32 devices in a mesh: row: 8 (over z, y), col: 4 (over x, core).
Axes of the slice: x: 2, y: 2, z: 4, core: 2. Of those that a mesh axis runs over, the one named last changes fastest.
Arguments:
- frames_in: bfloat16 [24000, 1024], P(('col', 'row')), may hold values from -6 to 6
- text_states: bfloat16 [1024, 1024], P(('col', 'row')), may hold values from -6 to 6
- self_query: bfloat16 [1024, 1024], P('row', 'col'), may hold values from -0.1875 to 0.1875
- self_key: bfloat16 [1024, 1024], P('row', 'col'), may hold values from -0.1875 to 0.1875
- self_value: bfloat16 [1024, 1024], P('row', 'col'), may hold values from -0.1875 to 0.1875
- self_output: bfloat16 [1024, 1024], P('row', 'col'), may hold values from -0.75 to 0.75
- cross_query: bfloat16 [1024, 1024], P('row', 'col'), may hold values from -0.1875 to 0.1875
- cross_key: bfloat16 [1024, 1024], P('row', 'col'), may hold values from -0.1875 to 0.1875
- cross_value: bfloat16 [1024, 1024], P('row', 'col'), may hold values from -0.1875 to 0.1875
- cross_output: bfloat16 [1024, 1024], P('row', 'col'), may hold values from -0.5 to 0.5
- up_weight: bfloat16 [1024, 4096], P('row', 'col'), may hold values from -0.1875 to 0.1875
- down_weight: bfloat16 [4096, 1024], P('row', 'col'), may hold values from -0.09375 to 0.09375
- first_gain: bfloat16 [1024], P(('row', 'col')), may hold values from 0.5 to 1.5
- first_bias: bfloat16 [1024], P(('row', 'col')), may hold values from -2.5 to 2.5
- second_gain: bfloat16 [1024], P(('row', 'col')), may hold values from 0.5 to 1.5
- second_bias: bfloat16 [1024], P(('row', 'col')), may hold values from -2.5 to 2.5
- third_gain: bfloat16 [1024], P(('row', 'col')), may hold values from 0.5 to 1.5
- third_bias: bfloat16 [1024], P(('row', 'col')), may hold values from -2.5 to 2.5
- cotangent: bfloat16 [24000, 1024], P(('col', 'row')), may hold values from -6 to 6
Outputs:
- layer_out: bfloat16 [24000, 1024], P(('col', 'row'))
- input_grad: float32 [24000, 1024], P(('col', 'row'))
- text_grad: float32 [1024, 1024], P(('col', 'row'))
- self_query_grad: float32 [1024, 1024], P('row', 'col')
- self_key_grad: float32 [1024, 1024], P('row', 'col')
- self_value_grad: float32 [1024, 1024], P('row', 'col')
- self_output_grad: float32 [1024, 1024], P('row', 'col')
- cross_query_grad: float32 [1024, 1024], P('row', 'col')
- cross_key_grad: float32 [1024, 1024], P('row', 'col')
- cross_value_grad: float32 [1024, 1024], P('row', 'col')
- cross_output_grad: float32 [1024, 1024], P('row', 'col')
- up_weight_grad: float32 [1024, 4096], P('row', 'col')
- down_weight_grad: float32 [4096, 1024], P('row', 'col')
- first_gain_grad: float32 [1024], P(('row', 'col'))
- first_bias_grad: float32 [1024], P(('row', 'col'))
- second_gain_grad: float32 [1024], P(('row', 'col'))
- second_bias_grad: float32 [1024], P(('row', 'col'))
- third_gain_grad: float32 [1024], P(('row', 'col'))
- third_bias_grad: float32 [1024], P(('row', 'col'))
The draws below stay inside these ranges and needn't reach their ends.
All inputs are finite; a program needn't handle non-finite values.
Results may differ from the reference program's by a relative error of at most 0.023.
Values may be sent and summed in bfloat16 or wider, within the bound.
A program may use at most 256 MiB of HBM per device.

```python
import jax
import jax.numpy as jnp
from jax import lax

D = 1024
HEADS = 16
HEAD_DIM = 64
FF = 4096
FRAMES = 1500
TEXT = 64
CLIPS = 16
TOKENS = 24000
TEXT_ROWS = 1024


def block_scale(key, extent, shards, low, top_value):
    factor_of = 1.0
    for axis_at, blocks in shards:
        heights = jax.random.uniform(jax.random.fold_in(jax.random.fold_in(key, 6), axis_at), (blocks,), jnp.float32, low / len(shards), top_value / len(shards))
        factor_of = factor_of * jnp.repeat(jnp.exp(heights), extent[axis_at] // blocks).reshape((-1,) + (1,) * (len(extent) - 1 - axis_at))
    return factor_of


def gaussian(stream_key, shape, deviation, limit, pieces=(), held_as=jnp.bfloat16):
    level = block_scale(stream_key, shape, pieces, -0.22, 0.18) if pieces else 1.0
    values = jax.random.normal(stream_key, shape, jnp.float32) * deviation * level
    return jnp.minimum(jnp.maximum(values, -limit), limit).astype(held_as)


def setup_inputs(seed: int = 0) -> dict:
    keys = jax.random.split(jax.random.key(seed), 20)
    return {
        "frames_in": gaussian(keys[0], (TOKENS, D), 1.0, 6.0, ((0, 32),)),
        "text_states": gaussian(keys[1], (TEXT_ROWS, D), 1.0, 6.0, ((0, 32),)),
        "self_query": gaussian(keys[2], (D, D), D ** -0.5, 0.1875, ((0, 8), (1, 4))),
        "self_key": gaussian(keys[3], (D, D), D ** -0.5, 0.1875, ((0, 8), (1, 4))),
        "self_value": gaussian(keys[4], (D, D), D ** -0.5, 0.1875, ((0, 8), (1, 4))),
        "self_output": gaussian(keys[5], (D, D), (D // 16) ** -0.5, 0.75, ((0, 8), (1, 4))),
        "cross_query": gaussian(keys[6], (D, D), D ** -0.5, 0.1875, ((0, 8), (1, 4))),
        "cross_key": gaussian(keys[7], (D, D), D ** -0.5, 0.1875, ((0, 8), (1, 4))),
        "cross_value": gaussian(keys[8], (D, D), D ** -0.5, 0.1875, ((0, 8), (1, 4))),
        "cross_output": gaussian(keys[9], (D, D), (D // 8) ** -0.5, 0.5, ((0, 8), (1, 4))),
        "up_weight": gaussian(keys[10], (D, FF), D ** -0.5, 0.1875, ((0, 8), (1, 4))),
        "down_weight": gaussian(keys[11], (FF, D), FF ** -0.5, 0.09375, ((0, 8), (1, 4))),
        "first_gain": jnp.clip(1.0 + 0.1 * jax.random.normal(keys[12], (D,), jnp.float32), 0.5, 1.5).astype(jnp.bfloat16),
        "first_bias": gaussian(keys[13], (D,), 0.3, 2.5, ((0, 32),)),
        "second_gain": jnp.clip(1.0 + 0.1 * jax.random.normal(keys[14], (D,), jnp.float32), 0.5, 1.5).astype(jnp.bfloat16),
        "second_bias": gaussian(keys[15], (D,), 0.3, 2.5, ((0, 32),)),
        "third_gain": jnp.clip(1.0 + 0.1 * jax.random.normal(keys[16], (D,), jnp.float32), 0.5, 1.5).astype(jnp.bfloat16),
        "third_bias": gaussian(keys[17], (D,), 0.3, 2.5, ((0, 32),)),
        "cotangent": gaussian(keys[18], (TOKENS, D), 1.0, 6.0, ((0, 32),)),
    }


@jax.custom_vjp
def low(v):
    return lax.optimization_barrier(v.astype(jnp.bfloat16)).astype(jnp.float32)

@jax.custom_vjp
def low_back(v):
    return v

def low_keep(v):
    return (low(v), None)

def low_pass(kept, grad):
    return (grad,)

def back_keep(v):
    return (v, None)

def back_low(kept, grad):
    return (low(grad),)
low.defvjp(low_keep, low_pass)
low_back.defvjp(back_keep, back_low)

def matmul(left, right):
    return jnp.dot(left, right, precision=lax.Precision.HIGHEST)

def layer_norm(values, norm_gain, norm_bias):
    center = values - lax.optimization_barrier(jnp.mean(values, axis=-1, keepdims=True))
    variance = lax.optimization_barrier(jnp.mean(center * center, axis=-1, keepdims=True))
    return center * lax.rsqrt(variance + 1e-05) * norm_gain + norm_bias

def softmax_rows(scores):
    highest = lax.optimization_barrier(jnp.max(scores, axis=-1, keepdims=True))
    powers = jnp.exp(scores - highest)
    return powers / lax.optimization_barrier(jnp.sum(powers, axis=-1, keepdims=True))

def attend(query_rows, key_rows, value_rows, causal):

    def one_head(operands):
        query_head, key_head, value_head = operands
        scores = low_back(matmul(query_head, key_head.T) * HEAD_DIM ** (-0.5))
        if causal:
            allowed = jnp.arange(scores.shape[0])[:, None] >= jnp.arange(scores.shape[1])[None, :]
            scores = jnp.where(allowed, scores, -1e+30)
        return matmul(low(softmax_rows(scores)), value_head)

    def by_heads(row_block):
        return row_block.reshape(row_block.shape[0], HEADS, HEAD_DIM).transpose(1, 0, 2)
    mixture = lax.map(jax.checkpoint(one_head), (by_heads(query_rows), by_heads(key_rows), by_heads(value_rows)))
    return mixture.transpose(1, 0, 2).reshape(query_rows.shape[0], HEADS * HEAD_DIM)

def forward(frames, text_clip, params):
    self_query, self_key, self_value, self_output, cross_query, cross_key, cross_value, cross_output, up_weight, down_weight, first_gain, first_bias, second_gain, second_bias, third_gain, third_bias = params
    hidden_one = low(layer_norm(frames, first_gain, first_bias))
    queries = low_back(low(matmul(hidden_one, self_query)))
    key_self = low_back(low(matmul(hidden_one, self_key)))
    value_self = low_back(low(matmul(hidden_one, self_value)))
    self_mix = low_back(low(attend(queries, key_self, value_self, True)))
    resid_one = frames + low_back(matmul(self_mix, self_output))
    hidden_two = low(layer_norm(resid_one, second_gain, second_bias))
    cross_q = low_back(low(matmul(hidden_two, cross_query)))
    text_k = low_back(low(matmul(text_clip, cross_key)))
    text_v = low_back(low(matmul(text_clip, cross_value)))
    cross_mix = low_back(low(attend(cross_q, text_k, text_v, False)))
    resid_two = resid_one + low_back(matmul(cross_mix, cross_output))
    hidden_three = low(layer_norm(resid_two, third_gain, third_bias))
    inner = low(jax.nn.gelu(low_back(matmul(hidden_three, up_weight)), approximate=False))
    return resid_two + low_back(matmul(inner, down_weight))

def reference(frames_in, text_states, self_query, self_key, self_value, self_output, cross_query, cross_key, cross_value, cross_output, up_weight, down_weight, first_gain, first_bias, second_gain, second_bias, third_gain, third_bias, cotangent):
    params = jax.tree.map(lambda array: array.astype(jnp.float32), (self_query, self_key, self_value, self_output, cross_query, cross_key, cross_value, cross_output, up_weight, down_weight, first_gain, first_bias, second_gain, second_bias, third_gain, third_bias))
    frames_all = frames_in.astype(jnp.float32).reshape(CLIPS, FRAMES, D)
    text_all = text_states.astype(jnp.float32).reshape(CLIPS, TEXT, D)
    cotan_all = cotangent.astype(jnp.float32).reshape(CLIPS, FRAMES, D)

    def per_clip(totals, inputs):
        frames, text_clip, cotan_clip = inputs
        result, pullback = jax.vjp(forward, frames, text_clip, params)
        frame_grad, text_part, param_grads = pullback(cotan_clip)
        totals = jax.tree.map(jnp.add, totals, param_grads)
        return (totals, (result.astype(jnp.bfloat16), frame_grad, text_part))
    zero_grads = jax.tree.map(jnp.zeros_like, params)
    totals, (layer_outs, frame_grads, text_grads) = lax.scan(per_clip, zero_grads, (frames_all, text_all, cotan_all))
    return (layer_outs.reshape(TOKENS, D), frame_grads.reshape(TOKENS, D), text_grads.reshape(TEXT_ROWS, D), totals[0], totals[1], totals[2], totals[3], totals[4], totals[5], totals[6], totals[7], totals[8], totals[9], totals[10], totals[11], totals[12], totals[13], totals[14], totals[15])
```

```python
import functools
from functools import partial

import jax
import jax.numpy as jnp
from jax import lax
from jax.experimental import pallas as pl
from jax.experimental.pallas import tpu as pltpu
from jax.sharding import PartitionSpec as P

HEADS = 16
HEAD_DIM = 64
FRAMES = 1500
TEXT = 64


def norm_forward(values, norm_gain, norm_bias):
    center = values - jnp.mean(values, axis=-1, keepdims=True)
    variance = jnp.mean(center * center, axis=-1, keepdims=True)
    return center * lax.rsqrt(variance + 1e-05) * norm_gain + norm_bias


def matmul(left, right):
    return jnp.dot(left, right, preferred_element_type=jnp.float32)


def by_transposed(left, right):
    return lax.dot_general(
        left, right, (((1,), (1,)), ((), ())), preferred_element_type=jnp.float32
    )


def over_tokens(left, right):
    return lax.dot_general(
        left, right, (((0,), (0,)), ((), ())), preferred_element_type=jnp.float32
    )


def collect(blocks):
    partly = (
        lax.all_gather(blocks[0], "col", axis=1, tiled=True),
        lax.all_gather(blocks[1], "col", axis=1, tiled=True),
        lax.all_gather(blocks[2], "col", axis=1, tiled=True),
        lax.all_gather(blocks[3], "col", axis=1, tiled=True),
        lax.all_gather(blocks[4], "col", axis=1, tiled=True),
        lax.all_gather(blocks[5], "col", axis=1, tiled=True),
        lax.all_gather(blocks[6], "col", axis=1, tiled=True),
        lax.all_gather(blocks[7], "col", axis=1, tiled=True),
        lax.all_gather(blocks[8], "col", axis=1, tiled=True),
        lax.all_gather(blocks[9], "col", axis=1, tiled=True),
        lax.all_gather(blocks[10], "col", axis=1, tiled=True),
    )
    return (
        lax.all_gather(partly[0], "row", axis=0, tiled=True),
        lax.all_gather(partly[1], "row", axis=0, tiled=True),
        lax.all_gather(partly[2], "row", axis=0, tiled=True),
        lax.all_gather(partly[3], "row", axis=0, tiled=True),
        lax.all_gather(partly[4], "row", axis=0, tiled=True),
        lax.all_gather(partly[5], "row", axis=0, tiled=True),
        lax.all_gather(partly[6], "row", axis=0, tiled=True),
        lax.all_gather(partly[7], "row", axis=0, tiled=True),
        lax.all_gather(partly[8], "row", axis=0, tiled=True),
        lax.all_gather(partly[9], "row", axis=0, tiled=True),
        lax.all_gather(partly[10], "row", axis=0, tiled=True),
    )


def spread(grads):
    partly = (
        lax.psum_scatter(
            grads[0].astype(jnp.bfloat16), "row", scatter_dimension=0, tiled=True
        ).astype(jnp.float32),
        lax.psum_scatter(
            grads[1].astype(jnp.bfloat16), "row", scatter_dimension=0, tiled=True
        ).astype(jnp.float32),
        lax.psum_scatter(
            grads[2].astype(jnp.bfloat16), "row", scatter_dimension=0, tiled=True
        ).astype(jnp.float32),
        lax.psum_scatter(
            grads[3].astype(jnp.bfloat16), "row", scatter_dimension=0, tiled=True
        ).astype(jnp.float32),
        lax.psum_scatter(
            grads[4].astype(jnp.bfloat16), "row", scatter_dimension=0, tiled=True
        ).astype(jnp.float32),
        lax.psum_scatter(
            grads[5].astype(jnp.bfloat16), "row", scatter_dimension=0, tiled=True
        ).astype(jnp.float32),
        lax.psum_scatter(
            grads[6].astype(jnp.bfloat16), "row", scatter_dimension=0, tiled=True
        ).astype(jnp.float32),
        lax.psum_scatter(
            grads[7].astype(jnp.bfloat16), "row", scatter_dimension=0, tiled=True
        ).astype(jnp.float32),
        lax.psum_scatter(
            grads[8].astype(jnp.bfloat16), "row", scatter_dimension=0, tiled=True
        ).astype(jnp.float32),
        lax.psum_scatter(
            grads[9].astype(jnp.bfloat16), "row", scatter_dimension=0, tiled=True
        ).astype(jnp.float32),
        lax.psum_scatter(
            grads[10].astype(jnp.bfloat16), "row", scatter_dimension=0, tiled=True
        ).astype(jnp.float32),
    )
    return (
        lax.psum_scatter(
            partly[0].astype(jnp.bfloat16), "col", scatter_dimension=1, tiled=True
        ).astype(jnp.float32),
        lax.psum_scatter(
            partly[1].astype(jnp.bfloat16), "col", scatter_dimension=1, tiled=True
        ).astype(jnp.float32),
        lax.psum_scatter(
            partly[2].astype(jnp.bfloat16), "col", scatter_dimension=1, tiled=True
        ).astype(jnp.float32),
        lax.psum_scatter(
            partly[3].astype(jnp.bfloat16), "col", scatter_dimension=1, tiled=True
        ).astype(jnp.float32),
        lax.psum_scatter(
            partly[4].astype(jnp.bfloat16), "col", scatter_dimension=1, tiled=True
        ).astype(jnp.float32),
        lax.psum_scatter(
            partly[5].astype(jnp.bfloat16), "col", scatter_dimension=1, tiled=True
        ).astype(jnp.float32),
        lax.psum_scatter(
            partly[6].astype(jnp.bfloat16), "col", scatter_dimension=1, tiled=True
        ).astype(jnp.float32),
        lax.psum_scatter(
            partly[7].astype(jnp.bfloat16), "col", scatter_dimension=1, tiled=True
        ).astype(jnp.float32),
        lax.psum_scatter(
            partly[8].astype(jnp.bfloat16), "col", scatter_dimension=1, tiled=True
        ).astype(jnp.float32),
        lax.psum_scatter(
            partly[9].astype(jnp.bfloat16), "col", scatter_dimension=1, tiled=True
        ).astype(jnp.float32),
        lax.psum_scatter(
            partly[10].astype(jnp.bfloat16), "col", scatter_dimension=1, tiled=True
        ).astype(jnp.float32),
    )


def heads_layout(stacked):
    return lax.all_to_all(stacked, "row", split_axis=1, concat_axis=0, tiled=True)


def tokens_layout(stacked):
    return lax.all_to_all(stacked, "row", split_axis=0, concat_axis=2, tiled=True)


def by_clips(arranged, start, count, length, heads_dev):
    section = arranged[:, start : start + count]
    return section.reshape(-1, length, heads_dev, HEAD_DIM)


def causal_scores(query_clip, key_clip, causal):
    scores = jnp.einsum(
        "qhd,khd->hqk", query_clip, key_clip, preferred_element_type=jnp.float32
    ) * HEAD_DIM ** (-0.5)
    if causal:
        allowed = jnp.arange(scores.shape[1])[:, None] >= jnp.arange(scores.shape[2])[None, :]
        scores = jnp.where(allowed, scores, -1e30)
    return scores


def attend_forward(query_clips, key_clips, value_clips, causal):

    def one_clip(operands):
        query_clip, key_clip, value_clip = operands
        scores = causal_scores(query_clip, key_clip, causal)
        highest = jnp.max(scores, axis=-1, keepdims=True)
        powers = jnp.exp(scores - highest)
        totals = jnp.sum(powers, axis=-1, keepdims=True)
        weights_low = (powers / totals).astype(jnp.bfloat16)
        mixture = jnp.einsum(
            "hqk,khd->qhd", weights_low, value_clip, preferred_element_type=jnp.float32
        )
        return (mixture.astype(jnp.bfloat16), (highest + jnp.log(totals))[..., 0])

    return lax.map(one_clip, (query_clips, key_clips, value_clips))


def attend_backward(query_clips, key_clips, value_clips, log_sums, grad_clips, causal):

    def one_clip(operands):
        query_clip, key_clip, value_clip, log_clip, grad_clip = operands
        scores = causal_scores(query_clip, key_clip, causal)
        probs_full = jnp.exp(scores - log_clip[..., None])
        grad_probs = jnp.einsum(
            "qhd,khd->hqk", grad_clip, value_clip, preferred_element_type=jnp.float32
        )
        grad_value = jnp.einsum(
            "hqk,qhd->khd",
            probs_full.astype(jnp.bfloat16),
            grad_clip,
            preferred_element_type=jnp.float32,
        )
        centered = grad_probs - jnp.sum(probs_full * grad_probs, axis=-1, keepdims=True)
        grad_scores = (probs_full * centered).astype(jnp.bfloat16)
        grad_query = jnp.einsum(
            "hqk,khd->qhd", grad_scores, key_clip, preferred_element_type=jnp.float32
        ) * HEAD_DIM ** (-0.5)
        grad_key = jnp.einsum(
            "hqk,qhd->khd", grad_scores, query_clip, preferred_element_type=jnp.float32
        ) * HEAD_DIM ** (-0.5)
        return (
            grad_query.astype(jnp.bfloat16),
            grad_key.astype(jnp.bfloat16),
            grad_value.astype(jnp.bfloat16),
        )

    return lax.map(one_clip, (query_clips, key_clips, value_clips, log_sums, grad_clips))


def general(
    frames_in,
    text_states,
    self_query,
    self_key,
    self_value,
    self_output,
    cross_query,
    cross_key,
    cross_value,
    cross_output,
    up_weight,
    down_weight,
    first_gain,
    first_bias,
    second_gain,
    second_bias,
    third_gain,
    third_bias,
    cotangent,
):
    row_count = lax.axis_size("row")
    col_count = lax.axis_size("col")
    heads_dev = HEADS // row_count
    width_dev = heads_dev * HEAD_DIM
    tok_rows = frames_in.shape[0]
    text_rows = text_states.shape[0]
    piece_len = first_gain.shape[0]
    gain_block = jnp.stack(
        [first_gain, first_bias, second_gain, second_bias, third_gain, third_bias]
    ).reshape(1, 6 * piece_len)
    param_blocks = (
        self_query,
        self_key,
        self_value,
        self_output,
        cross_query,
        cross_key,
        cross_value,
        cross_output,
        up_weight,
        down_weight,
        gain_block,
    )

    def unpack_gains(gathered_gains):
        arranged = gathered_gains.reshape(row_count, col_count, 6, piece_len).transpose(2, 0, 1, 3)
        return arranged.reshape(6, row_count * col_count * piece_len).astype(jnp.float32)

    gathered = collect(param_blocks)
    (
        query_self,
        key_self,
        value_self,
        out_self,
        query_cross,
        key_cross,
        value_cross,
        out_cross,
        up_full,
        down_full,
    ) = gathered[:10]
    norm_params = unpack_gains(gathered[10])
    frames = frames_in.astype(jnp.float32)
    hidden_one = norm_forward(frames, norm_params[0], norm_params[1]).astype(jnp.bfloat16)
    self_q = matmul(hidden_one, query_self).astype(jnp.bfloat16)
    self_k = matmul(hidden_one, key_self).astype(jnp.bfloat16)
    self_v = matmul(hidden_one, value_self).astype(jnp.bfloat16)
    text_k = matmul(text_states, key_cross).astype(jnp.bfloat16)
    text_v = matmul(text_states, value_cross).astype(jnp.bfloat16)
    sent_rows = 3 * tok_rows + 2 * text_rows
    arranged = heads_layout(jnp.concatenate([self_q, self_k, self_v, text_k, text_v], axis=0))
    arranged = arranged.reshape(row_count, sent_rows, width_dev)
    query_clips = by_clips(arranged, 0, tok_rows, FRAMES, heads_dev)
    key_clips = by_clips(arranged, tok_rows, tok_rows, FRAMES, heads_dev)
    value_clips = by_clips(arranged, 2 * tok_rows, tok_rows, FRAMES, heads_dev)
    text_keys = by_clips(arranged, 3 * tok_rows, text_rows, TEXT, heads_dev)
    text_values = by_clips(arranged, 3 * tok_rows + text_rows, text_rows, TEXT, heads_dev)
    self_clips, self_logs = attend_forward(query_clips, key_clips, value_clips, True)
    self_mix = tokens_layout(self_clips.reshape(row_count, tok_rows, width_dev))[0]
    resid_one = frames + matmul(self_mix, out_self)
    hidden_two = norm_forward(resid_one, norm_params[2], norm_params[3]).astype(jnp.bfloat16)
    cross_q = matmul(hidden_two, query_cross).astype(jnp.bfloat16)
    cross_arranged = heads_layout(cross_q).reshape(row_count, tok_rows, width_dev)
    cross_queries = by_clips(cross_arranged, 0, tok_rows, FRAMES, heads_dev)
    cross_clips, cross_logs = attend_forward(cross_queries, text_keys, text_values, False)
    cross_mix = tokens_layout(cross_clips.reshape(row_count, tok_rows, width_dev))[0]
    resid_two = resid_one + matmul(cross_mix, out_cross)
    hidden_three = norm_forward(resid_two, norm_params[4], norm_params[5]).astype(jnp.bfloat16)
    pre_act = matmul(hidden_three, up_full)
    inner = jax.nn.gelu(pre_act, approximate=False).astype(jnp.bfloat16)
    layer_out = (resid_two + matmul(inner, down_full)).astype(jnp.bfloat16)
    gathered = collect(param_blocks)
    (
        query_self,
        key_self,
        value_self,
        out_self,
        query_cross,
        key_cross,
        value_cross,
        out_cross,
        up_full,
        down_full,
    ) = gathered[:10]
    norm_params = unpack_gains(gathered[10])
    cotan_full = cotangent.astype(jnp.float32)
    down_grad = over_tokens(inner, cotangent)
    grad_inner = by_transposed(cotangent, down_full)
    unused_gelu, gelu_pull = jax.vjp(partial(jax.nn.gelu, approximate=False), pre_act)
    grad_pre = gelu_pull(grad_inner)[0].astype(jnp.bfloat16)
    up_grad = over_tokens(hidden_three, grad_pre)
    grad_three = by_transposed(grad_pre, up_full)
    unused_three, pull_three = jax.vjp(norm_forward, resid_two, norm_params[4], norm_params[5])
    through_three, third_gain_part, third_bias_part = pull_three(grad_three)
    grad_resid_two = cotan_full + through_three
    grad_cross = grad_resid_two.astype(jnp.bfloat16)
    cross_out_grad = over_tokens(cross_mix, grad_cross)
    grad_cross_mix = by_transposed(grad_cross, out_cross).astype(jnp.bfloat16)
    grad_cross_arr = heads_layout(grad_cross_mix).reshape(row_count, tok_rows, width_dev)
    grad_cross_clips = by_clips(grad_cross_arr, 0, tok_rows, FRAMES, heads_dev)
    cq_clips, tk_clips, tv_clips = attend_backward(
        cross_queries, text_keys, text_values, cross_logs, grad_cross_clips, False
    )
    back_cross = jnp.concatenate(
        [
            cq_clips.reshape(row_count, tok_rows, width_dev),
            tk_clips.reshape(row_count, text_rows, width_dev),
            tv_clips.reshape(row_count, text_rows, width_dev),
        ],
        axis=1,
    )
    back_cross = tokens_layout(back_cross)[0]
    grad_cross_q = back_cross[:tok_rows]
    grad_text_k = back_cross[tok_rows : tok_rows + text_rows]
    grad_text_v = back_cross[tok_rows + text_rows :]
    cross_query_part = over_tokens(hidden_two, grad_cross_q)
    cross_key_part = over_tokens(text_states, grad_text_k)
    cross_value_part = over_tokens(text_states, grad_text_v)
    text_grad = by_transposed(grad_text_k, key_cross) + by_transposed(grad_text_v, value_cross)
    grad_two = by_transposed(grad_cross_q, query_cross)
    unused_two, pull_two = jax.vjp(norm_forward, resid_one, norm_params[2], norm_params[3])
    through_two, second_gain_part, second_bias_part = pull_two(grad_two)
    grad_resid_one = grad_resid_two + through_two
    grad_self = grad_resid_one.astype(jnp.bfloat16)
    self_out_grad = over_tokens(self_mix, grad_self)
    grad_self_mix = by_transposed(grad_self, out_self).astype(jnp.bfloat16)
    grad_self_arr = heads_layout(grad_self_mix).reshape(row_count, tok_rows, width_dev)
    grad_self_clips = by_clips(grad_self_arr, 0, tok_rows, FRAMES, heads_dev)
    sq_clips, sk_clips, sv_clips = attend_backward(
        query_clips, key_clips, value_clips, self_logs, grad_self_clips, True
    )
    back_self = jnp.concatenate(
        [
            sq_clips.reshape(row_count, tok_rows, width_dev),
            sk_clips.reshape(row_count, tok_rows, width_dev),
            sv_clips.reshape(row_count, tok_rows, width_dev),
        ],
        axis=1,
    )
    back_self = tokens_layout(back_self)[0]
    grad_self_q = back_self[:tok_rows]
    grad_self_k = back_self[tok_rows : 2 * tok_rows]
    grad_self_v = back_self[2 * tok_rows :]
    self_query_part = over_tokens(hidden_one, grad_self_q)
    self_key_part = over_tokens(hidden_one, grad_self_k)
    self_value_part = over_tokens(hidden_one, grad_self_v)
    grad_one = (
        by_transposed(grad_self_q, query_self)
        + by_transposed(grad_self_k, key_self)
        + by_transposed(grad_self_v, value_self)
    )
    unused_one, pull_one = jax.vjp(norm_forward, frames, norm_params[0], norm_params[1])
    through_one, first_gain_part, first_bias_part = pull_one(grad_one)
    input_grad = grad_resid_one + through_one
    norm_grads = jnp.stack(
        [
            first_gain_part,
            first_bias_part,
            second_gain_part,
            second_bias_part,
            third_gain_part,
            third_bias_part,
        ]
    )
    norm_grads = norm_grads.reshape(6, row_count, col_count, piece_len).transpose(1, 2, 0, 3)
    norm_grads = norm_grads.reshape(row_count, col_count * 6 * piece_len)
    summed = spread(
        (
            self_query_part,
            self_key_part,
            self_value_part,
            self_out_grad,
            cross_query_part,
            cross_key_part,
            cross_value_part,
            cross_out_grad,
            up_grad,
            down_grad,
            norm_grads,
        )
    )
    norm_parts = summed[10].reshape(6, piece_len)
    return (
        layer_out,
        input_grad,
        text_grad,
        summed[0],
        summed[1],
        summed[2],
        summed[3],
        summed[4],
        summed[5],
        summed[6],
        summed[7],
        summed[8],
        summed[9],
        norm_parts[0],
        norm_parts[1],
        norm_parts[2],
        norm_parts[3],
        norm_parts[4],
        norm_parts[5],
    )


NT=(((1,),(1,)),((),())); NN=(((1,),(0,)),((),())); TN=(((0,),(0,)),((),()))
def dg(a,b,dims): return lax.dot_general(a,b,dims,preferred_element_type=jnp.float32)

def attend_kernel(causal,tile,q_ref,k_ref,v_ref,o_ref,lse_ref):
    pair=pl.program_id(0)
    rows=q_ref.shape[0]
    low=lax.broadcasted_iota(jnp.int32,(1,128),1)<HEAD_DIM
    lane=lax.broadcasted_iota(jnp.int32,(1,128),1)
    value=v_ref[...]
    ones=jnp.ones_like(value)
    @pl.when(pair==0)
    def _(): lse_ref[...]=jnp.zeros_like(lse_ref)
    for start in range(0,rows,tile):
        n=min(tile,rows-start)
        q=q_ref[start:start+n,:]*jnp.bfloat16(HEAD_DIM**-0.5)
        mixed=[]; sums=[]
        lse=lse_ref[start:start+n,:]
        for h in range(2):
            mine=low if h==0 else jnp.logical_not(low)
            qh=jnp.where(mine,q,jnp.bfloat16(0))
            vh=jnp.where(mine,value,ones)
            if causal:
                spans=([(0,start)] if start else [])+[(start,n)]
            else: spans=[(0,k_ref.shape[0])]
            scores=[]
            for at,length in spans:
                s=dg(qh,k_ref[at:at+length,:],NT)
                if causal and at==start:
                    ok=lax.broadcasted_iota(jnp.int32,s.shape,0)>=lax.broadcasted_iota(jnp.int32,s.shape,1)
                    s=jnp.where(ok,s,-1e30)
                scores.append(s)
            top=functools.reduce(jnp.maximum,[jnp.max(s,axis=1,keepdims=True) for s in scores])
            out=None
            for (at,length),s in zip(spans,scores):
                p=jnp.exp(s-top).astype(jnp.bfloat16)
                part=dg(p,vh[at:at+length,:],NN)
                out=part if out is None else out+part
            total=out[:,HEAD_DIM:HEAD_DIM+1] if h==0 else out[:,0:1]
            mixed.append(out/total)
            lse=jnp.where(lane==2*pair+h,top+jnp.log(total),lse)
        lse_ref[start:start+n,:]=lse
        o_ref[start:start+n,:]=jnp.where(low,mixed[0],mixed[1]).astype(o_ref.dtype)

def attend(q,k,v,causal,out_dtype,tile=256):
    rows,width=q.shape; keys=k.shape[0]
    return pl.pallas_call(functools.partial(attend_kernel,causal,tile),grid=(width//128,),
        in_specs=[pl.BlockSpec((rows,128),lambda i:(0,i)),pl.BlockSpec((keys,128),lambda i:(0,i)),pl.BlockSpec((keys,128),lambda i:(0,i))],
        out_specs=[pl.BlockSpec((rows,128),lambda i:(0,i)),pl.BlockSpec((rows,128),lambda i:(0,0))],
        out_shape=[jax.ShapeDtypeStruct((rows,width),out_dtype),jax.ShapeDtypeStruct((rows,128),jnp.float32)],
        compiler_params=pltpu.CompilerParams(vmem_limit_bytes=40<<20),
        cost_estimate=pl.CostEstimate(flops=4*rows*keys*width,bytes_accessed=8*rows*width,transcendentals=rows*keys*width//64))(q,k,v)

def attend_back_kernel(causal,tile,q_ref,k_ref,v_ref,do_ref,st_ref,dq_ref,dk_ref,dv_ref,acc):
    rows=q_ref.shape[0]; keys=k_ref.shape[0]
    low=lax.broadcasted_iota(jnp.int32,(1,128),1)<HEAD_DIM
    acc[...]=jnp.zeros_like(acc)
    for start in range(0,keys,tile):
        n=min(tile,keys-start)
        k=k_ref[start:start+n,:]*jnp.bfloat16(HEAD_DIM**-0.5)
        v=v_ref[start:start+n,:]
        spans=[(0,rows)]
        if causal: spans=[(start,n)]+([(start+n,rows-start-n)] if start+n<rows else [])
        dks=[];dvs=[]
        for h in range(2):
            mine=low if h==0 else jnp.logical_not(low)
            kh=jnp.where(mine,k,jnp.bfloat16(0)); vh=jnp.where(mine,v,jnp.bfloat16(0))
            dk=dv=None
            for at,length in spans:
                qs=q_ref[at:at+length,:]; do=do_ref[at:at+length,:]
                s=dg(kh,qs,NT)
                p=jnp.exp(s-st_ref[0,h:h+1,at:at+length])
                if causal and at==start:
                    ok=lax.broadcasted_iota(jnp.int32,s.shape,0)<=lax.broadcasted_iota(jnp.int32,s.shape,1)
                    p=jnp.where(ok,p,0.0)
                dp=dg(vh,do,NT)
                ds=(p*(dp-st_ref[0,2+h:3+h,at:at+length])).astype(jnp.bfloat16)
                a=dg(p.astype(jnp.bfloat16),do,NN); b=dg(ds,qs,NN)
                dv=a if dv is None else dv+a
                dk=b if dk is None else dk+b
                acc[at:at+length,:]+=dg(ds,kh,TN)
            dks.append(dk);dvs.append(dv)
        dk_ref[start:start+n,:]=(jnp.where(low,dks[0],dks[1])*HEAD_DIM**-0.5).astype(dk_ref.dtype)
        dv_ref[start:start+n,:]=jnp.where(low,dvs[0],dvs[1]).astype(dv_ref.dtype)
    dq_ref[...]=acc[...].astype(dq_ref.dtype)

def attend_back(q,k,v,do,stats,causal,out_dtype,tile=256):
    rows,width=q.shape; keys=k.shape[0]
    bq=pl.BlockSpec((rows,128),lambda i:(0,i)); bk=pl.BlockSpec((keys,128),lambda i:(0,i))
    return pl.pallas_call(functools.partial(attend_back_kernel,causal,tile),grid=(width//128,),
        in_specs=[bq,bk,bk,bq,pl.BlockSpec((1,4,rows),lambda i:(i,0,0))],out_specs=[bq,bk,bk],
        out_shape=[jax.ShapeDtypeStruct((rows,width),out_dtype),jax.ShapeDtypeStruct((keys,width),out_dtype),jax.ShapeDtypeStruct((keys,width),out_dtype)],
        scratch_shapes=[pltpu.VMEM((rows,128),jnp.float32)],
        compiler_params=pltpu.CompilerParams(vmem_limit_bytes=40<<20),
        cost_estimate=pl.CostEstimate(flops=10*rows*keys*width,bytes_accessed=16*rows*width,transcendentals=rows*keys*width//64))(q,k,v,do,stats)

def feed_kernel(h_ref,cot_ref,res_ref,up_ref,down_ref,out_ref,g_ref,dup_ref,ddown_ref,acc):
    i=pl.program_id(0)
    @pl.when(i==0)
    def _():
        acc[...]=res_ref[...]
        g_ref[...]=jnp.zeros_like(g_ref)
    h=h_ref[...]; cot=cot_ref[...]
    pre=dg(h,up_ref[...],NN)
    cdf=0.5*(1.0+lax.erf(pre*0.7071067811865476))
    inner=(pre*cdf).astype(jnp.bfloat16)
    acc[...]+=dg(inner,down_ref[...],NN)
    ddown_ref[...]=dg(inner,cot,TN).astype(ddown_ref.dtype)
    slope=cdf+pre*(jnp.exp(-0.5*pre*pre)*0.3989422804014327)
    gpre=(dg(cot,down_ref[...],NT)*slope).astype(jnp.bfloat16)
    dup_ref[...]=dg(h,gpre,TN).astype(dup_ref.dtype)
    g_ref[...]+=dg(gpre,up_ref[...],NT)
    @pl.when(i==pl.num_programs(0)-1)
    def _(): out_ref[...]=acc[...].astype(out_ref.dtype)

def feed(h,cot,res,up,down,chunk=512):
    rows,d=h.shape; ff=up.shape[1]
    whole=pl.BlockSpec((rows,d),lambda i:(0,0))
    return pl.pallas_call(feed_kernel,grid=(ff//chunk,),
        in_specs=[whole,whole,whole,pl.BlockSpec((d,chunk),lambda i:(0,i)),pl.BlockSpec((chunk,d),lambda i:(i,0))],
        out_specs=[whole,whole,pl.BlockSpec((d,chunk),lambda i:(0,i)),pl.BlockSpec((chunk,d),lambda i:(i,0))],
        out_shape=[jax.ShapeDtypeStruct((rows,d),jnp.bfloat16),jax.ShapeDtypeStruct((rows,d),jnp.float32),jax.ShapeDtypeStruct((d,ff),jnp.bfloat16),jax.ShapeDtypeStruct((ff,d),jnp.bfloat16)],
        scratch_shapes=[pltpu.VMEM((rows,d),jnp.float32)],
        compiler_params=pltpu.CompilerParams(vmem_limit_bytes=56<<20),
        cost_estimate=pl.CostEstimate(flops=12*rows*d*ff,bytes_accessed=8*d*ff+16*rows*d,transcendentals=2*rows*ff))(h,cot,res,up,down)


MESH = pl.DeviceIdType.MESH
ORDERS = ("xzy", "yzx", "xzy", "yzx", "zxy", "zyx")


class Place:
    def __init__(self):
        row, col = lax.axis_index("row"), lax.axis_index("col")
        self.z, self.y, self.x, self.k = row // 2, row % 2, col // 2, col % 2
        self.along = lax.axis_size("row") // 2

    def device(self, dz=0, y=False, x=False, k=False):
        other_y = 1 - self.y if y else self.y
        other_x = 1 - self.x if x else self.x
        other_k = 1 - self.k if k else self.k
        return ((self.z + dz) * 2 + other_y, other_x * 2 + other_k)

    def across(self, axis):
        return self.device(y=axis == "y", x=axis == "x", k=axis == "k")

    def greet(self):
        barrier = pltpu.get_barrier_semaphore()
        for axis in "xyk":
            pl.semaphore_signal(barrier, inc=1, device_id=self.across(axis), device_id_type=MESH)

        @pl.when(self.z > 0)
        def _():
            pl.semaphore_signal(barrier, inc=1, device_id=self.device(dz=-1), device_id_type=MESH)

        @pl.when(self.z + 1 < self.along)
        def _():
            pl.semaphore_signal(barrier, inc=1, device_id=self.device(dz=1), device_id_type=MESH)

        below = jnp.where(self.z > 0, 1, 0)
        above = jnp.where(self.z + 1 < self.along, 1, 0)
        pl.semaphore_wait(barrier, 3 + below + above)


def when(condition, run):
    if condition is None:
        run()
    else:
        pl.when(condition)(run)


class Gather:
    def __init__(self, place, block, full, strip, order, send, recv):
        self.place, self.block, self.full, self.strip = place, block, full, strip
        turn = order.index("z")
        self.before, self.after = order[:turn], order[turn + 1 :]
        self.send, self.recv, self.used, self.sent, self.started = send, recv, 0, 0, []

    def region(self, z, y, x):
        part, start, count = self.strip
        column = (x * 2 + self.place.k) * self.block.shape[-1] + start
        return self.full.at[z, y, part, :, pl.ds(pl.multiple_of(column, 128), count)]

    def held(self, done, z):
        y = slice(None) if "y" in done else self.place.y
        return [self.region(z, y, x) for x in (range(2) if "x" in done else [self.place.x])]

    def pairs(self, done, z, first):
        if first:
            part, start, count = self.strip
            place = self.place
            return [(self.block.at[part, :, pl.ds(start, count)], self.region(place.z, place.y, place.x))]
        return [(region, region) for region in self.held(done, z)]

    def semaphore(self):
        self.used += 2
        return self.used - 2

    def copies(self, device, pairs, semaphore, send=0):
        return [
            pltpu.make_async_remote_copy(
                src_ref=source, dst_ref=target, send_sem=self.send.at[send + at],
                recv_sem=self.recv.at[semaphore + at], device_id=device, device_id_type=MESH)
            for at, (source, target) in enumerate(pairs)
        ]

    def start(self, device, pairs, condition, semaphore):
        copies = self.copies(device, pairs, semaphore, self.sent)
        self.sent += len(copies)
        when(condition, lambda: [copy.start() for copy in copies] and None)
        self.started.append((condition, copies))
        return condition, copies

    def arrive(self, sent):
        condition, copies = sent
        when(condition, lambda: [copy.wait_recv() for copy in copies] and None)

    def stages(self):
        place, along = self.place, self.place.along
        done = []
        for axis in self.before:
            sent = self.start(place.across(axis), self.pairs(done, place.z, not done), None, self.semaphore())
            yield
            self.arrive(sent)
            done.append(axis)
        first = not done
        from_left = [self.semaphore() for _ in range(along - 1)]
        from_right = [self.semaphore() for _ in range(along - 1)]

        def pass_on(turn, step):
            axes = done + list(self.after[:turn])
            device = place.across(self.after[turn])
            if step == 0:
                return turn, step, [self.start(device, self.pairs(axes, place.z, not axes), None, self.semaphore())]
            return turn, step, [
                self.start(device, self.pairs(axes, z, False), (z >= 0) & (z < along), self.semaphore())
                for z in (place.z - step, place.z + step)
            ]

        def step_out(step):
            left, right = place.z - (step - 1), place.z + (step - 1)
            self.start(place.device(dz=1), self.pairs(done, left, first and step == 1),
                       (left >= 0) & (place.z + 1 < along), from_left[step - 1])
            self.start(place.device(dz=-1), self.pairs(done, right, first and step == 1),
                       (right < along) & (place.z > 0), from_right[step - 1])

        def step_in(step):
            for z, semaphore in ((place.z - step, from_left), (place.z + step, from_right)):
                copies = self.copies(place.across("k"), self.pairs(done, z, False), semaphore[step - 1])
                self.arrive(((z >= 0) & (z < along), copies))

        step_out(1)
        waiting = [pass_on(0, 0)] if self.after else []
        for step in range(1, along + len(self.after)):
            yield
            if step < along:
                step_in(step)
                if step + 1 < along:
                    step_out(step + 1)
            following = []
            for turn, at, sent in waiting:
                for one in sent:
                    self.arrive(one)
                if turn + 1 < len(self.after):
                    following.append(pass_on(turn + 1, at))
            if self.after and step < along:
                following.append(pass_on(0, step))
            waiting = following
        everything = [self.region(slice(None), slice(None), x) for x in range(2)]
        sent = self.start(place.across("k"), [(r, r) for r in everything], None, self.semaphore())
        yield
        self.arrive(sent)

    def finish(self):
        for condition, copies in self.started:
            when(condition, lambda copies=copies: [copy.wait_send() for copy in copies] and None)


def gather_kernel(units, count, *refs):
    blocks, fulls = refs[:count], refs[count : 2 * count]
    send, recv, local_sem = refs[2 * count :]
    place = Place()
    place.greet()
    own = []
    for at, (block, full) in enumerate(zip(blocks, fulls)):
        width = block.shape[-1]
        columns = pl.ds(pl.multiple_of((place.x * 2 + place.k) * width, 128), width)
        copy = pltpu.make_async_copy(block, full.at[place.z, place.y, :, :, columns], local_sem.at[at])
        copy.start()
        own.append(copy)
    gathers = [
        Gather(place, blocks[which], fulls[which], strip, order, send.at[at], recv.at[at])
        for at, (which, strip, order) in enumerate(units)
    ]
    running = [gather.stages() for gather in gathers]
    while running:
        running = [stages for stages in running if next(stages, running) is not running]
        while own:
            own.pop().wait()
    for gather in gathers:
        gather.finish()


def gather_units(blocks, least):
    strips = []
    for which, block in enumerate(blocks):
        wide = min(least, block.shape[-1])
        for part in range(block.shape[0]):
            for start in range(0, block.shape[-1], wide):
                strips.append((which, (part, start, wide)))
    return [strip + (ORDERS[at % len(ORDERS)],) for at, strip in enumerate(strips)]


def gather_blocks(blocks, collective_id, least):
    along, cols = lax.axis_size("row") // 2, lax.axis_size("col")
    units = gather_units(blocks, least)
    count = len(blocks)
    anywhere = pl.BlockSpec(memory_space=pl.ANY)
    moved = sum(block.size for block in blocks) * 2 * along * 2 * cols
    return pl.pallas_call(
        functools.partial(gather_kernel, units, count),
        out_shape=[
            jax.ShapeDtypeStruct((along, 2) + b.shape[:2] + (cols * b.shape[2],), b.dtype) for b in blocks
        ],
        in_specs=[anywhere] * count,
        out_specs=[anywhere] * count,
        scratch_shapes=[
            pltpu.SemaphoreType.DMA((len(units), 8 * along)),
            pltpu.SemaphoreType.DMA((len(units), 12 * along)),
            pltpu.SemaphoreType.DMA((count,)),
        ],
        compiler_params=pltpu.CompilerParams(collective_id=collective_id, has_side_effects=True),
        cost_estimate=pl.CostEstimate(flops=0, bytes_accessed=2 * moved, transcendentals=0),
    )(*blocks)


class Scatter:
    def __init__(self, place, grad, out, strip, width, order, slots, send, recv, local):
        self.place, self.grad, self.out, self.strip, self.width = place, grad, out, strip, width
        self.order = order[::-1]
        self.slots, self.send, self.recv, self.local = slots, send, recv, local
        self.sent, self.used, self.started = 0, 0, []

    def columns(self, x, k):
        return pl.ds(pl.multiple_of((x * 2 + k) * self.width + self.strip[1], 128), self.strip[2])


def fast(
    frames_in, text_states, self_query, self_key, self_value, self_output, cross_query, cross_key, cross_value, cross_output,
    up_weight, down_weight, first_gain, first_bias, second_gain, second_bias, third_gain, third_bias, cotangent,
):
    row = lax.axis_index("row")
    rows, width = frames_in.shape
    half = width // 2
    piece = first_gain.shape[0]
    block_rows, block_cols = self_query.shape
    back = row % 2
    pairs = lax.axis_size("row") // 2
    forth_perm = [(2 * i, 2 * i + 1) for i in range(pairs)]
    back_perm = [(2 * i + 1, 2 * i) for i in range(pairs)]
    swap = forth_perm + back_perm

    def forth(array):
        return lax.ppermute(array, "row", forth_perm)

    def home(array):
        return lax.ppermute(array, "row", back_perm)

    def by_side(first, second):
        return jnp.where(back == 0, first, second)

    gains = jnp.zeros((1, 16, 128), jnp.bfloat16)
    gains = gains.at[0, :6, :piece].set(
        jnp.stack([first_gain, first_bias, second_gain, second_bias, third_gain, third_bias])
    )

    def small(block):
        return block.reshape(1, block_rows, block_cols)

    def flat(array):
        return array.reshape(-1, array.shape[-1])

    early = gather_blocks([small(self_query), small(self_key), small(self_value), gains], 1, 128)
    query_self, key_self, value_self = [flat(w) for w in early[:3]]
    late = gather_blocks(
        [small(self_output), small(cross_query), small(cross_key), small(cross_value), small(cross_output),
         up_weight.reshape(1, *up_weight.shape), down_weight.reshape(-1, block_rows, block_cols)], 2, 256)
    out_self, query_cross, key_cross, value_cross, out_cross, up_full, down_full = [flat(w) for w in late]
    norm_params = early[3].reshape(pairs * 2, 16, -1, 128)[:, :6, :, :piece].transpose(1, 0, 2, 3)
    norm_params = norm_params.reshape(6, width).astype(jnp.float32)

    frames = frames_in.astype(jnp.float32)
    hidden_one = norm_forward(frames, norm_params[0], norm_params[1]).astype(jnp.bfloat16)
    self_k = matmul(hidden_one, key_self).astype(jnp.bfloat16)
    self_v = matmul(hidden_one, value_self).astype(jnp.bfloat16)
    self_q = matmul(hidden_one, query_self).astype(jnp.bfloat16)
    sent_k, sent_v, sent_q = forth(self_k[:, :half]), forth(self_v[:, :half]), home(self_q[:, half:])
    near_mix, near_logs = attend(self_q, self_k, self_v, True, jnp.float32)
    far_q = by_side(sent_q, self_q[:, :half])
    far_k = by_side(self_k[:, half:], sent_k)
    far_v = by_side(self_v[:, half:], sent_v)
    far_mix, far_logs = attend(far_q, far_k, far_v, False, jnp.bfloat16)
    half_heads = half // HEAD_DIM
    far_logs = far_logs[:, :half_heads]
    near_logs = near_logs[:, : 2 * half_heads]
    far_mix = jnp.concatenate([far_mix, forth(far_mix)], axis=1)
    far_logs = by_side(-1e30, jnp.concatenate([far_logs, forth(far_logs)], axis=1))
    highest = jnp.maximum(near_logs, far_logs)
    self_logs = highest + jnp.log(jnp.exp(near_logs - highest) + jnp.exp(far_logs - highest))

    def per_feature(weights):
        return jnp.repeat(weights, HEAD_DIM, axis=1)

    self_mix = (
        near_mix * per_feature(jnp.exp(near_logs - self_logs))
        + by_side(0.0, far_mix.astype(jnp.float32)) * per_feature(jnp.exp(far_logs - self_logs))
    ).astype(jnp.bfloat16)
    resid_one = frames + matmul(self_mix, out_self)
    hidden_two = norm_forward(resid_one, norm_params[2], norm_params[3]).astype(jnp.bfloat16)
    cross_q = matmul(hidden_two, query_cross).astype(jnp.bfloat16)
    other_text = lax.ppermute(text_states, "row", swap)
    clip_text = by_side(
        jnp.concatenate([text_states, other_text]), jnp.concatenate([other_text, text_states])
    )
    text_k = matmul(clip_text, key_cross).astype(jnp.bfloat16)
    text_v = matmul(clip_text, value_cross).astype(jnp.bfloat16)
    cross_mix, cross_logs = attend(cross_q, text_k, text_v, False, jnp.bfloat16)
    cross_logs = cross_logs[:, : 2 * half_heads]
    resid_two = resid_one + matmul(cross_mix, out_cross)
    hidden_three = norm_forward(resid_two, norm_params[4], norm_params[5]).astype(jnp.bfloat16)
    layer_out, grad_three, up_grad, down_grad = feed(hidden_three, cotangent, resid_two, up_full, down_full)

    def stats_of(logs, mix, grad):
        products = mix.astype(jnp.float32) * grad.astype(jnp.float32)
        dots = jnp.sum(products.reshape(rows, -1, HEAD_DIM), axis=-1)
        both = jnp.stack([logs.T.reshape(-1, 2, rows), dots.T.reshape(-1, 2, rows)], axis=1)
        return both.reshape(-1, 4, rows)

    cotan_full = cotangent.astype(jnp.float32)
    unused_three, pull_three = jax.vjp(norm_forward, resid_two, norm_params[4], norm_params[5])
    through_three, third_gain_part, third_bias_part = pull_three(grad_three)
    grad_resid_two = cotan_full + through_three
    grad_cross = grad_resid_two.astype(jnp.bfloat16)
    cross_out_grad = over_tokens(cross_mix, grad_cross)
    grad_cross_mix = by_transposed(grad_cross, out_cross).astype(jnp.bfloat16)
    grad_cross_q, text_k_part, text_v_part = attend_back(
        cross_q, text_k, text_v, grad_cross_mix, stats_of(cross_logs, cross_mix, grad_cross_mix), False, jnp.bfloat16)
    text_rows = text_states.shape[0]
    text_parts = jnp.concatenate([text_k_part, text_v_part], axis=1)
    given = lax.ppermute(by_side(text_parts[text_rows:], text_parts[:text_rows]), "row", swap)
    kept = by_side(text_parts[:text_rows], text_parts[text_rows:])
    text_parts = (kept.astype(jnp.float32) + given.astype(jnp.float32)).astype(jnp.bfloat16)
    grad_text_k, grad_text_v = text_parts[:, :width], text_parts[:, width:]
    cross_query_part = over_tokens(hidden_two, grad_cross_q)
    cross_key_part = over_tokens(text_states, grad_text_k)
    cross_value_part = over_tokens(text_states, grad_text_v)
    text_grad = by_transposed(grad_text_k, key_cross) + by_transposed(grad_text_v, value_cross)
    grad_two = by_transposed(grad_cross_q, query_cross)
    unused_two, pull_two = jax.vjp(norm_forward, resid_one, norm_params[2], norm_params[3])
    through_two, second_gain_part, second_bias_part = pull_two(grad_two)
    grad_resid_one = grad_resid_two + through_two
    grad_self = grad_resid_one.astype(jnp.bfloat16)
    self_out_grad = over_tokens(self_mix, grad_self)
    grad_self_mix = by_transposed(grad_self, out_self).astype(jnp.bfloat16)
    stats = stats_of(self_logs, self_mix, grad_self_mix)
    far_pairs = half // 128
    sent_grad, sent_stats = home(grad_self_mix[:, half:]), home(stats[far_pairs:])
    near_dq, near_dk, near_dv = attend_back(self_q, self_k, self_v, grad_self_mix, stats, True, jnp.float32)
    far_grad = by_side(sent_grad, grad_self_mix[:, :half])
    far_stats = by_side(sent_stats, stats[:far_pairs])
    far_dq, far_dk, far_dv = attend_back(far_q, far_k, far_v, far_grad, far_stats, False, jnp.bfloat16)
    got_dq, got_dk, got_dv = forth(far_dq), home(far_dk), home(far_dv)

    def with_far(near, lower, upper):
        return (near + jnp.concatenate([lower, upper], axis=1).astype(jnp.float32)).astype(jnp.bfloat16)

    none = jnp.zeros_like(far_dq)
    grad_self_q = with_far(near_dq, by_side(none, far_dq), got_dq)
    grad_self_k = with_far(near_dk, got_dk, by_side(far_dk, none))
    grad_self_v = with_far(near_dv, got_dv, by_side(far_dv, none))
    self_query_part = over_tokens(hidden_one, grad_self_q)
    self_key_part = over_tokens(hidden_one, grad_self_k)
    self_value_part = over_tokens(hidden_one, grad_self_v)
    grad_one = (
        by_transposed(grad_self_q, query_self)
        + by_transposed(grad_self_k, key_self)
        + by_transposed(grad_self_v, value_self)
    )
    unused_one, pull_one = jax.vjp(norm_forward, frames, norm_params[0], norm_params[1])
    through_one, first_gain_part, first_bias_part = pull_one(grad_one)
    input_grad = grad_resid_one + through_one
    norm_grads = jnp.stack(
        [first_gain_part, first_bias_part, second_gain_part, second_bias_part, third_gain_part, third_bias_part]
    )
    col_count = lax.axis_size("col")
    norm_grads = norm_grads.reshape(6, 2 * pairs, col_count, piece).transpose(1, 2, 0, 3)
    norm_grads = norm_grads.reshape(2 * pairs, col_count * 6 * piece)
    summed = spread(
        (self_query_part, self_key_part, self_value_part, self_out_grad, cross_query_part, cross_key_part,
         cross_value_part, cross_out_grad, up_grad, down_grad, norm_grads))
    norm_parts = summed[10].reshape(6, piece)
    return (layer_out, input_grad, text_grad, *summed[:10], *norm_parts)


def local(*arrays):
    frames_in, self_query = arrays[0], arrays[2]
    halves = 2 * frames_in.shape[0] == FRAMES and lax.axis_size("row") % 2 == 0
    if halves and lax.axis_size("col") % 2 == 0 and self_query.shape[1] % 256 == 0 and self_query.shape[0] % 128 == 0:
        return fast(*arrays)
    return general(*arrays)


def solution(mesh):
    placed = (
        P(("col", "row"), None),
        P(("col", "row"), None),
        P("row", "col"),
        P("row", "col"),
        P("row", "col"),
        P("row", "col"),
        P("row", "col"),
        P("row", "col"),
        P("row", "col"),
        P("row", "col"),
        P("row", "col"),
        P("row", "col"),
        P(("row", "col")),
        P(("row", "col")),
        P(("row", "col")),
        P(("row", "col")),
        P(("row", "col")),
        P(("row", "col")),
        P(("col", "row"), None),
    )
    return jax.shard_map(
        local,
        mesh=mesh,
        in_specs=placed,
        out_specs=(
            P(("col", "row"), None),
            P(("col", "row"), None),
            P(("col", "row"), None),
            P("row", "col"),
            P("row", "col"),
            P("row", "col"),
            P("row", "col"),
            P("row", "col"),
            P("row", "col"),
            P("row", "col"),
            P("row", "col"),
            P("row", "col"),
            P("row", "col"),
            P(("row", "col")),
            P(("row", "col")),
            P(("row", "col")),
            P(("row", "col")),
            P(("row", "col")),
            P(("row", "col")),
        ),
        check_vma=False,
    )
```

```python
import functools
from functools import partial

import jax
import jax.numpy as jnp
from jax import lax
from jax.experimental import pallas as pl
from jax.experimental.pallas import tpu as pltpu
from jax.sharding import PartitionSpec as P

HEADS = 16
HEAD_DIM = 64
FRAMES = 1500
TEXT = 64


def norm_forward(values, norm_gain, norm_bias):
    center = values - jnp.mean(values, axis=-1, keepdims=True)
    variance = jnp.mean(center * center, axis=-1, keepdims=True)
    return center * lax.rsqrt(variance + 1e-05) * norm_gain + norm_bias


def matmul(left, right):
    return jnp.dot(left, right, preferred_element_type=jnp.float32)


def by_transposed(left, right):
    return lax.dot_general(
        left, right, (((1,), (1,)), ((), ())), preferred_element_type=jnp.float32
    )


def over_tokens(left, right):
    return lax.dot_general(
        left, right, (((0,), (0,)), ((), ())), preferred_element_type=jnp.float32
    )


def collect(blocks):
    partly = (
        lax.all_gather(blocks[0], "col", axis=1, tiled=True),
        lax.all_gather(blocks[1], "col", axis=1, tiled=True),
        lax.all_gather(blocks[2], "col", axis=1, tiled=True),
        lax.all_gather(blocks[3], "col", axis=1, tiled=True),
        lax.all_gather(blocks[4], "col", axis=1, tiled=True),
        lax.all_gather(blocks[5], "col", axis=1, tiled=True),
        lax.all_gather(blocks[6], "col", axis=1, tiled=True),
        lax.all_gather(blocks[7], "col", axis=1, tiled=True),
        lax.all_gather(blocks[8], "col", axis=1, tiled=True),
        lax.all_gather(blocks[9], "col", axis=1, tiled=True),
        lax.all_gather(blocks[10], "col", axis=1, tiled=True),
    )
    return (
        lax.all_gather(partly[0], "row", axis=0, tiled=True),
        lax.all_gather(partly[1], "row", axis=0, tiled=True),
        lax.all_gather(partly[2], "row", axis=0, tiled=True),
        lax.all_gather(partly[3], "row", axis=0, tiled=True),
        lax.all_gather(partly[4], "row", axis=0, tiled=True),
        lax.all_gather(partly[5], "row", axis=0, tiled=True),
        lax.all_gather(partly[6], "row", axis=0, tiled=True),
        lax.all_gather(partly[7], "row", axis=0, tiled=True),
        lax.all_gather(partly[8], "row", axis=0, tiled=True),
        lax.all_gather(partly[9], "row", axis=0, tiled=True),
        lax.all_gather(partly[10], "row", axis=0, tiled=True),
    )


def spread(grads):
    partly = (
        lax.psum_scatter(
            grads[0].astype(jnp.bfloat16), "row", scatter_dimension=0, tiled=True
        ).astype(jnp.float32),
        lax.psum_scatter(
            grads[1].astype(jnp.bfloat16), "row", scatter_dimension=0, tiled=True
        ).astype(jnp.float32),
        lax.psum_scatter(
            grads[2].astype(jnp.bfloat16), "row", scatter_dimension=0, tiled=True
        ).astype(jnp.float32),
        lax.psum_scatter(
            grads[3].astype(jnp.bfloat16), "row", scatter_dimension=0, tiled=True
        ).astype(jnp.float32),
        lax.psum_scatter(
            grads[4].astype(jnp.bfloat16), "row", scatter_dimension=0, tiled=True
        ).astype(jnp.float32),
        lax.psum_scatter(
            grads[5].astype(jnp.bfloat16), "row", scatter_dimension=0, tiled=True
        ).astype(jnp.float32),
        lax.psum_scatter(
            grads[6].astype(jnp.bfloat16), "row", scatter_dimension=0, tiled=True
        ).astype(jnp.float32),
        lax.psum_scatter(
            grads[7].astype(jnp.bfloat16), "row", scatter_dimension=0, tiled=True
        ).astype(jnp.float32),
        lax.psum_scatter(
            grads[8].astype(jnp.bfloat16), "row", scatter_dimension=0, tiled=True
        ).astype(jnp.float32),
        lax.psum_scatter(
            grads[9].astype(jnp.bfloat16), "row", scatter_dimension=0, tiled=True
        ).astype(jnp.float32),
        lax.psum_scatter(
            grads[10].astype(jnp.bfloat16), "row", scatter_dimension=0, tiled=True
        ).astype(jnp.float32),
    )
    return (
        lax.psum_scatter(
            partly[0].astype(jnp.bfloat16), "col", scatter_dimension=1, tiled=True
        ).astype(jnp.float32),
        lax.psum_scatter(
            partly[1].astype(jnp.bfloat16), "col", scatter_dimension=1, tiled=True
        ).astype(jnp.float32),
        lax.psum_scatter(
            partly[2].astype(jnp.bfloat16), "col", scatter_dimension=1, tiled=True
        ).astype(jnp.float32),
        lax.psum_scatter(
            partly[3].astype(jnp.bfloat16), "col", scatter_dimension=1, tiled=True
        ).astype(jnp.float32),
        lax.psum_scatter(
            partly[4].astype(jnp.bfloat16), "col", scatter_dimension=1, tiled=True
        ).astype(jnp.float32),
        lax.psum_scatter(
            partly[5].astype(jnp.bfloat16), "col", scatter_dimension=1, tiled=True
        ).astype(jnp.float32),
        lax.psum_scatter(
            partly[6].astype(jnp.bfloat16), "col", scatter_dimension=1, tiled=True
        ).astype(jnp.float32),
        lax.psum_scatter(
            partly[7].astype(jnp.bfloat16), "col", scatter_dimension=1, tiled=True
        ).astype(jnp.float32),
        lax.psum_scatter(
            partly[8].astype(jnp.bfloat16), "col", scatter_dimension=1, tiled=True
        ).astype(jnp.float32),
        lax.psum_scatter(
            partly[9].astype(jnp.bfloat16), "col", scatter_dimension=1, tiled=True
        ).astype(jnp.float32),
        lax.psum_scatter(
            partly[10].astype(jnp.bfloat16), "col", scatter_dimension=1, tiled=True
        ).astype(jnp.float32),
    )


def heads_layout(stacked):
    return lax.all_to_all(stacked, "row", split_axis=1, concat_axis=0, tiled=True)


def tokens_layout(stacked):
    return lax.all_to_all(stacked, "row", split_axis=0, concat_axis=2, tiled=True)


def by_clips(arranged, start, count, length, heads_dev):
    section = arranged[:, start : start + count]
    return section.reshape(-1, length, heads_dev, HEAD_DIM)


def causal_scores(query_clip, key_clip, causal):
    scores = jnp.einsum(
        "qhd,khd->hqk", query_clip, key_clip, preferred_element_type=jnp.float32
    ) * HEAD_DIM ** (-0.5)
    if causal:
        allowed = jnp.arange(scores.shape[1])[:, None] >= jnp.arange(scores.shape[2])[None, :]
        scores = jnp.where(allowed, scores, -1e30)
    return scores


def attend_forward(query_clips, key_clips, value_clips, causal):

    def one_clip(operands):
        query_clip, key_clip, value_clip = operands
        scores = causal_scores(query_clip, key_clip, causal)
        highest = jnp.max(scores, axis=-1, keepdims=True)
        powers = jnp.exp(scores - highest)
        totals = jnp.sum(powers, axis=-1, keepdims=True)
        weights_low = (powers / totals).astype(jnp.bfloat16)
        mixture = jnp.einsum(
            "hqk,khd->qhd", weights_low, value_clip, preferred_element_type=jnp.float32
        )
        return (mixture.astype(jnp.bfloat16), (highest + jnp.log(totals))[..., 0])

    return lax.map(one_clip, (query_clips, key_clips, value_clips))


def attend_backward(query_clips, key_clips, value_clips, log_sums, grad_clips, causal):

    def one_clip(operands):
        query_clip, key_clip, value_clip, log_clip, grad_clip = operands
        scores = causal_scores(query_clip, key_clip, causal)
        probs_full = jnp.exp(scores - log_clip[..., None])
        grad_probs = jnp.einsum(
            "qhd,khd->hqk", grad_clip, value_clip, preferred_element_type=jnp.float32
        )
        grad_value = jnp.einsum(
            "hqk,qhd->khd",
            probs_full.astype(jnp.bfloat16),
            grad_clip,
            preferred_element_type=jnp.float32,
        )
        centered = grad_probs - jnp.sum(probs_full * grad_probs, axis=-1, keepdims=True)
        grad_scores = (probs_full * centered).astype(jnp.bfloat16)
        grad_query = jnp.einsum(
            "hqk,khd->qhd", grad_scores, key_clip, preferred_element_type=jnp.float32
        ) * HEAD_DIM ** (-0.5)
        grad_key = jnp.einsum(
            "hqk,qhd->khd", grad_scores, query_clip, preferred_element_type=jnp.float32
        ) * HEAD_DIM ** (-0.5)
        return (
            grad_query.astype(jnp.bfloat16),
            grad_key.astype(jnp.bfloat16),
            grad_value.astype(jnp.bfloat16),
        )

    return lax.map(one_clip, (query_clips, key_clips, value_clips, log_sums, grad_clips))


def general(
    frames_in,
    text_states,
    self_query,
    self_key,
    self_value,
    self_output,
    cross_query,
    cross_key,
    cross_value,
    cross_output,
    up_weight,
    down_weight,
    first_gain,
    first_bias,
    second_gain,
    second_bias,
    third_gain,
    third_bias,
    cotangent,
):
    row_count = lax.axis_size("row")
    col_count = lax.axis_size("col")
    heads_dev = HEADS // row_count
    width_dev = heads_dev * HEAD_DIM
    tok_rows = frames_in.shape[0]
    text_rows = text_states.shape[0]
    piece_len = first_gain.shape[0]
    gain_block = jnp.stack(
        [first_gain, first_bias, second_gain, second_bias, third_gain, third_bias]
    ).reshape(1, 6 * piece_len)
    param_blocks = (
        self_query,
        self_key,
        self_value,
        self_output,
        cross_query,
        cross_key,
        cross_value,
        cross_output,
        up_weight,
        down_weight,
        gain_block,
    )

    def unpack_gains(gathered_gains):
        arranged = gathered_gains.reshape(row_count, col_count, 6, piece_len).transpose(2, 0, 1, 3)
        return arranged.reshape(6, row_count * col_count * piece_len).astype(jnp.float32)

    gathered = collect(param_blocks)
    (
        query_self,
        key_self,
        value_self,
        out_self,
        query_cross,
        key_cross,
        value_cross,
        out_cross,
        up_full,
        down_full,
    ) = gathered[:10]
    norm_params = unpack_gains(gathered[10])
    frames = frames_in.astype(jnp.float32)
    hidden_one = norm_forward(frames, norm_params[0], norm_params[1]).astype(jnp.bfloat16)
    self_q = matmul(hidden_one, query_self).astype(jnp.bfloat16)
    self_k = matmul(hidden_one, key_self).astype(jnp.bfloat16)
    self_v = matmul(hidden_one, value_self).astype(jnp.bfloat16)
    text_k = matmul(text_states, key_cross).astype(jnp.bfloat16)
    text_v = matmul(text_states, value_cross).astype(jnp.bfloat16)
    sent_rows = 3 * tok_rows + 2 * text_rows
    arranged = heads_layout(jnp.concatenate([self_q, self_k, self_v, text_k, text_v], axis=0))
    arranged = arranged.reshape(row_count, sent_rows, width_dev)
    query_clips = by_clips(arranged, 0, tok_rows, FRAMES, heads_dev)
    key_clips = by_clips(arranged, tok_rows, tok_rows, FRAMES, heads_dev)
    value_clips = by_clips(arranged, 2 * tok_rows, tok_rows, FRAMES, heads_dev)
    text_keys = by_clips(arranged, 3 * tok_rows, text_rows, TEXT, heads_dev)
    text_values = by_clips(arranged, 3 * tok_rows + text_rows, text_rows, TEXT, heads_dev)
    self_clips, self_logs = attend_forward(query_clips, key_clips, value_clips, True)
    self_mix = tokens_layout(self_clips.reshape(row_count, tok_rows, width_dev))[0]
    resid_one = frames + matmul(self_mix, out_self)
    hidden_two = norm_forward(resid_one, norm_params[2], norm_params[3]).astype(jnp.bfloat16)
    cross_q = matmul(hidden_two, query_cross).astype(jnp.bfloat16)
    cross_arranged = heads_layout(cross_q).reshape(row_count, tok_rows, width_dev)
    cross_queries = by_clips(cross_arranged, 0, tok_rows, FRAMES, heads_dev)
    cross_clips, cross_logs = attend_forward(cross_queries, text_keys, text_values, False)
    cross_mix = tokens_layout(cross_clips.reshape(row_count, tok_rows, width_dev))[0]
    resid_two = resid_one + matmul(cross_mix, out_cross)
    hidden_three = norm_forward(resid_two, norm_params[4], norm_params[5]).astype(jnp.bfloat16)
    pre_act = matmul(hidden_three, up_full)
    inner = jax.nn.gelu(pre_act, approximate=False).astype(jnp.bfloat16)
    layer_out = (resid_two + matmul(inner, down_full)).astype(jnp.bfloat16)
    gathered = collect(param_blocks)
    (
        query_self,
        key_self,
        value_self,
        out_self,
        query_cross,
        key_cross,
        value_cross,
        out_cross,
        up_full,
        down_full,
    ) = gathered[:10]
    norm_params = unpack_gains(gathered[10])
    cotan_full = cotangent.astype(jnp.float32)
    down_grad = over_tokens(inner, cotangent)
    grad_inner = by_transposed(cotangent, down_full)
    unused_gelu, gelu_pull = jax.vjp(partial(jax.nn.gelu, approximate=False), pre_act)
    grad_pre = gelu_pull(grad_inner)[0].astype(jnp.bfloat16)
    up_grad = over_tokens(hidden_three, grad_pre)
    grad_three = by_transposed(grad_pre, up_full)
    unused_three, pull_three = jax.vjp(norm_forward, resid_two, norm_params[4], norm_params[5])
    through_three, third_gain_part, third_bias_part = pull_three(grad_three)
    grad_resid_two = cotan_full + through_three
    grad_cross = grad_resid_two.astype(jnp.bfloat16)
    cross_out_grad = over_tokens(cross_mix, grad_cross)
    grad_cross_mix = by_transposed(grad_cross, out_cross).astype(jnp.bfloat16)
    grad_cross_arr = heads_layout(grad_cross_mix).reshape(row_count, tok_rows, width_dev)
    grad_cross_clips = by_clips(grad_cross_arr, 0, tok_rows, FRAMES, heads_dev)
    cq_clips, tk_clips, tv_clips = attend_backward(
        cross_queries, text_keys, text_values, cross_logs, grad_cross_clips, False
    )
    back_cross = jnp.concatenate(
        [
            cq_clips.reshape(row_count, tok_rows, width_dev),
            tk_clips.reshape(row_count, text_rows, width_dev),
            tv_clips.reshape(row_count, text_rows, width_dev),
        ],
        axis=1,
    )
    back_cross = tokens_layout(back_cross)[0]
    grad_cross_q = back_cross[:tok_rows]
    grad_text_k = back_cross[tok_rows : tok_rows + text_rows]
    grad_text_v = back_cross[tok_rows + text_rows :]
    cross_query_part = over_tokens(hidden_two, grad_cross_q)
    cross_key_part = over_tokens(text_states, grad_text_k)
    cross_value_part = over_tokens(text_states, grad_text_v)
    text_grad = by_transposed(grad_text_k, key_cross) + by_transposed(grad_text_v, value_cross)
    grad_two = by_transposed(grad_cross_q, query_cross)
    unused_two, pull_two = jax.vjp(norm_forward, resid_one, norm_params[2], norm_params[3])
    through_two, second_gain_part, second_bias_part = pull_two(grad_two)
    grad_resid_one = grad_resid_two + through_two
    grad_self = grad_resid_one.astype(jnp.bfloat16)
    self_out_grad = over_tokens(self_mix, grad_self)
    grad_self_mix = by_transposed(grad_self, out_self).astype(jnp.bfloat16)
    grad_self_arr = heads_layout(grad_self_mix).reshape(row_count, tok_rows, width_dev)
    grad_self_clips = by_clips(grad_self_arr, 0, tok_rows, FRAMES, heads_dev)
    sq_clips, sk_clips, sv_clips = attend_backward(
        query_clips, key_clips, value_clips, self_logs, grad_self_clips, True
    )
    back_self = jnp.concatenate(
        [
            sq_clips.reshape(row_count, tok_rows, width_dev),
            sk_clips.reshape(row_count, tok_rows, width_dev),
            sv_clips.reshape(row_count, tok_rows, width_dev),
        ],
        axis=1,
    )
    back_self = tokens_layout(back_self)[0]
    grad_self_q = back_self[:tok_rows]
    grad_self_k = back_self[tok_rows : 2 * tok_rows]
    grad_self_v = back_self[2 * tok_rows :]
    self_query_part = over_tokens(hidden_one, grad_self_q)
    self_key_part = over_tokens(hidden_one, grad_self_k)
    self_value_part = over_tokens(hidden_one, grad_self_v)
    grad_one = (
        by_transposed(grad_self_q, query_self)
        + by_transposed(grad_self_k, key_self)
        + by_transposed(grad_self_v, value_self)
    )
    unused_one, pull_one = jax.vjp(norm_forward, frames, norm_params[0], norm_params[1])
    through_one, first_gain_part, first_bias_part = pull_one(grad_one)
    input_grad = grad_resid_one + through_one
    norm_grads = jnp.stack(
        [
            first_gain_part,
            first_bias_part,
            second_gain_part,
            second_bias_part,
            third_gain_part,
            third_bias_part,
        ]
    )
    norm_grads = norm_grads.reshape(6, row_count, col_count, piece_len).transpose(1, 2, 0, 3)
    norm_grads = norm_grads.reshape(row_count, col_count * 6 * piece_len)
    summed = spread(
        (
            self_query_part,
            self_key_part,
            self_value_part,
            self_out_grad,
            cross_query_part,
            cross_key_part,
            cross_value_part,
            cross_out_grad,
            up_grad,
            down_grad,
            norm_grads,
        )
    )
    norm_parts = summed[10].reshape(6, piece_len)
    return (
        layer_out,
        input_grad,
        text_grad,
        summed[0],
        summed[1],
        summed[2],
        summed[3],
        summed[4],
        summed[5],
        summed[6],
        summed[7],
        summed[8],
        summed[9],
        norm_parts[0],
        norm_parts[1],
        norm_parts[2],
        norm_parts[3],
        norm_parts[4],
        norm_parts[5],
    )


NT=(((1,),(1,)),((),())); NN=(((1,),(0,)),((),())); TN=(((0,),(0,)),((),()))
def dg(a,b,dims): return lax.dot_general(a,b,dims,preferred_element_type=jnp.float32)

def attend_kernel(causal,tile,q_ref,k_ref,v_ref,o_ref,lse_ref):
    pair=pl.program_id(0)
    rows=q_ref.shape[0]
    low=lax.broadcasted_iota(jnp.int32,(1,128),1)<HEAD_DIM
    lane=lax.broadcasted_iota(jnp.int32,(1,128),1)
    value=v_ref[...]
    ones=jnp.ones_like(value)
    @pl.when(pair==0)
    def _(): lse_ref[...]=jnp.zeros_like(lse_ref)
    for start in range(0,rows,tile):
        n=min(tile,rows-start)
        q=q_ref[start:start+n,:]*jnp.bfloat16(HEAD_DIM**-0.5)
        mixed=[]; sums=[]
        lse=lse_ref[start:start+n,:]
        for h in range(2):
            mine=low if h==0 else jnp.logical_not(low)
            qh=jnp.where(mine,q,jnp.bfloat16(0))
            vh=jnp.where(mine,value,ones)
            if causal:
                spans=([(0,start)] if start else [])+[(start,n)]
            else: spans=[(0,k_ref.shape[0])]
            scores=[]
            for at,length in spans:
                s=dg(qh,k_ref[at:at+length,:],NT)
                if causal and at==start:
                    ok=lax.broadcasted_iota(jnp.int32,s.shape,0)>=lax.broadcasted_iota(jnp.int32,s.shape,1)
                    s=jnp.where(ok,s,-1e30)
                scores.append(s)
            top=functools.reduce(jnp.maximum,[jnp.max(s,axis=1,keepdims=True) for s in scores])
            out=None
            for (at,length),s in zip(spans,scores):
                p=jnp.exp(s-top).astype(jnp.bfloat16)
                part=dg(p,vh[at:at+length,:],NN)
                out=part if out is None else out+part
            total=out[:,HEAD_DIM:HEAD_DIM+1] if h==0 else out[:,0:1]
            mixed.append(out/total)
            lse=jnp.where(lane==2*pair+h,top+jnp.log(total),lse)
        lse_ref[start:start+n,:]=lse
        o_ref[start:start+n,:]=jnp.where(low,mixed[0],mixed[1]).astype(o_ref.dtype)

def attend(q,k,v,causal,out_dtype,tile=256):
    rows,width=q.shape; keys=k.shape[0]
    return pl.pallas_call(functools.partial(attend_kernel,causal,tile),grid=(width//128,),
        in_specs=[pl.BlockSpec((rows,128),lambda i:(0,i)),pl.BlockSpec((keys,128),lambda i:(0,i)),pl.BlockSpec((keys,128),lambda i:(0,i))],
        out_specs=[pl.BlockSpec((rows,128),lambda i:(0,i)),pl.BlockSpec((rows,128),lambda i:(0,0))],
        out_shape=[jax.ShapeDtypeStruct((rows,width),out_dtype),jax.ShapeDtypeStruct((rows,128),jnp.float32)],
        compiler_params=pltpu.CompilerParams(vmem_limit_bytes=40<<20),
        cost_estimate=pl.CostEstimate(flops=4*rows*keys*width,bytes_accessed=8*rows*width,transcendentals=rows*keys*width//64))(q,k,v)

def attend_back_kernel(causal,tile,q_ref,k_ref,v_ref,do_ref,st_ref,dq_ref,dk_ref,dv_ref,acc):
    rows=q_ref.shape[0]; keys=k_ref.shape[0]
    low=lax.broadcasted_iota(jnp.int32,(1,128),1)<HEAD_DIM
    acc[...]=jnp.zeros_like(acc)
    for start in range(0,keys,tile):
        n=min(tile,keys-start)
        k=k_ref[start:start+n,:]*jnp.bfloat16(HEAD_DIM**-0.5)
        v=v_ref[start:start+n,:]
        spans=[(0,rows)]
        if causal: spans=[(start,n)]+([(start+n,rows-start-n)] if start+n<rows else [])
        dks=[];dvs=[]
        for h in range(2):
            mine=low if h==0 else jnp.logical_not(low)
            kh=jnp.where(mine,k,jnp.bfloat16(0)); vh=jnp.where(mine,v,jnp.bfloat16(0))
            dk=dv=None
            for at,length in spans:
                qs=q_ref[at:at+length,:]; do=do_ref[at:at+length,:]
                s=dg(kh,qs,NT)
                p=jnp.exp(s-st_ref[0,h:h+1,at:at+length])
                if causal and at==start:
                    ok=lax.broadcasted_iota(jnp.int32,s.shape,0)<=lax.broadcasted_iota(jnp.int32,s.shape,1)
                    p=jnp.where(ok,p,0.0)
                dp=dg(vh,do,NT)
                ds=(p*(dp-st_ref[0,2+h:3+h,at:at+length])).astype(jnp.bfloat16)
                a=dg(p.astype(jnp.bfloat16),do,NN); b=dg(ds,qs,NN)
                dv=a if dv is None else dv+a
                dk=b if dk is None else dk+b
                acc[at:at+length,:]+=dg(ds,kh,TN)
            dks.append(dk);dvs.append(dv)
        dk_ref[start:start+n,:]=(jnp.where(low,dks[0],dks[1])*HEAD_DIM**-0.5).astype(dk_ref.dtype)
        dv_ref[start:start+n,:]=jnp.where(low,dvs[0],dvs[1]).astype(dv_ref.dtype)
    dq_ref[...]=acc[...].astype(dq_ref.dtype)

def attend_back(q,k,v,do,stats,causal,out_dtype,tile=256):
    rows,width=q.shape; keys=k.shape[0]
    bq=pl.BlockSpec((rows,128),lambda i:(0,i)); bk=pl.BlockSpec((keys,128),lambda i:(0,i))
    return pl.pallas_call(functools.partial(attend_back_kernel,causal,tile),grid=(width//128,),
        in_specs=[bq,bk,bk,bq,pl.BlockSpec((1,4,rows),lambda i:(i,0,0))],out_specs=[bq,bk,bk],
        out_shape=[jax.ShapeDtypeStruct((rows,width),out_dtype),jax.ShapeDtypeStruct((keys,width),out_dtype),jax.ShapeDtypeStruct((keys,width),out_dtype)],
        scratch_shapes=[pltpu.VMEM((rows,128),jnp.float32)],
        compiler_params=pltpu.CompilerParams(vmem_limit_bytes=40<<20),
        cost_estimate=pl.CostEstimate(flops=10*rows*keys*width,bytes_accessed=16*rows*width,transcendentals=rows*keys*width//64))(q,k,v,do,stats)

def feed_kernel(h_ref,cot_ref,res_ref,up_ref,down_ref,out_ref,g_ref,dup_ref,ddown_ref,acc):
    i=pl.program_id(0)
    @pl.when(i==0)
    def _():
        acc[...]=res_ref[...]
        g_ref[...]=jnp.zeros_like(g_ref)
    h=h_ref[...]; cot=cot_ref[...]
    pre=dg(h,up_ref[...],NN)
    cdf=0.5*(1.0+lax.erf(pre*0.7071067811865476))
    inner=(pre*cdf).astype(jnp.bfloat16)
    acc[...]+=dg(inner,down_ref[...],NN)
    ddown_ref[...]=dg(inner,cot,TN).astype(ddown_ref.dtype)
    slope=cdf+pre*(jnp.exp(-0.5*pre*pre)*0.3989422804014327)
    gpre=(dg(cot,down_ref[...],NT)*slope).astype(jnp.bfloat16)
    dup_ref[...]=dg(h,gpre,TN).astype(dup_ref.dtype)
    g_ref[...]+=dg(gpre,up_ref[...],NT)
    @pl.when(i==pl.num_programs(0)-1)
    def _(): out_ref[...]=acc[...].astype(out_ref.dtype)

def feed(h,cot,res,up,down,chunk=512):
    rows,d=h.shape; ff=up.shape[1]
    whole=pl.BlockSpec((rows,d),lambda i:(0,0))
    return pl.pallas_call(feed_kernel,grid=(ff//chunk,),
        in_specs=[whole,whole,whole,pl.BlockSpec((d,chunk),lambda i:(0,i)),pl.BlockSpec((chunk,d),lambda i:(i,0))],
        out_specs=[whole,whole,pl.BlockSpec((d,chunk),lambda i:(0,i)),pl.BlockSpec((chunk,d),lambda i:(i,0))],
        out_shape=[jax.ShapeDtypeStruct((rows,d),jnp.bfloat16),jax.ShapeDtypeStruct((rows,d),jnp.float32),jax.ShapeDtypeStruct((d,ff),jnp.bfloat16),jax.ShapeDtypeStruct((ff,d),jnp.bfloat16)],
        scratch_shapes=[pltpu.VMEM((rows,d),jnp.float32)],
        compiler_params=pltpu.CompilerParams(vmem_limit_bytes=56<<20),
        cost_estimate=pl.CostEstimate(flops=12*rows*d*ff,bytes_accessed=8*d*ff+16*rows*d,transcendentals=2*rows*ff))(h,cot,res,up,down)


MESH = pl.DeviceIdType.MESH
ORDERS = ("xzy", "yzx", "xzy", "yzx", "zxy", "zyx")


class Place:
    def __init__(self):
        row, col = lax.axis_index("row"), lax.axis_index("col")
        self.z, self.y, self.x, self.k = row // 2, row % 2, col // 2, col % 2
        self.along = lax.axis_size("row") // 2

    def device(self, dz=0, y=False, x=False, k=False):
        other_y = 1 - self.y if y else self.y
        other_x = 1 - self.x if x else self.x
        other_k = 1 - self.k if k else self.k
        return ((self.z + dz) * 2 + other_y, other_x * 2 + other_k)

    def across(self, axis):
        return self.device(y=axis == "y", x=axis == "x", k=axis == "k")

    def greet(self):
        barrier = pltpu.get_barrier_semaphore()
        for axis in "xyk":
            pl.semaphore_signal(barrier, inc=1, device_id=self.across(axis), device_id_type=MESH)

        @pl.when(self.z > 0)
        def _():
            pl.semaphore_signal(barrier, inc=1, device_id=self.device(dz=-1), device_id_type=MESH)

        @pl.when(self.z + 1 < self.along)
        def _():
            pl.semaphore_signal(barrier, inc=1, device_id=self.device(dz=1), device_id_type=MESH)

        below = jnp.where(self.z > 0, 1, 0)
        above = jnp.where(self.z + 1 < self.along, 1, 0)
        pl.semaphore_wait(barrier, 3 + below + above)


def when(condition, run):
    if condition is None:
        run()
    else:
        pl.when(condition)(run)


class Gather:
    def __init__(self, place, block, full, strip, order, send, recv):
        self.place, self.block, self.full, self.strip = place, block, full, strip
        turn = order.index("z")
        self.before, self.after = order[:turn], order[turn + 1 :]
        self.send, self.recv, self.used, self.sent, self.started = send, recv, 0, 0, []

    def region(self, z, y, x):
        part, start, count = self.strip
        column = (x * 2 + self.place.k) * self.block.shape[-1] + start
        return self.full.at[z, y, part, :, pl.ds(pl.multiple_of(column, 128), count)]

    def held(self, done, z):
        y = slice(None) if "y" in done else self.place.y
        return [self.region(z, y, x) for x in (range(2) if "x" in done else [self.place.x])]

    def pairs(self, done, z, first):
        if first:
            part, start, count = self.strip
            place = self.place
            return [(self.block.at[part, :, pl.ds(start, count)], self.region(place.z, place.y, place.x))]
        return [(region, region) for region in self.held(done, z)]

    def semaphore(self):
        self.used += 2
        return self.used - 2

    def copies(self, device, pairs, semaphore, send=0):
        return [
            pltpu.make_async_remote_copy(
                src_ref=source, dst_ref=target, send_sem=self.send.at[send + at],
                recv_sem=self.recv.at[semaphore + at], device_id=device, device_id_type=MESH)
            for at, (source, target) in enumerate(pairs)
        ]

    def start(self, device, pairs, condition, semaphore):
        copies = self.copies(device, pairs, semaphore, self.sent)
        self.sent += len(copies)
        when(condition, lambda: [copy.start() for copy in copies] and None)
        self.started.append((condition, copies))
        return condition, copies

    def arrive(self, sent):
        condition, copies = sent
        when(condition, lambda: [copy.wait_recv() for copy in copies] and None)

    def stages(self):
        place, along = self.place, self.place.along
        done = []
        for axis in self.before:
            sent = self.start(place.across(axis), self.pairs(done, place.z, not done), None, self.semaphore())
            yield
            self.arrive(sent)
            done.append(axis)
        first = not done
        from_left = [self.semaphore() for _ in range(along - 1)]
        from_right = [self.semaphore() for _ in range(along - 1)]

        def pass_on(turn, step):
            axes = done + list(self.after[:turn])
            device = place.across(self.after[turn])
            if step == 0:
                return turn, step, [self.start(device, self.pairs(axes, place.z, not axes), None, self.semaphore())]
            return turn, step, [
                self.start(device, self.pairs(axes, z, False), (z >= 0) & (z < along), self.semaphore())
                for z in (place.z - step, place.z + step)
            ]

        def step_out(step):
            left, right = place.z - (step - 1), place.z + (step - 1)
            self.start(place.device(dz=1), self.pairs(done, left, first and step == 1),
                       (left >= 0) & (place.z + 1 < along), from_left[step - 1])
            self.start(place.device(dz=-1), self.pairs(done, right, first and step == 1),
                       (right < along) & (place.z > 0), from_right[step - 1])

        def step_in(step):
            for z, semaphore in ((place.z - step, from_left), (place.z + step, from_right)):
                copies = self.copies(place.across("k"), self.pairs(done, z, False), semaphore[step - 1])
                self.arrive(((z >= 0) & (z < along), copies))

        step_out(1)
        waiting = [pass_on(0, 0)] if self.after else []
        for step in range(1, along + len(self.after)):
            yield
            if step < along:
                step_in(step)
                if step + 1 < along:
                    step_out(step + 1)
            following = []
            for turn, at, sent in waiting:
                for one in sent:
                    self.arrive(one)
                if turn + 1 < len(self.after):
                    following.append(pass_on(turn + 1, at))
            if self.after and step < along:
                following.append(pass_on(0, step))
            waiting = following
        everything = [self.region(slice(None), slice(None), x) for x in range(2)]
        sent = self.start(place.across("k"), [(r, r) for r in everything], None, self.semaphore())
        yield
        self.arrive(sent)

    def finish(self):
        for condition, copies in self.started:
            when(condition, lambda copies=copies: [copy.wait_send() for copy in copies] and None)


def gather_kernel(units, count, *refs):
    blocks, fulls = refs[:count], refs[count : 2 * count]
    send, recv, local_sem = refs[2 * count :]
    place = Place()
    place.greet()
    own = []
    for at, (block, full) in enumerate(zip(blocks, fulls)):
        width = block.shape[-1]
        columns = pl.ds(pl.multiple_of((place.x * 2 + place.k) * width, 128), width)
        copy = pltpu.make_async_copy(block, full.at[place.z, place.y, :, :, columns], local_sem.at[at])
        copy.start()
        own.append(copy)
    gathers = [
        Gather(place, blocks[which], fulls[which], strip, order, send.at[at], recv.at[at])
        for at, (which, strip, order) in enumerate(units)
    ]
    running = [gather.stages() for gather in gathers]
    while running:
        running = [stages for stages in running if next(stages, running) is not running]
        while own:
            own.pop().wait()
    for gather in gathers:
        gather.finish()


def gather_units(blocks, least):
    strips = []
    for which, block in enumerate(blocks):
        wide = min(least, block.shape[-1])
        for part in range(block.shape[0]):
            for start in range(0, block.shape[-1], wide):
                strips.append((which, (part, start, wide)))
    return [strip + (ORDERS[at % len(ORDERS)],) for at, strip in enumerate(strips)]


def gather_blocks(blocks, collective_id, least):
    along, cols = lax.axis_size("row") // 2, lax.axis_size("col")
    units = gather_units(blocks, least)
    count = len(blocks)
    anywhere = pl.BlockSpec(memory_space=pl.ANY)
    moved = sum(block.size for block in blocks) * 2 * along * 2 * cols
    return pl.pallas_call(
        functools.partial(gather_kernel, units, count),
        out_shape=[
            jax.ShapeDtypeStruct((along, 2) + b.shape[:2] + (cols * b.shape[2],), b.dtype) for b in blocks
        ],
        in_specs=[anywhere] * count,
        out_specs=[anywhere] * count,
        scratch_shapes=[
            pltpu.SemaphoreType.DMA((len(units), 8 * along)),
            pltpu.SemaphoreType.DMA((len(units), 12 * along)),
            pltpu.SemaphoreType.DMA((count,)),
        ],
        compiler_params=pltpu.CompilerParams(collective_id=collective_id, has_side_effects=True),
        cost_estimate=pl.CostEstimate(flops=0, bytes_accessed=2 * moved, transcendentals=0),
    )(*blocks)


def add_blocks(total, extra, leading):
    def one(at, unused):
        place = []
        for size in leading[::-1]:
            place.append(at % size)
            at = at // size
        place = tuple(place[::-1])
        total[place] = (total[place].astype(jnp.float32) + extra[place].astype(jnp.float32)).astype(total.dtype)
        return unused

    if not leading:
        total[...] = (total[...].astype(jnp.float32) + extra[...].astype(jnp.float32)).astype(total.dtype)
        return
    count = 1
    for size in leading:
        count *= size
    lax.fori_loop(0, count, one, 0)


class Scatter:
    def __init__(self, place, grad, out, strip, width, order, slots, send, recv, local):
        self.place, self.grad, self.out, self.strip, self.width = place, grad, out, strip, width
        self.order = order[::-1]
        self.total, self.other_core, self.halves, self.steps = slots
        self.send, self.recv, self.local = send, recv, local
        self.used, self.started = 0, []

    def region(self, x, k):
        part, start, count = self.strip
        column = (x * 2 + k) * self.width + start
        return self.grad.at[:, :, part, :, pl.ds(pl.multiple_of(column, 128), count)]

    def copy(self, device, source, target, semaphore=None):
        if semaphore is None:
            semaphore = self.used
            self.used += 1
        return pltpu.make_async_remote_copy(
            src_ref=source, dst_ref=target, send_sem=self.send.at[semaphore], recv_sem=self.recv.at[semaphore],
            device_id=device, device_id_type=MESH)

    def start(self, copy, condition=None):
        when(condition, lambda: copy.start())
        self.started.append((condition, copy))

    def stages(self):
        place, along = self.place, self.place.along
        rows, columns = self.total.shape[-2:]
        own = [
            pltpu.make_async_copy(self.region(x, place.k), self.total.at[:, :, x], self.local.at[x]) for x in range(2)
        ]
        swapped = [
            self.copy(place.across("k"), self.region(x, 1 - place.k), self.other_core.at[:, :, x]) for x in range(2)
        ]
        for copy in own:
            copy.start()
        for copy in swapped:
            self.start(copy)
        yield
        for copy in own:
            copy.wait()
        for copy in swapped:
            copy.wait_recv()
        add_blocks(self.total, self.other_core, (along, 2, 2))
        left = {"z": slice(None), "y": slice(None), "x": slice(None)}
        at = {"y": place.y, "x": place.x}

        def view(ref, **places):
            return ref.at[tuple({**left, **places}[axis] for axis in "zyx")]

        def sizes():
            return tuple(size for axis, size in zip("zyx", (along, 2, 2)) if isinstance(left[axis], slice))

        exchanges = 0
        for axis in self.order:
            if axis == "z":
                shape = tuple(2 for name in "yx" if isinstance(left[name], slice))
                landing = self.steps.at[(slice(None),) * 2 + tuple(slice(None) if isinstance(left[name], slice) else 0 for name in "yx")]
                right, leftward = [self.used + at for at in range(along)], [self.used + along + at for at in range(along)]
                self.used += 2 * along
                for step in range(along):
                    if step:
                        yield
                    for way, names, first in ((1, right, place.z), (-1, leftward, along - 1 - place.z)):
                        goal = along - 1 - step + place.z if way == 1 else step - along + 1 + place.z
                        side = 0 if way == 1 else 1
                        if step:
                            arrived = self.copy(
                                place.across("k"), landing.at[side, step - 1], landing.at[side, step - 1], names[step - 1])

                            def take(arrived=arrived, goal=goal, side=side, step=step):
                                arrived.wait_recv()
                                add_blocks(view(self.total, z=goal), landing.at[side, step - 1], shape)

                            pl.when((first >= 1) & (first <= step))(take)
                        if step < along - 1:
                            onward = self.copy(
                                place.device(dz=way), view(self.total, z=jnp.clip(goal, 0, along - 1)), landing.at[side, step], names[step])
                            self.start(onward, (first <= step) & (first < along - 1))
                left["z"] = place.z
            else:
                landing = self.halves[exchanges]
                exchanges += 1
                target = landing.at[tuple(slice(None) if isinstance(left[name], slice) and name != axis else 0 for name in "zyx")]
                swap = self.copy(place.across(axis), view(self.total, **{axis: 1 - at[axis]}), target)
                self.start(swap)
                yield
                swap.wait_recv()
                left[axis] = at[axis]
                add_blocks(view(self.total), target, sizes())
        part, start, count = self.strip
        self.out[part, :, start : start + count] = view(self.total)[...].astype(jnp.float32)

    def finish(self):
        for condition, copy in self.started:
            when(condition, lambda copy=copy: copy.wait_send())


def scatter_slots(along, rows, columns, order):
    left = {"z": along, "y": 2, "x": 2}
    whole = (along, 2, 2, rows, columns)
    shapes = [whole, whole]
    steps = None
    for axis in order[::-1]:
        if axis == "z":
            steps = (2, along - 1, left["y"], left["x"], rows, columns)
        left[axis] = 1
        if axis != "z":
            shapes.append((left["z"], left["y"], left["x"], rows, columns))
    return shapes + [steps]


def scatter_kernel(units, count, *refs):
    grads, outs = refs[:count], refs[count : 2 * count]
    send, recv, local = refs[2 * count : 2 * count + 3]
    slots = refs[2 * count + 3 :]
    place = Place()
    place.greet()
    scatters = []
    for at, (which, strip, order) in enumerate(units):
        total, other_core, first, second, steps = slots[5 * at : 5 * at + 5]
        scatters.append(
            Scatter(place, grads[which], outs[which], strip, outs[which].shape[-1], order,
                    (total, other_core, (first, second), steps), send.at[at], recv.at[at], local.at[at]))
    running = [scatter.stages() for scatter in scatters]
    while running:
        running = [stages for stages in running if next(stages, running) is not running]
    for scatter in scatters:
        scatter.finish()


def scatter_blocks(grads, collective_id, least):
    along, cols = lax.axis_size("row") // 2, lax.axis_size("col")
    blocks = [jax.ShapeDtypeStruct(g.shape[2:4] + (g.shape[4] // cols,), jnp.float32) for g in grads]
    units = gather_units(blocks, least)
    count = len(grads)
    slots = []
    for which, strip, order in units:
        slots += [pltpu.VMEM(shape, jnp.bfloat16) for shape in scatter_slots(along, blocks[which].shape[1], strip[2], order)]
    anywhere = pl.BlockSpec(memory_space=pl.ANY)
    return pl.pallas_call(
        functools.partial(scatter_kernel, units, count),
        out_shape=blocks,
        in_specs=[anywhere] * count,
        out_specs=[pl.BlockSpec(memory_space=pltpu.VMEM)] * count,
        scratch_shapes=[
            pltpu.SemaphoreType.DMA((len(units), 2 * along + 4)),
            pltpu.SemaphoreType.DMA((len(units), 2 * along + 4)),
            pltpu.SemaphoreType.DMA((len(units), 2)),
            *slots,
        ],
        compiler_params=pltpu.CompilerParams(
            collective_id=collective_id, has_side_effects=True, vmem_limit_bytes=60 << 20),
        cost_estimate=pl.CostEstimate(
            flops=sum(g.size for g in grads), bytes_accessed=4 * sum(g.size for g in grads), transcendentals=0),
    )(*grads)


def fast(
    frames_in, text_states, self_query, self_key, self_value, self_output, cross_query, cross_key, cross_value, cross_output,
    up_weight, down_weight, first_gain, first_bias, second_gain, second_bias, third_gain, third_bias, cotangent,
):
    row = lax.axis_index("row")
    rows, width = frames_in.shape
    half = width // 2
    piece = first_gain.shape[0]
    block_rows, block_cols = self_query.shape
    back = row % 2
    pairs = lax.axis_size("row") // 2
    forth_perm = [(2 * i, 2 * i + 1) for i in range(pairs)]
    back_perm = [(2 * i + 1, 2 * i) for i in range(pairs)]
    swap = forth_perm + back_perm

    def forth(array):
        return lax.ppermute(array, "row", forth_perm)

    def home(array):
        return lax.ppermute(array, "row", back_perm)

    def by_side(first, second):
        return jnp.where(back == 0, first, second)

    gains = jnp.zeros((1, 16, 128), jnp.bfloat16)
    gains = gains.at[0, :6, :piece].set(
        jnp.stack([first_gain, first_bias, second_gain, second_bias, third_gain, third_bias])
    )

    def small(block):
        return block.reshape(1, block_rows, block_cols)

    def flat(array):
        return array.reshape(-1, array.shape[-1])

    early = gather_blocks([small(self_query), small(self_key), small(self_value), gains], 1, 128)
    query_self, key_self, value_self = [flat(w) for w in early[:3]]
    late = gather_blocks(
        [small(self_output), small(cross_query), small(cross_key), small(cross_value), small(cross_output),
         up_weight.reshape(1, *up_weight.shape), down_weight.reshape(-1, block_rows, block_cols)], 2, 256)
    out_self, query_cross, key_cross, value_cross, out_cross, up_full, down_full = [flat(w) for w in late]
    norm_params = early[3].reshape(pairs * 2, 16, -1, 128)[:, :6, :, :piece].transpose(1, 0, 2, 3)
    norm_params = norm_params.reshape(6, width).astype(jnp.float32)

    frames = frames_in.astype(jnp.float32)
    hidden_one = norm_forward(frames, norm_params[0], norm_params[1]).astype(jnp.bfloat16)
    self_k = matmul(hidden_one, key_self).astype(jnp.bfloat16)
    self_v = matmul(hidden_one, value_self).astype(jnp.bfloat16)
    self_q = matmul(hidden_one, query_self).astype(jnp.bfloat16)
    sent_k, sent_v, sent_q = forth(self_k[:, :half]), forth(self_v[:, :half]), home(self_q[:, half:])
    near_mix, near_logs = attend(self_q, self_k, self_v, True, jnp.float32)
    far_q = by_side(sent_q, self_q[:, :half])
    far_k = by_side(self_k[:, half:], sent_k)
    far_v = by_side(self_v[:, half:], sent_v)
    far_mix, far_logs = attend(far_q, far_k, far_v, False, jnp.bfloat16)
    half_heads = half // HEAD_DIM
    far_logs = far_logs[:, :half_heads]
    near_logs = near_logs[:, : 2 * half_heads]
    far_mix = jnp.concatenate([far_mix, forth(far_mix)], axis=1)
    far_logs = by_side(-1e30, jnp.concatenate([far_logs, forth(far_logs)], axis=1))
    highest = jnp.maximum(near_logs, far_logs)
    self_logs = highest + jnp.log(jnp.exp(near_logs - highest) + jnp.exp(far_logs - highest))

    def per_feature(weights):
        return jnp.repeat(weights, HEAD_DIM, axis=1)

    self_mix = (
        near_mix * per_feature(jnp.exp(near_logs - self_logs))
        + by_side(0.0, far_mix.astype(jnp.float32)) * per_feature(jnp.exp(far_logs - self_logs))
    ).astype(jnp.bfloat16)
    resid_one = frames + matmul(self_mix, out_self)
    hidden_two = norm_forward(resid_one, norm_params[2], norm_params[3]).astype(jnp.bfloat16)
    cross_q = matmul(hidden_two, query_cross).astype(jnp.bfloat16)
    other_text = lax.ppermute(text_states, "row", swap)
    clip_text = by_side(
        jnp.concatenate([text_states, other_text]), jnp.concatenate([other_text, text_states])
    )
    text_k = matmul(clip_text, key_cross).astype(jnp.bfloat16)
    text_v = matmul(clip_text, value_cross).astype(jnp.bfloat16)
    cross_mix, cross_logs = attend(cross_q, text_k, text_v, False, jnp.bfloat16)
    cross_logs = cross_logs[:, : 2 * half_heads]
    resid_two = resid_one + matmul(cross_mix, out_cross)
    hidden_three = norm_forward(resid_two, norm_params[4], norm_params[5]).astype(jnp.bfloat16)
    layer_out, grad_three, up_grad, down_grad = feed(hidden_three, cotangent, resid_two, up_full, down_full)

    def stats_of(logs, mix, grad):
        products = mix.astype(jnp.float32) * grad.astype(jnp.float32)
        dots = jnp.sum(products.reshape(rows, -1, HEAD_DIM), axis=-1)
        both = jnp.stack([logs.T.reshape(-1, 2, rows), dots.T.reshape(-1, 2, rows)], axis=1)
        return both.reshape(-1, 4, rows)

    cotan_full = cotangent.astype(jnp.float32)
    unused_three, pull_three = jax.vjp(norm_forward, resid_two, norm_params[4], norm_params[5])
    through_three, third_gain_part, third_bias_part = pull_three(grad_three)
    grad_resid_two = cotan_full + through_three
    grad_cross = grad_resid_two.astype(jnp.bfloat16)
    cross_out_grad = over_tokens(cross_mix, grad_cross)
    grad_cross_mix = by_transposed(grad_cross, out_cross).astype(jnp.bfloat16)
    grad_cross_q, text_k_part, text_v_part = attend_back(
        cross_q, text_k, text_v, grad_cross_mix, stats_of(cross_logs, cross_mix, grad_cross_mix), False, jnp.bfloat16)
    text_rows = text_states.shape[0]
    text_parts = jnp.concatenate([text_k_part, text_v_part], axis=1)
    given = lax.ppermute(by_side(text_parts[text_rows:], text_parts[:text_rows]), "row", swap)
    kept = by_side(text_parts[:text_rows], text_parts[text_rows:])
    text_parts = (kept.astype(jnp.float32) + given.astype(jnp.float32)).astype(jnp.bfloat16)
    grad_text_k, grad_text_v = text_parts[:, :width], text_parts[:, width:]
    cross_query_part = over_tokens(hidden_two, grad_cross_q)
    cross_key_part = over_tokens(text_states, grad_text_k)
    cross_value_part = over_tokens(text_states, grad_text_v)
    text_grad = by_transposed(grad_text_k, key_cross) + by_transposed(grad_text_v, value_cross)
    grad_two = by_transposed(grad_cross_q, query_cross)
    unused_two, pull_two = jax.vjp(norm_forward, resid_one, norm_params[2], norm_params[3])
    through_two, second_gain_part, second_bias_part = pull_two(grad_two)
    grad_resid_one = grad_resid_two + through_two
    grad_self = grad_resid_one.astype(jnp.bfloat16)
    self_out_grad = over_tokens(self_mix, grad_self)
    grad_self_mix = by_transposed(grad_self, out_self).astype(jnp.bfloat16)
    stats = stats_of(self_logs, self_mix, grad_self_mix)
    far_pairs = half // 128
    sent_grad, sent_stats = home(grad_self_mix[:, half:]), home(stats[far_pairs:])
    near_dq, near_dk, near_dv = attend_back(self_q, self_k, self_v, grad_self_mix, stats, True, jnp.float32)
    far_grad = by_side(sent_grad, grad_self_mix[:, :half])
    far_stats = by_side(sent_stats, stats[:far_pairs])
    far_dq, far_dk, far_dv = attend_back(far_q, far_k, far_v, far_grad, far_stats, False, jnp.bfloat16)
    got_dq, got_dk, got_dv = forth(far_dq), home(far_dk), home(far_dv)

    def with_far(near, lower, upper):
        return (near + jnp.concatenate([lower, upper], axis=1).astype(jnp.float32)).astype(jnp.bfloat16)

    none = jnp.zeros_like(far_dq)
    grad_self_q = with_far(near_dq, by_side(none, far_dq), got_dq)
    grad_self_k = with_far(near_dk, got_dk, by_side(far_dk, none))
    grad_self_v = with_far(near_dv, got_dv, by_side(far_dv, none))
    self_query_part = over_tokens(hidden_one, grad_self_q)
    self_key_part = over_tokens(hidden_one, grad_self_k)
    self_value_part = over_tokens(hidden_one, grad_self_v)
    grad_one = (
        by_transposed(grad_self_q, query_self)
        + by_transposed(grad_self_k, key_self)
        + by_transposed(grad_self_v, value_self)
    )
    unused_one, pull_one = jax.vjp(norm_forward, frames, norm_params[0], norm_params[1])
    through_one, first_gain_part, first_bias_part = pull_one(grad_one)
    input_grad = grad_resid_one + through_one
    norm_grads = jnp.stack(
        [first_gain_part, first_bias_part, second_gain_part, second_bias_part, third_gain_part, third_bias_part]
    )
    norm_grads = norm_grads.reshape(6, 2 * pairs, -1, piece).transpose(1, 0, 2, 3)
    norm_grads = jnp.pad(norm_grads, ((0, 0), (0, 10), (0, 0), (0, 128 - piece)))

    def by_place(grad, parts):
        return grad.astype(jnp.bfloat16).reshape(pairs, 2, parts, -1, grad.shape[-1])

    early_sums = scatter_blocks(
        [by_place(g, 1) for g in (self_out_grad, cross_query_part, cross_key_part, cross_value_part, cross_out_grad, up_grad)]
        + [by_place(down_grad, down_weight.shape[0] // block_rows)], 4, 256)
    late_sums = scatter_blocks(
        [by_place(g, 1) for g in (self_query_part, self_key_part, self_value_part)]
        + [by_place(norm_grads.reshape(2 * pairs * 16, -1), 1)], 3, 128)
    norm_parts = late_sums[3][0, :6, :piece]
    sums = late_sums[:3] + early_sums
    sums = [total.reshape(-1, total.shape[-1]) for total in sums]
    return (layer_out, input_grad, text_grad, *sums, *norm_parts)


def local(*arrays):
    frames_in, self_query = arrays[0], arrays[2]
    halves = 2 * frames_in.shape[0] == FRAMES and lax.axis_size("row") % 2 == 0
    if halves and lax.axis_size("col") % 2 == 0 and self_query.shape[1] % 256 == 0 and self_query.shape[0] % 128 == 0:
        return fast(*arrays)
    return general(*arrays)


def solution(mesh):
    placed = (
        P(("col", "row"), None),
        P(("col", "row"), None),
        P("row", "col"),
        P("row", "col"),
        P("row", "col"),
        P("row", "col"),
        P("row", "col"),
        P("row", "col"),
        P("row", "col"),
        P("row", "col"),
        P("row", "col"),
        P("row", "col"),
        P(("row", "col")),
        P(("row", "col")),
        P(("row", "col")),
        P(("row", "col")),
        P(("row", "col")),
        P(("row", "col")),
        P(("col", "row"), None),
    )
    return jax.shard_map(
        local,
        mesh=mesh,
        in_specs=placed,
        out_specs=(
            P(("col", "row"), None),
            P(("col", "row"), None),
            P(("col", "row"), None),
            P("row", "col"),
            P("row", "col"),
            P("row", "col"),
            P("row", "col"),
            P("row", "col"),
            P("row", "col"),
            P("row", "col"),
            P("row", "col"),
            P("row", "col"),
            P("row", "col"),
            P(("row", "col")),
            P(("row", "col")),
            P(("row", "col")),
            P(("row", "col")),
            P(("row", "col")),
            P(("row", "col")),
        ),
        check_vma=False,
    )
```

```python
import functools
from functools import partial

import jax
import jax.numpy as jnp
from jax import lax
from jax.experimental import pallas as pl
from jax.experimental.pallas import tpu as pltpu
from jax.sharding import PartitionSpec as P

HEADS = 16
HEAD_DIM = 64
FRAMES = 1500
TEXT = 64


def norm_forward(values, norm_gain, norm_bias):
    center = values - jnp.mean(values, axis=-1, keepdims=True)
    variance = jnp.mean(center * center, axis=-1, keepdims=True)
    return center * lax.rsqrt(variance + 1e-05) * norm_gain + norm_bias


def matmul(left, right):
    return jnp.dot(left, right, preferred_element_type=jnp.float32)


def by_transposed(left, right):
    return lax.dot_general(
        left, right, (((1,), (1,)), ((), ())), preferred_element_type=jnp.float32
    )


def over_tokens(left, right):
    return lax.dot_general(
        left, right, (((0,), (0,)), ((), ())), preferred_element_type=jnp.float32
    )


def collect(blocks):
    partly = (
        lax.all_gather(blocks[0], "col", axis=1, tiled=True),
        lax.all_gather(blocks[1], "col", axis=1, tiled=True),
        lax.all_gather(blocks[2], "col", axis=1, tiled=True),
        lax.all_gather(blocks[3], "col", axis=1, tiled=True),
        lax.all_gather(blocks[4], "col", axis=1, tiled=True),
        lax.all_gather(blocks[5], "col", axis=1, tiled=True),
        lax.all_gather(blocks[6], "col", axis=1, tiled=True),
        lax.all_gather(blocks[7], "col", axis=1, tiled=True),
        lax.all_gather(blocks[8], "col", axis=1, tiled=True),
        lax.all_gather(blocks[9], "col", axis=1, tiled=True),
        lax.all_gather(blocks[10], "col", axis=1, tiled=True),
    )
    return (
        lax.all_gather(partly[0], "row", axis=0, tiled=True),
        lax.all_gather(partly[1], "row", axis=0, tiled=True),
        lax.all_gather(partly[2], "row", axis=0, tiled=True),
        lax.all_gather(partly[3], "row", axis=0, tiled=True),
        lax.all_gather(partly[4], "row", axis=0, tiled=True),
        lax.all_gather(partly[5], "row", axis=0, tiled=True),
        lax.all_gather(partly[6], "row", axis=0, tiled=True),
        lax.all_gather(partly[7], "row", axis=0, tiled=True),
        lax.all_gather(partly[8], "row", axis=0, tiled=True),
        lax.all_gather(partly[9], "row", axis=0, tiled=True),
        lax.all_gather(partly[10], "row", axis=0, tiled=True),
    )


def spread(grads):
    partly = (
        lax.psum_scatter(
            grads[0].astype(jnp.bfloat16), "row", scatter_dimension=0, tiled=True
        ).astype(jnp.float32),
        lax.psum_scatter(
            grads[1].astype(jnp.bfloat16), "row", scatter_dimension=0, tiled=True
        ).astype(jnp.float32),
        lax.psum_scatter(
            grads[2].astype(jnp.bfloat16), "row", scatter_dimension=0, tiled=True
        ).astype(jnp.float32),
        lax.psum_scatter(
            grads[3].astype(jnp.bfloat16), "row", scatter_dimension=0, tiled=True
        ).astype(jnp.float32),
        lax.psum_scatter(
            grads[4].astype(jnp.bfloat16), "row", scatter_dimension=0, tiled=True
        ).astype(jnp.float32),
        lax.psum_scatter(
            grads[5].astype(jnp.bfloat16), "row", scatter_dimension=0, tiled=True
        ).astype(jnp.float32),
        lax.psum_scatter(
            grads[6].astype(jnp.bfloat16), "row", scatter_dimension=0, tiled=True
        ).astype(jnp.float32),
        lax.psum_scatter(
            grads[7].astype(jnp.bfloat16), "row", scatter_dimension=0, tiled=True
        ).astype(jnp.float32),
        lax.psum_scatter(
            grads[8].astype(jnp.bfloat16), "row", scatter_dimension=0, tiled=True
        ).astype(jnp.float32),
        lax.psum_scatter(
            grads[9].astype(jnp.bfloat16), "row", scatter_dimension=0, tiled=True
        ).astype(jnp.float32),
        lax.psum_scatter(
            grads[10].astype(jnp.bfloat16), "row", scatter_dimension=0, tiled=True
        ).astype(jnp.float32),
    )
    return (
        lax.psum_scatter(
            partly[0].astype(jnp.bfloat16), "col", scatter_dimension=1, tiled=True
        ).astype(jnp.float32),
        lax.psum_scatter(
            partly[1].astype(jnp.bfloat16), "col", scatter_dimension=1, tiled=True
        ).astype(jnp.float32),
        lax.psum_scatter(
            partly[2].astype(jnp.bfloat16), "col", scatter_dimension=1, tiled=True
        ).astype(jnp.float32),
        lax.psum_scatter(
            partly[3].astype(jnp.bfloat16), "col", scatter_dimension=1, tiled=True
        ).astype(jnp.float32),
        lax.psum_scatter(
            partly[4].astype(jnp.bfloat16), "col", scatter_dimension=1, tiled=True
        ).astype(jnp.float32),
        lax.psum_scatter(
            partly[5].astype(jnp.bfloat16), "col", scatter_dimension=1, tiled=True
        ).astype(jnp.float32),
        lax.psum_scatter(
            partly[6].astype(jnp.bfloat16), "col", scatter_dimension=1, tiled=True
        ).astype(jnp.float32),
        lax.psum_scatter(
            partly[7].astype(jnp.bfloat16), "col", scatter_dimension=1, tiled=True
        ).astype(jnp.float32),
        lax.psum_scatter(
            partly[8].astype(jnp.bfloat16), "col", scatter_dimension=1, tiled=True
        ).astype(jnp.float32),
        lax.psum_scatter(
            partly[9].astype(jnp.bfloat16), "col", scatter_dimension=1, tiled=True
        ).astype(jnp.float32),
        lax.psum_scatter(
            partly[10].astype(jnp.bfloat16), "col", scatter_dimension=1, tiled=True
        ).astype(jnp.float32),
    )


def heads_layout(stacked):
    return lax.all_to_all(stacked, "row", split_axis=1, concat_axis=0, tiled=True)


def tokens_layout(stacked):
    return lax.all_to_all(stacked, "row", split_axis=0, concat_axis=2, tiled=True)


def by_clips(arranged, start, count, length, heads_dev):
    section = arranged[:, start : start + count]
    return section.reshape(-1, length, heads_dev, HEAD_DIM)


def causal_scores(query_clip, key_clip, causal):
    scores = jnp.einsum(
        "qhd,khd->hqk", query_clip, key_clip, preferred_element_type=jnp.float32
    ) * HEAD_DIM ** (-0.5)
    if causal:
        allowed = jnp.arange(scores.shape[1])[:, None] >= jnp.arange(scores.shape[2])[None, :]
        scores = jnp.where(allowed, scores, -1e30)
    return scores


def attend_forward(query_clips, key_clips, value_clips, causal):

    def one_clip(operands):
        query_clip, key_clip, value_clip = operands
        scores = causal_scores(query_clip, key_clip, causal)
        highest = jnp.max(scores, axis=-1, keepdims=True)
        powers = jnp.exp(scores - highest)
        totals = jnp.sum(powers, axis=-1, keepdims=True)
        weights_low = (powers / totals).astype(jnp.bfloat16)
        mixture = jnp.einsum(
            "hqk,khd->qhd", weights_low, value_clip, preferred_element_type=jnp.float32
        )
        return (mixture.astype(jnp.bfloat16), (highest + jnp.log(totals))[..., 0])

    return lax.map(one_clip, (query_clips, key_clips, value_clips))


def attend_backward(query_clips, key_clips, value_clips, log_sums, grad_clips, causal):

    def one_clip(operands):
        query_clip, key_clip, value_clip, log_clip, grad_clip = operands
        scores = causal_scores(query_clip, key_clip, causal)
        probs_full = jnp.exp(scores - log_clip[..., None])
        grad_probs = jnp.einsum(
            "qhd,khd->hqk", grad_clip, value_clip, preferred_element_type=jnp.float32
        )
        grad_value = jnp.einsum(
            "hqk,qhd->khd",
            probs_full.astype(jnp.bfloat16),
            grad_clip,
            preferred_element_type=jnp.float32,
        )
        centered = grad_probs - jnp.sum(probs_full * grad_probs, axis=-1, keepdims=True)
        grad_scores = (probs_full * centered).astype(jnp.bfloat16)
        grad_query = jnp.einsum(
            "hqk,khd->qhd", grad_scores, key_clip, preferred_element_type=jnp.float32
        ) * HEAD_DIM ** (-0.5)
        grad_key = jnp.einsum(
            "hqk,qhd->khd", grad_scores, query_clip, preferred_element_type=jnp.float32
        ) * HEAD_DIM ** (-0.5)
        return (
            grad_query.astype(jnp.bfloat16),
            grad_key.astype(jnp.bfloat16),
            grad_value.astype(jnp.bfloat16),
        )

    return lax.map(one_clip, (query_clips, key_clips, value_clips, log_sums, grad_clips))


def general(
    frames_in,
    text_states,
    self_query,
    self_key,
    self_value,
    self_output,
    cross_query,
    cross_key,
    cross_value,
    cross_output,
    up_weight,
    down_weight,
    first_gain,
    first_bias,
    second_gain,
    second_bias,
    third_gain,
    third_bias,
    cotangent,
):
    row_count = lax.axis_size("row")
    col_count = lax.axis_size("col")
    heads_dev = HEADS // row_count
    width_dev = heads_dev * HEAD_DIM
    tok_rows = frames_in.shape[0]
    text_rows = text_states.shape[0]
    piece_len = first_gain.shape[0]
    gain_block = jnp.stack(
        [first_gain, first_bias, second_gain, second_bias, third_gain, third_bias]
    ).reshape(1, 6 * piece_len)
    param_blocks = (
        self_query,
        self_key,
        self_value,
        self_output,
        cross_query,
        cross_key,
        cross_value,
        cross_output,
        up_weight,
        down_weight,
        gain_block,
    )

    def unpack_gains(gathered_gains):
        arranged = gathered_gains.reshape(row_count, col_count, 6, piece_len).transpose(2, 0, 1, 3)
        return arranged.reshape(6, row_count * col_count * piece_len).astype(jnp.float32)

    gathered = collect(param_blocks)
    (
        query_self,
        key_self,
        value_self,
        out_self,
        query_cross,
        key_cross,
        value_cross,
        out_cross,
        up_full,
        down_full,
    ) = gathered[:10]
    norm_params = unpack_gains(gathered[10])
    frames = frames_in.astype(jnp.float32)
    hidden_one = norm_forward(frames, norm_params[0], norm_params[1]).astype(jnp.bfloat16)
    self_q = matmul(hidden_one, query_self).astype(jnp.bfloat16)
    self_k = matmul(hidden_one, key_self).astype(jnp.bfloat16)
    self_v = matmul(hidden_one, value_self).astype(jnp.bfloat16)
    text_k = matmul(text_states, key_cross).astype(jnp.bfloat16)
    text_v = matmul(text_states, value_cross).astype(jnp.bfloat16)
    sent_rows = 3 * tok_rows + 2 * text_rows
    arranged = heads_layout(jnp.concatenate([self_q, self_k, self_v, text_k, text_v], axis=0))
    arranged = arranged.reshape(row_count, sent_rows, width_dev)
    query_clips = by_clips(arranged, 0, tok_rows, FRAMES, heads_dev)
    key_clips = by_clips(arranged, tok_rows, tok_rows, FRAMES, heads_dev)
    value_clips = by_clips(arranged, 2 * tok_rows, tok_rows, FRAMES, heads_dev)
    text_keys = by_clips(arranged, 3 * tok_rows, text_rows, TEXT, heads_dev)
    text_values = by_clips(arranged, 3 * tok_rows + text_rows, text_rows, TEXT, heads_dev)
    self_clips, self_logs = attend_forward(query_clips, key_clips, value_clips, True)
    self_mix = tokens_layout(self_clips.reshape(row_count, tok_rows, width_dev))[0]
    resid_one = frames + matmul(self_mix, out_self)
    hidden_two = norm_forward(resid_one, norm_params[2], norm_params[3]).astype(jnp.bfloat16)
    cross_q = matmul(hidden_two, query_cross).astype(jnp.bfloat16)
    cross_arranged = heads_layout(cross_q).reshape(row_count, tok_rows, width_dev)
    cross_queries = by_clips(cross_arranged, 0, tok_rows, FRAMES, heads_dev)
    cross_clips, cross_logs = attend_forward(cross_queries, text_keys, text_values, False)
    cross_mix = tokens_layout(cross_clips.reshape(row_count, tok_rows, width_dev))[0]
    resid_two = resid_one + matmul(cross_mix, out_cross)
    hidden_three = norm_forward(resid_two, norm_params[4], norm_params[5]).astype(jnp.bfloat16)
    pre_act = matmul(hidden_three, up_full)
    inner = jax.nn.gelu(pre_act, approximate=False).astype(jnp.bfloat16)
    layer_out = (resid_two + matmul(inner, down_full)).astype(jnp.bfloat16)
    gathered = collect(param_blocks)
    (
        query_self,
        key_self,
        value_self,
        out_self,
        query_cross,
        key_cross,
        value_cross,
        out_cross,
        up_full,
        down_full,
    ) = gathered[:10]
    norm_params = unpack_gains(gathered[10])
    cotan_full = cotangent.astype(jnp.float32)
    down_grad = over_tokens(inner, cotangent)
    grad_inner = by_transposed(cotangent, down_full)
    unused_gelu, gelu_pull = jax.vjp(partial(jax.nn.gelu, approximate=False), pre_act)
    grad_pre = gelu_pull(grad_inner)[0].astype(jnp.bfloat16)
    up_grad = over_tokens(hidden_three, grad_pre)
    grad_three = by_transposed(grad_pre, up_full)
    unused_three, pull_three = jax.vjp(norm_forward, resid_two, norm_params[4], norm_params[5])
    through_three, third_gain_part, third_bias_part = pull_three(grad_three)
    grad_resid_two = cotan_full + through_three
    grad_cross = grad_resid_two.astype(jnp.bfloat16)
    cross_out_grad = over_tokens(cross_mix, grad_cross)
    grad_cross_mix = by_transposed(grad_cross, out_cross).astype(jnp.bfloat16)
    grad_cross_arr = heads_layout(grad_cross_mix).reshape(row_count, tok_rows, width_dev)
    grad_cross_clips = by_clips(grad_cross_arr, 0, tok_rows, FRAMES, heads_dev)
    cq_clips, tk_clips, tv_clips = attend_backward(
        cross_queries, text_keys, text_values, cross_logs, grad_cross_clips, False
    )
    back_cross = jnp.concatenate(
        [
            cq_clips.reshape(row_count, tok_rows, width_dev),
            tk_clips.reshape(row_count, text_rows, width_dev),
            tv_clips.reshape(row_count, text_rows, width_dev),
        ],
        axis=1,
    )
    back_cross = tokens_layout(back_cross)[0]
    grad_cross_q = back_cross[:tok_rows]
    grad_text_k = back_cross[tok_rows : tok_rows + text_rows]
    grad_text_v = back_cross[tok_rows + text_rows :]
    cross_query_part = over_tokens(hidden_two, grad_cross_q)
    cross_key_part = over_tokens(text_states, grad_text_k)
    cross_value_part = over_tokens(text_states, grad_text_v)
    text_grad = by_transposed(grad_text_k, key_cross) + by_transposed(grad_text_v, value_cross)
    grad_two = by_transposed(grad_cross_q, query_cross)
    unused_two, pull_two = jax.vjp(norm_forward, resid_one, norm_params[2], norm_params[3])
    through_two, second_gain_part, second_bias_part = pull_two(grad_two)
    grad_resid_one = grad_resid_two + through_two
    grad_self = grad_resid_one.astype(jnp.bfloat16)
    self_out_grad = over_tokens(self_mix, grad_self)
    grad_self_mix = by_transposed(grad_self, out_self).astype(jnp.bfloat16)
    grad_self_arr = heads_layout(grad_self_mix).reshape(row_count, tok_rows, width_dev)
    grad_self_clips = by_clips(grad_self_arr, 0, tok_rows, FRAMES, heads_dev)
    sq_clips, sk_clips, sv_clips = attend_backward(
        query_clips, key_clips, value_clips, self_logs, grad_self_clips, True
    )
    back_self = jnp.concatenate(
        [
            sq_clips.reshape(row_count, tok_rows, width_dev),
            sk_clips.reshape(row_count, tok_rows, width_dev),
            sv_clips.reshape(row_count, tok_rows, width_dev),
        ],
        axis=1,
    )
    back_self = tokens_layout(back_self)[0]
    grad_self_q = back_self[:tok_rows]
    grad_self_k = back_self[tok_rows : 2 * tok_rows]
    grad_self_v = back_self[2 * tok_rows :]
    self_query_part = over_tokens(hidden_one, grad_self_q)
    self_key_part = over_tokens(hidden_one, grad_self_k)
    self_value_part = over_tokens(hidden_one, grad_self_v)
    grad_one = (
        by_transposed(grad_self_q, query_self)
        + by_transposed(grad_self_k, key_self)
        + by_transposed(grad_self_v, value_self)
    )
    unused_one, pull_one = jax.vjp(norm_forward, frames, norm_params[0], norm_params[1])
    through_one, first_gain_part, first_bias_part = pull_one(grad_one)
    input_grad = grad_resid_one + through_one
    norm_grads = jnp.stack(
        [
            first_gain_part,
            first_bias_part,
            second_gain_part,
            second_bias_part,
            third_gain_part,
            third_bias_part,
        ]
    )
    norm_grads = norm_grads.reshape(6, row_count, col_count, piece_len).transpose(1, 2, 0, 3)
    norm_grads = norm_grads.reshape(row_count, col_count * 6 * piece_len)
    summed = spread(
        (
            self_query_part,
            self_key_part,
            self_value_part,
            self_out_grad,
            cross_query_part,
            cross_key_part,
            cross_value_part,
            cross_out_grad,
            up_grad,
            down_grad,
            norm_grads,
        )
    )
    norm_parts = summed[10].reshape(6, piece_len)
    return (
        layer_out,
        input_grad,
        text_grad,
        summed[0],
        summed[1],
        summed[2],
        summed[3],
        summed[4],
        summed[5],
        summed[6],
        summed[7],
        summed[8],
        summed[9],
        norm_parts[0],
        norm_parts[1],
        norm_parts[2],
        norm_parts[3],
        norm_parts[4],
        norm_parts[5],
    )


NT=(((1,),(1,)),((),())); NN=(((1,),(0,)),((),())); TN=(((0,),(0,)),((),()))
def dg(a,b,dims): return lax.dot_general(a,b,dims,preferred_element_type=jnp.float32)

def attend_kernel(causal,tile,q_ref,k_ref,v_ref,o_ref,lse_ref):
    pair=pl.program_id(0)
    rows=q_ref.shape[0]
    low=lax.broadcasted_iota(jnp.int32,(1,128),1)<HEAD_DIM
    lane=lax.broadcasted_iota(jnp.int32,(1,128),1)
    value=v_ref[...]
    ones=jnp.ones_like(value)
    @pl.when(pair==0)
    def _(): lse_ref[...]=jnp.zeros_like(lse_ref)
    for start in range(0,rows,tile):
        n=min(tile,rows-start)
        q=q_ref[start:start+n,:]*jnp.bfloat16(HEAD_DIM**-0.5)
        mixed=[]; sums=[]
        lse=lse_ref[start:start+n,:]
        for h in range(2):
            mine=low if h==0 else jnp.logical_not(low)
            qh=jnp.where(mine,q,jnp.bfloat16(0))
            vh=jnp.where(mine,value,ones)
            if causal:
                spans=([(0,start)] if start else [])+[(start,n)]
            else: spans=[(0,k_ref.shape[0])]
            scores=[]
            for at,length in spans:
                s=dg(qh,k_ref[at:at+length,:],NT)
                if causal and at==start:
                    ok=lax.broadcasted_iota(jnp.int32,s.shape,0)>=lax.broadcasted_iota(jnp.int32,s.shape,1)
                    s=jnp.where(ok,s,-1e30)
                scores.append(s)
            top=functools.reduce(jnp.maximum,[jnp.max(s,axis=1,keepdims=True) for s in scores])
            out=None
            for (at,length),s in zip(spans,scores):
                p=jnp.exp(s-top).astype(jnp.bfloat16)
                part=dg(p,vh[at:at+length,:],NN)
                out=part if out is None else out+part
            total=out[:,HEAD_DIM:HEAD_DIM+1] if h==0 else out[:,0:1]
            mixed.append(out/total)
            lse=jnp.where(lane==2*pair+h,top+jnp.log(total),lse)
        lse_ref[start:start+n,:]=lse
        o_ref[start:start+n,:]=jnp.where(low,mixed[0],mixed[1]).astype(o_ref.dtype)

def attend(q,k,v,causal,out_dtype,tile=256):
    rows,width=q.shape; keys=k.shape[0]
    return pl.pallas_call(functools.partial(attend_kernel,causal,tile),grid=(width//128,),
        in_specs=[pl.BlockSpec((rows,128),lambda i:(0,i)),pl.BlockSpec((keys,128),lambda i:(0,i)),pl.BlockSpec((keys,128),lambda i:(0,i))],
        out_specs=[pl.BlockSpec((rows,128),lambda i:(0,i)),pl.BlockSpec((rows,128),lambda i:(0,0))],
        out_shape=[jax.ShapeDtypeStruct((rows,width),out_dtype),jax.ShapeDtypeStruct((rows,128),jnp.float32)],
        compiler_params=pltpu.CompilerParams(vmem_limit_bytes=40<<20),
        cost_estimate=pl.CostEstimate(flops=4*rows*keys*width,bytes_accessed=8*rows*width,transcendentals=rows*keys*width//64))(q,k,v)

def attend_back_kernel(causal,tile,q_ref,k_ref,v_ref,do_ref,st_ref,dq_ref,dk_ref,dv_ref,acc):
    rows=q_ref.shape[0]; keys=k_ref.shape[0]
    low=lax.broadcasted_iota(jnp.int32,(1,128),1)<HEAD_DIM
    acc[...]=jnp.zeros_like(acc)
    for start in range(0,keys,tile):
        n=min(tile,keys-start)
        k=k_ref[start:start+n,:]*jnp.bfloat16(HEAD_DIM**-0.5)
        v=v_ref[start:start+n,:]
        spans=[(0,rows)]
        if causal: spans=[(start,n)]+([(start+n,rows-start-n)] if start+n<rows else [])
        dks=[];dvs=[]
        for h in range(2):
            mine=low if h==0 else jnp.logical_not(low)
            kh=jnp.where(mine,k,jnp.bfloat16(0)); vh=jnp.where(mine,v,jnp.bfloat16(0))
            dk=dv=None
            for at,length in spans:
                qs=q_ref[at:at+length,:]; do=do_ref[at:at+length,:]
                s=dg(kh,qs,NT)
                p=jnp.exp(s-st_ref[0,h:h+1,at:at+length])
                if causal and at==start:
                    ok=lax.broadcasted_iota(jnp.int32,s.shape,0)<=lax.broadcasted_iota(jnp.int32,s.shape,1)
                    p=jnp.where(ok,p,0.0)
                dp=dg(vh,do,NT)
                ds=(p*(dp-st_ref[0,2+h:3+h,at:at+length])).astype(jnp.bfloat16)
                a=dg(p.astype(jnp.bfloat16),do,NN); b=dg(ds,qs,NN)
                dv=a if dv is None else dv+a
                dk=b if dk is None else dk+b
                acc[at:at+length,:]+=dg(ds,kh,TN)
            dks.append(dk);dvs.append(dv)
        dk_ref[start:start+n,:]=(jnp.where(low,dks[0],dks[1])*HEAD_DIM**-0.5).astype(dk_ref.dtype)
        dv_ref[start:start+n,:]=jnp.where(low,dvs[0],dvs[1]).astype(dv_ref.dtype)
    dq_ref[...]=acc[...].astype(dq_ref.dtype)

def attend_back(q,k,v,do,stats,causal,out_dtype,tile=256):
    rows,width=q.shape; keys=k.shape[0]
    bq=pl.BlockSpec((rows,128),lambda i:(0,i)); bk=pl.BlockSpec((keys,128),lambda i:(0,i))
    return pl.pallas_call(functools.partial(attend_back_kernel,causal,tile),grid=(width//128,),
        in_specs=[bq,bk,bk,bq,pl.BlockSpec((1,4,rows),lambda i:(i,0,0))],out_specs=[bq,bk,bk],
        out_shape=[jax.ShapeDtypeStruct((rows,width),out_dtype),jax.ShapeDtypeStruct((keys,width),out_dtype),jax.ShapeDtypeStruct((keys,width),out_dtype)],
        scratch_shapes=[pltpu.VMEM((rows,128),jnp.float32)],
        compiler_params=pltpu.CompilerParams(vmem_limit_bytes=40<<20),
        cost_estimate=pl.CostEstimate(flops=10*rows*keys*width,bytes_accessed=16*rows*width,transcendentals=rows*keys*width//64))(q,k,v,do,stats)

def feed_kernel(h_ref,cot_ref,res_ref,up_ref,down_ref,out_ref,g_ref,dup_ref,ddown_ref,acc):
    i=pl.program_id(0)
    @pl.when(i==0)
    def _():
        acc[...]=res_ref[...]
        g_ref[...]=jnp.zeros_like(g_ref)
    h=h_ref[...]
    up=up_ref[:,0].reshape(h.shape[1],-1)
    blocks,wide=down_ref.shape[1],down_ref.shape[3]
    pre=dg(h,up,NN)
    cdf=0.5*(1.0+lax.erf(pre*0.7071067811865476))
    inner=(pre*cdf).astype(jnp.bfloat16)
    slope=cdf+pre*(jnp.exp(-0.5*pre*pre)*0.3989422804014327)
    grad=None
    for at in range(blocks):
        columns=slice(at*wide,(at+1)*wide)
        cot=cot_ref[:,columns]
        acc[:,columns]+=dg(inner,down_ref[0,at],NN)
        ddown_ref[0,at]=dg(inner,cot,TN).astype(ddown_ref.dtype)
        part=dg(cot,down_ref[0,at],NT)
        grad=part if grad is None else grad+part
    gpre=(grad*slope).astype(jnp.bfloat16)
    dup_ref[:,0]=dg(h,gpre,TN).astype(dup_ref.dtype).reshape(dup_ref.shape[0],dup_ref.shape[2],dup_ref.shape[3])
    g_ref[...]+=dg(gpre,up,NT)
    @pl.when(i==pl.num_programs(0)-1)
    def _(): out_ref[...]=acc[...].astype(out_ref.dtype)

def feed(h,cot,res,up,down):
    rows,d=h.shape; chunk=down.shape[2]; strips=up.shape[3]//chunk; ff=down.shape[0]*chunk
    whole=pl.BlockSpec((rows,d),lambda i:(0,0))
    up_spec=pl.BlockSpec((up.shape[0],1,up.shape[2],chunk),lambda i:(0,i//strips,0,i%strips))
    down_spec=pl.BlockSpec((1,)+down.shape[1:],lambda i:(i,0,0,0))
    return pl.pallas_call(feed_kernel,grid=(ff//chunk,),
        in_specs=[whole,whole,whole,up_spec,down_spec],
        out_specs=[whole,whole,up_spec,down_spec],
        out_shape=[jax.ShapeDtypeStruct((rows,d),jnp.bfloat16),jax.ShapeDtypeStruct((rows,d),jnp.float32),jax.ShapeDtypeStruct(up.shape,jnp.bfloat16),jax.ShapeDtypeStruct(down.shape,jnp.bfloat16)],
        scratch_shapes=[pltpu.VMEM((rows,d),jnp.float32)],
        compiler_params=pltpu.CompilerParams(vmem_limit_bytes=56<<20),
        cost_estimate=pl.CostEstimate(flops=12*rows*d*ff,bytes_accessed=8*d*ff+16*rows*d,transcendentals=2*rows*ff))(h,cot,res,up,down)


MESH = pl.DeviceIdType.MESH
ORDERS = ("xzy", "yzx", "xzy", "yzx", "zxy", "zyx")


class Place:
    def __init__(self):
        row, col = lax.axis_index("row"), lax.axis_index("col")
        self.z, self.y, self.x, self.k = row // 2, row % 2, col // 2, col % 2
        self.along = lax.axis_size("row") // 2

    def device(self, dz=0, y=False, x=False, k=False):
        other_y = 1 - self.y if y else self.y
        other_x = 1 - self.x if x else self.x
        other_k = 1 - self.k if k else self.k
        return ((self.z + dz) * 2 + other_y, other_x * 2 + other_k)

    def across(self, axis):
        return self.device(y=axis == "y", x=axis == "x", k=axis == "k")

    def greet(self):
        barrier = pltpu.get_barrier_semaphore()
        for axis in "xyk":
            pl.semaphore_signal(barrier, inc=1, device_id=self.across(axis), device_id_type=MESH)

        @pl.when(self.z > 0)
        def _():
            pl.semaphore_signal(barrier, inc=1, device_id=self.device(dz=-1), device_id_type=MESH)

        @pl.when(self.z + 1 < self.along)
        def _():
            pl.semaphore_signal(barrier, inc=1, device_id=self.device(dz=1), device_id_type=MESH)

        below = jnp.where(self.z > 0, 1, 0)
        above = jnp.where(self.z + 1 < self.along, 1, 0)
        pl.semaphore_wait(barrier, 3 + below + above)


def when(condition, run):
    if condition is None:
        run()
    else:
        pl.when(condition)(run)


def in_turn(units, lag):
    ready = [(lag * at, at) for at in range(len(units))]
    while ready:
        turn, at = min(ready)
        ready.remove((turn, at))
        if next(units[at], units) is not units:
            ready.append((turn + 1, at))
        yield


class Gather:
    def __init__(self, place, block, full, strip, order, send, recv):
        self.place, self.block, self.full, self.strip = place, block, full, strip
        turn = order.index("z")
        self.before, self.after = order[:turn], order[turn + 1 :]
        self.send, self.recv, self.used, self.sent, self.started = send, recv, 0, 0, []

    def region(self, z, y, x):
        part, start, count = self.strip
        column = (x * 2 + self.place.k) * self.block.shape[-1] + start
        return self.full.at[z, y, part, :, pl.ds(pl.multiple_of(column, 128), count)]

    def held(self, done, z):
        y = slice(None) if "y" in done else self.place.y
        return [self.region(z, y, x) for x in (range(2) if "x" in done else [self.place.x])]

    def pairs(self, done, z, first):
        if first:
            part, start, count = self.strip
            place = self.place
            return [(self.block.at[part, :, pl.ds(start, count)], self.region(place.z, place.y, place.x))]
        return [(region, region) for region in self.held(done, z)]

    def semaphore(self):
        self.used += 2
        return self.used - 2

    def copies(self, device, pairs, semaphore, send=0):
        return [
            pltpu.make_async_remote_copy(
                src_ref=source, dst_ref=target, send_sem=self.send.at[send + at],
                recv_sem=self.recv.at[semaphore + at], device_id=device, device_id_type=MESH)
            for at, (source, target) in enumerate(pairs)
        ]

    def start(self, device, pairs, condition, semaphore):
        copies = self.copies(device, pairs, semaphore, self.sent)
        self.sent += len(copies)
        when(condition, lambda: [copy.start() for copy in copies] and None)
        self.started.append((condition, copies))
        return condition, copies

    def arrive(self, sent):
        condition, copies = sent
        when(condition, lambda: [copy.wait_recv() for copy in copies] and None)

    def stages(self):
        place, along = self.place, self.place.along
        done = []
        for axis in self.before:
            sent = self.start(place.across(axis), self.pairs(done, place.z, not done), None, self.semaphore())
            yield
            self.arrive(sent)
            done.append(axis)
        first = not done
        from_left = [self.semaphore() for _ in range(along - 1)]
        from_right = [self.semaphore() for _ in range(along - 1)]

        def pass_on(turn, step):
            axes = done + list(self.after[:turn])
            device = place.across(self.after[turn])
            if step == 0:
                return turn, step, [self.start(device, self.pairs(axes, place.z, not axes), None, self.semaphore())]
            return turn, step, [
                self.start(device, self.pairs(axes, z, False), (z >= 0) & (z < along), self.semaphore())
                for z in (place.z - step, place.z + step)
            ]

        def step_out(step):
            left, right = place.z - (step - 1), place.z + (step - 1)
            self.start(place.device(dz=1), self.pairs(done, left, first and step == 1),
                       (left >= 0) & (place.z + 1 < along), from_left[step - 1])
            self.start(place.device(dz=-1), self.pairs(done, right, first and step == 1),
                       (right < along) & (place.z > 0), from_right[step - 1])

        def step_in(step):
            for z, semaphore in ((place.z - step, from_left), (place.z + step, from_right)):
                copies = self.copies(place.across("k"), self.pairs(done, z, False), semaphore[step - 1])
                self.arrive(((z >= 0) & (z < along), copies))

        step_out(1)
        waiting = [pass_on(0, 0)] if self.after else []
        for step in range(1, along + len(self.after)):
            yield
            if step < along:
                step_in(step)
                if step + 1 < along:
                    step_out(step + 1)
            following = []
            for turn, at, sent in waiting:
                for one in sent:
                    self.arrive(one)
                if turn + 1 < len(self.after):
                    following.append(pass_on(turn + 1, at))
            if self.after and step < along:
                following.append(pass_on(0, step))
            waiting = following
        everything = [self.region(slice(None), slice(None), x) for x in range(2)]
        sent = self.start(place.across("k"), [(r, r) for r in everything], None, self.semaphore())
        yield
        self.arrive(sent)

    def finish(self):
        for condition, copies in self.started:
            when(condition, lambda copies=copies: [copy.wait_send() for copy in copies] and None)


def gather_kernel(units, count, *refs):
    blocks, fulls = refs[:count], refs[count : 2 * count]
    send, recv, local_sem = refs[2 * count :]
    place = Place()
    place.greet()
    own = []
    for at, (block, full) in enumerate(zip(blocks, fulls)):
        width = block.shape[-1]
        columns = pl.ds(pl.multiple_of((place.x * 2 + place.k) * width, 128), width)
        copy = pltpu.make_async_copy(block, full.at[place.z, place.y, :, :, columns], local_sem.at[at])
        copy.start()
        own.append(copy)
    gathers = [
        Gather(place, blocks[which], fulls[which], strip, order, send.at[at], recv.at[at])
        for at, (which, strip, order) in enumerate(units)
    ]
    for unused in in_turn([gather.stages() for gather in gathers], 0.0):
        while own:
            own.pop().wait()
    for gather in gathers:
        gather.finish()


def gather_units(blocks, least):
    strips = []
    for which, block in enumerate(blocks):
        wide = min(least, block.shape[-1])
        for part in range(block.shape[0]):
            for start in range(0, block.shape[-1], wide):
                strips.append((which, (part, start, wide)))
    return [strip + (ORDERS[at % len(ORDERS)],) for at, strip in enumerate(strips)]


def gather_blocks(blocks, collective_id, least):
    along, cols = lax.axis_size("row") // 2, lax.axis_size("col")
    units = gather_units(blocks, least)
    count = len(blocks)
    anywhere = pl.BlockSpec(memory_space=pl.ANY)
    moved = sum(block.size for block in blocks) * 2 * along * 2 * cols
    return pl.pallas_call(
        functools.partial(gather_kernel, units, count),
        out_shape=[
            jax.ShapeDtypeStruct((along, 2) + b.shape[:2] + (cols * b.shape[2],), b.dtype) for b in blocks
        ],
        in_specs=[anywhere] * count,
        out_specs=[anywhere] * count,
        scratch_shapes=[
            pltpu.SemaphoreType.DMA((len(units), 8 * along)),
            pltpu.SemaphoreType.DMA((len(units), 12 * along)),
            pltpu.SemaphoreType.DMA((count,)),
        ],
        compiler_params=pltpu.CompilerParams(collective_id=collective_id, has_side_effects=True),
        cost_estimate=pl.CostEstimate(flops=0, bytes_accessed=2 * moved, transcendentals=0),
    )(*blocks)


def add_blocks(total, extra, leading):
    def one(at, unused):
        place = []
        for size in leading[::-1]:
            place.append(at % size)
            at = at // size
        place = tuple(place[::-1])
        total[place] = total[place] + extra[place]
        return unused

    if not leading:
        total[...] = total[...] + extra[...]
        return
    count = 1
    for size in leading:
        count *= size
    lax.fori_loop(0, count, one, 0)


class Scatter:
    def __init__(self, place, grad, out, strip, width, order, slots, send, recv, local):
        self.place, self.grad, self.out, self.strip, self.width = place, grad, out, strip, width
        self.order = order[::-1]
        self.total, self.other_core, self.halves, self.steps = slots
        self.send, self.recv, self.local = send, recv, local
        self.used, self.started = 0, []

    def region(self, x, k):
        part, start, count = self.strip
        column = (x * 2 + k) * self.width + start
        return self.grad.at[:, :, part, :, pl.ds(pl.multiple_of(column, 128), count)]

    def copy(self, device, source, target, semaphore=None):
        if semaphore is None:
            semaphore = self.used
            self.used += 1
        return pltpu.make_async_remote_copy(
            src_ref=source, dst_ref=target, send_sem=self.send.at[semaphore], recv_sem=self.recv.at[semaphore],
            device_id=device, device_id_type=MESH)

    def start(self, copy, condition=None):
        when(condition, lambda: copy.start())
        self.started.append((condition, copy))

    def stages(self):
        place, along = self.place, self.place.along
        rows, columns = self.total.shape[-2:]
        own = [
            pltpu.make_async_copy(self.region(x, place.k), self.total.at[:, :, x], self.local.at[x]) for x in range(2)
        ]
        swapped = [
            self.copy(place.across("k"), self.region(x, 1 - place.k), self.other_core.at[:, :, x]) for x in range(2)
        ]
        for copy in own:
            copy.start()
        for copy in swapped:
            self.start(copy)
        yield
        for copy in own:
            copy.wait()
        for copy in swapped:
            copy.wait_recv()
        add_blocks(self.total, self.other_core, (along, 2, 2))
        left = {"z": slice(None), "y": slice(None), "x": slice(None)}
        at = {"y": place.y, "x": place.x}

        def view(ref, **places):
            return ref.at[tuple({**left, **places}[axis] for axis in "zyx")]

        def sizes():
            return tuple(size for axis, size in zip("zyx", (along, 2, 2)) if isinstance(left[axis], slice))

        exchanges = 0
        for axis in self.order:
            if axis == "z":
                shape = tuple(2 for name in "yx" if isinstance(left[name], slice))
                landing = self.steps.at[(slice(None),) * 2 + tuple(slice(None) if isinstance(left[name], slice) else 0 for name in "yx")]
                right, leftward = [self.used + at for at in range(along)], [self.used + along + at for at in range(along)]
                self.used += 2 * along
                for step in range(along):
                    if step:
                        yield
                    for way, names, first in ((1, right, place.z), (-1, leftward, along - 1 - place.z)):
                        goal = along - 1 - step + place.z if way == 1 else step - along + 1 + place.z
                        side = 0 if way == 1 else 1
                        if step:
                            arrived = self.copy(
                                place.across("k"), landing.at[side, step - 1], landing.at[side, step - 1], names[step - 1])

                            def take(arrived=arrived, goal=goal, side=side, step=step):
                                arrived.wait_recv()
                                add_blocks(view(self.total, z=goal), landing.at[side, step - 1], shape)

                            pl.when((first >= 1) & (first <= step))(take)
                        if step < along - 1:
                            onward = self.copy(
                                place.device(dz=way), view(self.total, z=jnp.clip(goal, 0, along - 1)), landing.at[side, step], names[step])
                            self.start(onward, (first <= step) & (first < along - 1))
                left["z"] = place.z
            else:
                landing = self.halves[exchanges]
                exchanges += 1
                target = landing.at[tuple(slice(None) if isinstance(left[name], slice) and name != axis else 0 for name in "zyx")]
                swap = self.copy(place.across(axis), view(self.total, **{axis: 1 - at[axis]}), target)
                self.start(swap)
                yield
                swap.wait_recv()
                left[axis] = at[axis]
                add_blocks(view(self.total), target, sizes())
        part, start, count = self.strip
        self.out[part, :, start : start + count] = view(self.total)[...].astype(jnp.float32)

    def finish(self):
        for condition, copy in self.started:
            when(condition, lambda copy=copy: copy.wait_send())


def scatter_slots(along, rows, columns, order):
    left = {"z": along, "y": 2, "x": 2}
    whole = (along, 2, 2, rows, columns)
    shapes = [whole, whole]
    steps = None
    for axis in order[::-1]:
        if axis == "z":
            steps = (2, along - 1, left["y"], left["x"], rows, columns)
        left[axis] = 1
        if axis != "z":
            shapes.append((left["z"], left["y"], left["x"], rows, columns))
    return shapes + [steps]


def scatter_kernel(units, count, *refs):
    grads, outs = refs[:count], refs[count : 2 * count]
    send, recv, local = refs[2 * count : 2 * count + 3]
    slots = refs[2 * count + 3 :]
    place = Place()
    place.greet()
    scatters = []
    for at, (which, strip, order) in enumerate(units):
        total, other_core, first, second, steps = slots[5 * at : 5 * at + 5]
        scatters.append(
            Scatter(place, grads[which], outs[which], strip, outs[which].shape[-1], order,
                    (total, other_core, (first, second), steps), send.at[at], recv.at[at], local.at[at]))
    for unused in in_turn([scatter.stages() for scatter in scatters], 0.5):
        pass
    for scatter in scatters:
        scatter.finish()


def scatter_blocks(grads, collective_id, least):
    along, cols = lax.axis_size("row") // 2, lax.axis_size("col")
    blocks = [jax.ShapeDtypeStruct(g.shape[2:4] + (g.shape[4] // cols,), jnp.float32) for g in grads]
    units = gather_units(blocks, least)
    count = len(grads)
    slots = []
    for which, strip, order in units:
        slots += [pltpu.VMEM(shape, jnp.bfloat16) for shape in scatter_slots(along, blocks[which].shape[1], strip[2], order)]
    anywhere = pl.BlockSpec(memory_space=pl.ANY)
    return pl.pallas_call(
        functools.partial(scatter_kernel, units, count),
        out_shape=blocks,
        in_specs=[anywhere] * count,
        out_specs=[pl.BlockSpec(memory_space=pltpu.VMEM)] * count,
        scratch_shapes=[
            pltpu.SemaphoreType.DMA((len(units), 2 * along + 4)),
            pltpu.SemaphoreType.DMA((len(units), 2 * along + 4)),
            pltpu.SemaphoreType.DMA((len(units), 2)),
            *slots,
        ],
        compiler_params=pltpu.CompilerParams(
            collective_id=collective_id, has_side_effects=True, vmem_limit_bytes=60 << 20),
        cost_estimate=pl.CostEstimate(
            flops=sum(g.size for g in grads), bytes_accessed=4 * sum(g.size for g in grads), transcendentals=0),
    )(*grads)


def fast(
    frames_in, text_states, self_query, self_key, self_value, self_output, cross_query, cross_key, cross_value, cross_output,
    up_weight, down_weight, first_gain, first_bias, second_gain, second_bias, third_gain, third_bias, cotangent,
):
    row = lax.axis_index("row")
    rows, width = frames_in.shape
    half = width // 2
    piece = first_gain.shape[0]
    block_rows, block_cols = self_query.shape
    back = row % 2
    pairs = lax.axis_size("row") // 2
    forth_perm = [(2 * i, 2 * i + 1) for i in range(pairs)]
    back_perm = [(2 * i + 1, 2 * i) for i in range(pairs)]
    swap = forth_perm + back_perm

    def forth(array):
        return lax.ppermute(array, "row", forth_perm)

    def home(array):
        return lax.ppermute(array, "row", back_perm)

    def by_side(first, second):
        return jnp.where(back == 0, first, second)

    gains = jnp.zeros((1, 16, 128), jnp.bfloat16)
    gains = gains.at[0, :6, :piece].set(
        jnp.stack([first_gain, first_bias, second_gain, second_bias, third_gain, third_bias])
    )

    everyone = ("row", "col")
    places = (lax.axis_size("row"), lax.axis_size("col"))
    up_blocks = lax.all_gather(up_weight, everyone).reshape(*places, *up_weight.shape)
    down_blocks = lax.all_gather(down_weight, everyone).reshape(*places, *down_weight.shape)

    def small(block):
        return block.reshape(1, block_rows, block_cols)

    def flat(array):
        return array.reshape(-1, array.shape[-1])

    early = gather_blocks([small(self_query), small(self_key), small(self_value), gains], 1, 128)
    query_self, key_self, value_self = [flat(w) for w in early[:3]]
    late = gather_blocks(
        [small(self_output), small(cross_query), small(cross_key), small(cross_value), small(cross_output)],
        2, 128)
    out_self, query_cross, key_cross, value_cross, out_cross = [flat(w) for w in late]
    norm_params = early[3].reshape(pairs * 2, 16, -1, 128)[:, :6, :, :piece].transpose(1, 0, 2, 3)
    norm_params = norm_params.reshape(6, width).astype(jnp.float32)

    frames = frames_in.astype(jnp.float32)
    hidden_one = norm_forward(frames, norm_params[0], norm_params[1]).astype(jnp.bfloat16)
    self_k = matmul(hidden_one, key_self).astype(jnp.bfloat16)
    self_v = matmul(hidden_one, value_self).astype(jnp.bfloat16)
    self_q = matmul(hidden_one, query_self).astype(jnp.bfloat16)
    sent_k, sent_v, sent_q = forth(self_k[:, :half]), forth(self_v[:, :half]), home(self_q[:, half:])
    near_mix, near_logs = attend(self_q, self_k, self_v, True, jnp.float32)
    far_q = by_side(sent_q, self_q[:, :half])
    far_k = by_side(self_k[:, half:], sent_k)
    far_v = by_side(self_v[:, half:], sent_v)
    far_mix, far_logs = attend(far_q, far_k, far_v, False, jnp.bfloat16)
    half_heads = half // HEAD_DIM
    far_logs = far_logs[:, :half_heads]
    near_logs = near_logs[:, : 2 * half_heads]
    far_mix = jnp.concatenate([far_mix, forth(far_mix)], axis=1)
    far_logs = by_side(-1e30, jnp.concatenate([far_logs, forth(far_logs)], axis=1))
    highest = jnp.maximum(near_logs, far_logs)
    self_logs = highest + jnp.log(jnp.exp(near_logs - highest) + jnp.exp(far_logs - highest))

    def per_feature(weights):
        return jnp.repeat(weights, HEAD_DIM, axis=1)

    self_mix = (
        near_mix * per_feature(jnp.exp(near_logs - self_logs))
        + by_side(0.0, far_mix.astype(jnp.float32)) * per_feature(jnp.exp(far_logs - self_logs))
    ).astype(jnp.bfloat16)
    resid_one = frames + matmul(self_mix, out_self)
    hidden_two = norm_forward(resid_one, norm_params[2], norm_params[3]).astype(jnp.bfloat16)
    cross_q = matmul(hidden_two, query_cross).astype(jnp.bfloat16)
    other_text = lax.ppermute(text_states, "row", swap)
    clip_text = by_side(
        jnp.concatenate([text_states, other_text]), jnp.concatenate([other_text, text_states])
    )
    text_k = matmul(clip_text, key_cross).astype(jnp.bfloat16)
    text_v = matmul(clip_text, value_cross).astype(jnp.bfloat16)
    cross_mix, cross_logs = attend(cross_q, text_k, text_v, False, jnp.bfloat16)
    cross_logs = cross_logs[:, : 2 * half_heads]
    resid_two = resid_one + matmul(cross_mix, out_cross)
    hidden_three = norm_forward(resid_two, norm_params[4], norm_params[5]).astype(jnp.bfloat16)
    layer_out, grad_three, up_grad, down_grad = feed(hidden_three, cotangent, resid_two, up_blocks, down_blocks)
    up_sum, down_sum = [
        lax.psum_scatter(g.reshape(-1, *g.shape[2:]), everyone, scatter_dimension=0).astype(jnp.float32)
        for g in (up_grad, down_grad)
    ]

    def stats_of(logs, mix, grad):
        products = mix.astype(jnp.float32) * grad.astype(jnp.float32)
        dots = jnp.sum(products.reshape(rows, -1, HEAD_DIM), axis=-1)
        both = jnp.stack([logs.T.reshape(-1, 2, rows), dots.T.reshape(-1, 2, rows)], axis=1)
        return both.reshape(-1, 4, rows)

    cotan_full = cotangent.astype(jnp.float32)
    unused_three, pull_three = jax.vjp(norm_forward, resid_two, norm_params[4], norm_params[5])
    through_three, third_gain_part, third_bias_part = pull_three(grad_three)
    grad_resid_two = cotan_full + through_three
    grad_cross = grad_resid_two.astype(jnp.bfloat16)
    cross_out_grad = over_tokens(cross_mix, grad_cross)
    grad_cross_mix = by_transposed(grad_cross, out_cross).astype(jnp.bfloat16)
    grad_cross_q, text_k_part, text_v_part = attend_back(
        cross_q, text_k, text_v, grad_cross_mix, stats_of(cross_logs, cross_mix, grad_cross_mix), False, jnp.bfloat16)
    text_rows = text_states.shape[0]
    text_parts = jnp.concatenate([text_k_part, text_v_part], axis=1)
    given = lax.ppermute(by_side(text_parts[text_rows:], text_parts[:text_rows]), "row", swap)
    kept = by_side(text_parts[:text_rows], text_parts[text_rows:])
    text_parts = (kept.astype(jnp.float32) + given.astype(jnp.float32)).astype(jnp.bfloat16)
    grad_text_k, grad_text_v = text_parts[:, :width], text_parts[:, width:]
    cross_query_part = over_tokens(hidden_two, grad_cross_q)
    cross_key_part = over_tokens(text_states, grad_text_k)
    cross_value_part = over_tokens(text_states, grad_text_v)
    text_grad = by_transposed(grad_text_k, key_cross) + by_transposed(grad_text_v, value_cross)
    grad_two = by_transposed(grad_cross_q, query_cross)
    unused_two, pull_two = jax.vjp(norm_forward, resid_one, norm_params[2], norm_params[3])
    through_two, second_gain_part, second_bias_part = pull_two(grad_two)
    grad_resid_one = grad_resid_two + through_two
    grad_self = grad_resid_one.astype(jnp.bfloat16)
    self_out_grad = over_tokens(self_mix, grad_self)
    grad_self_mix = by_transposed(grad_self, out_self).astype(jnp.bfloat16)
    stats = stats_of(self_logs, self_mix, grad_self_mix)
    far_pairs = half // 128
    sent_grad, sent_stats = home(grad_self_mix[:, half:]), home(stats[far_pairs:])
    near_dq, near_dk, near_dv = attend_back(self_q, self_k, self_v, grad_self_mix, stats, True, jnp.float32)
    far_grad = by_side(sent_grad, grad_self_mix[:, :half])
    far_stats = by_side(sent_stats, stats[:far_pairs])
    far_dq, far_dk, far_dv = attend_back(far_q, far_k, far_v, far_grad, far_stats, False, jnp.bfloat16)
    got_dq, got_dk, got_dv = forth(far_dq), home(far_dk), home(far_dv)

    def with_far(near, lower, upper):
        return (near + jnp.concatenate([lower, upper], axis=1).astype(jnp.float32)).astype(jnp.bfloat16)

    none = jnp.zeros_like(far_dq)
    grad_self_q = with_far(near_dq, by_side(none, far_dq), got_dq)
    grad_self_k = with_far(near_dk, got_dk, by_side(far_dk, none))
    grad_self_v = with_far(near_dv, got_dv, by_side(far_dv, none))
    self_query_part = over_tokens(hidden_one, grad_self_q)
    self_key_part = over_tokens(hidden_one, grad_self_k)
    self_value_part = over_tokens(hidden_one, grad_self_v)
    grad_one = (
        by_transposed(grad_self_q, query_self)
        + by_transposed(grad_self_k, key_self)
        + by_transposed(grad_self_v, value_self)
    )
    unused_one, pull_one = jax.vjp(norm_forward, frames, norm_params[0], norm_params[1])
    through_one, first_gain_part, first_bias_part = pull_one(grad_one)
    input_grad = grad_resid_one + through_one
    norm_grads = jnp.stack(
        [first_gain_part, first_bias_part, second_gain_part, second_bias_part, third_gain_part, third_bias_part]
    )
    norm_grads = norm_grads.reshape(6, 2 * pairs, -1, piece).transpose(1, 0, 2, 3)
    norm_grads = jnp.pad(norm_grads, ((0, 0), (0, 10), (0, 0), (0, 128 - piece)))

    def by_place(grad, parts):
        return grad.astype(jnp.bfloat16).reshape(pairs, 2, parts, -1, grad.shape[-1])

    early_sums = scatter_blocks(
        [by_place(g, 1) for g in (self_out_grad, cross_query_part, cross_key_part, cross_value_part, cross_out_grad)], 4, 128)
    late_sums = scatter_blocks(
        [by_place(g, 1) for g in (self_query_part, self_key_part, self_value_part)]
        + [by_place(norm_grads.reshape(2 * pairs * 16, -1), 1)], 3, 128)
    norm_parts = late_sums[3][0, :6, :piece]
    sums = late_sums[:3] + early_sums
    sums = [total.reshape(-1, total.shape[-1]) for total in sums]
    return (layer_out, input_grad, text_grad, *sums, up_sum, down_sum, *norm_parts)


def local(*arrays):
    frames_in, self_query = arrays[0], arrays[2]
    halves = 2 * frames_in.shape[0] == FRAMES and lax.axis_size("row") % 2 == 0
    if halves and lax.axis_size("col") % 2 == 0 and self_query.shape[1] % 256 == 0 and self_query.shape[0] % 128 == 0:
        return fast(*arrays)
    return general(*arrays)


def solution(mesh):
    placed = (
        P(("col", "row"), None),
        P(("col", "row"), None),
        P("row", "col"),
        P("row", "col"),
        P("row", "col"),
        P("row", "col"),
        P("row", "col"),
        P("row", "col"),
        P("row", "col"),
        P("row", "col"),
        P("row", "col"),
        P("row", "col"),
        P(("row", "col")),
        P(("row", "col")),
        P(("row", "col")),
        P(("row", "col")),
        P(("row", "col")),
        P(("row", "col")),
        P(("col", "row"), None),
    )
    return jax.shard_map(
        local,
        mesh=mesh,
        in_specs=placed,
        out_specs=(
            P(("col", "row"), None),
            P(("col", "row"), None),
            P(("col", "row"), None),
            P("row", "col"),
            P("row", "col"),
            P("row", "col"),
            P("row", "col"),
            P("row", "col"),
            P("row", "col"),
            P("row", "col"),
            P("row", "col"),
            P("row", "col"),
            P("row", "col"),
            P(("row", "col")),
            P(("row", "col")),
            P(("row", "col")),
            P(("row", "col")),
            P(("row", "col")),
            P(("row", "col")),
        ),
        check_vma=False,
    )
```

```python
import functools
from functools import partial

import jax
import jax.numpy as jnp
from jax import lax
from jax.experimental import pallas as pl
from jax.experimental.pallas import tpu as pltpu
from jax.sharding import PartitionSpec as P

HEADS = 16
HEAD_DIM = 64
FRAMES = 1500
TEXT = 64


def norm_forward(values, norm_gain, norm_bias):
    center = values - jnp.mean(values, axis=-1, keepdims=True)
    variance = jnp.mean(center * center, axis=-1, keepdims=True)
    return center * lax.rsqrt(variance + 1e-05) * norm_gain + norm_bias


def matmul(left, right):
    return jnp.dot(left, right, preferred_element_type=jnp.float32)


def by_transposed(left, right):
    return lax.dot_general(
        left, right, (((1,), (1,)), ((), ())), preferred_element_type=jnp.float32
    )


def over_tokens(left, right):
    return lax.dot_general(
        left, right, (((0,), (0,)), ((), ())), preferred_element_type=jnp.float32
    )


def collect(blocks):
    partly = (
        lax.all_gather(blocks[0], "col", axis=1, tiled=True),
        lax.all_gather(blocks[1], "col", axis=1, tiled=True),
        lax.all_gather(blocks[2], "col", axis=1, tiled=True),
        lax.all_gather(blocks[3], "col", axis=1, tiled=True),
        lax.all_gather(blocks[4], "col", axis=1, tiled=True),
        lax.all_gather(blocks[5], "col", axis=1, tiled=True),
        lax.all_gather(blocks[6], "col", axis=1, tiled=True),
        lax.all_gather(blocks[7], "col", axis=1, tiled=True),
        lax.all_gather(blocks[8], "col", axis=1, tiled=True),
        lax.all_gather(blocks[9], "col", axis=1, tiled=True),
        lax.all_gather(blocks[10], "col", axis=1, tiled=True),
    )
    return (
        lax.all_gather(partly[0], "row", axis=0, tiled=True),
        lax.all_gather(partly[1], "row", axis=0, tiled=True),
        lax.all_gather(partly[2], "row", axis=0, tiled=True),
        lax.all_gather(partly[3], "row", axis=0, tiled=True),
        lax.all_gather(partly[4], "row", axis=0, tiled=True),
        lax.all_gather(partly[5], "row", axis=0, tiled=True),
        lax.all_gather(partly[6], "row", axis=0, tiled=True),
        lax.all_gather(partly[7], "row", axis=0, tiled=True),
        lax.all_gather(partly[8], "row", axis=0, tiled=True),
        lax.all_gather(partly[9], "row", axis=0, tiled=True),
        lax.all_gather(partly[10], "row", axis=0, tiled=True),
    )


def spread(grads):
    partly = (
        lax.psum_scatter(
            grads[0].astype(jnp.bfloat16), "row", scatter_dimension=0, tiled=True
        ).astype(jnp.float32),
        lax.psum_scatter(
            grads[1].astype(jnp.bfloat16), "row", scatter_dimension=0, tiled=True
        ).astype(jnp.float32),
        lax.psum_scatter(
            grads[2].astype(jnp.bfloat16), "row", scatter_dimension=0, tiled=True
        ).astype(jnp.float32),
        lax.psum_scatter(
            grads[3].astype(jnp.bfloat16), "row", scatter_dimension=0, tiled=True
        ).astype(jnp.float32),
        lax.psum_scatter(
            grads[4].astype(jnp.bfloat16), "row", scatter_dimension=0, tiled=True
        ).astype(jnp.float32),
        lax.psum_scatter(
            grads[5].astype(jnp.bfloat16), "row", scatter_dimension=0, tiled=True
        ).astype(jnp.float32),
        lax.psum_scatter(
            grads[6].astype(jnp.bfloat16), "row", scatter_dimension=0, tiled=True
        ).astype(jnp.float32),
        lax.psum_scatter(
            grads[7].astype(jnp.bfloat16), "row", scatter_dimension=0, tiled=True
        ).astype(jnp.float32),
        lax.psum_scatter(
            grads[8].astype(jnp.bfloat16), "row", scatter_dimension=0, tiled=True
        ).astype(jnp.float32),
        lax.psum_scatter(
            grads[9].astype(jnp.bfloat16), "row", scatter_dimension=0, tiled=True
        ).astype(jnp.float32),
        lax.psum_scatter(
            grads[10].astype(jnp.bfloat16), "row", scatter_dimension=0, tiled=True
        ).astype(jnp.float32),
    )
    return (
        lax.psum_scatter(
            partly[0].astype(jnp.bfloat16), "col", scatter_dimension=1, tiled=True
        ).astype(jnp.float32),
        lax.psum_scatter(
            partly[1].astype(jnp.bfloat16), "col", scatter_dimension=1, tiled=True
        ).astype(jnp.float32),
        lax.psum_scatter(
            partly[2].astype(jnp.bfloat16), "col", scatter_dimension=1, tiled=True
        ).astype(jnp.float32),
        lax.psum_scatter(
            partly[3].astype(jnp.bfloat16), "col", scatter_dimension=1, tiled=True
        ).astype(jnp.float32),
        lax.psum_scatter(
            partly[4].astype(jnp.bfloat16), "col", scatter_dimension=1, tiled=True
        ).astype(jnp.float32),
        lax.psum_scatter(
            partly[5].astype(jnp.bfloat16), "col", scatter_dimension=1, tiled=True
        ).astype(jnp.float32),
        lax.psum_scatter(
            partly[6].astype(jnp.bfloat16), "col", scatter_dimension=1, tiled=True
        ).astype(jnp.float32),
        lax.psum_scatter(
            partly[7].astype(jnp.bfloat16), "col", scatter_dimension=1, tiled=True
        ).astype(jnp.float32),
        lax.psum_scatter(
            partly[8].astype(jnp.bfloat16), "col", scatter_dimension=1, tiled=True
        ).astype(jnp.float32),
        lax.psum_scatter(
            partly[9].astype(jnp.bfloat16), "col", scatter_dimension=1, tiled=True
        ).astype(jnp.float32),
        lax.psum_scatter(
            partly[10].astype(jnp.bfloat16), "col", scatter_dimension=1, tiled=True
        ).astype(jnp.float32),
    )


def heads_layout(stacked):
    return lax.all_to_all(stacked, "row", split_axis=1, concat_axis=0, tiled=True)


def tokens_layout(stacked):
    return lax.all_to_all(stacked, "row", split_axis=0, concat_axis=2, tiled=True)


def by_clips(arranged, start, count, length, heads_dev):
    section = arranged[:, start : start + count]
    return section.reshape(-1, length, heads_dev, HEAD_DIM)


def causal_scores(query_clip, key_clip, causal):
    scores = jnp.einsum(
        "qhd,khd->hqk", query_clip, key_clip, preferred_element_type=jnp.float32
    ) * HEAD_DIM ** (-0.5)
    if causal:
        allowed = jnp.arange(scores.shape[1])[:, None] >= jnp.arange(scores.shape[2])[None, :]
        scores = jnp.where(allowed, scores, -1e30)
    return scores


def attend_forward(query_clips, key_clips, value_clips, causal):

    def one_clip(operands):
        query_clip, key_clip, value_clip = operands
        scores = causal_scores(query_clip, key_clip, causal)
        highest = jnp.max(scores, axis=-1, keepdims=True)
        powers = jnp.exp(scores - highest)
        totals = jnp.sum(powers, axis=-1, keepdims=True)
        weights_low = (powers / totals).astype(jnp.bfloat16)
        mixture = jnp.einsum(
            "hqk,khd->qhd", weights_low, value_clip, preferred_element_type=jnp.float32
        )
        return (mixture.astype(jnp.bfloat16), (highest + jnp.log(totals))[..., 0])

    return lax.map(one_clip, (query_clips, key_clips, value_clips))


def attend_backward(query_clips, key_clips, value_clips, log_sums, grad_clips, causal):

    def one_clip(operands):
        query_clip, key_clip, value_clip, log_clip, grad_clip = operands
        scores = causal_scores(query_clip, key_clip, causal)
        probs_full = jnp.exp(scores - log_clip[..., None])
        grad_probs = jnp.einsum(
            "qhd,khd->hqk", grad_clip, value_clip, preferred_element_type=jnp.float32
        )
        grad_value = jnp.einsum(
            "hqk,qhd->khd",
            probs_full.astype(jnp.bfloat16),
            grad_clip,
            preferred_element_type=jnp.float32,
        )
        centered = grad_probs - jnp.sum(probs_full * grad_probs, axis=-1, keepdims=True)
        grad_scores = (probs_full * centered).astype(jnp.bfloat16)
        grad_query = jnp.einsum(
            "hqk,khd->qhd", grad_scores, key_clip, preferred_element_type=jnp.float32
        ) * HEAD_DIM ** (-0.5)
        grad_key = jnp.einsum(
            "hqk,qhd->khd", grad_scores, query_clip, preferred_element_type=jnp.float32
        ) * HEAD_DIM ** (-0.5)
        return (
            grad_query.astype(jnp.bfloat16),
            grad_key.astype(jnp.bfloat16),
            grad_value.astype(jnp.bfloat16),
        )

    return lax.map(one_clip, (query_clips, key_clips, value_clips, log_sums, grad_clips))


def general(
    frames_in,
    text_states,
    self_query,
    self_key,
    self_value,
    self_output,
    cross_query,
    cross_key,
    cross_value,
    cross_output,
    up_weight,
    down_weight,
    first_gain,
    first_bias,
    second_gain,
    second_bias,
    third_gain,
    third_bias,
    cotangent,
):
    row_count = lax.axis_size("row")
    col_count = lax.axis_size("col")
    heads_dev = HEADS // row_count
    width_dev = heads_dev * HEAD_DIM
    tok_rows = frames_in.shape[0]
    text_rows = text_states.shape[0]
    piece_len = first_gain.shape[0]
    gain_block = jnp.stack(
        [first_gain, first_bias, second_gain, second_bias, third_gain, third_bias]
    ).reshape(1, 6 * piece_len)
    param_blocks = (
        self_query,
        self_key,
        self_value,
        self_output,
        cross_query,
        cross_key,
        cross_value,
        cross_output,
        up_weight,
        down_weight,
        gain_block,
    )

    def unpack_gains(gathered_gains):
        arranged = gathered_gains.reshape(row_count, col_count, 6, piece_len).transpose(2, 0, 1, 3)
        return arranged.reshape(6, row_count * col_count * piece_len).astype(jnp.float32)

    gathered = collect(param_blocks)
    (
        query_self,
        key_self,
        value_self,
        out_self,
        query_cross,
        key_cross,
        value_cross,
        out_cross,
        up_full,
        down_full,
    ) = gathered[:10]
    norm_params = unpack_gains(gathered[10])
    frames = frames_in.astype(jnp.float32)
    hidden_one = norm_forward(frames, norm_params[0], norm_params[1]).astype(jnp.bfloat16)
    self_q = matmul(hidden_one, query_self).astype(jnp.bfloat16)
    self_k = matmul(hidden_one, key_self).astype(jnp.bfloat16)
    self_v = matmul(hidden_one, value_self).astype(jnp.bfloat16)
    text_k = matmul(text_states, key_cross).astype(jnp.bfloat16)
    text_v = matmul(text_states, value_cross).astype(jnp.bfloat16)
    sent_rows = 3 * tok_rows + 2 * text_rows
    arranged = heads_layout(jnp.concatenate([self_q, self_k, self_v, text_k, text_v], axis=0))
    arranged = arranged.reshape(row_count, sent_rows, width_dev)
    query_clips = by_clips(arranged, 0, tok_rows, FRAMES, heads_dev)
    key_clips = by_clips(arranged, tok_rows, tok_rows, FRAMES, heads_dev)
    value_clips = by_clips(arranged, 2 * tok_rows, tok_rows, FRAMES, heads_dev)
    text_keys = by_clips(arranged, 3 * tok_rows, text_rows, TEXT, heads_dev)
    text_values = by_clips(arranged, 3 * tok_rows + text_rows, text_rows, TEXT, heads_dev)
    self_clips, self_logs = attend_forward(query_clips, key_clips, value_clips, True)
    self_mix = tokens_layout(self_clips.reshape(row_count, tok_rows, width_dev))[0]
    resid_one = frames + matmul(self_mix, out_self)
    hidden_two = norm_forward(resid_one, norm_params[2], norm_params[3]).astype(jnp.bfloat16)
    cross_q = matmul(hidden_two, query_cross).astype(jnp.bfloat16)
    cross_arranged = heads_layout(cross_q).reshape(row_count, tok_rows, width_dev)
    cross_queries = by_clips(cross_arranged, 0, tok_rows, FRAMES, heads_dev)
    cross_clips, cross_logs = attend_forward(cross_queries, text_keys, text_values, False)
    cross_mix = tokens_layout(cross_clips.reshape(row_count, tok_rows, width_dev))[0]
    resid_two = resid_one + matmul(cross_mix, out_cross)
    hidden_three = norm_forward(resid_two, norm_params[4], norm_params[5]).astype(jnp.bfloat16)
    pre_act = matmul(hidden_three, up_full)
    inner = jax.nn.gelu(pre_act, approximate=False).astype(jnp.bfloat16)
    layer_out = (resid_two + matmul(inner, down_full)).astype(jnp.bfloat16)
    gathered = collect(param_blocks)
    (
        query_self,
        key_self,
        value_self,
        out_self,
        query_cross,
        key_cross,
        value_cross,
        out_cross,
        up_full,
        down_full,
    ) = gathered[:10]
    norm_params = unpack_gains(gathered[10])
    cotan_full = cotangent.astype(jnp.float32)
    down_grad = over_tokens(inner, cotangent)
    grad_inner = by_transposed(cotangent, down_full)
    unused_gelu, gelu_pull = jax.vjp(partial(jax.nn.gelu, approximate=False), pre_act)
    grad_pre = gelu_pull(grad_inner)[0].astype(jnp.bfloat16)
    up_grad = over_tokens(hidden_three, grad_pre)
    grad_three = by_transposed(grad_pre, up_full)
    unused_three, pull_three = jax.vjp(norm_forward, resid_two, norm_params[4], norm_params[5])
    through_three, third_gain_part, third_bias_part = pull_three(grad_three)
    grad_resid_two = cotan_full + through_three
    grad_cross = grad_resid_two.astype(jnp.bfloat16)
    cross_out_grad = over_tokens(cross_mix, grad_cross)
    grad_cross_mix = by_transposed(grad_cross, out_cross).astype(jnp.bfloat16)
    grad_cross_arr = heads_layout(grad_cross_mix).reshape(row_count, tok_rows, width_dev)
    grad_cross_clips = by_clips(grad_cross_arr, 0, tok_rows, FRAMES, heads_dev)
    cq_clips, tk_clips, tv_clips = attend_backward(
        cross_queries, text_keys, text_values, cross_logs, grad_cross_clips, False
    )
    back_cross = jnp.concatenate(
        [
            cq_clips.reshape(row_count, tok_rows, width_dev),
            tk_clips.reshape(row_count, text_rows, width_dev),
            tv_clips.reshape(row_count, text_rows, width_dev),
        ],
        axis=1,
    )
    back_cross = tokens_layout(back_cross)[0]
    grad_cross_q = back_cross[:tok_rows]
    grad_text_k = back_cross[tok_rows : tok_rows + text_rows]
    grad_text_v = back_cross[tok_rows + text_rows :]
    cross_query_part = over_tokens(hidden_two, grad_cross_q)
    cross_key_part = over_tokens(text_states, grad_text_k)
    cross_value_part = over_tokens(text_states, grad_text_v)
    text_grad = by_transposed(grad_text_k, key_cross) + by_transposed(grad_text_v, value_cross)
    grad_two = by_transposed(grad_cross_q, query_cross)
    unused_two, pull_two = jax.vjp(norm_forward, resid_one, norm_params[2], norm_params[3])
    through_two, second_gain_part, second_bias_part = pull_two(grad_two)
    grad_resid_one = grad_resid_two + through_two
    grad_self = grad_resid_one.astype(jnp.bfloat16)
    self_out_grad = over_tokens(self_mix, grad_self)
    grad_self_mix = by_transposed(grad_self, out_self).astype(jnp.bfloat16)
    grad_self_arr = heads_layout(grad_self_mix).reshape(row_count, tok_rows, width_dev)
    grad_self_clips = by_clips(grad_self_arr, 0, tok_rows, FRAMES, heads_dev)
    sq_clips, sk_clips, sv_clips = attend_backward(
        query_clips, key_clips, value_clips, self_logs, grad_self_clips, True
    )
    back_self = jnp.concatenate(
        [
            sq_clips.reshape(row_count, tok_rows, width_dev),
            sk_clips.reshape(row_count, tok_rows, width_dev),
            sv_clips.reshape(row_count, tok_rows, width_dev),
        ],
        axis=1,
    )
    back_self = tokens_layout(back_self)[0]
    grad_self_q = back_self[:tok_rows]
    grad_self_k = back_self[tok_rows : 2 * tok_rows]
    grad_self_v = back_self[2 * tok_rows :]
    self_query_part = over_tokens(hidden_one, grad_self_q)
    self_key_part = over_tokens(hidden_one, grad_self_k)
    self_value_part = over_tokens(hidden_one, grad_self_v)
    grad_one = (
        by_transposed(grad_self_q, query_self)
        + by_transposed(grad_self_k, key_self)
        + by_transposed(grad_self_v, value_self)
    )
    unused_one, pull_one = jax.vjp(norm_forward, frames, norm_params[0], norm_params[1])
    through_one, first_gain_part, first_bias_part = pull_one(grad_one)
    input_grad = grad_resid_one + through_one
    norm_grads = jnp.stack(
        [
            first_gain_part,
            first_bias_part,
            second_gain_part,
            second_bias_part,
            third_gain_part,
            third_bias_part,
        ]
    )
    norm_grads = norm_grads.reshape(6, row_count, col_count, piece_len).transpose(1, 2, 0, 3)
    norm_grads = norm_grads.reshape(row_count, col_count * 6 * piece_len)
    summed = spread(
        (
            self_query_part,
            self_key_part,
            self_value_part,
            self_out_grad,
            cross_query_part,
            cross_key_part,
            cross_value_part,
            cross_out_grad,
            up_grad,
            down_grad,
            norm_grads,
        )
    )
    norm_parts = summed[10].reshape(6, piece_len)
    return (
        layer_out,
        input_grad,
        text_grad,
        summed[0],
        summed[1],
        summed[2],
        summed[3],
        summed[4],
        summed[5],
        summed[6],
        summed[7],
        summed[8],
        summed[9],
        norm_parts[0],
        norm_parts[1],
        norm_parts[2],
        norm_parts[3],
        norm_parts[4],
        norm_parts[5],
    )


NT=(((1,),(1,)),((),())); NN=(((1,),(0,)),((),())); TN=(((0,),(0,)),((),()))
def dg(a,b,dims): return lax.dot_general(a,b,dims,preferred_element_type=jnp.float32)

def attend_kernel(causal,tile,q_ref,k_ref,v_ref,o_ref,lse_ref):
    pair=pl.program_id(0)
    rows=q_ref.shape[0]
    low=lax.broadcasted_iota(jnp.int32,(1,128),1)<HEAD_DIM
    lane=lax.broadcasted_iota(jnp.int32,(1,128),1)
    value=v_ref[...]
    ones=jnp.ones_like(value)
    @pl.when(pair==0)
    def _(): lse_ref[...]=jnp.zeros_like(lse_ref)
    for start in range(0,rows,tile):
        n=min(tile,rows-start)
        q=q_ref[start:start+n,:]*jnp.bfloat16(HEAD_DIM**-0.5)
        mixed=[]; sums=[]
        lse=lse_ref[start:start+n,:]
        for h in range(2):
            mine=low if h==0 else jnp.logical_not(low)
            qh=jnp.where(mine,q,jnp.bfloat16(0))
            vh=jnp.where(mine,value,ones)
            if causal:
                spans=([(0,start)] if start else [])+[(start,n)]
            else: spans=[(0,k_ref.shape[0])]
            scores=[]
            for at,length in spans:
                s=dg(qh,k_ref[at:at+length,:],NT)
                if causal and at==start:
                    ok=lax.broadcasted_iota(jnp.int32,s.shape,0)>=lax.broadcasted_iota(jnp.int32,s.shape,1)
                    s=jnp.where(ok,s,-1e30)
                scores.append(s)
            top=functools.reduce(jnp.maximum,[jnp.max(s,axis=1,keepdims=True) for s in scores])
            out=None
            for (at,length),s in zip(spans,scores):
                p=jnp.exp(s-top).astype(jnp.bfloat16)
                part=dg(p,vh[at:at+length,:],NN)
                out=part if out is None else out+part
            total=out[:,HEAD_DIM:HEAD_DIM+1] if h==0 else out[:,0:1]
            mixed.append(out/total)
            lse=jnp.where(lane==2*pair+h,top+jnp.log(total),lse)
        lse_ref[start:start+n,:]=lse
        o_ref[start:start+n,:]=jnp.where(low,mixed[0],mixed[1]).astype(o_ref.dtype)

def attend(q,k,v,causal,out_dtype,tile=256):
    rows,width=q.shape; keys=k.shape[0]
    return pl.pallas_call(functools.partial(attend_kernel,causal,tile),grid=(width//128,),
        in_specs=[pl.BlockSpec((rows,128),lambda i:(0,i)),pl.BlockSpec((keys,128),lambda i:(0,i)),pl.BlockSpec((keys,128),lambda i:(0,i))],
        out_specs=[pl.BlockSpec((rows,128),lambda i:(0,i)),pl.BlockSpec((rows,128),lambda i:(0,0))],
        out_shape=[jax.ShapeDtypeStruct((rows,width),out_dtype),jax.ShapeDtypeStruct((rows,128),jnp.float32)],
        compiler_params=pltpu.CompilerParams(vmem_limit_bytes=40<<20),
        cost_estimate=pl.CostEstimate(flops=4*rows*keys*width,bytes_accessed=8*rows*width,transcendentals=rows*keys*width//64))(q,k,v)

def attend_back_kernel(causal,tile,q_ref,k_ref,v_ref,do_ref,st_ref,dq_ref,dk_ref,dv_ref,acc):
    rows=q_ref.shape[0]; keys=k_ref.shape[0]
    low=lax.broadcasted_iota(jnp.int32,(1,128),1)<HEAD_DIM
    acc[...]=jnp.zeros_like(acc)
    for start in range(0,keys,tile):
        n=min(tile,keys-start)
        k=k_ref[start:start+n,:]*jnp.bfloat16(HEAD_DIM**-0.5)
        v=v_ref[start:start+n,:]
        spans=[(0,rows)]
        if causal: spans=[(start,n)]+([(start+n,rows-start-n)] if start+n<rows else [])
        dks=[];dvs=[]
        for h in range(2):
            mine=low if h==0 else jnp.logical_not(low)
            kh=jnp.where(mine,k,jnp.bfloat16(0)); vh=jnp.where(mine,v,jnp.bfloat16(0))
            dk=dv=None
            for at,length in spans:
                qs=q_ref[at:at+length,:]; do=do_ref[at:at+length,:]
                s=dg(kh,qs,NT)
                p=jnp.exp(s-st_ref[0,h:h+1,at:at+length])
                if causal and at==start:
                    ok=lax.broadcasted_iota(jnp.int32,s.shape,0)<=lax.broadcasted_iota(jnp.int32,s.shape,1)
                    p=jnp.where(ok,p,0.0)
                dp=dg(vh,do,NT)
                ds=(p*(dp-st_ref[0,2+h:3+h,at:at+length])).astype(jnp.bfloat16)
                a=dg(p.astype(jnp.bfloat16),do,NN); b=dg(ds,qs,NN)
                dv=a if dv is None else dv+a
                dk=b if dk is None else dk+b
                acc[at:at+length,:]+=dg(ds,kh,TN)
            dks.append(dk);dvs.append(dv)
        dk_ref[start:start+n,:]=(jnp.where(low,dks[0],dks[1])*HEAD_DIM**-0.5).astype(dk_ref.dtype)
        dv_ref[start:start+n,:]=jnp.where(low,dvs[0],dvs[1]).astype(dv_ref.dtype)
    dq_ref[...]=acc[...].astype(dq_ref.dtype)

def attend_back(q,k,v,do,stats,causal,out_dtype,tile=256):
    rows,width=q.shape; keys=k.shape[0]
    bq=pl.BlockSpec((rows,128),lambda i:(0,i)); bk=pl.BlockSpec((keys,128),lambda i:(0,i))
    return pl.pallas_call(functools.partial(attend_back_kernel,causal,tile),grid=(width//128,),
        in_specs=[bq,bk,bk,bq,pl.BlockSpec((1,4,rows),lambda i:(i,0,0))],out_specs=[bq,bk,bk],
        out_shape=[jax.ShapeDtypeStruct((rows,width),out_dtype),jax.ShapeDtypeStruct((keys,width),out_dtype),jax.ShapeDtypeStruct((keys,width),out_dtype)],
        scratch_shapes=[pltpu.VMEM((rows,128),jnp.float32)],
        compiler_params=pltpu.CompilerParams(vmem_limit_bytes=40<<20),
        cost_estimate=pl.CostEstimate(flops=10*rows*keys*width,bytes_accessed=16*rows*width,transcendentals=rows*keys*width//64))(q,k,v,do,stats)

def feed_kernel(h_ref,cot_ref,res_ref,up_ref,down_ref,out_ref,g_ref,dup_ref,ddown_ref,acc):
    i=pl.program_id(0)
    @pl.when(i==0)
    def _():
        acc[...]=res_ref[...]
        g_ref[...]=jnp.zeros_like(g_ref)
    h=h_ref[...]
    up=up_ref[:,0].reshape(h.shape[1],-1)
    blocks,wide=down_ref.shape[1],down_ref.shape[3]
    pre=dg(h,up,NN)
    cdf=0.5*(1.0+lax.erf(pre*0.7071067811865476))
    inner=(pre*cdf).astype(jnp.bfloat16)
    slope=cdf+pre*(jnp.exp(-0.5*pre*pre)*0.3989422804014327)
    grad=None
    for at in range(blocks):
        columns=slice(at*wide,(at+1)*wide)
        cot=cot_ref[:,columns]
        acc[:,columns]+=dg(inner,down_ref[0,at],NN)
        ddown_ref[0,at]=dg(inner,cot,TN).astype(ddown_ref.dtype)
        part=dg(cot,down_ref[0,at],NT)
        grad=part if grad is None else grad+part
    gpre=(grad*slope).astype(jnp.bfloat16)
    dup_ref[:,0]=dg(h,gpre,TN).astype(dup_ref.dtype).reshape(dup_ref.shape[0],dup_ref.shape[2],dup_ref.shape[3])
    g_ref[...]+=dg(gpre,up,NT)
    @pl.when(i==pl.num_programs(0)-1)
    def _(): out_ref[...]=acc[...].astype(out_ref.dtype)

def feed(h,cot,res,up,down):
    rows,d=h.shape; chunk=down.shape[2]; strips=up.shape[3]//chunk; ff=down.shape[0]*chunk
    whole=pl.BlockSpec((rows,d),lambda i:(0,0))
    up_spec=pl.BlockSpec((up.shape[0],1,up.shape[2],chunk),lambda i:(0,i//strips,0,i%strips))
    down_spec=pl.BlockSpec((1,)+down.shape[1:],lambda i:(i,0,0,0))
    return pl.pallas_call(feed_kernel,grid=(ff//chunk,),
        in_specs=[whole,whole,whole,up_spec,down_spec],
        out_specs=[whole,whole,up_spec,down_spec],
        out_shape=[jax.ShapeDtypeStruct((rows,d),jnp.bfloat16),jax.ShapeDtypeStruct((rows,d),jnp.float32),jax.ShapeDtypeStruct(up.shape,jnp.bfloat16),jax.ShapeDtypeStruct(down.shape,jnp.bfloat16)],
        scratch_shapes=[pltpu.VMEM((rows,d),jnp.float32)],
        compiler_params=pltpu.CompilerParams(vmem_limit_bytes=56<<20),
        cost_estimate=pl.CostEstimate(flops=12*rows*d*ff,bytes_accessed=8*d*ff+16*rows*d,transcendentals=2*rows*ff))(h,cot,res,up,down)


MESH = pl.DeviceIdType.MESH
ORDERS = ("xzy", "yzx", "xzy", "yzx", "zxy", "zyx")


class Place:
    def __init__(self):
        row, col = lax.axis_index("row"), lax.axis_index("col")
        self.z, self.y, self.x, self.k = row // 2, row % 2, col // 2, col % 2
        self.along = lax.axis_size("row") // 2

    def device(self, dz=0, y=False, x=False, k=False):
        other_y = 1 - self.y if y else self.y
        other_x = 1 - self.x if x else self.x
        other_k = 1 - self.k if k else self.k
        return ((self.z + dz) * 2 + other_y, other_x * 2 + other_k)

    def across(self, axis):
        return self.device(y=axis == "y", x=axis == "x", k=axis == "k")

    def greet(self):
        barrier = pltpu.get_barrier_semaphore()
        for axis in "xyk":
            pl.semaphore_signal(barrier, inc=1, device_id=self.across(axis), device_id_type=MESH)

        @pl.when(self.z > 0)
        def _():
            pl.semaphore_signal(barrier, inc=1, device_id=self.device(dz=-1), device_id_type=MESH)

        @pl.when(self.z + 1 < self.along)
        def _():
            pl.semaphore_signal(barrier, inc=1, device_id=self.device(dz=1), device_id_type=MESH)

        below = jnp.where(self.z > 0, 1, 0)
        above = jnp.where(self.z + 1 < self.along, 1, 0)
        pl.semaphore_wait(barrier, 3 + below + above)


def when(condition, run):
    if condition is None:
        run()
    else:
        pl.when(condition)(run)


def in_turn(units, lag):
    ready = [(lag * at, at) for at in range(len(units))]
    while ready:
        turn, at = min(ready)
        ready.remove((turn, at))
        if next(units[at], units) is not units:
            ready.append((turn + 1, at))
        yield


class Gather:
    def __init__(self, place, block, full, strip, order, send, recv):
        self.place, self.block, self.full, self.strip = place, block, full, strip
        turn = order.index("z")
        self.before, self.after = order[:turn], order[turn + 1 :]
        self.send, self.recv, self.used, self.sent, self.started = send, recv, 0, 0, []

    def region(self, z, y, x):
        part, start, count = self.strip
        column = (x * 2 + self.place.k) * self.block.shape[-1] + start
        return self.full.at[z, y, part, :, pl.ds(pl.multiple_of(column, 128), count)]

    def held(self, done, z):
        y = slice(None) if "y" in done else self.place.y
        return [self.region(z, y, x) for x in (range(2) if "x" in done else [self.place.x])]

    def pairs(self, done, z, first):
        if first:
            part, start, count = self.strip
            place = self.place
            return [(self.block.at[part, :, pl.ds(start, count)], self.region(place.z, place.y, place.x))]
        return [(region, region) for region in self.held(done, z)]

    def semaphore(self):
        self.used += 2
        return self.used - 2

    def copies(self, device, pairs, semaphore, send=0):
        return [
            pltpu.make_async_remote_copy(
                src_ref=source, dst_ref=target, send_sem=self.send.at[send + at],
                recv_sem=self.recv.at[semaphore + at], device_id=device, device_id_type=MESH)
            for at, (source, target) in enumerate(pairs)
        ]

    def start(self, device, pairs, condition, semaphore):
        copies = self.copies(device, pairs, semaphore, self.sent)
        self.sent += len(copies)
        when(condition, lambda: [copy.start() for copy in copies] and None)
        self.started.append((condition, copies))
        return condition, copies

    def arrive(self, sent):
        condition, copies = sent
        when(condition, lambda: [copy.wait_recv() for copy in copies] and None)

    def stages(self):
        place, along = self.place, self.place.along
        done = []
        for axis in self.before:
            sent = self.start(place.across(axis), self.pairs(done, place.z, not done), None, self.semaphore())
            yield
            self.arrive(sent)
            done.append(axis)
        first = not done
        from_left = [self.semaphore() for _ in range(along - 1)]
        from_right = [self.semaphore() for _ in range(along - 1)]

        def pass_on(turn, step):
            axes = done + list(self.after[:turn])
            device = place.across(self.after[turn])
            if step == 0:
                return turn, step, [self.start(device, self.pairs(axes, place.z, not axes), None, self.semaphore())]
            return turn, step, [
                self.start(device, self.pairs(axes, z, False), (z >= 0) & (z < along), self.semaphore())
                for z in (place.z - step, place.z + step)
            ]

        def step_out(step):
            left, right = place.z - (step - 1), place.z + (step - 1)
            self.start(place.device(dz=1), self.pairs(done, left, first and step == 1),
                       (left >= 0) & (place.z + 1 < along), from_left[step - 1])
            self.start(place.device(dz=-1), self.pairs(done, right, first and step == 1),
                       (right < along) & (place.z > 0), from_right[step - 1])

        def step_in(step):
            for z, semaphore in ((place.z - step, from_left), (place.z + step, from_right)):
                copies = self.copies(place.across("k"), self.pairs(done, z, False), semaphore[step - 1])
                self.arrive(((z >= 0) & (z < along), copies))

        step_out(1)
        waiting = [pass_on(0, 0)] if self.after else []
        for step in range(1, along + len(self.after)):
            yield
            if step < along:
                step_in(step)
                if step + 1 < along:
                    step_out(step + 1)
            following = []
            for turn, at, sent in waiting:
                for one in sent:
                    self.arrive(one)
                if turn + 1 < len(self.after):
                    following.append(pass_on(turn + 1, at))
            if self.after and step < along:
                following.append(pass_on(0, step))
            waiting = following
        everything = [self.region(slice(None), slice(None), x) for x in range(2)]
        sent = self.start(place.across("k"), [(r, r) for r in everything], None, self.semaphore())
        yield
        self.arrive(sent)

    def finish(self):
        for condition, copies in self.started:
            when(condition, lambda copies=copies: [copy.wait_send() for copy in copies] and None)


def gather_kernel(units, count, *refs):
    blocks, fulls = refs[:count], refs[count : 2 * count]
    send, recv, local_sem = refs[2 * count :]
    place = Place()
    place.greet()
    own = []
    for at, (block, full) in enumerate(zip(blocks, fulls)):
        width = block.shape[-1]
        columns = pl.ds(pl.multiple_of((place.x * 2 + place.k) * width, 128), width)
        copy = pltpu.make_async_copy(block, full.at[place.z, place.y, :, :, columns], local_sem.at[at])
        copy.start()
        own.append(copy)
    gathers = [
        Gather(place, blocks[which], fulls[which], strip, order, send.at[at], recv.at[at])
        for at, (which, strip, order) in enumerate(units)
    ]
    for unused in in_turn([gather.stages() for gather in gathers], 0.0):
        while own:
            own.pop().wait()
    for gather in gathers:
        gather.finish()


def gather_units(blocks, least):
    strips = []
    for which, block in enumerate(blocks):
        wide = min(least, block.shape[-1])
        for part in range(block.shape[0]):
            for start in range(0, block.shape[-1], wide):
                strips.append((which, (part, start, wide)))
    return [strip + (ORDERS[at % len(ORDERS)],) for at, strip in enumerate(strips)]


def gather_blocks(blocks, collective_id, least):
    along, cols = lax.axis_size("row") // 2, lax.axis_size("col")
    units = gather_units(blocks, least)
    count = len(blocks)
    anywhere = pl.BlockSpec(memory_space=pl.ANY)
    moved = sum(block.size for block in blocks) * 2 * along * 2 * cols
    return pl.pallas_call(
        functools.partial(gather_kernel, units, count),
        out_shape=[
            jax.ShapeDtypeStruct((along, 2) + b.shape[:2] + (cols * b.shape[2],), b.dtype) for b in blocks
        ],
        in_specs=[anywhere] * count,
        out_specs=[anywhere] * count,
        scratch_shapes=[
            pltpu.SemaphoreType.DMA((len(units), 8 * along)),
            pltpu.SemaphoreType.DMA((len(units), 12 * along)),
            pltpu.SemaphoreType.DMA((count,)),
        ],
        compiler_params=pltpu.CompilerParams(collective_id=collective_id, has_side_effects=True),
        cost_estimate=pl.CostEstimate(flops=0, bytes_accessed=2 * moved, transcendentals=0),
    )(*blocks)


def add_blocks(total, extra, leading):
    def one(at, unused):
        place = []
        for size in leading[::-1]:
            place.append(at % size)
            at = at // size
        place = tuple(place[::-1])
        total[place] = total[place] + extra[place]
        return unused

    if not leading:
        total[...] = total[...] + extra[...]
        return
    count = 1
    for size in leading:
        count *= size
    lax.fori_loop(0, count, one, 0)


class Scatter:
    def __init__(self, place, grad, out, strip, width, order, slots, send, recv, local):
        self.place, self.grad, self.out, self.strip, self.width = place, grad, out, strip, width
        self.order = order[::-1]
        self.total, self.other_core, self.halves, self.steps = slots
        self.send, self.recv, self.local = send, recv, local
        self.used, self.started = 0, []

    def region(self, x, k):
        part, start, count = self.strip
        column = (x * 2 + k) * self.width + start
        return self.grad.at[:, :, part, :, pl.ds(pl.multiple_of(column, 128), count)]

    def copy(self, device, source, target, semaphore=None):
        if semaphore is None:
            semaphore = self.used
            self.used += 1
        return pltpu.make_async_remote_copy(
            src_ref=source, dst_ref=target, send_sem=self.send.at[semaphore], recv_sem=self.recv.at[semaphore],
            device_id=device, device_id_type=MESH)

    def start(self, copy, condition=None):
        when(condition, lambda: copy.start())
        self.started.append((condition, copy))

    def stages(self):
        place, along = self.place, self.place.along
        rows, columns = self.total.shape[-2:]
        own = [
            pltpu.make_async_copy(self.region(x, place.k), self.total.at[:, :, x], self.local.at[x]) for x in range(2)
        ]
        swapped = [
            self.copy(place.across("k"), self.region(x, 1 - place.k), self.other_core.at[:, :, x]) for x in range(2)
        ]
        for copy in own:
            copy.start()
        for copy in swapped:
            self.start(copy)
        yield
        for copy in own:
            copy.wait()
        for copy in swapped:
            copy.wait_recv()
        add_blocks(self.total, self.other_core, (along, 2, 2))
        left = {"z": slice(None), "y": slice(None), "x": slice(None)}
        at = {"y": place.y, "x": place.x}

        def view(ref, **places):
            return ref.at[tuple({**left, **places}[axis] for axis in "zyx")]

        def sizes():
            return tuple(size for axis, size in zip("zyx", (along, 2, 2)) if isinstance(left[axis], slice))

        exchanges = 0
        for axis in self.order:
            if axis == "z":
                shape = tuple(2 for name in "yx" if isinstance(left[name], slice))
                landing = self.steps.at[(slice(None),) * 2 + tuple(slice(None) if isinstance(left[name], slice) else 0 for name in "yx")]
                right, leftward = [self.used + at for at in range(along)], [self.used + along + at for at in range(along)]
                self.used += 2 * along
                for step in range(along):
                    if step:
                        yield
                    for way, names, first in ((1, right, place.z), (-1, leftward, along - 1 - place.z)):
                        goal = along - 1 - step + place.z if way == 1 else step - along + 1 + place.z
                        side = 0 if way == 1 else 1
                        if step:
                            arrived = self.copy(
                                place.across("k"), landing.at[side, step - 1], landing.at[side, step - 1], names[step - 1])

                            def take(arrived=arrived, goal=goal, side=side, step=step):
                                arrived.wait_recv()
                                add_blocks(view(self.total, z=goal), landing.at[side, step - 1], shape)

                            pl.when((first >= 1) & (first <= step))(take)
                        if step < along - 1:
                            onward = self.copy(
                                place.device(dz=way), view(self.total, z=jnp.clip(goal, 0, along - 1)), landing.at[side, step], names[step])
                            self.start(onward, (first <= step) & (first < along - 1))
                left["z"] = place.z
            else:
                landing = self.halves[exchanges]
                exchanges += 1
                target = landing.at[tuple(slice(None) if isinstance(left[name], slice) and name != axis else 0 for name in "zyx")]
                swap = self.copy(place.across(axis), view(self.total, **{axis: 1 - at[axis]}), target)
                self.start(swap)
                yield
                swap.wait_recv()
                left[axis] = at[axis]
                add_blocks(view(self.total), target, sizes())
        part, start, count = self.strip
        self.out[part, :, start : start + count] = view(self.total)[...].astype(jnp.float32)

    def finish(self):
        for condition, copy in self.started:
            when(condition, lambda copy=copy: copy.wait_send())


def scatter_slots(along, rows, columns, order):
    left = {"z": along, "y": 2, "x": 2}
    whole = (along, 2, 2, rows, columns)
    shapes = [whole, whole]
    steps = None
    for axis in order[::-1]:
        if axis == "z":
            steps = (2, along - 1, left["y"], left["x"], rows, columns)
        left[axis] = 1
        if axis != "z":
            shapes.append((left["z"], left["y"], left["x"], rows, columns))
    return shapes + [steps]


def scatter_kernel(units, count, *refs):
    grads, outs = refs[:count], refs[count : 2 * count]
    send, recv, local = refs[2 * count : 2 * count + 3]
    slots = refs[2 * count + 3 :]
    place = Place()
    place.greet()
    scatters = []
    for at, (which, strip, order) in enumerate(units):
        total, other_core, first, second, steps = slots[5 * at : 5 * at + 5]
        scatters.append(
            Scatter(place, grads[which], outs[which], strip, outs[which].shape[-1], order,
                    (total, other_core, (first, second), steps), send.at[at], recv.at[at], local.at[at]))
    for unused in in_turn([scatter.stages() for scatter in scatters], 0.5):
        pass
    for scatter in scatters:
        scatter.finish()


def scatter_blocks(grads, collective_id, least):
    along, cols = lax.axis_size("row") // 2, lax.axis_size("col")
    blocks = [jax.ShapeDtypeStruct(g.shape[2:4] + (g.shape[4] // cols,), jnp.float32) for g in grads]
    units = gather_units(blocks, least)
    count = len(grads)
    slots = []
    for which, strip, order in units:
        slots += [pltpu.VMEM(shape, jnp.bfloat16) for shape in scatter_slots(along, blocks[which].shape[1], strip[2], order)]
    anywhere = pl.BlockSpec(memory_space=pl.ANY)
    return pl.pallas_call(
        functools.partial(scatter_kernel, units, count),
        out_shape=blocks,
        in_specs=[anywhere] * count,
        out_specs=[pl.BlockSpec(memory_space=pltpu.VMEM)] * count,
        scratch_shapes=[
            pltpu.SemaphoreType.DMA((len(units), 2 * along + 4)),
            pltpu.SemaphoreType.DMA((len(units), 2 * along + 4)),
            pltpu.SemaphoreType.DMA((len(units), 2)),
            *slots,
        ],
        compiler_params=pltpu.CompilerParams(
            collective_id=collective_id, has_side_effects=True, vmem_limit_bytes=60 << 20),
        cost_estimate=pl.CostEstimate(
            flops=sum(g.size for g in grads), bytes_accessed=4 * sum(g.size for g in grads), transcendentals=0),
    )(*grads)


def attend_rows(q, key_ref, value_ref, spans, diagonal, put):
    low = lax.broadcasted_iota(jnp.int32, (1, 128), 1) < HEAD_DIM
    mixed, logs = [], []
    for h in range(2):
        mine = low if h == 0 else jnp.logical_not(low)
        qh = jnp.where(mine, q, jnp.bfloat16(0))
        scores = []
        for at, length in spans:
            s = dg(qh, key_ref[at : at + length, :], NT)
            if at == diagonal:
                allowed = lax.broadcasted_iota(jnp.int32, s.shape, 0) >= lax.broadcasted_iota(jnp.int32, s.shape, 1)
                s = jnp.where(allowed, s, -1e30)
            scores.append(s)
        top = functools.reduce(jnp.maximum, [jnp.max(s, axis=1, keepdims=True) for s in scores])
        out = None
        for (at, length), s in zip(spans, scores):
            p = jnp.exp(s - top).astype(jnp.bfloat16)
            value = value_ref[at : at + length, :]
            part = dg(p, jnp.where(mine, value, jnp.ones_like(value)), NN)
            out = part if out is None else out + part
        total = out[:, HEAD_DIM : HEAD_DIM + 1] if h == 0 else out[:, 0:1]
        mixed.append(out / total)
        logs.append(top + jnp.log(total))
    put(logs)
    return jnp.where(low, mixed[0], mixed[1])


def rows_of(lanes_ref, first):
    picked = lax.broadcasted_iota(jnp.int32, (8, 128), 0) + first == lax.broadcasted_iota(jnp.int32, (8, 128), 1)
    return lax.dot_general(
        picked.astype(jnp.float32), lanes_ref[...], NT, precision=lax.Precision.HIGHEST,
        preferred_element_type=jnp.float32)


def pair_attend_kernel(tile, q_ref, k_ref, v_ref, q_any, k_any, v_any, mix_ref, logs_ref, fq_out, fk_out, fv_out,
                       near, near_logs, far_q, far_k, far_v, far, far_logs, got, far_rows, got_rows,
                       send, recv, local, keep):
    step = pl.program_id(0)
    place = Place()
    pairs = near.shape[0]
    fars = pairs // 2
    rows = q_ref.shape[0]
    first, second = place.y == 0, place.y == 1
    partner = place.across("y")
    lane = lax.broadcasted_iota(jnp.int32, (1, 128), 1)
    scale = jnp.bfloat16(HEAD_DIM**-0.5)
    plan = ((q_any, far_q, False), (k_any, far_k, True), (v_any, far_v, True))

    def columns(pair):
        return pl.ds(pl.multiple_of(pair * 128, 128), 128)

    def sending(which, j):
        array, landing, by_first = plan[which]
        return pltpu.make_async_remote_copy(
            src_ref=array.at[:, columns(j if by_first else fars + j)], dst_ref=landing.at[j],
            send_sem=send.at[which, j], recv_sem=recv.at[which, j], device_id=partner, device_id_type=MESH)

    def keeping(which, j):
        array, landing, by_first = plan[which]
        return pltpu.make_async_copy(
            array.at[:, columns(fars + j if by_first else j)], landing.at[j], local.at[which, j])

    def mixture_out(j):
        return pltpu.make_async_remote_copy(
            src_ref=far.at[j], dst_ref=got.at[j], send_sem=send.at[3, j], recv_sem=recv.at[3, j],
            device_id=partner, device_id_type=MESH)

    def logs_out():
        return pltpu.make_async_remote_copy(
            src_ref=far_rows, dst_ref=got_rows, send_sem=send.at[4, 0], recv_sem=recv.at[4, 0],
            device_id=partner, device_id_type=MESH)

    def saving(which):
        return pltpu.make_async_copy(plan[which][1], (fq_out, fk_out, fv_out)[which], keep.at[which])

    @pl.when(step == 0)
    def _():
        barrier = pltpu.get_barrier_semaphore()
        pl.semaphore_signal(barrier, inc=1, device_id=partner, device_id_type=MESH)
        pl.semaphore_wait(barrier, 1)
        near_logs[...] = jnp.zeros_like(near_logs)
        far_logs[...] = jnp.zeros_like(far_logs)
        for j in range(fars):
            for which in range(3):

                @pl.when(first if plan[which][2] else second)
                def _(which=which, j=j):
                    keeping(which, j).start()

    @pl.when((step % 3 == 0) & (step < 3 * fars))
    def _():
        j = step // 3
        for which in range(3):

            @pl.when(first if plan[which][2] else second)
            def _(which=which):
                @pl.when(j > 0)
                def _():
                    sending(which, j - 1).wait_send()

                sending(which, j).start()

    @pl.when(step < pairs)
    def _():
        for start in range(0, rows, tile):
            n = min(tile, rows - start)

            def put(logs, start=start, n=n):
                kept = near_logs[start : start + n, :]
                for h in range(2):
                    kept = jnp.where(lane == 2 * step + h, logs[h], kept)
                near_logs[start : start + n, :] = kept

            spans = ([(0, start)] if start else []) + [(start, n)]
            near[step, start : start + n, :] = attend_rows(
                q_ref[start : start + n, :] * scale, k_ref, v_ref, spans, start, put)

    @pl.when((step >= pairs) & (step < pairs + fars))
    def _():
        j = step - pairs
        for which in range(3):
            by_first = plan[which][2]

            @pl.when(first if by_first else second)
            def _(which=which):
                keeping(which, j).wait()

            @pl.when(second if by_first else first)
            def _(which=which):
                sending(which, j).wait_recv()

        base = jnp.where(first, 2 * fars, 0)
        for start in range(0, rows, tile):
            n = min(tile, rows - start)

            def put(logs, start=start, n=n):
                kept = far_logs[start : start + n, :]
                for h in range(2):
                    kept = jnp.where(lane == base + 2 * j + h, logs[h], kept)
                far_logs[start : start + n, :] = kept

            far[j, start : start + n, :] = attend_rows(
                far_q[j, start : start + n, :] * scale, far_k.at[j], far_v.at[j], [(0, rows)], None, put
            ).astype(far.dtype)

        @pl.when(first)
        def _():
            mixture_out(j).start()

    @pl.when(step == pairs + fars)
    def _():
        for which in range(3):
            saving(which).start()

        @pl.when(first)
        def _():
            far_rows[...] = rows_of(far_logs, 2 * fars)
            logs_out().start()
            for pair in range(pairs):
                mix_ref[:, pair * 128 : (pair + 1) * 128] = near[pair].astype(mix_ref.dtype)
            logs_ref[...] = near_logs[...]
            logs_out().wait_send()
            for j in range(fars):
                mixture_out(j).wait_send()
            for which in (1, 2):
                sending(which, fars - 1).wait_send()

        @pl.when(second)
        def _():
            logs_out().wait_recv()
            for j in range(fars):
                mixture_out(j).wait_recv()
            sending(0, fars - 1).wait_send()
            spread_out = (lax.broadcasted_iota(jnp.int32, (8, 128), 0) + 2 * fars == lane).astype(jnp.float32)
            theirs = lax.dot_general(
                got_rows[...], spread_out, TN, precision=lax.Precision.HIGHEST, preferred_element_type=jnp.float32)
            logs_far = far_logs[...] + theirs
            logs_near = near_logs[...]
            top = jnp.maximum(logs_near, logs_far)
            total = top + jnp.log(jnp.exp(logs_near - top) + jnp.exp(logs_far - top))
            logs_ref[...] = total
            share = jnp.exp(logs_near - total)
            low = lane < HEAD_DIM
            for pair in range(pairs):
                part = jnp.where(low, share[:, 2 * pair : 2 * pair + 1], share[:, 2 * pair + 1 : 2 * pair + 2])
                other = (far[pair] if pair < fars else got[pair - fars]).astype(jnp.float32)
                mix_ref[:, pair * 128 : (pair + 1) * 128] = (other + (near[pair] - other) * part).astype(mix_ref.dtype)

        for which in range(3):
            saving(which).wait()


def pair_attend(q, k, v, collective_id, tile=384):
    rows, width = q.shape
    pairs = width // 128
    fars = pairs // 2
    block = pl.BlockSpec((rows, 128), lambda i: (0, jnp.minimum(i, pairs - 1)))
    anywhere = pl.BlockSpec(memory_space=pl.ANY)
    kept = jax.ShapeDtypeStruct((fars, rows, 128), jnp.bfloat16)
    half = pltpu.VMEM((fars, rows, 128), jnp.bfloat16)
    return pl.pallas_call(
        functools.partial(pair_attend_kernel, tile),
        grid=(pairs + fars + 1,),
        in_specs=[block] * 3 + [anywhere] * 3,
        out_specs=[pl.BlockSpec((rows, width), lambda i: (0, 0)), pl.BlockSpec((rows, 128), lambda i: (0, 0))] + [anywhere] * 3,
        out_shape=[
            jax.ShapeDtypeStruct((rows, width), jnp.bfloat16), jax.ShapeDtypeStruct((rows, 128), jnp.float32), kept, kept, kept],
        scratch_shapes=[
            pltpu.VMEM((pairs, rows, 128), jnp.float32), pltpu.VMEM((rows, 128), jnp.float32),
            half, half, half, half, pltpu.VMEM((rows, 128), jnp.float32), half,
            pltpu.VMEM((8, rows), jnp.float32), pltpu.VMEM((8, rows), jnp.float32),
            pltpu.SemaphoreType.DMA((5, fars)), pltpu.SemaphoreType.DMA((5, fars)),
            pltpu.SemaphoreType.DMA((3, fars)), pltpu.SemaphoreType.DMA((3,)),
        ],
        compiler_params=pltpu.CompilerParams(
            collective_id=collective_id, has_side_effects=True, vmem_limit_bytes=48 << 20),
        cost_estimate=pl.CostEstimate(
            flops=4 * rows * rows * width, bytes_accessed=16 * rows * width, transcendentals=rows * rows * pairs * 2),
    )(q, k, v, q, k, v)


def fast(
    frames_in, text_states, self_query, self_key, self_value, self_output, cross_query, cross_key, cross_value, cross_output,
    up_weight, down_weight, first_gain, first_bias, second_gain, second_bias, third_gain, third_bias, cotangent,
):
    row = lax.axis_index("row")
    rows, width = frames_in.shape
    half = width // 2
    piece = first_gain.shape[0]
    block_rows, block_cols = self_query.shape
    back = row % 2
    pairs = lax.axis_size("row") // 2
    forth_perm = [(2 * i, 2 * i + 1) for i in range(pairs)]
    back_perm = [(2 * i + 1, 2 * i) for i in range(pairs)]
    swap = forth_perm + back_perm

    def forth(array):
        return lax.ppermute(array, "row", forth_perm)

    def home(array):
        return lax.ppermute(array, "row", back_perm)

    def by_side(first, second):
        return jnp.where(back == 0, first, second)

    gains = jnp.zeros((1, 16, 128), jnp.bfloat16)
    gains = gains.at[0, :6, :piece].set(
        jnp.stack([first_gain, first_bias, second_gain, second_bias, third_gain, third_bias])
    )

    everyone = ("row", "col")
    places = (lax.axis_size("row"), lax.axis_size("col"))
    up_blocks = lax.all_gather(up_weight, everyone).reshape(*places, *up_weight.shape)
    down_blocks = lax.all_gather(down_weight, everyone).reshape(*places, *down_weight.shape)

    def small(block):
        return block.reshape(1, block_rows, block_cols)

    def flat(array):
        return array.reshape(-1, array.shape[-1])

    early = gather_blocks([small(self_query), small(self_key), small(self_value), gains], 1, 128)
    query_self, key_self, value_self = [flat(w) for w in early[:3]]
    between = jnp.stack([self_output, cross_query, cross_key, cross_value, cross_output])
    between = lax.all_gather(between, everyone).reshape(*places, *between.shape).transpose(2, 0, 3, 1, 4)
    out_self, query_cross, key_cross, value_cross, out_cross = between.reshape(-1, width, width)
    norm_params = early[3].reshape(pairs * 2, 16, -1, 128)[:, :6, :, :piece].transpose(1, 0, 2, 3)
    norm_params = norm_params.reshape(6, width).astype(jnp.float32)

    frames = frames_in.astype(jnp.float32)
    hidden_one = norm_forward(frames, norm_params[0], norm_params[1]).astype(jnp.bfloat16)
    self_k = matmul(hidden_one, key_self).astype(jnp.bfloat16)
    self_v = matmul(hidden_one, value_self).astype(jnp.bfloat16)
    self_q = matmul(hidden_one, query_self).astype(jnp.bfloat16)
    self_mix, log_lanes, far_q, far_k, far_v = pair_attend(self_q, self_k, self_v, 5)
    half_heads = half // HEAD_DIM
    self_logs = log_lanes[:, : 2 * half_heads]
    far_q, far_k, far_v = [a.transpose(1, 0, 2).reshape(rows, half) for a in (far_q, far_k, far_v)]
    resid_one = frames + matmul(self_mix, out_self)
    hidden_two = norm_forward(resid_one, norm_params[2], norm_params[3]).astype(jnp.bfloat16)
    cross_q = matmul(hidden_two, query_cross).astype(jnp.bfloat16)
    other_text = lax.ppermute(text_states, "row", swap)
    clip_text = by_side(
        jnp.concatenate([text_states, other_text]), jnp.concatenate([other_text, text_states])
    )
    text_k = matmul(clip_text, key_cross).astype(jnp.bfloat16)
    text_v = matmul(clip_text, value_cross).astype(jnp.bfloat16)
    cross_mix, cross_logs = attend(cross_q, text_k, text_v, False, jnp.bfloat16)
    cross_logs = cross_logs[:, : 2 * half_heads]
    resid_two = resid_one + matmul(cross_mix, out_cross)
    hidden_three = norm_forward(resid_two, norm_params[4], norm_params[5]).astype(jnp.bfloat16)
    layer_out, grad_three, up_grad, down_grad = feed(hidden_three, cotangent, resid_two, up_blocks, down_blocks)
    up_sum, down_sum = [
        lax.psum_scatter(g.reshape(-1, *g.shape[2:]), everyone, scatter_dimension=0).astype(jnp.float32)
        for g in (up_grad, down_grad)
    ]

    def stats_of(logs, mix, grad):
        products = mix.astype(jnp.float32) * grad.astype(jnp.float32)
        dots = jnp.sum(products.reshape(rows, -1, HEAD_DIM), axis=-1)
        both = jnp.stack([logs.T.reshape(-1, 2, rows), dots.T.reshape(-1, 2, rows)], axis=1)
        return both.reshape(-1, 4, rows)

    cotan_full = cotangent.astype(jnp.float32)
    unused_three, pull_three = jax.vjp(norm_forward, resid_two, norm_params[4], norm_params[5])
    through_three, third_gain_part, third_bias_part = pull_three(grad_three)
    grad_resid_two = cotan_full + through_three
    grad_cross = grad_resid_two.astype(jnp.bfloat16)
    cross_out_grad = over_tokens(cross_mix, grad_cross)
    grad_cross_mix = by_transposed(grad_cross, out_cross).astype(jnp.bfloat16)
    grad_cross_q, text_k_part, text_v_part = attend_back(
        cross_q, text_k, text_v, grad_cross_mix, stats_of(cross_logs, cross_mix, grad_cross_mix), False, jnp.bfloat16)
    text_rows = text_states.shape[0]
    text_parts = jnp.concatenate([text_k_part, text_v_part], axis=1)
    given = lax.ppermute(by_side(text_parts[text_rows:], text_parts[:text_rows]), "row", swap)
    kept = by_side(text_parts[:text_rows], text_parts[text_rows:])
    text_parts = (kept.astype(jnp.float32) + given.astype(jnp.float32)).astype(jnp.bfloat16)
    grad_text_k, grad_text_v = text_parts[:, :width], text_parts[:, width:]
    cross_query_part = over_tokens(hidden_two, grad_cross_q)
    cross_key_part = over_tokens(text_states, grad_text_k)
    cross_value_part = over_tokens(text_states, grad_text_v)
    text_grad = by_transposed(grad_text_k, key_cross) + by_transposed(grad_text_v, value_cross)
    grad_two = by_transposed(grad_cross_q, query_cross)
    unused_two, pull_two = jax.vjp(norm_forward, resid_one, norm_params[2], norm_params[3])
    through_two, second_gain_part, second_bias_part = pull_two(grad_two)
    grad_resid_one = grad_resid_two + through_two
    grad_self = grad_resid_one.astype(jnp.bfloat16)
    self_out_grad = over_tokens(self_mix, grad_self)
    grad_self_mix = by_transposed(grad_self, out_self).astype(jnp.bfloat16)
    stats = stats_of(self_logs, self_mix, grad_self_mix)
    far_pairs = half // 128
    sent_grad, sent_stats = home(grad_self_mix[:, half:]), home(stats[far_pairs:])
    near_dq, near_dk, near_dv = attend_back(self_q, self_k, self_v, grad_self_mix, stats, True, jnp.float32)
    far_grad = by_side(sent_grad, grad_self_mix[:, :half])
    far_stats = by_side(sent_stats, stats[:far_pairs])
    far_dq, far_dk, far_dv = attend_back(far_q, far_k, far_v, far_grad, far_stats, False, jnp.bfloat16)
    got_dq, got_dk, got_dv = forth(far_dq), home(far_dk), home(far_dv)

    def with_far(near, lower, upper):
        return (near + jnp.concatenate([lower, upper], axis=1).astype(jnp.float32)).astype(jnp.bfloat16)

    none = jnp.zeros_like(far_dq)
    grad_self_q = with_far(near_dq, by_side(none, far_dq), got_dq)
    grad_self_k = with_far(near_dk, got_dk, by_side(far_dk, none))
    grad_self_v = with_far(near_dv, got_dv, by_side(far_dv, none))
    self_query_part = over_tokens(hidden_one, grad_self_q)
    self_key_part = over_tokens(hidden_one, grad_self_k)
    self_value_part = over_tokens(hidden_one, grad_self_v)
    grad_one = (
        by_transposed(grad_self_q, query_self)
        + by_transposed(grad_self_k, key_self)
        + by_transposed(grad_self_v, value_self)
    )
    unused_one, pull_one = jax.vjp(norm_forward, frames, norm_params[0], norm_params[1])
    through_one, first_gain_part, first_bias_part = pull_one(grad_one)
    input_grad = grad_resid_one + through_one
    norm_grads = jnp.stack(
        [first_gain_part, first_bias_part, second_gain_part, second_bias_part, third_gain_part, third_bias_part]
    )
    norm_grads = norm_grads.reshape(6, 2 * pairs, -1, piece).transpose(1, 0, 2, 3)
    norm_grads = jnp.pad(norm_grads, ((0, 0), (0, 10), (0, 0), (0, 128 - piece)))

    def by_place(grad, parts):
        return grad.astype(jnp.bfloat16).reshape(pairs, 2, parts, -1, grad.shape[-1])

    early_sums = scatter_blocks(
        [by_place(g, 1) for g in (self_out_grad, cross_query_part, cross_key_part, cross_value_part, cross_out_grad)], 4, 128)
    late_sums = scatter_blocks(
        [by_place(g, 1) for g in (self_query_part, self_key_part, self_value_part)]
        + [by_place(norm_grads.reshape(2 * pairs * 16, -1), 1)], 3, 128)
    norm_parts = late_sums[3][0, :6, :piece]
    sums = late_sums[:3] + early_sums
    sums = [total.reshape(-1, total.shape[-1]) for total in sums]
    return (layer_out, input_grad, text_grad, *sums, up_sum, down_sum, *norm_parts)


def local(*arrays):
    frames_in, self_query = arrays[0], arrays[2]
    halves = 2 * frames_in.shape[0] == FRAMES and lax.axis_size("row") % 2 == 0
    if halves and lax.axis_size("col") % 2 == 0 and self_query.shape[1] % 256 == 0 and self_query.shape[0] % 128 == 0:
        return fast(*arrays)
    return general(*arrays)


def solution(mesh):
    placed = (
        P(("col", "row"), None),
        P(("col", "row"), None),
        P("row", "col"),
        P("row", "col"),
        P("row", "col"),
        P("row", "col"),
        P("row", "col"),
        P("row", "col"),
        P("row", "col"),
        P("row", "col"),
        P("row", "col"),
        P("row", "col"),
        P(("row", "col")),
        P(("row", "col")),
        P(("row", "col")),
        P(("row", "col")),
        P(("row", "col")),
        P(("row", "col")),
        P(("col", "row"), None),
    )
    return jax.shard_map(
        local,
        mesh=mesh,
        in_specs=placed,
        out_specs=(
            P(("col", "row"), None),
            P(("col", "row"), None),
            P(("col", "row"), None),
            P("row", "col"),
            P("row", "col"),
            P("row", "col"),
            P("row", "col"),
            P("row", "col"),
            P("row", "col"),
            P("row", "col"),
            P("row", "col"),
            P("row", "col"),
            P("row", "col"),
            P(("row", "col")),
            P(("row", "col")),
            P(("row", "col")),
            P(("row", "col")),
            P(("row", "col")),
            P(("row", "col")),
        ),
        check_vma=False,
    )
```

```python
import functools
from functools import partial

import jax
import jax.numpy as jnp
from jax import lax
from jax.experimental import pallas as pl
from jax.experimental.pallas import tpu as pltpu
from jax.sharding import PartitionSpec as P

HEADS = 16
HEAD_DIM = 64
FRAMES = 1500
TEXT = 64


def norm_forward(values, norm_gain, norm_bias):
    center = values - jnp.mean(values, axis=-1, keepdims=True)
    variance = jnp.mean(center * center, axis=-1, keepdims=True)
    return center * lax.rsqrt(variance + 1e-05) * norm_gain + norm_bias


def matmul(left, right):
    return jnp.dot(left, right, preferred_element_type=jnp.float32)


def by_transposed(left, right):
    return lax.dot_general(
        left, right, (((1,), (1,)), ((), ())), preferred_element_type=jnp.float32
    )


def over_tokens(left, right):
    return lax.dot_general(
        left, right, (((0,), (0,)), ((), ())), preferred_element_type=jnp.float32
    )


def collect(blocks):
    partly = (
        lax.all_gather(blocks[0], "col", axis=1, tiled=True),
        lax.all_gather(blocks[1], "col", axis=1, tiled=True),
        lax.all_gather(blocks[2], "col", axis=1, tiled=True),
        lax.all_gather(blocks[3], "col", axis=1, tiled=True),
        lax.all_gather(blocks[4], "col", axis=1, tiled=True),
        lax.all_gather(blocks[5], "col", axis=1, tiled=True),
        lax.all_gather(blocks[6], "col", axis=1, tiled=True),
        lax.all_gather(blocks[7], "col", axis=1, tiled=True),
        lax.all_gather(blocks[8], "col", axis=1, tiled=True),
        lax.all_gather(blocks[9], "col", axis=1, tiled=True),
        lax.all_gather(blocks[10], "col", axis=1, tiled=True),
    )
    return (
        lax.all_gather(partly[0], "row", axis=0, tiled=True),
        lax.all_gather(partly[1], "row", axis=0, tiled=True),
        lax.all_gather(partly[2], "row", axis=0, tiled=True),
        lax.all_gather(partly[3], "row", axis=0, tiled=True),
        lax.all_gather(partly[4], "row", axis=0, tiled=True),
        lax.all_gather(partly[5], "row", axis=0, tiled=True),
        lax.all_gather(partly[6], "row", axis=0, tiled=True),
        lax.all_gather(partly[7], "row", axis=0, tiled=True),
        lax.all_gather(partly[8], "row", axis=0, tiled=True),
        lax.all_gather(partly[9], "row", axis=0, tiled=True),
        lax.all_gather(partly[10], "row", axis=0, tiled=True),
    )


def spread(grads):
    partly = (
        lax.psum_scatter(
            grads[0].astype(jnp.bfloat16), "row", scatter_dimension=0, tiled=True
        ).astype(jnp.float32),
        lax.psum_scatter(
            grads[1].astype(jnp.bfloat16), "row", scatter_dimension=0, tiled=True
        ).astype(jnp.float32),
        lax.psum_scatter(
            grads[2].astype(jnp.bfloat16), "row", scatter_dimension=0, tiled=True
        ).astype(jnp.float32),
        lax.psum_scatter(
            grads[3].astype(jnp.bfloat16), "row", scatter_dimension=0, tiled=True
        ).astype(jnp.float32),
        lax.psum_scatter(
            grads[4].astype(jnp.bfloat16), "row", scatter_dimension=0, tiled=True
        ).astype(jnp.float32),
        lax.psum_scatter(
            grads[5].astype(jnp.bfloat16), "row", scatter_dimension=0, tiled=True
        ).astype(jnp.float32),
        lax.psum_scatter(
            grads[6].astype(jnp.bfloat16), "row", scatter_dimension=0, tiled=True
        ).astype(jnp.float32),
        lax.psum_scatter(
            grads[7].astype(jnp.bfloat16), "row", scatter_dimension=0, tiled=True
        ).astype(jnp.float32),
        lax.psum_scatter(
            grads[8].astype(jnp.bfloat16), "row", scatter_dimension=0, tiled=True
        ).astype(jnp.float32),
        lax.psum_scatter(
            grads[9].astype(jnp.bfloat16), "row", scatter_dimension=0, tiled=True
        ).astype(jnp.float32),
        lax.psum_scatter(
            grads[10].astype(jnp.bfloat16), "row", scatter_dimension=0, tiled=True
        ).astype(jnp.float32),
    )
    return (
        lax.psum_scatter(
            partly[0].astype(jnp.bfloat16), "col", scatter_dimension=1, tiled=True
        ).astype(jnp.float32),
        lax.psum_scatter(
            partly[1].astype(jnp.bfloat16), "col", scatter_dimension=1, tiled=True
        ).astype(jnp.float32),
        lax.psum_scatter(
            partly[2].astype(jnp.bfloat16), "col", scatter_dimension=1, tiled=True
        ).astype(jnp.float32),
        lax.psum_scatter(
            partly[3].astype(jnp.bfloat16), "col", scatter_dimension=1, tiled=True
        ).astype(jnp.float32),
        lax.psum_scatter(
            partly[4].astype(jnp.bfloat16), "col", scatter_dimension=1, tiled=True
        ).astype(jnp.float32),
        lax.psum_scatter(
            partly[5].astype(jnp.bfloat16), "col", scatter_dimension=1, tiled=True
        ).astype(jnp.float32),
        lax.psum_scatter(
            partly[6].astype(jnp.bfloat16), "col", scatter_dimension=1, tiled=True
        ).astype(jnp.float32),
        lax.psum_scatter(
            partly[7].astype(jnp.bfloat16), "col", scatter_dimension=1, tiled=True
        ).astype(jnp.float32),
        lax.psum_scatter(
            partly[8].astype(jnp.bfloat16), "col", scatter_dimension=1, tiled=True
        ).astype(jnp.float32),
        lax.psum_scatter(
            partly[9].astype(jnp.bfloat16), "col", scatter_dimension=1, tiled=True
        ).astype(jnp.float32),
        lax.psum_scatter(
            partly[10].astype(jnp.bfloat16), "col", scatter_dimension=1, tiled=True
        ).astype(jnp.float32),
    )


def heads_layout(stacked):
    return lax.all_to_all(stacked, "row", split_axis=1, concat_axis=0, tiled=True)


def tokens_layout(stacked):
    return lax.all_to_all(stacked, "row", split_axis=0, concat_axis=2, tiled=True)


def by_clips(arranged, start, count, length, heads_dev):
    section = arranged[:, start : start + count]
    return section.reshape(-1, length, heads_dev, HEAD_DIM)


def causal_scores(query_clip, key_clip, causal):
    scores = jnp.einsum(
        "qhd,khd->hqk", query_clip, key_clip, preferred_element_type=jnp.float32
    ) * HEAD_DIM ** (-0.5)
    if causal:
        allowed = jnp.arange(scores.shape[1])[:, None] >= jnp.arange(scores.shape[2])[None, :]
        scores = jnp.where(allowed, scores, -1e30)
    return scores


def attend_forward(query_clips, key_clips, value_clips, causal):

    def one_clip(operands):
        query_clip, key_clip, value_clip = operands
        scores = causal_scores(query_clip, key_clip, causal)
        highest = jnp.max(scores, axis=-1, keepdims=True)
        powers = jnp.exp(scores - highest)
        totals = jnp.sum(powers, axis=-1, keepdims=True)
        weights_low = (powers / totals).astype(jnp.bfloat16)
        mixture = jnp.einsum(
            "hqk,khd->qhd", weights_low, value_clip, preferred_element_type=jnp.float32
        )
        return (mixture.astype(jnp.bfloat16), (highest + jnp.log(totals))[..., 0])

    return lax.map(one_clip, (query_clips, key_clips, value_clips))


def attend_backward(query_clips, key_clips, value_clips, log_sums, grad_clips, causal):

    def one_clip(operands):
        query_clip, key_clip, value_clip, log_clip, grad_clip = operands
        scores = causal_scores(query_clip, key_clip, causal)
        probs_full = jnp.exp(scores - log_clip[..., None])
        grad_probs = jnp.einsum(
            "qhd,khd->hqk", grad_clip, value_clip, preferred_element_type=jnp.float32
        )
        grad_value = jnp.einsum(
            "hqk,qhd->khd",
            probs_full.astype(jnp.bfloat16),
            grad_clip,
            preferred_element_type=jnp.float32,
        )
        centered = grad_probs - jnp.sum(probs_full * grad_probs, axis=-1, keepdims=True)
        grad_scores = (probs_full * centered).astype(jnp.bfloat16)
        grad_query = jnp.einsum(
            "hqk,khd->qhd", grad_scores, key_clip, preferred_element_type=jnp.float32
        ) * HEAD_DIM ** (-0.5)
        grad_key = jnp.einsum(
            "hqk,qhd->khd", grad_scores, query_clip, preferred_element_type=jnp.float32
        ) * HEAD_DIM ** (-0.5)
        return (
            grad_query.astype(jnp.bfloat16),
            grad_key.astype(jnp.bfloat16),
            grad_value.astype(jnp.bfloat16),
        )

    return lax.map(one_clip, (query_clips, key_clips, value_clips, log_sums, grad_clips))


def general(
    frames_in,
    text_states,
    self_query,
    self_key,
    self_value,
    self_output,
    cross_query,
    cross_key,
    cross_value,
    cross_output,
    up_weight,
    down_weight,
    first_gain,
    first_bias,
    second_gain,
    second_bias,
    third_gain,
    third_bias,
    cotangent,
):
    row_count = lax.axis_size("row")
    col_count = lax.axis_size("col")
    heads_dev = HEADS // row_count
    width_dev = heads_dev * HEAD_DIM
    tok_rows = frames_in.shape[0]
    text_rows = text_states.shape[0]
    piece_len = first_gain.shape[0]
    gain_block = jnp.stack(
        [first_gain, first_bias, second_gain, second_bias, third_gain, third_bias]
    ).reshape(1, 6 * piece_len)
    param_blocks = (
        self_query,
        self_key,
        self_value,
        self_output,
        cross_query,
        cross_key,
        cross_value,
        cross_output,
        up_weight,
        down_weight,
        gain_block,
    )

    def unpack_gains(gathered_gains):
        arranged = gathered_gains.reshape(row_count, col_count, 6, piece_len).transpose(2, 0, 1, 3)
        return arranged.reshape(6, row_count * col_count * piece_len).astype(jnp.float32)

    gathered = collect(param_blocks)
    (
        query_self,
        key_self,
        value_self,
        out_self,
        query_cross,
        key_cross,
        value_cross,
        out_cross,
        up_full,
        down_full,
    ) = gathered[:10]
    norm_params = unpack_gains(gathered[10])
    frames = frames_in.astype(jnp.float32)
    hidden_one = norm_forward(frames, norm_params[0], norm_params[1]).astype(jnp.bfloat16)
    self_q = matmul(hidden_one, query_self).astype(jnp.bfloat16)
    self_k = matmul(hidden_one, key_self).astype(jnp.bfloat16)
    self_v = matmul(hidden_one, value_self).astype(jnp.bfloat16)
    text_k = matmul(text_states, key_cross).astype(jnp.bfloat16)
    text_v = matmul(text_states, value_cross).astype(jnp.bfloat16)
    sent_rows = 3 * tok_rows + 2 * text_rows
    arranged = heads_layout(jnp.concatenate([self_q, self_k, self_v, text_k, text_v], axis=0))
    arranged = arranged.reshape(row_count, sent_rows, width_dev)
    query_clips = by_clips(arranged, 0, tok_rows, FRAMES, heads_dev)
    key_clips = by_clips(arranged, tok_rows, tok_rows, FRAMES, heads_dev)
    value_clips = by_clips(arranged, 2 * tok_rows, tok_rows, FRAMES, heads_dev)
    text_keys = by_clips(arranged, 3 * tok_rows, text_rows, TEXT, heads_dev)
    text_values = by_clips(arranged, 3 * tok_rows + text_rows, text_rows, TEXT, heads_dev)
    self_clips, self_logs = attend_forward(query_clips, key_clips, value_clips, True)
    self_mix = tokens_layout(self_clips.reshape(row_count, tok_rows, width_dev))[0]
    resid_one = frames + matmul(self_mix, out_self)
    hidden_two = norm_forward(resid_one, norm_params[2], norm_params[3]).astype(jnp.bfloat16)
    cross_q = matmul(hidden_two, query_cross).astype(jnp.bfloat16)
    cross_arranged = heads_layout(cross_q).reshape(row_count, tok_rows, width_dev)
    cross_queries = by_clips(cross_arranged, 0, tok_rows, FRAMES, heads_dev)
    cross_clips, cross_logs = attend_forward(cross_queries, text_keys, text_values, False)
    cross_mix = tokens_layout(cross_clips.reshape(row_count, tok_rows, width_dev))[0]
    resid_two = resid_one + matmul(cross_mix, out_cross)
    hidden_three = norm_forward(resid_two, norm_params[4], norm_params[5]).astype(jnp.bfloat16)
    pre_act = matmul(hidden_three, up_full)
    inner = jax.nn.gelu(pre_act, approximate=False).astype(jnp.bfloat16)
    layer_out = (resid_two + matmul(inner, down_full)).astype(jnp.bfloat16)
    gathered = collect(param_blocks)
    (
        query_self,
        key_self,
        value_self,
        out_self,
        query_cross,
        key_cross,
        value_cross,
        out_cross,
        up_full,
        down_full,
    ) = gathered[:10]
    norm_params = unpack_gains(gathered[10])
    cotan_full = cotangent.astype(jnp.float32)
    down_grad = over_tokens(inner, cotangent)
    grad_inner = by_transposed(cotangent, down_full)
    unused_gelu, gelu_pull = jax.vjp(partial(jax.nn.gelu, approximate=False), pre_act)
    grad_pre = gelu_pull(grad_inner)[0].astype(jnp.bfloat16)
    up_grad = over_tokens(hidden_three, grad_pre)
    grad_three = by_transposed(grad_pre, up_full)
    unused_three, pull_three = jax.vjp(norm_forward, resid_two, norm_params[4], norm_params[5])
    through_three, third_gain_part, third_bias_part = pull_three(grad_three)
    grad_resid_two = cotan_full + through_three
    grad_cross = grad_resid_two.astype(jnp.bfloat16)
    cross_out_grad = over_tokens(cross_mix, grad_cross)
    grad_cross_mix = by_transposed(grad_cross, out_cross).astype(jnp.bfloat16)
    grad_cross_arr = heads_layout(grad_cross_mix).reshape(row_count, tok_rows, width_dev)
    grad_cross_clips = by_clips(grad_cross_arr, 0, tok_rows, FRAMES, heads_dev)
    cq_clips, tk_clips, tv_clips = attend_backward(
        cross_queries, text_keys, text_values, cross_logs, grad_cross_clips, False
    )
    back_cross = jnp.concatenate(
        [
            cq_clips.reshape(row_count, tok_rows, width_dev),
            tk_clips.reshape(row_count, text_rows, width_dev),
            tv_clips.reshape(row_count, text_rows, width_dev),
        ],
        axis=1,
    )
    back_cross = tokens_layout(back_cross)[0]
    grad_cross_q = back_cross[:tok_rows]
    grad_text_k = back_cross[tok_rows : tok_rows + text_rows]
    grad_text_v = back_cross[tok_rows + text_rows :]
    cross_query_part = over_tokens(hidden_two, grad_cross_q)
    cross_key_part = over_tokens(text_states, grad_text_k)
    cross_value_part = over_tokens(text_states, grad_text_v)
    text_grad = by_transposed(grad_text_k, key_cross) + by_transposed(grad_text_v, value_cross)
    grad_two = by_transposed(grad_cross_q, query_cross)
    unused_two, pull_two = jax.vjp(norm_forward, resid_one, norm_params[2], norm_params[3])
    through_two, second_gain_part, second_bias_part = pull_two(grad_two)
    grad_resid_one = grad_resid_two + through_two
    grad_self = grad_resid_one.astype(jnp.bfloat16)
    self_out_grad = over_tokens(self_mix, grad_self)
    grad_self_mix = by_transposed(grad_self, out_self).astype(jnp.bfloat16)
    grad_self_arr = heads_layout(grad_self_mix).reshape(row_count, tok_rows, width_dev)
    grad_self_clips = by_clips(grad_self_arr, 0, tok_rows, FRAMES, heads_dev)
    sq_clips, sk_clips, sv_clips = attend_backward(
        query_clips, key_clips, value_clips, self_logs, grad_self_clips, True
    )
    back_self = jnp.concatenate(
        [
            sq_clips.reshape(row_count, tok_rows, width_dev),
            sk_clips.reshape(row_count, tok_rows, width_dev),
            sv_clips.reshape(row_count, tok_rows, width_dev),
        ],
        axis=1,
    )
    back_self = tokens_layout(back_self)[0]
    grad_self_q = back_self[:tok_rows]
    grad_self_k = back_self[tok_rows : 2 * tok_rows]
    grad_self_v = back_self[2 * tok_rows :]
    self_query_part = over_tokens(hidden_one, grad_self_q)
    self_key_part = over_tokens(hidden_one, grad_self_k)
    self_value_part = over_tokens(hidden_one, grad_self_v)
    grad_one = (
        by_transposed(grad_self_q, query_self)
        + by_transposed(grad_self_k, key_self)
        + by_transposed(grad_self_v, value_self)
    )
    unused_one, pull_one = jax.vjp(norm_forward, frames, norm_params[0], norm_params[1])
    through_one, first_gain_part, first_bias_part = pull_one(grad_one)
    input_grad = grad_resid_one + through_one
    norm_grads = jnp.stack(
        [
            first_gain_part,
            first_bias_part,
            second_gain_part,
            second_bias_part,
            third_gain_part,
            third_bias_part,
        ]
    )
    norm_grads = norm_grads.reshape(6, row_count, col_count, piece_len).transpose(1, 2, 0, 3)
    norm_grads = norm_grads.reshape(row_count, col_count * 6 * piece_len)
    summed = spread(
        (
            self_query_part,
            self_key_part,
            self_value_part,
            self_out_grad,
            cross_query_part,
            cross_key_part,
            cross_value_part,
            cross_out_grad,
            up_grad,
            down_grad,
            norm_grads,
        )
    )
    norm_parts = summed[10].reshape(6, piece_len)
    return (
        layer_out,
        input_grad,
        text_grad,
        summed[0],
        summed[1],
        summed[2],
        summed[3],
        summed[4],
        summed[5],
        summed[6],
        summed[7],
        summed[8],
        summed[9],
        norm_parts[0],
        norm_parts[1],
        norm_parts[2],
        norm_parts[3],
        norm_parts[4],
        norm_parts[5],
    )


NT=(((1,),(1,)),((),())); NN=(((1,),(0,)),((),())); TN=(((0,),(0,)),((),()))
def dg(a,b,dims): return lax.dot_general(a,b,dims,preferred_element_type=jnp.float32)

def attend_kernel(causal,tile,q_ref,k_ref,v_ref,o_ref,lse_ref):
    pair=pl.program_id(0)
    rows=q_ref.shape[0]
    low=lax.broadcasted_iota(jnp.int32,(1,128),1)<HEAD_DIM
    lane=lax.broadcasted_iota(jnp.int32,(1,128),1)
    value=v_ref[...]
    ones=jnp.ones_like(value)
    @pl.when(pair==0)
    def _(): lse_ref[...]=jnp.zeros_like(lse_ref)
    for start in range(0,rows,tile):
        n=min(tile,rows-start)
        q=q_ref[start:start+n,:]*jnp.bfloat16(HEAD_DIM**-0.5)
        mixed=[]; sums=[]
        lse=lse_ref[start:start+n,:]
        for h in range(2):
            mine=low if h==0 else jnp.logical_not(low)
            qh=jnp.where(mine,q,jnp.bfloat16(0))
            vh=jnp.where(mine,value,ones)
            if causal:
                spans=([(0,start)] if start else [])+[(start,n)]
            else: spans=[(0,k_ref.shape[0])]
            scores=[]
            for at,length in spans:
                s=dg(qh,k_ref[at:at+length,:],NT)
                if causal and at==start:
                    ok=lax.broadcasted_iota(jnp.int32,s.shape,0)>=lax.broadcasted_iota(jnp.int32,s.shape,1)
                    s=jnp.where(ok,s,-1e30)
                scores.append(s)
            top=functools.reduce(jnp.maximum,[jnp.max(s,axis=1,keepdims=True) for s in scores])
            out=None
            for (at,length),s in zip(spans,scores):
                p=jnp.exp(s-top).astype(jnp.bfloat16)
                part=dg(p,vh[at:at+length,:],NN)
                out=part if out is None else out+part
            total=out[:,HEAD_DIM:HEAD_DIM+1] if h==0 else out[:,0:1]
            mixed.append(out/total)
            lse=jnp.where(lane==2*pair+h,top+jnp.log(total),lse)
        lse_ref[start:start+n,:]=lse
        o_ref[start:start+n,:]=jnp.where(low,mixed[0],mixed[1]).astype(o_ref.dtype)

def attend(q,k,v,causal,out_dtype,tile=256):
    rows,width=q.shape; keys=k.shape[0]
    return pl.pallas_call(functools.partial(attend_kernel,causal,tile),grid=(width//128,),
        in_specs=[pl.BlockSpec((rows,128),lambda i:(0,i)),pl.BlockSpec((keys,128),lambda i:(0,i)),pl.BlockSpec((keys,128),lambda i:(0,i))],
        out_specs=[pl.BlockSpec((rows,128),lambda i:(0,i)),pl.BlockSpec((rows,128),lambda i:(0,0))],
        out_shape=[jax.ShapeDtypeStruct((rows,width),out_dtype),jax.ShapeDtypeStruct((rows,128),jnp.float32)],
        compiler_params=pltpu.CompilerParams(vmem_limit_bytes=40<<20),
        cost_estimate=pl.CostEstimate(flops=4*rows*keys*width,bytes_accessed=8*rows*width,transcendentals=rows*keys*width//64))(q,k,v)

def attend_back_kernel(causal,tile,q_ref,k_ref,v_ref,do_ref,st_ref,dq_ref,dk_ref,dv_ref,acc):
    rows=q_ref.shape[0]; keys=k_ref.shape[0]
    low=lax.broadcasted_iota(jnp.int32,(1,128),1)<HEAD_DIM
    acc[...]=jnp.zeros_like(acc)
    for start in range(0,keys,tile):
        n=min(tile,keys-start)
        k=k_ref[start:start+n,:]*jnp.bfloat16(HEAD_DIM**-0.5)
        v=v_ref[start:start+n,:]
        spans=[(0,rows)]
        if causal: spans=[(start,n)]+([(start+n,rows-start-n)] if start+n<rows else [])
        dks=[];dvs=[]
        for h in range(2):
            mine=low if h==0 else jnp.logical_not(low)
            kh=jnp.where(mine,k,jnp.bfloat16(0)); vh=jnp.where(mine,v,jnp.bfloat16(0))
            dk=dv=None
            for at,length in spans:
                qs=q_ref[at:at+length,:]; do=do_ref[at:at+length,:]
                s=dg(kh,qs,NT)
                p=jnp.exp(s-st_ref[0,h:h+1,at:at+length])
                if causal and at==start:
                    ok=lax.broadcasted_iota(jnp.int32,s.shape,0)<=lax.broadcasted_iota(jnp.int32,s.shape,1)
                    p=jnp.where(ok,p,0.0)
                dp=dg(vh,do,NT)
                ds=(p*(dp-st_ref[0,2+h:3+h,at:at+length])).astype(jnp.bfloat16)
                a=dg(p.astype(jnp.bfloat16),do,NN); b=dg(ds,qs,NN)
                dv=a if dv is None else dv+a
                dk=b if dk is None else dk+b
                acc[at:at+length,:]+=dg(ds,kh,TN)
            dks.append(dk);dvs.append(dv)
        dk_ref[start:start+n,:]=(jnp.where(low,dks[0],dks[1])*HEAD_DIM**-0.5).astype(dk_ref.dtype)
        dv_ref[start:start+n,:]=jnp.where(low,dvs[0],dvs[1]).astype(dv_ref.dtype)
    dq_ref[...]=acc[...].astype(dq_ref.dtype)

def attend_back(q,k,v,do,stats,causal,out_dtype,tile=256):
    rows,width=q.shape; keys=k.shape[0]
    bq=pl.BlockSpec((rows,128),lambda i:(0,i)); bk=pl.BlockSpec((keys,128),lambda i:(0,i))
    return pl.pallas_call(functools.partial(attend_back_kernel,causal,tile),grid=(width//128,),
        in_specs=[bq,bk,bk,bq,pl.BlockSpec((1,4,rows),lambda i:(i,0,0))],out_specs=[bq,bk,bk],
        out_shape=[jax.ShapeDtypeStruct((rows,width),out_dtype),jax.ShapeDtypeStruct((keys,width),out_dtype),jax.ShapeDtypeStruct((keys,width),out_dtype)],
        scratch_shapes=[pltpu.VMEM((rows,128),jnp.float32)],
        compiler_params=pltpu.CompilerParams(vmem_limit_bytes=40<<20),
        cost_estimate=pl.CostEstimate(flops=10*rows*keys*width,bytes_accessed=16*rows*width,transcendentals=rows*keys*width//64))(q,k,v,do,stats)

def feed_kernel(h_ref,cot_ref,res_ref,up_ref,down_ref,out_ref,g_ref,dup_ref,ddown_ref,acc):
    i=pl.program_id(0)
    @pl.when(i==0)
    def _():
        acc[...]=res_ref[...]
        g_ref[...]=jnp.zeros_like(g_ref)
    h=h_ref[...]
    up=up_ref[:,0].reshape(h.shape[1],-1)
    blocks,wide=down_ref.shape[1],down_ref.shape[3]
    pre=dg(h,up,NN)
    cdf=0.5*(1.0+lax.erf(pre*0.7071067811865476))
    inner=(pre*cdf).astype(jnp.bfloat16)
    slope=cdf+pre*(jnp.exp(-0.5*pre*pre)*0.3989422804014327)
    grad=None
    for at in range(blocks):
        columns=slice(at*wide,(at+1)*wide)
        cot=cot_ref[:,columns]
        acc[:,columns]+=dg(inner,down_ref[0,at],NN)
        ddown_ref[:,columns]=dg(inner,cot,TN).astype(ddown_ref.dtype)
        part=dg(cot,down_ref[0,at],NT)
        grad=part if grad is None else grad+part
    gpre=(grad*slope).astype(jnp.bfloat16)
    dup_ref[:,0]=dg(h,gpre,TN).astype(dup_ref.dtype).reshape(dup_ref.shape[0],dup_ref.shape[2],dup_ref.shape[3])
    g_ref[...]+=dg(gpre,up,NT)
    @pl.when(i==pl.num_programs(0)-1)
    def _(): out_ref[...]=acc[...].astype(out_ref.dtype)

def feed(h,cot,res,up,down):
    rows,d=h.shape; chunk=down.shape[2]; strips=up.shape[3]//chunk; ff=down.shape[0]*chunk
    whole=pl.BlockSpec((rows,d),lambda i:(0,0))
    up_spec=pl.BlockSpec((up.shape[0],1,up.shape[2],chunk),lambda i:(0,i//strips,0,i%strips))
    down_spec=pl.BlockSpec((1,)+down.shape[1:],lambda i:(i,0,0,0))
    return pl.pallas_call(feed_kernel,grid=(ff//chunk,),
        in_specs=[whole,whole,whole,up_spec,down_spec],
        out_specs=[whole,whole,up_spec,pl.BlockSpec((chunk,d),lambda i:(i,0))],
        out_shape=[jax.ShapeDtypeStruct((rows,d),jnp.bfloat16),jax.ShapeDtypeStruct((rows,d),jnp.float32),jax.ShapeDtypeStruct(up.shape,jnp.bfloat16),jax.ShapeDtypeStruct((ff,d),jnp.bfloat16)],
        scratch_shapes=[pltpu.VMEM((rows,d),jnp.float32)],
        compiler_params=pltpu.CompilerParams(vmem_limit_bytes=56<<20),
        cost_estimate=pl.CostEstimate(flops=12*rows*d*ff,bytes_accessed=8*d*ff+16*rows*d,transcendentals=2*rows*ff))(h,cot,res,up,down)


MESH = pl.DeviceIdType.MESH
ORDERS = ("xzy", "yzx", "xzy", "yzx", "zxy", "zyx")


class Place:
    def __init__(self):
        row, col = lax.axis_index("row"), lax.axis_index("col")
        self.z, self.y, self.x, self.k = row // 2, row % 2, col // 2, col % 2
        self.along = lax.axis_size("row") // 2

    def device(self, dz=0, y=False, x=False, k=False):
        other_y = 1 - self.y if y else self.y
        other_x = 1 - self.x if x else self.x
        other_k = 1 - self.k if k else self.k
        return ((self.z + dz) * 2 + other_y, other_x * 2 + other_k)

    def across(self, axis):
        return self.device(y=axis == "y", x=axis == "x", k=axis == "k")

    def greet(self):
        barrier = pltpu.get_barrier_semaphore()
        for axis in "xyk":
            pl.semaphore_signal(barrier, inc=1, device_id=self.across(axis), device_id_type=MESH)

        @pl.when(self.z > 0)
        def _():
            pl.semaphore_signal(barrier, inc=1, device_id=self.device(dz=-1), device_id_type=MESH)

        @pl.when(self.z + 1 < self.along)
        def _():
            pl.semaphore_signal(barrier, inc=1, device_id=self.device(dz=1), device_id_type=MESH)

        below = jnp.where(self.z > 0, 1, 0)
        above = jnp.where(self.z + 1 < self.along, 1, 0)
        pl.semaphore_wait(barrier, 3 + below + above)


def when(condition, run):
    if condition is None:
        run()
    else:
        pl.when(condition)(run)


def in_turn(units, lag):
    ready = [(lag * at, at) for at in range(len(units))]
    while ready:
        turn, at = min(ready)
        ready.remove((turn, at))
        if next(units[at], units) is not units:
            ready.append((turn + 1, at))
        yield


class Gather:
    def __init__(self, place, block, full, strip, order, send, recv):
        self.place, self.block, self.full, self.strip = place, block, full, strip
        turn = order.index("z")
        self.before, self.after = order[:turn], order[turn + 1 :]
        self.send, self.recv, self.used, self.sent, self.started = send, recv, 0, 0, []

    def region(self, z, y, x):
        part, start, count = self.strip
        column = (x * 2 + self.place.k) * self.block.shape[-1] + start
        return self.full.at[z, y, part, :, pl.ds(pl.multiple_of(column, 128), count)]

    def held(self, done, z):
        y = slice(None) if "y" in done else self.place.y
        return [self.region(z, y, x) for x in (range(2) if "x" in done else [self.place.x])]

    def pairs(self, done, z, first):
        if first:
            part, start, count = self.strip
            place = self.place
            return [(self.block.at[part, :, pl.ds(start, count)], self.region(place.z, place.y, place.x))]
        return [(region, region) for region in self.held(done, z)]

    def semaphore(self):
        self.used += 2
        return self.used - 2

    def copies(self, device, pairs, semaphore, send=0):
        return [
            pltpu.make_async_remote_copy(
                src_ref=source, dst_ref=target, send_sem=self.send.at[send + at],
                recv_sem=self.recv.at[semaphore + at], device_id=device, device_id_type=MESH)
            for at, (source, target) in enumerate(pairs)
        ]

    def start(self, device, pairs, condition, semaphore):
        copies = self.copies(device, pairs, semaphore, self.sent)
        self.sent += len(copies)
        when(condition, lambda: [copy.start() for copy in copies] and None)
        self.started.append((condition, copies))
        return condition, copies

    def arrive(self, sent):
        condition, copies = sent
        when(condition, lambda: [copy.wait_recv() for copy in copies] and None)

    def stages(self):
        place, along = self.place, self.place.along
        done = []
        for axis in self.before:
            sent = self.start(place.across(axis), self.pairs(done, place.z, not done), None, self.semaphore())
            yield
            self.arrive(sent)
            done.append(axis)
        first = not done
        from_left = [self.semaphore() for _ in range(along - 1)]
        from_right = [self.semaphore() for _ in range(along - 1)]

        def pass_on(turn, step):
            axes = done + list(self.after[:turn])
            device = place.across(self.after[turn])
            if step == 0:
                return turn, step, [self.start(device, self.pairs(axes, place.z, not axes), None, self.semaphore())]
            return turn, step, [
                self.start(device, self.pairs(axes, z, False), (z >= 0) & (z < along), self.semaphore())
                for z in (place.z - step, place.z + step)
            ]

        def step_out(step):
            left, right = place.z - (step - 1), place.z + (step - 1)
            self.start(place.device(dz=1), self.pairs(done, left, first and step == 1),
                       (left >= 0) & (place.z + 1 < along), from_left[step - 1])
            self.start(place.device(dz=-1), self.pairs(done, right, first and step == 1),
                       (right < along) & (place.z > 0), from_right[step - 1])

        def step_in(step):
            for z, semaphore in ((place.z - step, from_left), (place.z + step, from_right)):
                copies = self.copies(place.across("k"), self.pairs(done, z, False), semaphore[step - 1])
                self.arrive(((z >= 0) & (z < along), copies))

        step_out(1)
        waiting = [pass_on(0, 0)] if self.after else []
        for step in range(1, along + len(self.after)):
            yield
            if step < along:
                step_in(step)
                if step + 1 < along:
                    step_out(step + 1)
            following = []
            for turn, at, sent in waiting:
                for one in sent:
                    self.arrive(one)
                if turn + 1 < len(self.after):
                    following.append(pass_on(turn + 1, at))
            if self.after and step < along:
                following.append(pass_on(0, step))
            waiting = following
        everything = [self.region(slice(None), slice(None), x) for x in range(2)]
        sent = self.start(place.across("k"), [(r, r) for r in everything], None, self.semaphore())
        yield
        self.arrive(sent)

    def finish(self):
        for condition, copies in self.started:
            when(condition, lambda copies=copies: [copy.wait_send() for copy in copies] and None)


def gather_kernel(units, count, *refs):
    blocks, fulls = refs[:count], refs[count : 2 * count]
    send, recv, local_sem = refs[2 * count :]
    place = Place()
    place.greet()
    own = []
    for at, (block, full) in enumerate(zip(blocks, fulls)):
        width = block.shape[-1]
        columns = pl.ds(pl.multiple_of((place.x * 2 + place.k) * width, 128), width)
        copy = pltpu.make_async_copy(block, full.at[place.z, place.y, :, :, columns], local_sem.at[at])
        copy.start()
        own.append(copy)
    gathers = [
        Gather(place, blocks[which], fulls[which], strip, order, send.at[at], recv.at[at])
        for at, (which, strip, order) in enumerate(units)
    ]
    for unused in in_turn([gather.stages() for gather in gathers], 0.0):
        while own:
            own.pop().wait()
    for gather in gathers:
        gather.finish()


def gather_units(blocks, least, orders):
    strips = []
    for which, block in enumerate(blocks):
        wide = min(least, block.shape[-1])
        for part in range(block.shape[0]):
            for start in range(0, block.shape[-1], wide):
                strips.append((which, (part, start, wide)))
    return [strip + (orders[at % len(orders)],) for at, strip in enumerate(strips)]


def gather_blocks(blocks, collective_id, least):
    along, cols = lax.axis_size("row") // 2, lax.axis_size("col")
    units = gather_units(blocks, least, ORDERS)
    count = len(blocks)
    anywhere = pl.BlockSpec(memory_space=pl.ANY)
    moved = sum(block.size for block in blocks) * 2 * along * 2 * cols
    return pl.pallas_call(
        functools.partial(gather_kernel, units, count),
        out_shape=[
            jax.ShapeDtypeStruct((along, 2) + b.shape[:2] + (cols * b.shape[2],), b.dtype) for b in blocks
        ],
        in_specs=[anywhere] * count,
        out_specs=[anywhere] * count,
        scratch_shapes=[
            pltpu.SemaphoreType.DMA((len(units), 8 * along)),
            pltpu.SemaphoreType.DMA((len(units), 12 * along)),
            pltpu.SemaphoreType.DMA((count,)),
        ],
        compiler_params=pltpu.CompilerParams(collective_id=collective_id, has_side_effects=True),
        cost_estimate=pl.CostEstimate(flops=0, bytes_accessed=2 * moved, transcendentals=0),
    )(*blocks)


def add_blocks(total, extra, leading):
    def one(at, unused):
        place = []
        for size in leading[::-1]:
            place.append(at % size)
            at = at // size
        place = tuple(place[::-1])
        total[place] = total[place] + extra[place]
        return unused

    if not leading:
        total[...] = total[...] + extra[...]
        return
    count = 1
    for size in leading:
        count *= size
    lax.fori_loop(0, count, one, 0)


class Scatter:
    def __init__(self, place, grad, out, strip, width, order, slots, send, recv, local):
        self.place, self.grad, self.out, self.strip, self.width = place, grad, out, strip, width
        self.order = order[::-1]
        self.total, self.other_core, self.halves, self.steps = slots
        self.send, self.recv, self.local = send, recv, local
        self.used, self.started = 0, []

    def region(self, x, k):
        part, start, count = self.strip
        column = (x * 2 + k) * self.width + start
        return self.grad.at[:, :, part, :, pl.ds(pl.multiple_of(column, 128), count)]

    def copy(self, device, source, target, semaphore):
        return pltpu.make_async_remote_copy(
            src_ref=source, dst_ref=target, send_sem=self.send.at[semaphore], recv_sem=self.recv.at[semaphore],
            device_id=device, device_id_type=MESH)

    def reserve(self, count):
        self.used += count
        return self.used - count

    def start(self, make, condition=lambda: None):
        when(condition(), lambda: make().start())
        self.started.append((condition, make))

    def stages(self):
        place, along = self.place, self.place.along
        rows, columns = self.total.shape[-2:]
        core = self.reserve(2)

        def own(x):
            return pltpu.make_async_copy(self.region(x, place.k), self.total.at[:, :, x], self.local.at[x])

        def swapped(x):
            return self.copy(
                place.across("k"), self.region(x, 1 - place.k), self.other_core.at[:, :, x], core + x)

        for x in range(2):
            own(x).start()
            self.start(functools.partial(swapped, x))
        yield
        for x in range(2):
            own(x).wait()
            swapped(x).wait_recv()
        add_blocks(self.total, self.other_core, (along, 2, 2))
        left = {"z": slice(None), "y": slice(None), "x": slice(None)}
        at = {"y": place.y, "x": place.x}

        def view(ref, kept=None, **places):
            return ref.at[tuple({**(left if kept is None else kept), **places}[axis] for axis in "zyx")]

        def sizes():
            return tuple(size for axis, size in zip("zyx", (along, 2, 2)) if isinstance(left[axis], slice))

        exchanges = 0
        for axis in self.order:
            if axis == "z":
                shape = tuple(2 for name in "yx" if isinstance(left[name], slice))
                inner = tuple(slice(None) if isinstance(left[name], slice) else 0 for name in "yx")

                def landing(side, step, inner=inner):
                    return self.steps.at[(side, step) + inner]

                base = self.reserve(2 * along)
                right, leftward = range(base, base + along), range(base + along, base + 2 * along)
                for step in range(along):
                    if step:
                        yield
                    for way, names, first in ((1, right, place.z), (-1, leftward, along - 1 - place.z)):
                        goal = along - 1 - step + place.z if way == 1 else step - along + 1 + place.z
                        side = 0 if way == 1 else 1
                        if step:
                            arrived = landing(side, step - 1)

                            def take(arrived=arrived, goal=goal, side=side, step=step, names=names):
                                self.copy(place.across("k"), arrived, arrived, names[step - 1]).wait_recv()
                                add_blocks(view(self.total, z=goal), arrived, shape)

                            pl.when((first >= 1) & (first <= step))(take)
                        if step < along - 1:
                            kept = dict(left)

                            def onward(way=way, step=step, kept=kept, landing=landing, side=side, names=names):
                                goal = along - 1 - step + place.z if way == 1 else step - along + 1 + place.z
                                source = view(self.total, kept, z=jnp.clip(goal, 0, along - 1))
                                return self.copy(place.device(dz=way), source, landing(side, step), names[step])

                            def reached(way=way, step=step):
                                first = place.z if way == 1 else along - 1 - place.z
                                return (first <= step) & (first < along - 1)

                            self.start(onward, reached)
                left["z"] = place.z
            else:
                landing = self.halves[exchanges]
                exchanges += 1
                inner = tuple(slice(None) if isinstance(left[name], slice) and name != axis else 0 for name in "zyx")
                semaphore, kept = self.reserve(1), dict(left)

                def swap(axis=axis, kept=kept, landing=landing, inner=inner, semaphore=semaphore):
                    source = view(self.total, kept, **{axis: 1 - at[axis]})
                    return self.copy(place.across(axis), source, landing.at[inner], semaphore)

                self.start(swap)
                yield
                swap().wait_recv()
                left[axis] = at[axis]
                add_blocks(view(self.total), landing.at[inner], sizes())
        part, start, count = self.strip
        self.out[part, :, start : start + count] = view(self.total)[...].astype(jnp.float32)

    def finish(self):
        for condition, make in self.started:
            when(condition(), lambda make=make: make().wait_send())


def scatter_slots(along, rows, columns, order):
    left = {"z": along, "y": 2, "x": 2}
    whole = (along, 2, 2, rows, columns)
    shapes = [whole, whole]
    steps = None
    for axis in order[::-1]:
        if axis == "z":
            steps = (2, along - 1, left["y"], left["x"], rows, columns)
        left[axis] = 1
        if axis != "z":
            shapes.append((left["z"], left["y"], left["x"], rows, columns))
    return shapes + [steps]


def scatters_of(place, units, grads, outs, send, recv, local, slots):
    scatters = []
    for at, (which, strip, order) in enumerate(units):
        total, other_core, first, second, steps = slots[5 * at : 5 * at + 5]
        scatters.append(
            Scatter(place, grads[which], outs[which], strip, outs[which].shape[-1], order,
                    (total, other_core, (first, second), steps), send.at[at], recv.at[at], local.at[at]))
    return scatters


def scatter_kernel(units, count, *refs):
    grads, outs = refs[:count], refs[count : 2 * count]
    place = Place()
    place.greet()
    scatters = scatters_of(place, units, grads, outs, *refs[2 * count : 2 * count + 3], refs[2 * count + 3 :])
    for unused in in_turn([scatter.stages() for scatter in scatters], 0.5):
        pass
    for scatter in scatters:
        scatter.finish()


def scatter_plan(grads, least, orders):
    along, cols = lax.axis_size("row") // 2, lax.axis_size("col")
    blocks = [jax.ShapeDtypeStruct(g.shape[2:4] + (g.shape[4] // cols,), jnp.float32) for g in grads]
    units = gather_units(blocks, least, orders)
    scratch = [pltpu.SemaphoreType.DMA((len(units), 2 * along + 4))] * 2 + [pltpu.SemaphoreType.DMA((len(units), 2))]
    for which, strip, order in units:
        shapes = scatter_slots(along, blocks[which].shape[1], strip[2], order)
        scratch += [pltpu.VMEM(shape, jnp.bfloat16) for shape in shapes]
    return blocks, units, scratch


def scatter_blocks(grads, collective_id, least):
    blocks, units, scratch = scatter_plan(grads, least, ORDERS)
    count = len(grads)
    anywhere = pl.BlockSpec(memory_space=pl.ANY)
    return pl.pallas_call(
        functools.partial(scatter_kernel, units, count),
        out_shape=blocks,
        in_specs=[anywhere] * count,
        out_specs=[pl.BlockSpec(memory_space=pltpu.VMEM)] * count,
        scratch_shapes=scratch,
        compiler_params=pltpu.CompilerParams(
            collective_id=collective_id, has_side_effects=True, vmem_limit_bytes=60 << 20),
        cost_estimate=pl.CostEstimate(
            flops=sum(g.size for g in grads), bytes_accessed=4 * sum(g.size for g in grads), transcendentals=0),
    )(*grads)


def attend_rows(q, key_ref, value_ref, spans, diagonal, put):
    low = lax.broadcasted_iota(jnp.int32, (1, 128), 1) < HEAD_DIM
    mixed, logs = [], []
    for h in range(2):
        mine = low if h == 0 else jnp.logical_not(low)
        qh = jnp.where(mine, q, jnp.bfloat16(0))
        scores = []
        for at, length in spans:
            s = dg(qh, key_ref[at : at + length, :], NT)
            if at == diagonal:
                allowed = lax.broadcasted_iota(jnp.int32, s.shape, 0) >= lax.broadcasted_iota(jnp.int32, s.shape, 1)
                s = jnp.where(allowed, s, -1e30)
            scores.append(s)
        top = functools.reduce(jnp.maximum, [jnp.max(s, axis=1, keepdims=True) for s in scores])
        out = None
        for (at, length), s in zip(spans, scores):
            p = jnp.exp(s - top).astype(jnp.bfloat16)
            value = value_ref[at : at + length, :]
            part = dg(p, jnp.where(mine, value, jnp.ones_like(value)), NN)
            out = part if out is None else out + part
        total = out[:, HEAD_DIM : HEAD_DIM + 1] if h == 0 else out[:, 0:1]
        mixed.append(out / total)
        logs.append(top + jnp.log(total))
    put(logs)
    return jnp.where(low, mixed[0], mixed[1])


def rows_of(lanes_ref, first):
    picked = lax.broadcasted_iota(jnp.int32, (8, 128), 0) + first == lax.broadcasted_iota(jnp.int32, (8, 128), 1)
    return lax.dot_general(
        picked.astype(jnp.float32), lanes_ref[...], NT, precision=lax.Precision.HIGHEST,
        preferred_element_type=jnp.float32)


def pair_attend_kernel(tile, q_ref, k_ref, v_ref, q_any, k_any, v_any, mix_ref, logs_ref, fq_out, fk_out, fv_out,
                       near, near_logs, far_q, far_k, far_v, far, far_logs, got, far_rows, got_rows,
                       send, recv, local, keep):
    step = pl.program_id(0)
    place = Place()
    pairs = near.shape[0]
    fars = pairs // 2
    rows = q_ref.shape[0]
    first, second = place.y == 0, place.y == 1
    partner = place.across("y")
    lane = lax.broadcasted_iota(jnp.int32, (1, 128), 1)
    scale = jnp.bfloat16(HEAD_DIM**-0.5)
    plan = ((q_any, far_q, False), (k_any, far_k, True), (v_any, far_v, True))

    def columns(pair):
        return pl.ds(pl.multiple_of(pair * 128, 128), 128)

    def sending(which, j):
        array, landing, by_first = plan[which]
        return pltpu.make_async_remote_copy(
            src_ref=array.at[:, columns(j if by_first else fars + j)], dst_ref=landing.at[j],
            send_sem=send.at[which, j], recv_sem=recv.at[which, j], device_id=partner, device_id_type=MESH)

    def keeping(which, j):
        array, landing, by_first = plan[which]
        return pltpu.make_async_copy(
            array.at[:, columns(fars + j if by_first else j)], landing.at[j], local.at[which, j])

    def mixture_out(j):
        return pltpu.make_async_remote_copy(
            src_ref=far.at[j], dst_ref=got.at[j], send_sem=send.at[3, j], recv_sem=recv.at[3, j],
            device_id=partner, device_id_type=MESH)

    def logs_out():
        return pltpu.make_async_remote_copy(
            src_ref=far_rows, dst_ref=got_rows, send_sem=send.at[4, 0], recv_sem=recv.at[4, 0],
            device_id=partner, device_id_type=MESH)

    def saving(which):
        return pltpu.make_async_copy(plan[which][1], (fq_out, fk_out, fv_out)[which], keep.at[which])

    @pl.when(step == 0)
    def _():
        barrier = pltpu.get_barrier_semaphore()
        pl.semaphore_signal(barrier, inc=1, device_id=partner, device_id_type=MESH)
        pl.semaphore_wait(barrier, 1)
        near_logs[...] = jnp.zeros_like(near_logs)
        far_logs[...] = jnp.zeros_like(far_logs)
        for j in range(fars):
            for which in range(3):

                @pl.when(first if plan[which][2] else second)
                def _(which=which, j=j):
                    keeping(which, j).start()

    @pl.when((step % 3 == 0) & (step < 3 * fars))
    def _():
        j = step // 3
        for which in range(3):

            @pl.when(first if plan[which][2] else second)
            def _(which=which):
                @pl.when(j > 0)
                def _():
                    sending(which, j - 1).wait_send()

                sending(which, j).start()

    @pl.when(step < pairs)
    def _():
        for start in range(0, rows, tile):
            n = min(tile, rows - start)

            def put(logs, start=start, n=n):
                kept = near_logs[start : start + n, :]
                for h in range(2):
                    kept = jnp.where(lane == 2 * step + h, logs[h], kept)
                near_logs[start : start + n, :] = kept

            spans = ([(0, start)] if start else []) + [(start, n)]
            near[step, start : start + n, :] = attend_rows(
                q_ref[start : start + n, :] * scale, k_ref, v_ref, spans, start, put)

    @pl.when((step >= pairs) & (step < pairs + fars))
    def _():
        j = step - pairs
        for which in range(3):
            by_first = plan[which][2]

            @pl.when(first if by_first else second)
            def _(which=which):
                keeping(which, j).wait()

            @pl.when(second if by_first else first)
            def _(which=which):
                sending(which, j).wait_recv()

        base = jnp.where(first, 2 * fars, 0)
        for start in range(0, rows, tile):
            n = min(tile, rows - start)

            def put(logs, start=start, n=n):
                kept = far_logs[start : start + n, :]
                for h in range(2):
                    kept = jnp.where(lane == base + 2 * j + h, logs[h], kept)
                far_logs[start : start + n, :] = kept

            far[j, start : start + n, :] = attend_rows(
                far_q[j, start : start + n, :] * scale, far_k.at[j], far_v.at[j], [(0, rows)], None, put
            ).astype(far.dtype)

        @pl.when(first)
        def _():
            mixture_out(j).start()

    @pl.when(step == pairs + fars)
    def _():
        for which in range(3):
            saving(which).start()

        @pl.when(first)
        def _():
            far_rows[...] = rows_of(far_logs, 2 * fars)
            logs_out().start()
            for pair in range(pairs):
                mix_ref[:, pair * 128 : (pair + 1) * 128] = near[pair].astype(mix_ref.dtype)
            logs_ref[...] = near_logs[...]
            logs_out().wait_send()
            for j in range(fars):
                mixture_out(j).wait_send()
            for which in (1, 2):
                sending(which, fars - 1).wait_send()

        @pl.when(second)
        def _():
            logs_out().wait_recv()
            for j in range(fars):
                mixture_out(j).wait_recv()
            sending(0, fars - 1).wait_send()
            spread_out = (lax.broadcasted_iota(jnp.int32, (8, 128), 0) + 2 * fars == lane).astype(jnp.float32)
            theirs = lax.dot_general(
                got_rows[...], spread_out, TN, precision=lax.Precision.HIGHEST, preferred_element_type=jnp.float32)
            logs_far = far_logs[...] + theirs
            logs_near = near_logs[...]
            top = jnp.maximum(logs_near, logs_far)
            total = top + jnp.log(jnp.exp(logs_near - top) + jnp.exp(logs_far - top))
            logs_ref[...] = total
            share = jnp.exp(logs_near - total)
            low = lane < HEAD_DIM
            for pair in range(pairs):
                part = jnp.where(low, share[:, 2 * pair : 2 * pair + 1], share[:, 2 * pair + 1 : 2 * pair + 2])
                other = (far[pair] if pair < fars else got[pair - fars]).astype(jnp.float32)
                mix_ref[:, pair * 128 : (pair + 1) * 128] = (other + (near[pair] - other) * part).astype(mix_ref.dtype)

        for which in range(3):
            saving(which).wait()


def pair_attend(q, k, v, collective_id, tile=384):
    rows, width = q.shape
    pairs = width // 128
    fars = pairs // 2
    block = pl.BlockSpec((rows, 128), lambda i: (0, jnp.minimum(i, pairs - 1)))
    anywhere = pl.BlockSpec(memory_space=pl.ANY)
    kept = jax.ShapeDtypeStruct((fars, rows, 128), jnp.bfloat16)
    half = pltpu.VMEM((fars, rows, 128), jnp.bfloat16)
    return pl.pallas_call(
        functools.partial(pair_attend_kernel, tile),
        grid=(pairs + fars + 1,),
        in_specs=[block] * 3 + [anywhere] * 3,
        out_specs=[pl.BlockSpec((rows, width), lambda i: (0, 0)), pl.BlockSpec((rows, 128), lambda i: (0, 0))] + [anywhere] * 3,
        out_shape=[
            jax.ShapeDtypeStruct((rows, width), jnp.bfloat16), jax.ShapeDtypeStruct((rows, 128), jnp.float32), kept, kept, kept],
        scratch_shapes=[
            pltpu.VMEM((pairs, rows, 128), jnp.float32), pltpu.VMEM((rows, 128), jnp.float32),
            half, half, half, half, pltpu.VMEM((rows, 128), jnp.float32), half,
            pltpu.VMEM((8, rows), jnp.float32), pltpu.VMEM((8, rows), jnp.float32),
            pltpu.SemaphoreType.DMA((5, fars)), pltpu.SemaphoreType.DMA((5, fars)),
            pltpu.SemaphoreType.DMA((3, fars)), pltpu.SemaphoreType.DMA((3,)),
        ],
        compiler_params=pltpu.CompilerParams(
            collective_id=collective_id, has_side_effects=True, vmem_limit_bytes=48 << 20),
        cost_estimate=pl.CostEstimate(
            flops=4 * rows * rows * width, bytes_accessed=16 * rows * width, transcendentals=rows * rows * pairs * 2),
    )(q, k, v, q, k, v)


def back_pair(tile, causal, q_ref, k_ref, v_ref, do_ref, stats, acc, put):
    rows, keys = q_ref.shape[0], k_ref.shape[0]
    low = lax.broadcasted_iota(jnp.int32, (1, 128), 1) < HEAD_DIM
    acc[...] = jnp.zeros_like(acc)
    for start in range(0, keys, tile):
        n = min(tile, keys - start)
        k = k_ref[start : start + n, :] * jnp.bfloat16(HEAD_DIM**-0.5)
        v = v_ref[start : start + n, :]
        spans = [(0, rows)]
        if causal:
            spans = [(start, n)] + ([(start + n, rows - start - n)] if start + n < rows else [])
        dks, dvs = [], []
        for h in range(2):
            mine = low if h == 0 else jnp.logical_not(low)
            kh, vh = jnp.where(mine, k, jnp.bfloat16(0)), jnp.where(mine, v, jnp.bfloat16(0))
            dk = dv = None
            for at, length in spans:
                qs, do = q_ref[at : at + length, :], do_ref[at : at + length, :]
                p = jnp.exp(dg(kh, qs, NT) - stats[h : h + 1, at : at + length])
                if causal and at == start:
                    allowed = lax.broadcasted_iota(jnp.int32, p.shape, 0) <= lax.broadcasted_iota(jnp.int32, p.shape, 1)
                    p = jnp.where(allowed, p, 0.0)
                ds = (p * (dg(vh, do, NT) - stats[2 + h : 3 + h, at : at + length])).astype(jnp.bfloat16)
                a, b = dg(p.astype(jnp.bfloat16), do, NN), dg(ds, qs, NN)
                dv = a if dv is None else dv + a
                dk = b if dk is None else dk + b
                acc[at : at + length, :] += dg(ds, kh, TN)
            dks.append(dk)
            dvs.append(dv)
        put(start, n, jnp.where(low, dks[0], dks[1]) * HEAD_DIM**-0.5, jnp.where(low, dvs[0], dvs[1]))


def pair_back_kernel(tile, far_tile, units, count, events, *refs):
    q_ref, k_ref, v_ref, do_ref, mix_ref, logs_ref, do_any, fq_any, fk_any, fv_any = refs[:10]
    grads, (dq_ref, dk_ref, dv_ref) = refs[10 : 10 + count], refs[10 + count : 13 + count]
    sums = refs[13 + count : 13 + 2 * count]
    (near, acc, stats, far_stats, used_stats, far_q, far_k, far_v, far_do, far_dq, far_dk, far_dv, got_q, got_k, got_v,
     send, recv, local, do_local) = refs[13 + 2 * count : 32 + 2 * count]
    scatter_refs = refs[32 + 2 * count :]
    step = pl.program_id(0)
    place = Place()
    pairs = near.shape[1]
    fars = pairs // 2
    first, second = place.y == 0, place.y == 1
    partner = place.across("y")
    lane = lax.broadcasted_iota(jnp.int32, (8, 128), 1)
    line = lax.broadcasted_iota(jnp.int32, (8, 128), 0)

    def columns(pair):
        return pl.ds(pl.multiple_of(pair * 128, 128), 128)

    def remote(source, target, which, j):
        return pltpu.make_async_remote_copy(
            src_ref=source, dst_ref=target, send_sem=send.at[which, j], recv_sem=recv.at[which, j],
            device_id=partner, device_id_type=MESH)

    def grad_over(j):
        return remote(do_any.at[:, columns(fars + j)], far_do.at[j], 0, j)

    def grad_kept(j):
        return pltpu.make_async_copy(do_any.at[:, columns(j)], far_do.at[j], do_local.at[j])

    def stats_over():
        return remote(stats.at[pl.ds(fars, fars)], far_stats, 4, 0)

    def back_over(which, j):
        source, target = ((far_dq, got_q), (far_dk, got_k), (far_dv, got_v))[which]
        return remote(source.at[j], target.at[j], 1 + which, j)

    def far_in(which):
        source, target = ((fq_any, far_q), (fk_any, far_k), (fv_any, far_v))[which]
        return pltpu.make_async_copy(source, target, local.at[which])

    scatters = scatters_of(place, units, grads, sums, *scatter_refs[:3], scatter_refs[3:])
    turns = in_turn([scatter.stages() for scatter in scatters], 0.5)

    @pl.when(step == 0)
    def _():
        place.greet()
        for which in range(3):
            far_in(which).start()
        for j in range(fars):

            @pl.when(second)
            def _(j=j):
                grad_over(j).start()

            @pl.when(second)
            def _(j=j):
                grad_kept(j).start()

    for at, number in enumerate(events):

        @pl.when(step == at)
        def _(number=number):
            for unused in range(number):
                next(turns, None)

    @pl.when((step == fars) & second)
    def _():
        stats_over().start()

    @pl.when(step < pairs)
    def _():
        pair = lax.rem(step + fars, pairs)
        picked = ((line < 2) & (line + 2 * pair == lane)).astype(jnp.float32)
        halves = (((line == 2) & (lane < HEAD_DIM)) | ((line == 3) & (lane >= HEAD_DIM))).astype(jnp.float32)
        products = mix_ref[...].astype(jnp.float32) * do_ref[...].astype(jnp.float32)
        both = lax.dot_general(
            picked, logs_ref[...], NT, precision=lax.Precision.HIGHEST, preferred_element_type=jnp.float32)
        both += lax.dot_general(
            halves, products, NT, precision=lax.Precision.HIGHEST, preferred_element_type=jnp.float32)
        stats[pair] = both

        def put(start, n, dk, dv):
            near[1, pair, start : start + n, :] = dk
            near[2, pair, start : start + n, :] = dv

        back_pair(tile, True, q_ref, k_ref, v_ref, do_ref, stats.at[pair], acc, put)
        near[0, pair] = acc[...]

    @pl.when((step >= pairs) & (step < pairs + fars))
    def _():
        j = step - pairs

        @pl.when(j == 0)
        def _():
            for which in range(3):
                far_in(which).wait()

            @pl.when(first)
            def _():
                stats_over().wait_recv()

        @pl.when(first)
        def _():
            grad_over(j).wait_recv()
            used_stats[...] = far_stats[j]

        @pl.when(second)
        def _():
            grad_kept(j).wait()
            used_stats[...] = stats[j]

        def put(start, n, dk, dv):
            far_dk[j, start : start + n, :] = dk.astype(far_dk.dtype)
            far_dv[j, start : start + n, :] = dv.astype(far_dv.dtype)

        back_pair(far_tile, False, far_q.at[j], far_k.at[j], far_v.at[j], far_do.at[j], used_stats, acc, put)
        far_dq[j] = acc[...].astype(far_dq.dtype)

        @pl.when(first)
        def _():
            back_over(0, j).start()

        @pl.when(second)
        def _():
            back_over(1, j).start()
            back_over(2, j).start()

    @pl.when(step >= pairs + fars)
    def _():
        pair = step - pairs - fars
        lower = pair < fars
        j = lax.rem(pair, fars)

        def write(ref, which, other):
            total = near[which, pair]
            if other is not None:
                total = total + other[j].astype(jnp.float32)
            ref[...] = total.astype(ref.dtype)

        @pl.when(first & lower)
        def _():
            for which in (1, 2):
                back_over(which, j).wait_recv()
            write(dq_ref, 0, None)
            write(dk_ref, 1, got_k)
            write(dv_ref, 2, got_v)

        @pl.when(first & jnp.logical_not(lower))
        def _():
            write(dq_ref, 0, None)
            write(dk_ref, 1, far_dk)
            write(dv_ref, 2, far_dv)

        @pl.when(second & lower)
        def _():
            write(dq_ref, 0, far_dq)
            write(dk_ref, 1, None)
            write(dv_ref, 2, None)

        @pl.when(second & jnp.logical_not(lower))
        def _():
            back_over(0, j).wait_recv()
            write(dq_ref, 0, got_q)
            write(dk_ref, 1, None)
            write(dv_ref, 2, None)

    @pl.when(step == 2 * pairs + fars - 1)
    def _():
        for unused in turns:
            pass
        for scatter in scatters:
            scatter.finish()

        @pl.when(first)
        def _():
            for j in range(fars):
                back_over(0, j).wait_send()

        @pl.when(second)
        def _():
            stats_over().wait_send()
            for j in range(fars):
                grad_over(j).wait_send()
                for which in (1, 2):
                    back_over(which, j).wait_send()


BACK_ORDERS = ("yzx", "yzx", "xzy", "yzx", "yzx", "zyx", "yzx", "yxz", "yzx")


def pair_back(q, k, v, do, mix, logs, far, grads, collective_id, events, tile=384, far_tile=256):
    rows, width = q.shape
    pairs = width // 128
    fars = pairs // 2
    blocks, units, scratch = scatter_plan(grads, 256, BACK_ORDERS)
    count = len(grads)
    block = pl.BlockSpec((rows, 128), lambda i: (0, lax.rem(jnp.minimum(i, pairs - 1) + fars, pairs)))
    joined = pl.BlockSpec((rows, 128), lambda i: (0, jnp.maximum(i - pairs - fars, 0)))
    anywhere = pl.BlockSpec(memory_space=pl.ANY)
    half = pltpu.VMEM((fars, rows, 128), jnp.bfloat16)
    out = jax.ShapeDtypeStruct((rows, width), jnp.bfloat16)
    result = pl.pallas_call(
        functools.partial(pair_back_kernel, tile, far_tile, units, count, events),
        grid=(2 * pairs + fars,),
        in_specs=[block] * 5 + [pl.BlockSpec((rows, 128), lambda i: (0, 0))] + [anywhere] * (4 + count),
        out_specs=[joined] * 3 + [pl.BlockSpec(memory_space=pltpu.VMEM)] * count,
        out_shape=[out] * 3 + blocks,
        scratch_shapes=[
            pltpu.VMEM((3, pairs, rows, 128), jnp.float32), pltpu.VMEM((rows, 128), jnp.float32),
            pltpu.VMEM((pairs, 8, rows), jnp.float32), pltpu.VMEM((fars, 8, rows), jnp.float32),
            pltpu.VMEM((8, rows), jnp.float32), *[half] * 10,
            pltpu.SemaphoreType.DMA((5, fars)), pltpu.SemaphoreType.DMA((5, fars)),
            pltpu.SemaphoreType.DMA((3,)), pltpu.SemaphoreType.DMA((fars,)), *scratch,
        ],
        compiler_params=pltpu.CompilerParams(
            collective_id=collective_id, has_side_effects=True, vmem_limit_bytes=62 << 20),
        cost_estimate=pl.CostEstimate(
            flops=10 * rows * rows * width, bytes_accessed=16 * rows * width, transcendentals=rows * rows * pairs * 2),
    )(q, k, v, do, mix, logs, do, *far, *grads)
    return result[:3], result[3:]


def fast(
    frames_in, text_states, self_query, self_key, self_value, self_output, cross_query, cross_key, cross_value, cross_output,
    up_weight, down_weight, first_gain, first_bias, second_gain, second_bias, third_gain, third_bias, cotangent,
):
    row = lax.axis_index("row")
    rows, width = frames_in.shape
    half = width // 2
    piece = first_gain.shape[0]
    block_rows, block_cols = self_query.shape
    back = row % 2
    pairs = lax.axis_size("row") // 2
    forth_perm = [(2 * i, 2 * i + 1) for i in range(pairs)]
    back_perm = [(2 * i + 1, 2 * i) for i in range(pairs)]
    swap = forth_perm + back_perm

    def forth(array):
        return lax.ppermute(array, "row", forth_perm)

    def home(array):
        return lax.ppermute(array, "row", back_perm)

    def by_side(first, second):
        return jnp.where(back == 0, first, second)

    gains = jnp.zeros((1, 16, 128), jnp.bfloat16)
    gains = gains.at[0, :6, :piece].set(
        jnp.stack([first_gain, first_bias, second_gain, second_bias, third_gain, third_bias])
    )

    everyone = ("row", "col")
    places = (lax.axis_size("row"), lax.axis_size("col"))
    up_blocks = lax.all_gather(up_weight, everyone).reshape(*places, *up_weight.shape)
    down_blocks = lax.all_gather(down_weight, everyone).reshape(*places, *down_weight.shape)

    def small(block):
        return block.reshape(1, block_rows, block_cols)

    def flat(array):
        return array.reshape(-1, array.shape[-1])

    early = gather_blocks([small(self_query), small(self_key), small(self_value), gains], 1, 128)
    query_self, key_self, value_self = [flat(w) for w in early[:3]]
    between = jnp.stack([self_output, cross_query, cross_key, cross_value, cross_output])
    between = lax.all_gather(between, everyone).reshape(*places, *between.shape).transpose(2, 0, 3, 1, 4)
    out_self, query_cross, key_cross, value_cross, out_cross = between.reshape(-1, width, width)
    norm_params = early[3].reshape(pairs * 2, 16, -1, 128)[:, :6, :, :piece].transpose(1, 0, 2, 3)
    norm_params = norm_params.reshape(6, width).astype(jnp.float32)

    frames = frames_in.astype(jnp.float32)
    hidden_one = norm_forward(frames, norm_params[0], norm_params[1]).astype(jnp.bfloat16)
    self_k = matmul(hidden_one, key_self).astype(jnp.bfloat16)
    self_v = matmul(hidden_one, value_self).astype(jnp.bfloat16)
    self_q = matmul(hidden_one, query_self).astype(jnp.bfloat16)
    self_mix, log_lanes, far_q, far_k, far_v = pair_attend(self_q, self_k, self_v, 5)
    half_heads = half // HEAD_DIM
    resid_one = frames + matmul(self_mix, out_self)
    hidden_two = norm_forward(resid_one, norm_params[2], norm_params[3]).astype(jnp.bfloat16)
    cross_q = matmul(hidden_two, query_cross).astype(jnp.bfloat16)
    other_text = lax.ppermute(text_states, "row", swap)
    clip_text = by_side(
        jnp.concatenate([text_states, other_text]), jnp.concatenate([other_text, text_states])
    )
    text_k = matmul(clip_text, key_cross).astype(jnp.bfloat16)
    text_v = matmul(clip_text, value_cross).astype(jnp.bfloat16)
    cross_mix, cross_logs = attend(cross_q, text_k, text_v, False, jnp.bfloat16)
    cross_logs = cross_logs[:, : 2 * half_heads]
    resid_two = resid_one + matmul(cross_mix, out_cross)
    hidden_three = norm_forward(resid_two, norm_params[4], norm_params[5]).astype(jnp.bfloat16)
    layer_out, grad_three, up_grad, down_grad = feed(hidden_three, cotangent, resid_two, up_blocks, down_blocks)
    up_sum = lax.psum_scatter(up_grad.reshape(-1, *up_weight.shape), everyone, scatter_dimension=0).astype(jnp.float32)

    def stats_of(logs, mix, grad):
        products = mix.astype(jnp.float32) * grad.astype(jnp.float32)
        dots = jnp.sum(products.reshape(rows, -1, HEAD_DIM), axis=-1)
        both = jnp.stack([logs.T.reshape(-1, 2, rows), dots.T.reshape(-1, 2, rows)], axis=1)
        return both.reshape(-1, 4, rows)

    cotan_full = cotangent.astype(jnp.float32)
    unused_three, pull_three = jax.vjp(norm_forward, resid_two, norm_params[4], norm_params[5])
    through_three, third_gain_part, third_bias_part = pull_three(grad_three)
    grad_resid_two = cotan_full + through_three
    grad_cross = grad_resid_two.astype(jnp.bfloat16)
    cross_out_grad = over_tokens(cross_mix, grad_cross)
    grad_cross_mix = by_transposed(grad_cross, out_cross).astype(jnp.bfloat16)
    grad_cross_q, text_k_part, text_v_part = attend_back(
        cross_q, text_k, text_v, grad_cross_mix, stats_of(cross_logs, cross_mix, grad_cross_mix), False, jnp.bfloat16)
    text_rows = text_states.shape[0]
    text_parts = jnp.concatenate([text_k_part, text_v_part], axis=1)
    given = lax.ppermute(by_side(text_parts[text_rows:], text_parts[:text_rows]), "row", swap)
    kept = by_side(text_parts[:text_rows], text_parts[text_rows:])
    text_parts = (kept.astype(jnp.float32) + given.astype(jnp.float32)).astype(jnp.bfloat16)
    grad_text_k, grad_text_v = text_parts[:, :width], text_parts[:, width:]
    cross_query_part = over_tokens(hidden_two, grad_cross_q)
    cross_key_part = over_tokens(text_states, grad_text_k)
    cross_value_part = over_tokens(text_states, grad_text_v)
    text_grad = by_transposed(grad_text_k, key_cross) + by_transposed(grad_text_v, value_cross)
    grad_two = by_transposed(grad_cross_q, query_cross)
    unused_two, pull_two = jax.vjp(norm_forward, resid_one, norm_params[2], norm_params[3])
    through_two, second_gain_part, second_bias_part = pull_two(grad_two)
    grad_resid_one = grad_resid_two + through_two
    grad_self = grad_resid_one.astype(jnp.bfloat16)
    self_out_grad = over_tokens(self_mix, grad_self)
    grad_self_mix = by_transposed(grad_self, out_self).astype(jnp.bfloat16)

    def by_place(grad, parts):
        return grad.astype(jnp.bfloat16).reshape(pairs, 2, parts, -1, grad.shape[-1])

    (grad_self_q, grad_self_k, grad_self_v), early_sums = pair_back(
        self_q, self_k, self_v, grad_self_mix, self_mix, log_lanes, (far_q, far_k, far_v),
        [by_place(g, 1) for g in (self_out_grad, cross_query_part, cross_key_part, cross_value_part, cross_out_grad)]
        + [by_place(down_grad, down_weight.shape[0] // block_rows)], 4, [4] * 12)
    self_query_part = over_tokens(hidden_one, grad_self_q)
    self_key_part = over_tokens(hidden_one, grad_self_k)
    self_value_part = over_tokens(hidden_one, grad_self_v)
    grad_one = (
        by_transposed(grad_self_q, query_self)
        + by_transposed(grad_self_k, key_self)
        + by_transposed(grad_self_v, value_self)
    )
    unused_one, pull_one = jax.vjp(norm_forward, frames, norm_params[0], norm_params[1])
    through_one, first_gain_part, first_bias_part = pull_one(grad_one)
    input_grad = grad_resid_one + through_one
    norm_grads = jnp.stack(
        [first_gain_part, first_bias_part, second_gain_part, second_bias_part, third_gain_part, third_bias_part]
    )
    norm_grads = norm_grads.reshape(6, 2 * pairs, -1, piece).transpose(1, 0, 2, 3)
    norm_grads = jnp.pad(norm_grads, ((0, 0), (0, 10), (0, 0), (0, 128 - piece)))

    late_sums = scatter_blocks(
        [by_place(g, 1) for g in (self_query_part, self_key_part, self_value_part)]
        + [by_place(norm_grads.reshape(2 * pairs * 16, -1), 1)], 3, 128)
    norm_parts = late_sums[3][0, :6, :piece]
    sums = [*late_sums[:3], *early_sums]
    sums = [total.reshape(-1, total.shape[-1]) for total in sums]
    return (layer_out, input_grad, text_grad, *sums[:-1], up_sum, sums[-1], *norm_parts)


def local(*arrays):
    frames_in, self_query = arrays[0], arrays[2]
    halves = 2 * frames_in.shape[0] == FRAMES and lax.axis_size("row") % 2 == 0
    if halves and lax.axis_size("col") % 2 == 0 and self_query.shape[1] % 256 == 0 and self_query.shape[0] % 128 == 0:
        return fast(*arrays)
    return general(*arrays)


def solution(mesh):
    placed = (
        P(("col", "row"), None),
        P(("col", "row"), None),
        P("row", "col"),
        P("row", "col"),
        P("row", "col"),
        P("row", "col"),
        P("row", "col"),
        P("row", "col"),
        P("row", "col"),
        P("row", "col"),
        P("row", "col"),
        P("row", "col"),
        P(("row", "col")),
        P(("row", "col")),
        P(("row", "col")),
        P(("row", "col")),
        P(("row", "col")),
        P(("row", "col")),
        P(("col", "row"), None),
    )
    return jax.shard_map(
        local,
        mesh=mesh,
        in_specs=placed,
        out_specs=(
            P(("col", "row"), None),
            P(("col", "row"), None),
            P(("col", "row"), None),
            P("row", "col"),
            P("row", "col"),
            P("row", "col"),
            P("row", "col"),
            P("row", "col"),
            P("row", "col"),
            P("row", "col"),
            P("row", "col"),
            P("row", "col"),
            P("row", "col"),
            P(("row", "col")),
            P(("row", "col")),
            P(("row", "col")),
            P(("row", "col")),
            P(("row", "col")),
            P(("row", "col")),
        ),
        check_vma=False,
    )
```

```python
import functools
from functools import partial

import jax
import jax.numpy as jnp
from jax import lax
from jax.experimental import pallas as pl
from jax.experimental.pallas import tpu as pltpu
from jax.sharding import PartitionSpec as P

HEADS = 16
HEAD_DIM = 64
FRAMES = 1500
TEXT = 64


def norm_forward(values, norm_gain, norm_bias):
    center = values - jnp.mean(values, axis=-1, keepdims=True)
    variance = jnp.mean(center * center, axis=-1, keepdims=True)
    return center * lax.rsqrt(variance + 1e-05) * norm_gain + norm_bias


def matmul(left, right):
    return jnp.dot(left, right, preferred_element_type=jnp.float32)


def by_transposed(left, right):
    return lax.dot_general(
        left, right, (((1,), (1,)), ((), ())), preferred_element_type=jnp.float32
    )


def over_tokens(left, right):
    return lax.dot_general(
        left, right, (((0,), (0,)), ((), ())), preferred_element_type=jnp.float32
    )


def collect(blocks):
    partly = (
        lax.all_gather(blocks[0], "col", axis=1, tiled=True),
        lax.all_gather(blocks[1], "col", axis=1, tiled=True),
        lax.all_gather(blocks[2], "col", axis=1, tiled=True),
        lax.all_gather(blocks[3], "col", axis=1, tiled=True),
        lax.all_gather(blocks[4], "col", axis=1, tiled=True),
        lax.all_gather(blocks[5], "col", axis=1, tiled=True),
        lax.all_gather(blocks[6], "col", axis=1, tiled=True),
        lax.all_gather(blocks[7], "col", axis=1, tiled=True),
        lax.all_gather(blocks[8], "col", axis=1, tiled=True),
        lax.all_gather(blocks[9], "col", axis=1, tiled=True),
        lax.all_gather(blocks[10], "col", axis=1, tiled=True),
    )
    return (
        lax.all_gather(partly[0], "row", axis=0, tiled=True),
        lax.all_gather(partly[1], "row", axis=0, tiled=True),
        lax.all_gather(partly[2], "row", axis=0, tiled=True),
        lax.all_gather(partly[3], "row", axis=0, tiled=True),
        lax.all_gather(partly[4], "row", axis=0, tiled=True),
        lax.all_gather(partly[5], "row", axis=0, tiled=True),
        lax.all_gather(partly[6], "row", axis=0, tiled=True),
        lax.all_gather(partly[7], "row", axis=0, tiled=True),
        lax.all_gather(partly[8], "row", axis=0, tiled=True),
        lax.all_gather(partly[9], "row", axis=0, tiled=True),
        lax.all_gather(partly[10], "row", axis=0, tiled=True),
    )


def spread(grads):
    partly = (
        lax.psum_scatter(
            grads[0].astype(jnp.bfloat16), "row", scatter_dimension=0, tiled=True
        ).astype(jnp.float32),
        lax.psum_scatter(
            grads[1].astype(jnp.bfloat16), "row", scatter_dimension=0, tiled=True
        ).astype(jnp.float32),
        lax.psum_scatter(
            grads[2].astype(jnp.bfloat16), "row", scatter_dimension=0, tiled=True
        ).astype(jnp.float32),
        lax.psum_scatter(
            grads[3].astype(jnp.bfloat16), "row", scatter_dimension=0, tiled=True
        ).astype(jnp.float32),
        lax.psum_scatter(
            grads[4].astype(jnp.bfloat16), "row", scatter_dimension=0, tiled=True
        ).astype(jnp.float32),
        lax.psum_scatter(
            grads[5].astype(jnp.bfloat16), "row", scatter_dimension=0, tiled=True
        ).astype(jnp.float32),
        lax.psum_scatter(
            grads[6].astype(jnp.bfloat16), "row", scatter_dimension=0, tiled=True
        ).astype(jnp.float32),
        lax.psum_scatter(
            grads[7].astype(jnp.bfloat16), "row", scatter_dimension=0, tiled=True
        ).astype(jnp.float32),
        lax.psum_scatter(
            grads[8].astype(jnp.bfloat16), "row", scatter_dimension=0, tiled=True
        ).astype(jnp.float32),
        lax.psum_scatter(
            grads[9].astype(jnp.bfloat16), "row", scatter_dimension=0, tiled=True
        ).astype(jnp.float32),
        lax.psum_scatter(
            grads[10].astype(jnp.bfloat16), "row", scatter_dimension=0, tiled=True
        ).astype(jnp.float32),
    )
    return (
        lax.psum_scatter(
            partly[0].astype(jnp.bfloat16), "col", scatter_dimension=1, tiled=True
        ).astype(jnp.float32),
        lax.psum_scatter(
            partly[1].astype(jnp.bfloat16), "col", scatter_dimension=1, tiled=True
        ).astype(jnp.float32),
        lax.psum_scatter(
            partly[2].astype(jnp.bfloat16), "col", scatter_dimension=1, tiled=True
        ).astype(jnp.float32),
        lax.psum_scatter(
            partly[3].astype(jnp.bfloat16), "col", scatter_dimension=1, tiled=True
        ).astype(jnp.float32),
        lax.psum_scatter(
            partly[4].astype(jnp.bfloat16), "col", scatter_dimension=1, tiled=True
        ).astype(jnp.float32),
        lax.psum_scatter(
            partly[5].astype(jnp.bfloat16), "col", scatter_dimension=1, tiled=True
        ).astype(jnp.float32),
        lax.psum_scatter(
            partly[6].astype(jnp.bfloat16), "col", scatter_dimension=1, tiled=True
        ).astype(jnp.float32),
        lax.psum_scatter(
            partly[7].astype(jnp.bfloat16), "col", scatter_dimension=1, tiled=True
        ).astype(jnp.float32),
        lax.psum_scatter(
            partly[8].astype(jnp.bfloat16), "col", scatter_dimension=1, tiled=True
        ).astype(jnp.float32),
        lax.psum_scatter(
            partly[9].astype(jnp.bfloat16), "col", scatter_dimension=1, tiled=True
        ).astype(jnp.float32),
        lax.psum_scatter(
            partly[10].astype(jnp.bfloat16), "col", scatter_dimension=1, tiled=True
        ).astype(jnp.float32),
    )


def heads_layout(stacked):
    return lax.all_to_all(stacked, "row", split_axis=1, concat_axis=0, tiled=True)


def tokens_layout(stacked):
    return lax.all_to_all(stacked, "row", split_axis=0, concat_axis=2, tiled=True)


def by_clips(arranged, start, count, length, heads_dev):
    section = arranged[:, start : start + count]
    return section.reshape(-1, length, heads_dev, HEAD_DIM)


def causal_scores(query_clip, key_clip, causal):
    scores = jnp.einsum(
        "qhd,khd->hqk", query_clip, key_clip, preferred_element_type=jnp.float32
    ) * HEAD_DIM ** (-0.5)
    if causal:
        allowed = jnp.arange(scores.shape[1])[:, None] >= jnp.arange(scores.shape[2])[None, :]
        scores = jnp.where(allowed, scores, -1e30)
    return scores


def attend_forward(query_clips, key_clips, value_clips, causal):

    def one_clip(operands):
        query_clip, key_clip, value_clip = operands
        scores = causal_scores(query_clip, key_clip, causal)
        highest = jnp.max(scores, axis=-1, keepdims=True)
        powers = jnp.exp(scores - highest)
        totals = jnp.sum(powers, axis=-1, keepdims=True)
        weights_low = (powers / totals).astype(jnp.bfloat16)
        mixture = jnp.einsum(
            "hqk,khd->qhd", weights_low, value_clip, preferred_element_type=jnp.float32
        )
        return (mixture.astype(jnp.bfloat16), (highest + jnp.log(totals))[..., 0])

    return lax.map(one_clip, (query_clips, key_clips, value_clips))


def attend_backward(query_clips, key_clips, value_clips, log_sums, grad_clips, causal):

    def one_clip(operands):
        query_clip, key_clip, value_clip, log_clip, grad_clip = operands
        scores = causal_scores(query_clip, key_clip, causal)
        probs_full = jnp.exp(scores - log_clip[..., None])
        grad_probs = jnp.einsum(
            "qhd,khd->hqk", grad_clip, value_clip, preferred_element_type=jnp.float32
        )
        grad_value = jnp.einsum(
            "hqk,qhd->khd",
            probs_full.astype(jnp.bfloat16),
            grad_clip,
            preferred_element_type=jnp.float32,
        )
        centered = grad_probs - jnp.sum(probs_full * grad_probs, axis=-1, keepdims=True)
        grad_scores = (probs_full * centered).astype(jnp.bfloat16)
        grad_query = jnp.einsum(
            "hqk,khd->qhd", grad_scores, key_clip, preferred_element_type=jnp.float32
        ) * HEAD_DIM ** (-0.5)
        grad_key = jnp.einsum(
            "hqk,qhd->khd", grad_scores, query_clip, preferred_element_type=jnp.float32
        ) * HEAD_DIM ** (-0.5)
        return (
            grad_query.astype(jnp.bfloat16),
            grad_key.astype(jnp.bfloat16),
            grad_value.astype(jnp.bfloat16),
        )

    return lax.map(one_clip, (query_clips, key_clips, value_clips, log_sums, grad_clips))


def general(
    frames_in,
    text_states,
    self_query,
    self_key,
    self_value,
    self_output,
    cross_query,
    cross_key,
    cross_value,
    cross_output,
    up_weight,
    down_weight,
    first_gain,
    first_bias,
    second_gain,
    second_bias,
    third_gain,
    third_bias,
    cotangent,
):
    row_count = lax.axis_size("row")
    col_count = lax.axis_size("col")
    heads_dev = HEADS // row_count
    width_dev = heads_dev * HEAD_DIM
    tok_rows = frames_in.shape[0]
    text_rows = text_states.shape[0]
    piece_len = first_gain.shape[0]
    gain_block = jnp.stack(
        [first_gain, first_bias, second_gain, second_bias, third_gain, third_bias]
    ).reshape(1, 6 * piece_len)
    param_blocks = (
        self_query,
        self_key,
        self_value,
        self_output,
        cross_query,
        cross_key,
        cross_value,
        cross_output,
        up_weight,
        down_weight,
        gain_block,
    )

    def unpack_gains(gathered_gains):
        arranged = gathered_gains.reshape(row_count, col_count, 6, piece_len).transpose(2, 0, 1, 3)
        return arranged.reshape(6, row_count * col_count * piece_len).astype(jnp.float32)

    gathered = collect(param_blocks)
    (
        query_self,
        key_self,
        value_self,
        out_self,
        query_cross,
        key_cross,
        value_cross,
        out_cross,
        up_full,
        down_full,
    ) = gathered[:10]
    norm_params = unpack_gains(gathered[10])
    frames = frames_in.astype(jnp.float32)
    hidden_one = norm_forward(frames, norm_params[0], norm_params[1]).astype(jnp.bfloat16)
    self_q = matmul(hidden_one, query_self).astype(jnp.bfloat16)
    self_k = matmul(hidden_one, key_self).astype(jnp.bfloat16)
    self_v = matmul(hidden_one, value_self).astype(jnp.bfloat16)
    text_k = matmul(text_states, key_cross).astype(jnp.bfloat16)
    text_v = matmul(text_states, value_cross).astype(jnp.bfloat16)
    sent_rows = 3 * tok_rows + 2 * text_rows
    arranged = heads_layout(jnp.concatenate([self_q, self_k, self_v, text_k, text_v], axis=0))
    arranged = arranged.reshape(row_count, sent_rows, width_dev)
    query_clips = by_clips(arranged, 0, tok_rows, FRAMES, heads_dev)
    key_clips = by_clips(arranged, tok_rows, tok_rows, FRAMES, heads_dev)
    value_clips = by_clips(arranged, 2 * tok_rows, tok_rows, FRAMES, heads_dev)
    text_keys = by_clips(arranged, 3 * tok_rows, text_rows, TEXT, heads_dev)
    text_values = by_clips(arranged, 3 * tok_rows + text_rows, text_rows, TEXT, heads_dev)
    self_clips, self_logs = attend_forward(query_clips, key_clips, value_clips, True)
    self_mix = tokens_layout(self_clips.reshape(row_count, tok_rows, width_dev))[0]
    resid_one = frames + matmul(self_mix, out_self)
    hidden_two = norm_forward(resid_one, norm_params[2], norm_params[3]).astype(jnp.bfloat16)
    cross_q = matmul(hidden_two, query_cross).astype(jnp.bfloat16)
    cross_arranged = heads_layout(cross_q).reshape(row_count, tok_rows, width_dev)
    cross_queries = by_clips(cross_arranged, 0, tok_rows, FRAMES, heads_dev)
    cross_clips, cross_logs = attend_forward(cross_queries, text_keys, text_values, False)
    cross_mix = tokens_layout(cross_clips.reshape(row_count, tok_rows, width_dev))[0]
    resid_two = resid_one + matmul(cross_mix, out_cross)
    hidden_three = norm_forward(resid_two, norm_params[4], norm_params[5]).astype(jnp.bfloat16)
    pre_act = matmul(hidden_three, up_full)
    inner = jax.nn.gelu(pre_act, approximate=False).astype(jnp.bfloat16)
    layer_out = (resid_two + matmul(inner, down_full)).astype(jnp.bfloat16)
    gathered = collect(param_blocks)
    (
        query_self,
        key_self,
        value_self,
        out_self,
        query_cross,
        key_cross,
        value_cross,
        out_cross,
        up_full,
        down_full,
    ) = gathered[:10]
    norm_params = unpack_gains(gathered[10])
    cotan_full = cotangent.astype(jnp.float32)
    down_grad = over_tokens(inner, cotangent)
    grad_inner = by_transposed(cotangent, down_full)
    unused_gelu, gelu_pull = jax.vjp(partial(jax.nn.gelu, approximate=False), pre_act)
    grad_pre = gelu_pull(grad_inner)[0].astype(jnp.bfloat16)
    up_grad = over_tokens(hidden_three, grad_pre)
    grad_three = by_transposed(grad_pre, up_full)
    unused_three, pull_three = jax.vjp(norm_forward, resid_two, norm_params[4], norm_params[5])
    through_three, third_gain_part, third_bias_part = pull_three(grad_three)
    grad_resid_two = cotan_full + through_three
    grad_cross = grad_resid_two.astype(jnp.bfloat16)
    cross_out_grad = over_tokens(cross_mix, grad_cross)
    grad_cross_mix = by_transposed(grad_cross, out_cross).astype(jnp.bfloat16)
    grad_cross_arr = heads_layout(grad_cross_mix).reshape(row_count, tok_rows, width_dev)
    grad_cross_clips = by_clips(grad_cross_arr, 0, tok_rows, FRAMES, heads_dev)
    cq_clips, tk_clips, tv_clips = attend_backward(
        cross_queries, text_keys, text_values, cross_logs, grad_cross_clips, False
    )
    back_cross = jnp.concatenate(
        [
            cq_clips.reshape(row_count, tok_rows, width_dev),
            tk_clips.reshape(row_count, text_rows, width_dev),
            tv_clips.reshape(row_count, text_rows, width_dev),
        ],
        axis=1,
    )
    back_cross = tokens_layout(back_cross)[0]
    grad_cross_q = back_cross[:tok_rows]
    grad_text_k = back_cross[tok_rows : tok_rows + text_rows]
    grad_text_v = back_cross[tok_rows + text_rows :]
    cross_query_part = over_tokens(hidden_two, grad_cross_q)
    cross_key_part = over_tokens(text_states, grad_text_k)
    cross_value_part = over_tokens(text_states, grad_text_v)
    text_grad = by_transposed(grad_text_k, key_cross) + by_transposed(grad_text_v, value_cross)
    grad_two = by_transposed(grad_cross_q, query_cross)
    unused_two, pull_two = jax.vjp(norm_forward, resid_one, norm_params[2], norm_params[3])
    through_two, second_gain_part, second_bias_part = pull_two(grad_two)
    grad_resid_one = grad_resid_two + through_two
    grad_self = grad_resid_one.astype(jnp.bfloat16)
    self_out_grad = over_tokens(self_mix, grad_self)
    grad_self_mix = by_transposed(grad_self, out_self).astype(jnp.bfloat16)
    grad_self_arr = heads_layout(grad_self_mix).reshape(row_count, tok_rows, width_dev)
    grad_self_clips = by_clips(grad_self_arr, 0, tok_rows, FRAMES, heads_dev)
    sq_clips, sk_clips, sv_clips = attend_backward(
        query_clips, key_clips, value_clips, self_logs, grad_self_clips, True
    )
    back_self = jnp.concatenate(
        [
            sq_clips.reshape(row_count, tok_rows, width_dev),
            sk_clips.reshape(row_count, tok_rows, width_dev),
            sv_clips.reshape(row_count, tok_rows, width_dev),
        ],
        axis=1,
    )
    back_self = tokens_layout(back_self)[0]
    grad_self_q = back_self[:tok_rows]
    grad_self_k = back_self[tok_rows : 2 * tok_rows]
    grad_self_v = back_self[2 * tok_rows :]
    self_query_part = over_tokens(hidden_one, grad_self_q)
    self_key_part = over_tokens(hidden_one, grad_self_k)
    self_value_part = over_tokens(hidden_one, grad_self_v)
    grad_one = (
        by_transposed(grad_self_q, query_self)
        + by_transposed(grad_self_k, key_self)
        + by_transposed(grad_self_v, value_self)
    )
    unused_one, pull_one = jax.vjp(norm_forward, frames, norm_params[0], norm_params[1])
    through_one, first_gain_part, first_bias_part = pull_one(grad_one)
    input_grad = grad_resid_one + through_one
    norm_grads = jnp.stack(
        [
            first_gain_part,
            first_bias_part,
            second_gain_part,
            second_bias_part,
            third_gain_part,
            third_bias_part,
        ]
    )
    norm_grads = norm_grads.reshape(6, row_count, col_count, piece_len).transpose(1, 2, 0, 3)
    norm_grads = norm_grads.reshape(row_count, col_count * 6 * piece_len)
    summed = spread(
        (
            self_query_part,
            self_key_part,
            self_value_part,
            self_out_grad,
            cross_query_part,
            cross_key_part,
            cross_value_part,
            cross_out_grad,
            up_grad,
            down_grad,
            norm_grads,
        )
    )
    norm_parts = summed[10].reshape(6, piece_len)
    return (
        layer_out,
        input_grad,
        text_grad,
        summed[0],
        summed[1],
        summed[2],
        summed[3],
        summed[4],
        summed[5],
        summed[6],
        summed[7],
        summed[8],
        summed[9],
        norm_parts[0],
        norm_parts[1],
        norm_parts[2],
        norm_parts[3],
        norm_parts[4],
        norm_parts[5],
    )


NT=(((1,),(1,)),((),())); NN=(((1,),(0,)),((),())); TN=(((0,),(0,)),((),()))
def dg(a,b,dims): return lax.dot_general(a,b,dims,preferred_element_type=jnp.float32)

def attend_kernel(causal,tile,q_ref,k_ref,v_ref,o_ref,lse_ref):
    pair=pl.program_id(0)
    rows=q_ref.shape[0]
    low=lax.broadcasted_iota(jnp.int32,(1,128),1)<HEAD_DIM
    lane=lax.broadcasted_iota(jnp.int32,(1,128),1)
    value=v_ref[...]
    ones=jnp.ones_like(value)
    @pl.when(pair==0)
    def _(): lse_ref[...]=jnp.zeros_like(lse_ref)
    for start in range(0,rows,tile):
        n=min(tile,rows-start)
        q=q_ref[start:start+n,:]*jnp.bfloat16(HEAD_DIM**-0.5)
        mixed=[]; sums=[]
        lse=lse_ref[start:start+n,:]
        for h in range(2):
            mine=low if h==0 else jnp.logical_not(low)
            qh=jnp.where(mine,q,jnp.bfloat16(0))
            vh=jnp.where(mine,value,ones)
            if causal:
                spans=([(0,start)] if start else [])+[(start,n)]
            else: spans=[(0,k_ref.shape[0])]
            scores=[]
            for at,length in spans:
                s=dg(qh,k_ref[at:at+length,:],NT)
                if causal and at==start:
                    ok=lax.broadcasted_iota(jnp.int32,s.shape,0)>=lax.broadcasted_iota(jnp.int32,s.shape,1)
                    s=jnp.where(ok,s,-1e30)
                scores.append(s)
            top=functools.reduce(jnp.maximum,[jnp.max(s,axis=1,keepdims=True) for s in scores])
            out=None
            for (at,length),s in zip(spans,scores):
                p=jnp.exp(s-top).astype(jnp.bfloat16)
                part=dg(p,vh[at:at+length,:],NN)
                out=part if out is None else out+part
            total=out[:,HEAD_DIM:HEAD_DIM+1] if h==0 else out[:,0:1]
            mixed.append(out/total)
            lse=jnp.where(lane==2*pair+h,top+jnp.log(total),lse)
        lse_ref[start:start+n,:]=lse
        o_ref[start:start+n,:]=jnp.where(low,mixed[0],mixed[1]).astype(o_ref.dtype)

def attend(q,k,v,causal,out_dtype,tile=256):
    rows,width=q.shape; keys=k.shape[0]
    return pl.pallas_call(functools.partial(attend_kernel,causal,tile),grid=(width//128,),
        in_specs=[pl.BlockSpec((rows,128),lambda i:(0,i)),pl.BlockSpec((keys,128),lambda i:(0,i)),pl.BlockSpec((keys,128),lambda i:(0,i))],
        out_specs=[pl.BlockSpec((rows,128),lambda i:(0,i)),pl.BlockSpec((rows,128),lambda i:(0,0))],
        out_shape=[jax.ShapeDtypeStruct((rows,width),out_dtype),jax.ShapeDtypeStruct((rows,128),jnp.float32)],
        compiler_params=pltpu.CompilerParams(vmem_limit_bytes=40<<20),
        cost_estimate=pl.CostEstimate(flops=4*rows*keys*width,bytes_accessed=8*rows*width,transcendentals=rows*keys*width//64))(q,k,v)

def feed_kernel(h_ref,cot_ref,res_ref,up_ref,down_ref,out_ref,g_ref,dup_ref,ddown_ref,acc):
    i=pl.program_id(0)
    @pl.when(i==0)
    def _():
        acc[...]=res_ref[...]
        g_ref[...]=jnp.zeros_like(g_ref)
    h=h_ref[...]
    up=up_ref[:,0].reshape(h.shape[1],-1)
    blocks,wide=down_ref.shape[1],down_ref.shape[3]
    pre=dg(h,up,NN)
    cdf=0.5*(1.0+lax.erf(pre*0.7071067811865476))
    inner=(pre*cdf).astype(jnp.bfloat16)
    slope=cdf+pre*(jnp.exp(-0.5*pre*pre)*0.3989422804014327)
    grad=None
    for at in range(blocks):
        columns=slice(at*wide,(at+1)*wide)
        cot=cot_ref[:,columns]
        acc[:,columns]+=dg(inner,down_ref[0,at],NN)
        ddown_ref[:,columns]=dg(inner,cot,TN).astype(ddown_ref.dtype)
        part=dg(cot,down_ref[0,at],NT)
        grad=part if grad is None else grad+part
    gpre=(grad*slope).astype(jnp.bfloat16)
    dup_ref[:,0]=dg(h,gpre,TN).astype(dup_ref.dtype).reshape(dup_ref.shape[0],dup_ref.shape[2],dup_ref.shape[3])
    g_ref[...]+=dg(gpre,up,NT)
    @pl.when(i==pl.num_programs(0)-1)
    def _(): out_ref[...]=acc[...].astype(out_ref.dtype)

def feed(h,cot,res,up,down):
    rows,d=h.shape; chunk=down.shape[2]; strips=up.shape[3]//chunk; ff=down.shape[0]*chunk
    whole=pl.BlockSpec((rows,d),lambda i:(0,0))
    up_spec=pl.BlockSpec((up.shape[0],1,up.shape[2],chunk),lambda i:(0,i//strips,0,i%strips))
    down_spec=pl.BlockSpec((1,)+down.shape[1:],lambda i:(i,0,0,0))
    return pl.pallas_call(feed_kernel,grid=(ff//chunk,),
        in_specs=[whole,whole,whole,up_spec,down_spec],
        out_specs=[whole,whole,up_spec,pl.BlockSpec((chunk,d),lambda i:(i,0))],
        out_shape=[jax.ShapeDtypeStruct((rows,d),jnp.bfloat16),jax.ShapeDtypeStruct((rows,d),jnp.float32),jax.ShapeDtypeStruct(up.shape,jnp.bfloat16),jax.ShapeDtypeStruct((ff,d),jnp.bfloat16)],
        scratch_shapes=[pltpu.VMEM((rows,d),jnp.float32)],
        compiler_params=pltpu.CompilerParams(vmem_limit_bytes=56<<20),
        cost_estimate=pl.CostEstimate(flops=12*rows*d*ff,bytes_accessed=8*d*ff+16*rows*d,transcendentals=2*rows*ff))(h,cot,res,up,down)


MESH = pl.DeviceIdType.MESH
ORDERS = ("xzy", "yzx", "xzy", "yzx", "zxy", "zyx")


class Place:
    def __init__(self):
        row, col = lax.axis_index("row"), lax.axis_index("col")
        self.z, self.y, self.x, self.k = row // 2, row % 2, col // 2, col % 2
        self.along = lax.axis_size("row") // 2

    def device(self, dz=0, y=False, x=False, k=False):
        other_y = 1 - self.y if y else self.y
        other_x = 1 - self.x if x else self.x
        other_k = 1 - self.k if k else self.k
        return ((self.z + dz) * 2 + other_y, other_x * 2 + other_k)

    def across(self, axis):
        return self.device(y=axis == "y", x=axis == "x", k=axis == "k")

    def greet(self):
        barrier = pltpu.get_barrier_semaphore()
        for axis in "xyk":
            pl.semaphore_signal(barrier, inc=1, device_id=self.across(axis), device_id_type=MESH)

        @pl.when(self.z > 0)
        def _():
            pl.semaphore_signal(barrier, inc=1, device_id=self.device(dz=-1), device_id_type=MESH)

        @pl.when(self.z + 1 < self.along)
        def _():
            pl.semaphore_signal(barrier, inc=1, device_id=self.device(dz=1), device_id_type=MESH)

        below = jnp.where(self.z > 0, 1, 0)
        above = jnp.where(self.z + 1 < self.along, 1, 0)
        pl.semaphore_wait(barrier, 3 + below + above)


def when(condition, run):
    if condition is None:
        run()
    else:
        pl.when(condition)(run)


def in_turn(units, lag):
    ready = [(lag * at, at) for at in range(len(units))]
    while ready:
        turn, at = min(ready)
        ready.remove((turn, at))
        if next(units[at], units) is not units:
            ready.append((turn + 1, at))
        yield


class Gather:
    def __init__(self, place, block, full, strip, order, send, recv):
        self.place, self.block, self.full, self.strip = place, block, full, strip
        turn = order.index("z")
        self.before, self.after = order[:turn], order[turn + 1 :]
        self.send, self.recv, self.used, self.sent, self.started = send, recv, 0, 0, []

    def region(self, z, y, x):
        part, start, count = self.strip
        column = (x * 2 + self.place.k) * self.block.shape[-1] + start
        return self.full.at[z, y, part, :, pl.ds(pl.multiple_of(column, 128), count)]

    def held(self, done, z):
        y = slice(None) if "y" in done else self.place.y
        return [self.region(z, y, x) for x in (range(2) if "x" in done else [self.place.x])]

    def pairs(self, done, z, first):
        if first:
            part, start, count = self.strip
            place = self.place
            return [(self.block.at[part, :, pl.ds(start, count)], self.region(place.z, place.y, place.x))]
        return [(region, region) for region in self.held(done, z)]

    def semaphore(self):
        self.used += 2
        return self.used - 2

    def copies(self, device, pairs, semaphore, send=0):
        return [
            pltpu.make_async_remote_copy(
                src_ref=source, dst_ref=target, send_sem=self.send.at[send + at],
                recv_sem=self.recv.at[semaphore + at], device_id=device, device_id_type=MESH)
            for at, (source, target) in enumerate(pairs)
        ]

    def start(self, device, pairs, condition, semaphore):
        copies = self.copies(device, pairs, semaphore, self.sent)
        self.sent += len(copies)
        when(condition, lambda: [copy.start() for copy in copies] and None)
        self.started.append((condition, copies))
        return condition, copies

    def arrive(self, sent):
        condition, copies = sent
        when(condition, lambda: [copy.wait_recv() for copy in copies] and None)

    def stages(self):
        place, along = self.place, self.place.along
        done = []
        for axis in self.before:
            sent = self.start(place.across(axis), self.pairs(done, place.z, not done), None, self.semaphore())
            yield
            self.arrive(sent)
            done.append(axis)
        first = not done
        from_left = [self.semaphore() for _ in range(along - 1)]
        from_right = [self.semaphore() for _ in range(along - 1)]

        def pass_on(turn, step):
            axes = done + list(self.after[:turn])
            device = place.across(self.after[turn])
            if step == 0:
                return turn, step, [self.start(device, self.pairs(axes, place.z, not axes), None, self.semaphore())]
            return turn, step, [
                self.start(device, self.pairs(axes, z, False), (z >= 0) & (z < along), self.semaphore())
                for z in (place.z - step, place.z + step)
            ]

        def step_out(step):
            left, right = place.z - (step - 1), place.z + (step - 1)
            self.start(place.device(dz=1), self.pairs(done, left, first and step == 1),
                       (left >= 0) & (place.z + 1 < along), from_left[step - 1])
            self.start(place.device(dz=-1), self.pairs(done, right, first and step == 1),
                       (right < along) & (place.z > 0), from_right[step - 1])

        def step_in(step):
            for z, semaphore in ((place.z - step, from_left), (place.z + step, from_right)):
                copies = self.copies(place.across("k"), self.pairs(done, z, False), semaphore[step - 1])
                self.arrive(((z >= 0) & (z < along), copies))

        step_out(1)
        waiting = [pass_on(0, 0)] if self.after else []
        for step in range(1, along + len(self.after)):
            yield
            if step < along:
                step_in(step)
                if step + 1 < along:
                    step_out(step + 1)
            following = []
            for turn, at, sent in waiting:
                for one in sent:
                    self.arrive(one)
                if turn + 1 < len(self.after):
                    following.append(pass_on(turn + 1, at))
            if self.after and step < along:
                following.append(pass_on(0, step))
            waiting = following
        everything = [self.region(slice(None), slice(None), x) for x in range(2)]
        sent = self.start(place.across("k"), [(r, r) for r in everything], None, self.semaphore())
        yield
        self.arrive(sent)

    def finish(self):
        for condition, copies in self.started:
            when(condition, lambda copies=copies: [copy.wait_send() for copy in copies] and None)


def gather_kernel(units, count, *refs):
    blocks, fulls = refs[:count], refs[count : 2 * count]
    send, recv, local_sem = refs[2 * count :]
    place = Place()
    place.greet()
    own = []
    for at, (block, full) in enumerate(zip(blocks, fulls)):
        width = block.shape[-1]
        columns = pl.ds(pl.multiple_of((place.x * 2 + place.k) * width, 128), width)
        copy = pltpu.make_async_copy(block, full.at[place.z, place.y, :, :, columns], local_sem.at[at])
        copy.start()
        own.append(copy)
    gathers = [
        Gather(place, blocks[which], fulls[which], strip, order, send.at[at], recv.at[at])
        for at, (which, strip, order) in enumerate(units)
    ]
    for unused in in_turn([gather.stages() for gather in gathers], 0.0):
        while own:
            own.pop().wait()
    for gather in gathers:
        gather.finish()


def gather_units(blocks, least, orders):
    strips = []
    for which, block in enumerate(blocks):
        wide = min(least, block.shape[-1])
        for part in range(block.shape[0]):
            for start in range(0, block.shape[-1], wide):
                strips.append((which, (part, start, wide)))
    return [strip + (orders[at % len(orders)],) for at, strip in enumerate(strips)]


def gather_blocks(blocks, collective_id, least):
    along, cols = lax.axis_size("row") // 2, lax.axis_size("col")
    units = gather_units(blocks, least, ORDERS)
    count = len(blocks)
    anywhere = pl.BlockSpec(memory_space=pl.ANY)
    moved = sum(block.size for block in blocks) * 2 * along * 2 * cols
    return pl.pallas_call(
        functools.partial(gather_kernel, units, count),
        out_shape=[
            jax.ShapeDtypeStruct((along, 2) + b.shape[:2] + (cols * b.shape[2],), b.dtype) for b in blocks
        ],
        in_specs=[anywhere] * count,
        out_specs=[anywhere] * count,
        scratch_shapes=[
            pltpu.SemaphoreType.DMA((len(units), 8 * along)),
            pltpu.SemaphoreType.DMA((len(units), 12 * along)),
            pltpu.SemaphoreType.DMA((count,)),
        ],
        compiler_params=pltpu.CompilerParams(collective_id=collective_id, has_side_effects=True),
        cost_estimate=pl.CostEstimate(flops=0, bytes_accessed=2 * moved, transcendentals=0),
    )(*blocks)


def add_blocks(total, extra, leading):
    def one(at, unused):
        place = []
        for size in leading[::-1]:
            place.append(at % size)
            at = at // size
        place = tuple(place[::-1])
        total[place] = total[place] + extra[place]
        return unused

    if not leading:
        total[...] = total[...] + extra[...]
        return
    count = 1
    for size in leading:
        count *= size
    lax.fori_loop(0, count, one, 0)


class Scatter:
    def __init__(self, place, grad, out, strip, width, order, slots, send, recv, local):
        self.place, self.grad, self.out, self.strip, self.width = place, grad, out, strip, width
        self.order = order[::-1]
        self.total, self.other_core, self.halves, self.steps = slots
        self.send, self.recv, self.local = send, recv, local
        self.used, self.started = 0, []

    def region(self, x, k):
        part, start, count = self.strip
        column = (x * 2 + k) * self.width + start
        return self.grad.at[:, :, part, :, pl.ds(pl.multiple_of(column, 128), count)]

    def copy(self, device, source, target, semaphore):
        return pltpu.make_async_remote_copy(
            src_ref=source, dst_ref=target, send_sem=self.send.at[semaphore], recv_sem=self.recv.at[semaphore],
            device_id=device, device_id_type=MESH)

    def reserve(self, count):
        self.used += count
        return self.used - count

    def start(self, make, condition=lambda: None):
        when(condition(), lambda: make().start())
        self.started.append((condition, make))

    def stages(self):
        place, along = self.place, self.place.along
        rows, columns = self.total.shape[-2:]
        core = self.reserve(2)

        def own(x):
            return pltpu.make_async_copy(self.region(x, place.k), self.total.at[:, :, x], self.local.at[x])

        def swapped(x):
            return self.copy(
                place.across("k"), self.region(x, 1 - place.k), self.other_core.at[:, :, x], core + x)

        for x in range(2):
            own(x).start()
            self.start(functools.partial(swapped, x))
        yield
        for x in range(2):
            own(x).wait()
            swapped(x).wait_recv()
        add_blocks(self.total, self.other_core, (along, 2, 2))
        left = {"z": slice(None), "y": slice(None), "x": slice(None)}
        at = {"y": place.y, "x": place.x}

        def view(ref, kept=None, **places):
            return ref.at[tuple({**(left if kept is None else kept), **places}[axis] for axis in "zyx")]

        def sizes():
            return tuple(size for axis, size in zip("zyx", (along, 2, 2)) if isinstance(left[axis], slice))

        exchanges = 0
        for axis in self.order:
            if axis == "z":
                shape = tuple(2 for name in "yx" if isinstance(left[name], slice))
                inner = tuple(slice(None) if isinstance(left[name], slice) else 0 for name in "yx")

                def landing(side, step, inner=inner):
                    return self.steps.at[(side, step) + inner]

                base = self.reserve(2 * along)
                right, leftward = range(base, base + along), range(base + along, base + 2 * along)
                for step in range(along):
                    if step:
                        yield
                    for way, names, first in ((1, right, place.z), (-1, leftward, along - 1 - place.z)):
                        goal = along - 1 - step + place.z if way == 1 else step - along + 1 + place.z
                        side = 0 if way == 1 else 1
                        if step:
                            arrived = landing(side, step - 1)

                            def take(arrived=arrived, goal=goal, side=side, step=step, names=names):
                                self.copy(place.across("k"), arrived, arrived, names[step - 1]).wait_recv()
                                add_blocks(view(self.total, z=goal), arrived, shape)

                            pl.when((first >= 1) & (first <= step))(take)
                        if step < along - 1:
                            kept = dict(left)

                            def onward(way=way, step=step, kept=kept, landing=landing, side=side, names=names):
                                goal = along - 1 - step + place.z if way == 1 else step - along + 1 + place.z
                                source = view(self.total, kept, z=jnp.clip(goal, 0, along - 1))
                                return self.copy(place.device(dz=way), source, landing(side, step), names[step])

                            def reached(way=way, step=step):
                                first = place.z if way == 1 else along - 1 - place.z
                                return (first <= step) & (first < along - 1)

                            self.start(onward, reached)
                left["z"] = place.z
            else:
                landing = self.halves[exchanges]
                exchanges += 1
                inner = tuple(slice(None) if isinstance(left[name], slice) and name != axis else 0 for name in "zyx")
                semaphore, kept = self.reserve(1), dict(left)

                def swap(axis=axis, kept=kept, landing=landing, inner=inner, semaphore=semaphore):
                    source = view(self.total, kept, **{axis: 1 - at[axis]})
                    return self.copy(place.across(axis), source, landing.at[inner], semaphore)

                self.start(swap)
                yield
                swap().wait_recv()
                left[axis] = at[axis]
                add_blocks(view(self.total), landing.at[inner], sizes())
        part, start, count = self.strip
        self.out[part, :, start : start + count] = view(self.total)[...].astype(jnp.float32)

    def finish(self):
        for condition, make in self.started:
            when(condition(), lambda make=make: make().wait_send())


def scatter_slots(along, rows, columns, order):
    left = {"z": along, "y": 2, "x": 2}
    whole = (along, 2, 2, rows, columns)
    shapes = [whole, whole]
    steps = None
    for axis in order[::-1]:
        if axis == "z":
            steps = (2, along - 1, left["y"], left["x"], rows, columns)
        left[axis] = 1
        if axis != "z":
            shapes.append((left["z"], left["y"], left["x"], rows, columns))
    return shapes + [steps]


def scatters_of(place, units, grads, outs, send, recv, local, slots):
    scatters = []
    for at, (which, strip, order) in enumerate(units):
        total, other_core, first, second, steps = slots[5 * at : 5 * at + 5]
        scatters.append(
            Scatter(place, grads[which], outs[which], strip, outs[which].shape[-1], order,
                    (total, other_core, (first, second), steps), send.at[at], recv.at[at], local.at[at]))
    return scatters


def scatter_kernel(units, count, *refs):
    grads, outs = refs[:count], refs[count : 2 * count]
    place = Place()
    place.greet()
    scatters = scatters_of(place, units, grads, outs, *refs[2 * count : 2 * count + 3], refs[2 * count + 3 :])
    for unused in in_turn([scatter.stages() for scatter in scatters], 0.5):
        pass
    for scatter in scatters:
        scatter.finish()


def scatter_plan(grads, least, orders):
    along, cols = lax.axis_size("row") // 2, lax.axis_size("col")
    blocks = [jax.ShapeDtypeStruct(g.shape[2:4] + (g.shape[4] // cols,), jnp.float32) for g in grads]
    units = gather_units(blocks, least, orders)
    scratch = [pltpu.SemaphoreType.DMA((len(units), 2 * along + 4))] * 2 + [pltpu.SemaphoreType.DMA((len(units), 2))]
    for which, strip, order in units:
        shapes = scatter_slots(along, blocks[which].shape[1], strip[2], order)
        scratch += [pltpu.VMEM(shape, jnp.bfloat16) for shape in shapes]
    return blocks, units, scratch


def scatter_blocks(grads, collective_id, least):
    blocks, units, scratch = scatter_plan(grads, least, ORDERS)
    count = len(grads)
    anywhere = pl.BlockSpec(memory_space=pl.ANY)
    return pl.pallas_call(
        functools.partial(scatter_kernel, units, count),
        out_shape=blocks,
        in_specs=[anywhere] * count,
        out_specs=[pl.BlockSpec(memory_space=pltpu.VMEM)] * count,
        scratch_shapes=scratch,
        compiler_params=pltpu.CompilerParams(
            collective_id=collective_id, has_side_effects=True, vmem_limit_bytes=60 << 20),
        cost_estimate=pl.CostEstimate(
            flops=sum(g.size for g in grads), bytes_accessed=4 * sum(g.size for g in grads), transcendentals=0),
    )(*grads)


def attend_rows(q, key_ref, value_ref, spans, diagonal, put):
    low = lax.broadcasted_iota(jnp.int32, (1, 128), 1) < HEAD_DIM
    mixed, logs = [], []
    for h in range(2):
        mine = low if h == 0 else jnp.logical_not(low)
        qh = jnp.where(mine, q, jnp.bfloat16(0))
        scores = []
        for at, length in spans:
            s = dg(qh, key_ref[at : at + length, :], NT)
            if at == diagonal:
                allowed = lax.broadcasted_iota(jnp.int32, s.shape, 0) >= lax.broadcasted_iota(jnp.int32, s.shape, 1)
                s = jnp.where(allowed, s, -1e30)
            scores.append(s)
        top = functools.reduce(jnp.maximum, [jnp.max(s, axis=1, keepdims=True) for s in scores])
        out = None
        for (at, length), s in zip(spans, scores):
            p = jnp.exp(s - top).astype(jnp.bfloat16)
            value = value_ref[at : at + length, :]
            part = dg(p, jnp.where(mine, value, jnp.ones_like(value)), NN)
            out = part if out is None else out + part
        total = out[:, HEAD_DIM : HEAD_DIM + 1] if h == 0 else out[:, 0:1]
        mixed.append(out / total)
        logs.append(top + jnp.log(total))
    put(logs)
    return jnp.where(low, mixed[0], mixed[1])


def rows_of(lanes_ref, first):
    picked = lax.broadcasted_iota(jnp.int32, (8, 128), 0) + first == lax.broadcasted_iota(jnp.int32, (8, 128), 1)
    return lax.dot_general(
        picked.astype(jnp.float32), lanes_ref[...], NT, precision=lax.Precision.HIGHEST,
        preferred_element_type=jnp.float32)


def pair_attend_kernel(tile, q_ref, k_ref, v_ref, q_any, k_any, v_any, mix_ref, logs_ref, fq_out, fk_out, fv_out,
                       near, near_logs, far_q, far_k, far_v, far, far_logs, got, far_rows, got_rows,
                       send, recv, local, keep):
    step = pl.program_id(0)
    place = Place()
    pairs = near.shape[0]
    fars = pairs // 2
    rows = q_ref.shape[0]
    first, second = place.y == 0, place.y == 1
    partner = place.across("y")
    lane = lax.broadcasted_iota(jnp.int32, (1, 128), 1)
    scale = jnp.bfloat16(HEAD_DIM**-0.5)
    plan = ((q_any, far_q, False), (k_any, far_k, True), (v_any, far_v, True))

    def columns(pair):
        return pl.ds(pl.multiple_of(pair * 128, 128), 128)

    def sending(which, j):
        array, landing, by_first = plan[which]
        return pltpu.make_async_remote_copy(
            src_ref=array.at[:, columns(j if by_first else fars + j)], dst_ref=landing.at[j],
            send_sem=send.at[which, j], recv_sem=recv.at[which, j], device_id=partner, device_id_type=MESH)

    def keeping(which, j):
        array, landing, by_first = plan[which]
        return pltpu.make_async_copy(
            array.at[:, columns(fars + j if by_first else j)], landing.at[j], local.at[which, j])

    def mixture_out(j):
        return pltpu.make_async_remote_copy(
            src_ref=far.at[j], dst_ref=got.at[j], send_sem=send.at[3, j], recv_sem=recv.at[3, j],
            device_id=partner, device_id_type=MESH)

    def logs_out():
        return pltpu.make_async_remote_copy(
            src_ref=far_rows, dst_ref=got_rows, send_sem=send.at[4, 0], recv_sem=recv.at[4, 0],
            device_id=partner, device_id_type=MESH)

    def saving(which):
        return pltpu.make_async_copy(plan[which][1], (fq_out, fk_out, fv_out)[which], keep.at[which])

    @pl.when(step == 0)
    def _():
        barrier = pltpu.get_barrier_semaphore()
        pl.semaphore_signal(barrier, inc=1, device_id=partner, device_id_type=MESH)
        pl.semaphore_wait(barrier, 1)
        near_logs[...] = jnp.zeros_like(near_logs)
        far_logs[...] = jnp.zeros_like(far_logs)
        for j in range(fars):
            for which in range(3):

                @pl.when(first if plan[which][2] else second)
                def _(which=which, j=j):
                    keeping(which, j).start()

    @pl.when((step % 3 == 0) & (step < 3 * fars))
    def _():
        j = step // 3
        for which in range(3):

            @pl.when(first if plan[which][2] else second)
            def _(which=which):
                @pl.when(j > 0)
                def _():
                    sending(which, j - 1).wait_send()

                sending(which, j).start()

    @pl.when(step < pairs)
    def _():
        for start in range(0, rows, tile):
            n = min(tile, rows - start)

            def put(logs, start=start, n=n):
                kept = near_logs[start : start + n, :]
                for h in range(2):
                    kept = jnp.where(lane == 2 * step + h, logs[h], kept)
                near_logs[start : start + n, :] = kept

            spans = ([(0, start)] if start else []) + [(start, n)]
            near[step, start : start + n, :] = attend_rows(
                q_ref[start : start + n, :] * scale, k_ref, v_ref, spans, start, put)

    @pl.when((step >= pairs) & (step < pairs + fars))
    def _():
        j = step - pairs
        for which in range(3):
            by_first = plan[which][2]

            @pl.when(first if by_first else second)
            def _(which=which):
                keeping(which, j).wait()

            @pl.when(second if by_first else first)
            def _(which=which):
                sending(which, j).wait_recv()

        base = jnp.where(first, 2 * fars, 0)
        for start in range(0, rows, tile):
            n = min(tile, rows - start)

            def put(logs, start=start, n=n):
                kept = far_logs[start : start + n, :]
                for h in range(2):
                    kept = jnp.where(lane == base + 2 * j + h, logs[h], kept)
                far_logs[start : start + n, :] = kept

            far[j, start : start + n, :] = attend_rows(
                far_q[j, start : start + n, :] * scale, far_k.at[j], far_v.at[j], [(0, rows)], None, put
            ).astype(far.dtype)

        @pl.when(first)
        def _():
            mixture_out(j).start()

    @pl.when(step == pairs + fars)
    def _():
        for which in range(3):
            saving(which).start()

        @pl.when(first)
        def _():
            far_rows[...] = rows_of(far_logs, 2 * fars)
            logs_out().start()
            for pair in range(pairs):
                mix_ref[:, pair * 128 : (pair + 1) * 128] = near[pair].astype(mix_ref.dtype)
            logs_ref[...] = near_logs[...]
            logs_out().wait_send()
            for j in range(fars):
                mixture_out(j).wait_send()
            for which in (1, 2):
                sending(which, fars - 1).wait_send()

        @pl.when(second)
        def _():
            logs_out().wait_recv()
            for j in range(fars):
                mixture_out(j).wait_recv()
            sending(0, fars - 1).wait_send()
            spread_out = (lax.broadcasted_iota(jnp.int32, (8, 128), 0) + 2 * fars == lane).astype(jnp.float32)
            theirs = lax.dot_general(
                got_rows[...], spread_out, TN, precision=lax.Precision.HIGHEST, preferred_element_type=jnp.float32)
            logs_far = far_logs[...] + theirs
            logs_near = near_logs[...]
            top = jnp.maximum(logs_near, logs_far)
            total = top + jnp.log(jnp.exp(logs_near - top) + jnp.exp(logs_far - top))
            logs_ref[...] = total
            share = jnp.exp(logs_near - total)
            low = lane < HEAD_DIM
            for pair in range(pairs):
                part = jnp.where(low, share[:, 2 * pair : 2 * pair + 1], share[:, 2 * pair + 1 : 2 * pair + 2])
                other = (far[pair] if pair < fars else got[pair - fars]).astype(jnp.float32)
                mix_ref[:, pair * 128 : (pair + 1) * 128] = (other + (near[pair] - other) * part).astype(mix_ref.dtype)

        for which in range(3):
            saving(which).wait()


def pair_attend(q, k, v, collective_id, tile=384):
    rows, width = q.shape
    pairs = width // 128
    fars = pairs // 2
    block = pl.BlockSpec((rows, 128), lambda i: (0, jnp.minimum(i, pairs - 1)))
    anywhere = pl.BlockSpec(memory_space=pl.ANY)
    kept = jax.ShapeDtypeStruct((fars, rows, 128), jnp.bfloat16)
    half = pltpu.VMEM((fars, rows, 128), jnp.bfloat16)
    return pl.pallas_call(
        functools.partial(pair_attend_kernel, tile),
        grid=(pairs + fars + 1,),
        in_specs=[block] * 3 + [anywhere] * 3,
        out_specs=[pl.BlockSpec((rows, width), lambda i: (0, 0)), pl.BlockSpec((rows, 128), lambda i: (0, 0))] + [anywhere] * 3,
        out_shape=[
            jax.ShapeDtypeStruct((rows, width), jnp.bfloat16), jax.ShapeDtypeStruct((rows, 128), jnp.float32), kept, kept, kept],
        scratch_shapes=[
            pltpu.VMEM((pairs, rows, 128), jnp.float32), pltpu.VMEM((rows, 128), jnp.float32),
            half, half, half, half, pltpu.VMEM((rows, 128), jnp.float32), half,
            pltpu.VMEM((8, rows), jnp.float32), pltpu.VMEM((8, rows), jnp.float32),
            pltpu.SemaphoreType.DMA((5, fars)), pltpu.SemaphoreType.DMA((5, fars)),
            pltpu.SemaphoreType.DMA((3, fars)), pltpu.SemaphoreType.DMA((3,)),
        ],
        compiler_params=pltpu.CompilerParams(
            collective_id=collective_id, has_side_effects=True, vmem_limit_bytes=48 << 20),
        cost_estimate=pl.CostEstimate(
            flops=4 * rows * rows * width, bytes_accessed=16 * rows * width, transcendentals=rows * rows * pairs * 2),
    )(q, k, v, q, k, v)


def back_pair(tile, causal, q_ref, k_ref, v_ref, do_ref, stats, acc, put):
    rows, keys = q_ref.shape[0], k_ref.shape[0]
    low = lax.broadcasted_iota(jnp.int32, (1, 128), 1) < HEAD_DIM
    acc[...] = jnp.zeros_like(acc)
    for start in range(0, keys, tile):
        n = min(tile, keys - start)
        k = k_ref[start : start + n, :] * jnp.bfloat16(HEAD_DIM**-0.5)
        v = v_ref[start : start + n, :]
        spans = [(0, rows)]
        if causal:
            spans = [(start, n)] + ([(start + n, rows - start - n)] if start + n < rows else [])
        dks, dvs = [], []
        for h in range(2):
            mine = low if h == 0 else jnp.logical_not(low)
            kh, vh = jnp.where(mine, k, jnp.bfloat16(0)), jnp.where(mine, v, jnp.bfloat16(0))
            dk = dv = None
            for at, length in spans:
                qs, do = q_ref[at : at + length, :], do_ref[at : at + length, :]
                p = jnp.exp(dg(kh, qs, NT) - stats[h : h + 1, at : at + length])
                if causal and at == start:
                    allowed = lax.broadcasted_iota(jnp.int32, p.shape, 0) <= lax.broadcasted_iota(jnp.int32, p.shape, 1)
                    p = jnp.where(allowed, p, 0.0)
                ds = (p * (dg(vh, do, NT) - stats[2 + h : 3 + h, at : at + length])).astype(jnp.bfloat16)
                a, b = dg(p.astype(jnp.bfloat16), do, NN), dg(ds, qs, NN)
                dv = a if dv is None else dv + a
                dk = b if dk is None else dk + b
                acc[at : at + length, :] += dg(ds, kh, TN)
            dks.append(dk)
            dvs.append(dv)
        put(start, n, jnp.where(low, dks[0], dks[1]) * HEAD_DIM**-0.5, jnp.where(low, dvs[0], dvs[1]))


def pair_stats(pair, mix_ref, do_ref, logs_ref):
    lane = lax.broadcasted_iota(jnp.int32, (8, 128), 1)
    line = lax.broadcasted_iota(jnp.int32, (8, 128), 0)
    picked = ((line < 2) & (line + 2 * pair == lane)).astype(jnp.float32)
    halves = (((line == 2) & (lane < HEAD_DIM)) | ((line == 3) & (lane >= HEAD_DIM))).astype(jnp.float32)
    products = mix_ref[...].astype(jnp.float32) * do_ref[...].astype(jnp.float32)
    logs = lax.dot_general(
        picked, logs_ref[...], NT, precision=lax.Precision.HIGHEST, preferred_element_type=jnp.float32)
    return logs + lax.dot_general(
        halves, products, NT, precision=lax.Precision.HIGHEST, preferred_element_type=jnp.float32)


def cross_back_kernel(q_ref, k_ref, v_ref, do_ref, mix_ref, logs_ref, dq_ref, dk_ref, dv_ref, acc, stats):
    stats[...] = pair_stats(pl.program_id(0), mix_ref, do_ref, logs_ref)

    def put(start, n, dk, dv):
        dk_ref[start : start + n, :] = dk.astype(dk_ref.dtype)
        dv_ref[start : start + n, :] = dv.astype(dv_ref.dtype)

    back_pair(k_ref.shape[0], False, q_ref, k_ref, v_ref, do_ref, stats, acc, put)
    dq_ref[...] = acc[...].astype(dq_ref.dtype)


def cross_back(q, k, v, do, mix, logs):
    rows, width = q.shape
    keys = k.shape[0]
    long, short = pl.BlockSpec((rows, 128), lambda i: (0, i)), pl.BlockSpec((keys, 128), lambda i: (0, i))
    return pl.pallas_call(
        cross_back_kernel,
        grid=(width // 128,),
        in_specs=[long, short, short, long, long, pl.BlockSpec((rows, 128), lambda i: (0, 0))],
        out_specs=[long, short, short],
        out_shape=[jax.ShapeDtypeStruct(a.shape, jnp.bfloat16) for a in (q, k, v)],
        scratch_shapes=[pltpu.VMEM((rows, 128), jnp.float32), pltpu.VMEM((8, rows), jnp.float32)],
        compiler_params=pltpu.CompilerParams(vmem_limit_bytes=40 << 20),
        cost_estimate=pl.CostEstimate(
            flops=10 * rows * keys * width, bytes_accessed=10 * rows * width, transcendentals=rows * keys * width // HEAD_DIM),
    )(q, k, v, do, mix, logs)


def pair_back_kernel(tile, far_tile, units, count, events, *refs):
    q_ref, k_ref, v_ref, do_ref, mix_ref, logs_ref, do_any, fq_any, fk_any, fv_any = refs[:10]
    grads, (dq_ref, dk_ref, dv_ref) = refs[10 : 10 + count], refs[10 + count : 13 + count]
    sums = refs[13 + count : 13 + 2 * count]
    (near, acc, stats, far_stats, used_stats, far_q, far_k, far_v, far_do, far_dq, far_dk, far_dv, got_q, got_k, got_v,
     send, recv, local, do_local) = refs[13 + 2 * count : 32 + 2 * count]
    scatter_refs = refs[32 + 2 * count :]
    step = pl.program_id(0)
    place = Place()
    pairs = near.shape[1]
    fars = pairs // 2
    first, second = place.y == 0, place.y == 1
    partner = place.across("y")

    def columns(pair):
        return pl.ds(pl.multiple_of(pair * 128, 128), 128)

    def remote(source, target, which, j):
        return pltpu.make_async_remote_copy(
            src_ref=source, dst_ref=target, send_sem=send.at[which, j], recv_sem=recv.at[which, j],
            device_id=partner, device_id_type=MESH)

    def grad_over(j):
        return remote(do_any.at[:, columns(fars + j)], far_do.at[j], 0, j)

    def grad_kept(j):
        return pltpu.make_async_copy(do_any.at[:, columns(j)], far_do.at[j], do_local.at[j])

    def stats_over():
        return remote(stats.at[pl.ds(fars, fars)], far_stats, 4, 0)

    def back_over(which, j):
        source, target = ((far_dq, got_q), (far_dk, got_k), (far_dv, got_v))[which]
        return remote(source.at[j], target.at[j], 1 + which, j)

    def far_in(which):
        source, target = ((fq_any, far_q), (fk_any, far_k), (fv_any, far_v))[which]
        return pltpu.make_async_copy(source, target, local.at[which])

    scatters = scatters_of(place, units, grads, sums, *scatter_refs[:3], scatter_refs[3:])
    turns = in_turn([scatter.stages() for scatter in scatters], 0.5)

    @pl.when(step == 0)
    def _():
        place.greet()
        for which in range(3):
            far_in(which).start()
        for j in range(fars):

            @pl.when(second)
            def _(j=j):
                grad_over(j).start()

            @pl.when(second)
            def _(j=j):
                grad_kept(j).start()

    for at, number in enumerate(events):

        @pl.when(step == at)
        def _(number=number):
            for unused in range(number):
                next(turns, None)

    @pl.when((step == fars) & second)
    def _():
        stats_over().start()

    @pl.when(step < pairs)
    def _():
        pair = lax.rem(step + fars, pairs)
        stats[pair] = pair_stats(pair, mix_ref, do_ref, logs_ref)

        def put(start, n, dk, dv):
            near[1, pair, start : start + n, :] = dk
            near[2, pair, start : start + n, :] = dv

        back_pair(tile, True, q_ref, k_ref, v_ref, do_ref, stats.at[pair], acc, put)
        near[0, pair] = acc[...]

    @pl.when((step >= pairs) & (step < pairs + fars))
    def _():
        j = step - pairs

        @pl.when(j == 0)
        def _():
            for which in range(3):
                far_in(which).wait()

            @pl.when(first)
            def _():
                stats_over().wait_recv()

        @pl.when(first)
        def _():
            grad_over(j).wait_recv()
            used_stats[...] = far_stats[j]

        @pl.when(second)
        def _():
            grad_kept(j).wait()
            used_stats[...] = stats[j]

        def put(start, n, dk, dv):
            far_dk[j, start : start + n, :] = dk.astype(far_dk.dtype)
            far_dv[j, start : start + n, :] = dv.astype(far_dv.dtype)

        back_pair(far_tile, False, far_q.at[j], far_k.at[j], far_v.at[j], far_do.at[j], used_stats, acc, put)
        far_dq[j] = acc[...].astype(far_dq.dtype)

        @pl.when(first)
        def _():
            back_over(0, j).start()

        @pl.when(second)
        def _():
            back_over(1, j).start()
            back_over(2, j).start()

    @pl.when(step >= pairs + fars)
    def _():
        pair = step - pairs - fars
        lower = pair < fars
        j = lax.rem(pair, fars)

        def write(ref, which, other):
            total = near[which, pair]
            if other is not None:
                total = total + other[j].astype(jnp.float32)
            ref[...] = total.astype(ref.dtype)

        @pl.when(first & lower)
        def _():
            for which in (1, 2):
                back_over(which, j).wait_recv()
            write(dq_ref, 0, None)
            write(dk_ref, 1, got_k)
            write(dv_ref, 2, got_v)

        @pl.when(first & jnp.logical_not(lower))
        def _():
            write(dq_ref, 0, None)
            write(dk_ref, 1, far_dk)
            write(dv_ref, 2, far_dv)

        @pl.when(second & lower)
        def _():
            write(dq_ref, 0, far_dq)
            write(dk_ref, 1, None)
            write(dv_ref, 2, None)

        @pl.when(second & jnp.logical_not(lower))
        def _():
            back_over(0, j).wait_recv()
            write(dq_ref, 0, got_q)
            write(dk_ref, 1, None)
            write(dv_ref, 2, None)

    @pl.when(step == 2 * pairs + fars - 1)
    def _():
        for unused in turns:
            pass
        for scatter in scatters:
            scatter.finish()

        @pl.when(first)
        def _():
            for j in range(fars):
                back_over(0, j).wait_send()

        @pl.when(second)
        def _():
            stats_over().wait_send()
            for j in range(fars):
                grad_over(j).wait_send()
                for which in (1, 2):
                    back_over(which, j).wait_send()


def pair_back(q, k, v, do, mix, logs, far, grads, collective_id, events, tile=384, far_tile=256):
    rows, width = q.shape
    pairs = width // 128
    fars = pairs // 2
    blocks, units, scratch = scatter_plan(grads, 256, ORDERS)
    count = len(grads)
    block = pl.BlockSpec((rows, 128), lambda i: (0, lax.rem(jnp.minimum(i, pairs - 1) + fars, pairs)))
    joined = pl.BlockSpec((rows, 128), lambda i: (0, jnp.maximum(i - pairs - fars, 0)))
    anywhere = pl.BlockSpec(memory_space=pl.ANY)
    half = pltpu.VMEM((fars, rows, 128), jnp.bfloat16)
    out = jax.ShapeDtypeStruct((rows, width), jnp.bfloat16)
    result = pl.pallas_call(
        functools.partial(pair_back_kernel, tile, far_tile, units, count, events),
        grid=(2 * pairs + fars,),
        in_specs=[block] * 5 + [pl.BlockSpec((rows, 128), lambda i: (0, 0))] + [anywhere] * (4 + count),
        out_specs=[joined] * 3 + [pl.BlockSpec(memory_space=pltpu.VMEM)] * count,
        out_shape=[out] * 3 + blocks,
        scratch_shapes=[
            pltpu.VMEM((3, pairs, rows, 128), jnp.float32), pltpu.VMEM((rows, 128), jnp.float32),
            pltpu.VMEM((pairs, 8, rows), jnp.float32), pltpu.VMEM((fars, 8, rows), jnp.float32),
            pltpu.VMEM((8, rows), jnp.float32), *[half] * 10,
            pltpu.SemaphoreType.DMA((5, fars)), pltpu.SemaphoreType.DMA((5, fars)),
            pltpu.SemaphoreType.DMA((3,)), pltpu.SemaphoreType.DMA((fars,)), *scratch,
        ],
        compiler_params=pltpu.CompilerParams(
            collective_id=collective_id, has_side_effects=True, vmem_limit_bytes=62 << 20),
        cost_estimate=pl.CostEstimate(
            flops=10 * rows * rows * width, bytes_accessed=16 * rows * width, transcendentals=rows * rows * pairs * 2),
    )(q, k, v, do, mix, logs, do, *far, *grads)
    return result[:3], result[3:]


def fast(
    frames_in, text_states, self_query, self_key, self_value, self_output, cross_query, cross_key, cross_value, cross_output,
    up_weight, down_weight, first_gain, first_bias, second_gain, second_bias, third_gain, third_bias, cotangent,
):
    row = lax.axis_index("row")
    rows, width = frames_in.shape
    half = width // 2
    piece = first_gain.shape[0]
    block_rows, block_cols = self_query.shape
    back = row % 2
    pairs = lax.axis_size("row") // 2
    forth_perm = [(2 * i, 2 * i + 1) for i in range(pairs)]
    back_perm = [(2 * i + 1, 2 * i) for i in range(pairs)]
    swap = forth_perm + back_perm

    def forth(array):
        return lax.ppermute(array, "row", forth_perm)

    def home(array):
        return lax.ppermute(array, "row", back_perm)

    def by_side(first, second):
        return jnp.where(back == 0, first, second)

    gains = jnp.zeros((1, 16, 128), jnp.bfloat16)
    gains = gains.at[0, :6, :piece].set(
        jnp.stack([first_gain, first_bias, second_gain, second_bias, third_gain, third_bias])
    )

    everyone = ("row", "col")
    places = (lax.axis_size("row"), lax.axis_size("col"))
    up_blocks = lax.all_gather(up_weight, everyone).reshape(*places, *up_weight.shape)
    down_blocks = lax.all_gather(down_weight, everyone).reshape(*places, *down_weight.shape)

    def small(block):
        return block.reshape(1, block_rows, block_cols)

    def flat(array):
        return array.reshape(-1, array.shape[-1])

    early = gather_blocks(
        [small(self_query), small(self_key), small(self_value), gains, small(self_output), small(cross_query),
         small(cross_key), small(cross_value), small(cross_output)], 1, 128)
    query_self, key_self, value_self = [flat(w) for w in early[:3]]
    out_self, query_cross, key_cross, value_cross, out_cross = [flat(w) for w in early[4:]]
    norm_params = early[3].reshape(pairs * 2, 16, -1, 128)[:, :6, :, :piece].transpose(1, 0, 2, 3)
    norm_params = norm_params.reshape(6, width).astype(jnp.float32)

    frames = frames_in.astype(jnp.float32)
    hidden_one = norm_forward(frames, norm_params[0], norm_params[1]).astype(jnp.bfloat16)
    self_k = matmul(hidden_one, key_self).astype(jnp.bfloat16)
    self_v = matmul(hidden_one, value_self).astype(jnp.bfloat16)
    self_q = matmul(hidden_one, query_self).astype(jnp.bfloat16)
    self_mix, log_lanes, far_q, far_k, far_v = pair_attend(self_q, self_k, self_v, 5)
    resid_one = frames + matmul(self_mix, out_self)
    hidden_two = norm_forward(resid_one, norm_params[2], norm_params[3]).astype(jnp.bfloat16)
    cross_q = matmul(hidden_two, query_cross).astype(jnp.bfloat16)
    other_text = lax.ppermute(text_states, "row", swap)
    clip_text = by_side(
        jnp.concatenate([text_states, other_text]), jnp.concatenate([other_text, text_states])
    )
    text_k = matmul(clip_text, key_cross).astype(jnp.bfloat16)
    text_v = matmul(clip_text, value_cross).astype(jnp.bfloat16)
    cross_mix, cross_logs = attend(cross_q, text_k, text_v, False, jnp.bfloat16)
    resid_two = resid_one + matmul(cross_mix, out_cross)
    hidden_three = norm_forward(resid_two, norm_params[4], norm_params[5]).astype(jnp.bfloat16)
    layer_out, grad_three, up_grad, down_grad = feed(hidden_three, cotangent, resid_two, up_blocks, down_blocks)
    up_sum = lax.psum_scatter(up_grad.reshape(-1, *up_weight.shape), everyone, scatter_dimension=0).astype(jnp.float32)

    cotan_full = cotangent.astype(jnp.float32)
    unused_three, pull_three = jax.vjp(norm_forward, resid_two, norm_params[4], norm_params[5])
    through_three, third_gain_part, third_bias_part = pull_three(grad_three)
    grad_resid_two = cotan_full + through_three
    grad_cross = grad_resid_two.astype(jnp.bfloat16)
    cross_out_grad = over_tokens(cross_mix, grad_cross)
    grad_cross_mix = by_transposed(grad_cross, out_cross).astype(jnp.bfloat16)
    grad_cross_q, text_k_part, text_v_part = cross_back(cross_q, text_k, text_v, grad_cross_mix, cross_mix, cross_logs)
    text_rows = text_states.shape[0]
    text_parts = jnp.concatenate([text_k_part, text_v_part], axis=1)
    given = lax.ppermute(by_side(text_parts[text_rows:], text_parts[:text_rows]), "row", swap)
    kept = by_side(text_parts[:text_rows], text_parts[text_rows:])
    text_parts = (kept.astype(jnp.float32) + given.astype(jnp.float32)).astype(jnp.bfloat16)
    grad_text_k, grad_text_v = text_parts[:, :width], text_parts[:, width:]
    cross_query_part = over_tokens(hidden_two, grad_cross_q)
    cross_key_part = over_tokens(text_states, grad_text_k)
    cross_value_part = over_tokens(text_states, grad_text_v)
    text_grad = by_transposed(grad_text_k, key_cross) + by_transposed(grad_text_v, value_cross)
    grad_two = by_transposed(grad_cross_q, query_cross)
    unused_two, pull_two = jax.vjp(norm_forward, resid_one, norm_params[2], norm_params[3])
    through_two, second_gain_part, second_bias_part = pull_two(grad_two)
    grad_resid_one = grad_resid_two + through_two
    grad_self = grad_resid_one.astype(jnp.bfloat16)
    self_out_grad = over_tokens(self_mix, grad_self)
    grad_self_mix = by_transposed(grad_self, out_self).astype(jnp.bfloat16)

    def by_place(grad, parts):
        return grad.astype(jnp.bfloat16).reshape(pairs, 2, parts, -1, grad.shape[-1])

    (grad_self_q, grad_self_k, grad_self_v), early_sums = pair_back(
        self_q, self_k, self_v, grad_self_mix, self_mix, log_lanes, (far_q, far_k, far_v),
        [by_place(g, 1) for g in (self_out_grad, cross_query_part, cross_key_part, cross_value_part, cross_out_grad)]
        + [by_place(down_grad, down_weight.shape[0] // block_rows)], 4, [5] * 12)
    self_query_part = over_tokens(hidden_one, grad_self_q)
    self_key_part = over_tokens(hidden_one, grad_self_k)
    self_value_part = over_tokens(hidden_one, grad_self_v)
    grad_one = (
        by_transposed(grad_self_q, query_self)
        + by_transposed(grad_self_k, key_self)
        + by_transposed(grad_self_v, value_self)
    )
    unused_one, pull_one = jax.vjp(norm_forward, frames, norm_params[0], norm_params[1])
    through_one, first_gain_part, first_bias_part = pull_one(grad_one)
    input_grad = grad_resid_one + through_one
    norm_grads = jnp.stack(
        [first_gain_part, first_bias_part, second_gain_part, second_bias_part, third_gain_part, third_bias_part]
    )
    norm_grads = norm_grads.reshape(6, 2 * pairs, -1, piece).transpose(1, 0, 2, 3)
    norm_grads = jnp.pad(norm_grads, ((0, 0), (0, 10), (0, 0), (0, 128 - piece)))

    late_sums = scatter_blocks(
        [by_place(g, 1) for g in (self_query_part, self_key_part, self_value_part)]
        + [by_place(norm_grads.reshape(2 * pairs * 16, -1), 1)], 3, 128)
    norm_parts = late_sums[3][0, :6, :piece]
    sums = [*late_sums[:3], *early_sums]
    sums = [total.reshape(-1, total.shape[-1]) for total in sums]
    return (layer_out, input_grad, text_grad, *sums[:-1], up_sum, sums[-1], *norm_parts)


def local(*arrays):
    frames_in, self_query = arrays[0], arrays[2]
    halves = 2 * frames_in.shape[0] == FRAMES and lax.axis_size("row") % 2 == 0
    if halves and lax.axis_size("col") % 2 == 0 and self_query.shape[1] % 256 == 0 and self_query.shape[0] % 128 == 0:
        return fast(*arrays)
    return general(*arrays)


def solution(mesh):
    placed = (
        P(("col", "row"), None),
        P(("col", "row"), None),
        P("row", "col"),
        P("row", "col"),
        P("row", "col"),
        P("row", "col"),
        P("row", "col"),
        P("row", "col"),
        P("row", "col"),
        P("row", "col"),
        P("row", "col"),
        P("row", "col"),
        P(("row", "col")),
        P(("row", "col")),
        P(("row", "col")),
        P(("row", "col")),
        P(("row", "col")),
        P(("row", "col")),
        P(("col", "row"), None),
    )
    return jax.shard_map(
        local,
        mesh=mesh,
        in_specs=placed,
        out_specs=(
            P(("col", "row"), None),
            P(("col", "row"), None),
            P(("col", "row"), None),
            P("row", "col"),
            P("row", "col"),
            P("row", "col"),
            P("row", "col"),
            P("row", "col"),
            P("row", "col"),
            P("row", "col"),
            P("row", "col"),
            P("row", "col"),
            P("row", "col"),
            P(("row", "col")),
            P(("row", "col")),
            P(("row", "col")),
            P(("row", "col")),
            P(("row", "col")),
            P(("row", "col")),
        ),
        check_vma=False,
    )
```

```python
import functools
from functools import partial

import jax
import jax.numpy as jnp
from jax import lax
from jax.experimental import pallas as pl
from jax.experimental.pallas import tpu as pltpu
from jax.sharding import PartitionSpec as P

HEADS = 16
HEAD_DIM = 64
FRAMES = 1500
TEXT = 64


def norm_forward(values, norm_gain, norm_bias):
    center = values - jnp.mean(values, axis=-1, keepdims=True)
    variance = jnp.mean(center * center, axis=-1, keepdims=True)
    return center * lax.rsqrt(variance + 1e-05) * norm_gain + norm_bias


def matmul(left, right):
    return jnp.dot(left, right, preferred_element_type=jnp.float32)


def by_transposed(left, right):
    return lax.dot_general(
        left, right, (((1,), (1,)), ((), ())), preferred_element_type=jnp.float32
    )


def over_tokens(left, right):
    return lax.dot_general(
        left, right, (((0,), (0,)), ((), ())), preferred_element_type=jnp.float32
    )


def collect(blocks):
    partly = (
        lax.all_gather(blocks[0], "col", axis=1, tiled=True),
        lax.all_gather(blocks[1], "col", axis=1, tiled=True),
        lax.all_gather(blocks[2], "col", axis=1, tiled=True),
        lax.all_gather(blocks[3], "col", axis=1, tiled=True),
        lax.all_gather(blocks[4], "col", axis=1, tiled=True),
        lax.all_gather(blocks[5], "col", axis=1, tiled=True),
        lax.all_gather(blocks[6], "col", axis=1, tiled=True),
        lax.all_gather(blocks[7], "col", axis=1, tiled=True),
        lax.all_gather(blocks[8], "col", axis=1, tiled=True),
        lax.all_gather(blocks[9], "col", axis=1, tiled=True),
        lax.all_gather(blocks[10], "col", axis=1, tiled=True),
    )
    return (
        lax.all_gather(partly[0], "row", axis=0, tiled=True),
        lax.all_gather(partly[1], "row", axis=0, tiled=True),
        lax.all_gather(partly[2], "row", axis=0, tiled=True),
        lax.all_gather(partly[3], "row", axis=0, tiled=True),
        lax.all_gather(partly[4], "row", axis=0, tiled=True),
        lax.all_gather(partly[5], "row", axis=0, tiled=True),
        lax.all_gather(partly[6], "row", axis=0, tiled=True),
        lax.all_gather(partly[7], "row", axis=0, tiled=True),
        lax.all_gather(partly[8], "row", axis=0, tiled=True),
        lax.all_gather(partly[9], "row", axis=0, tiled=True),
        lax.all_gather(partly[10], "row", axis=0, tiled=True),
    )


def spread(grads):
    partly = (
        lax.psum_scatter(
            grads[0].astype(jnp.bfloat16), "row", scatter_dimension=0, tiled=True
        ).astype(jnp.float32),
        lax.psum_scatter(
            grads[1].astype(jnp.bfloat16), "row", scatter_dimension=0, tiled=True
        ).astype(jnp.float32),
        lax.psum_scatter(
            grads[2].astype(jnp.bfloat16), "row", scatter_dimension=0, tiled=True
        ).astype(jnp.float32),
        lax.psum_scatter(
            grads[3].astype(jnp.bfloat16), "row", scatter_dimension=0, tiled=True
        ).astype(jnp.float32),
        lax.psum_scatter(
            grads[4].astype(jnp.bfloat16), "row", scatter_dimension=0, tiled=True
        ).astype(jnp.float32),
        lax.psum_scatter(
            grads[5].astype(jnp.bfloat16), "row", scatter_dimension=0, tiled=True
        ).astype(jnp.float32),
        lax.psum_scatter(
            grads[6].astype(jnp.bfloat16), "row", scatter_dimension=0, tiled=True
        ).astype(jnp.float32),
        lax.psum_scatter(
            grads[7].astype(jnp.bfloat16), "row", scatter_dimension=0, tiled=True
        ).astype(jnp.float32),
        lax.psum_scatter(
            grads[8].astype(jnp.bfloat16), "row", scatter_dimension=0, tiled=True
        ).astype(jnp.float32),
        lax.psum_scatter(
            grads[9].astype(jnp.bfloat16), "row", scatter_dimension=0, tiled=True
        ).astype(jnp.float32),
        lax.psum_scatter(
            grads[10].astype(jnp.bfloat16), "row", scatter_dimension=0, tiled=True
        ).astype(jnp.float32),
    )
    return (
        lax.psum_scatter(
            partly[0].astype(jnp.bfloat16), "col", scatter_dimension=1, tiled=True
        ).astype(jnp.float32),
        lax.psum_scatter(
            partly[1].astype(jnp.bfloat16), "col", scatter_dimension=1, tiled=True
        ).astype(jnp.float32),
        lax.psum_scatter(
            partly[2].astype(jnp.bfloat16), "col", scatter_dimension=1, tiled=True
        ).astype(jnp.float32),
        lax.psum_scatter(
            partly[3].astype(jnp.bfloat16), "col", scatter_dimension=1, tiled=True
        ).astype(jnp.float32),
        lax.psum_scatter(
            partly[4].astype(jnp.bfloat16), "col", scatter_dimension=1, tiled=True
        ).astype(jnp.float32),
        lax.psum_scatter(
            partly[5].astype(jnp.bfloat16), "col", scatter_dimension=1, tiled=True
        ).astype(jnp.float32),
        lax.psum_scatter(
            partly[6].astype(jnp.bfloat16), "col", scatter_dimension=1, tiled=True
        ).astype(jnp.float32),
        lax.psum_scatter(
            partly[7].astype(jnp.bfloat16), "col", scatter_dimension=1, tiled=True
        ).astype(jnp.float32),
        lax.psum_scatter(
            partly[8].astype(jnp.bfloat16), "col", scatter_dimension=1, tiled=True
        ).astype(jnp.float32),
        lax.psum_scatter(
            partly[9].astype(jnp.bfloat16), "col", scatter_dimension=1, tiled=True
        ).astype(jnp.float32),
        lax.psum_scatter(
            partly[10].astype(jnp.bfloat16), "col", scatter_dimension=1, tiled=True
        ).astype(jnp.float32),
    )


def heads_layout(stacked):
    return lax.all_to_all(stacked, "row", split_axis=1, concat_axis=0, tiled=True)


def tokens_layout(stacked):
    return lax.all_to_all(stacked, "row", split_axis=0, concat_axis=2, tiled=True)


def by_clips(arranged, start, count, length, heads_dev):
    section = arranged[:, start : start + count]
    return section.reshape(-1, length, heads_dev, HEAD_DIM)


def causal_scores(query_clip, key_clip, causal):
    scores = jnp.einsum(
        "qhd,khd->hqk", query_clip, key_clip, preferred_element_type=jnp.float32
    ) * HEAD_DIM ** (-0.5)
    if causal:
        allowed = jnp.arange(scores.shape[1])[:, None] >= jnp.arange(scores.shape[2])[None, :]
        scores = jnp.where(allowed, scores, -1e30)
    return scores


def attend_forward(query_clips, key_clips, value_clips, causal):

    def one_clip(operands):
        query_clip, key_clip, value_clip = operands
        scores = causal_scores(query_clip, key_clip, causal)
        highest = jnp.max(scores, axis=-1, keepdims=True)
        powers = jnp.exp(scores - highest)
        totals = jnp.sum(powers, axis=-1, keepdims=True)
        weights_low = (powers / totals).astype(jnp.bfloat16)
        mixture = jnp.einsum(
            "hqk,khd->qhd", weights_low, value_clip, preferred_element_type=jnp.float32
        )
        return (mixture.astype(jnp.bfloat16), (highest + jnp.log(totals))[..., 0])

    return lax.map(one_clip, (query_clips, key_clips, value_clips))


def attend_backward(query_clips, key_clips, value_clips, log_sums, grad_clips, causal):

    def one_clip(operands):
        query_clip, key_clip, value_clip, log_clip, grad_clip = operands
        scores = causal_scores(query_clip, key_clip, causal)
        probs_full = jnp.exp(scores - log_clip[..., None])
        grad_probs = jnp.einsum(
            "qhd,khd->hqk", grad_clip, value_clip, preferred_element_type=jnp.float32
        )
        grad_value = jnp.einsum(
            "hqk,qhd->khd",
            probs_full.astype(jnp.bfloat16),
            grad_clip,
            preferred_element_type=jnp.float32,
        )
        centered = grad_probs - jnp.sum(probs_full * grad_probs, axis=-1, keepdims=True)
        grad_scores = (probs_full * centered).astype(jnp.bfloat16)
        grad_query = jnp.einsum(
            "hqk,khd->qhd", grad_scores, key_clip, preferred_element_type=jnp.float32
        ) * HEAD_DIM ** (-0.5)
        grad_key = jnp.einsum(
            "hqk,qhd->khd", grad_scores, query_clip, preferred_element_type=jnp.float32
        ) * HEAD_DIM ** (-0.5)
        return (
            grad_query.astype(jnp.bfloat16),
            grad_key.astype(jnp.bfloat16),
            grad_value.astype(jnp.bfloat16),
        )

    return lax.map(one_clip, (query_clips, key_clips, value_clips, log_sums, grad_clips))


def general(
    frames_in,
    text_states,
    self_query,
    self_key,
    self_value,
    self_output,
    cross_query,
    cross_key,
    cross_value,
    cross_output,
    up_weight,
    down_weight,
    first_gain,
    first_bias,
    second_gain,
    second_bias,
    third_gain,
    third_bias,
    cotangent,
):
    row_count = lax.axis_size("row")
    col_count = lax.axis_size("col")
    heads_dev = HEADS // row_count
    width_dev = heads_dev * HEAD_DIM
    tok_rows = frames_in.shape[0]
    text_rows = text_states.shape[0]
    piece_len = first_gain.shape[0]
    gain_block = jnp.stack(
        [first_gain, first_bias, second_gain, second_bias, third_gain, third_bias]
    ).reshape(1, 6 * piece_len)
    param_blocks = (
        self_query,
        self_key,
        self_value,
        self_output,
        cross_query,
        cross_key,
        cross_value,
        cross_output,
        up_weight,
        down_weight,
        gain_block,
    )

    def unpack_gains(gathered_gains):
        arranged = gathered_gains.reshape(row_count, col_count, 6, piece_len).transpose(2, 0, 1, 3)
        return arranged.reshape(6, row_count * col_count * piece_len).astype(jnp.float32)

    gathered = collect(param_blocks)
    (
        query_self,
        key_self,
        value_self,
        out_self,
        query_cross,
        key_cross,
        value_cross,
        out_cross,
        up_full,
        down_full,
    ) = gathered[:10]
    norm_params = unpack_gains(gathered[10])
    frames = frames_in.astype(jnp.float32)
    hidden_one = norm_forward(frames, norm_params[0], norm_params[1]).astype(jnp.bfloat16)
    self_q = matmul(hidden_one, query_self).astype(jnp.bfloat16)
    self_k = matmul(hidden_one, key_self).astype(jnp.bfloat16)
    self_v = matmul(hidden_one, value_self).astype(jnp.bfloat16)
    text_k = matmul(text_states, key_cross).astype(jnp.bfloat16)
    text_v = matmul(text_states, value_cross).astype(jnp.bfloat16)
    sent_rows = 3 * tok_rows + 2 * text_rows
    arranged = heads_layout(jnp.concatenate([self_q, self_k, self_v, text_k, text_v], axis=0))
    arranged = arranged.reshape(row_count, sent_rows, width_dev)
    query_clips = by_clips(arranged, 0, tok_rows, FRAMES, heads_dev)
    key_clips = by_clips(arranged, tok_rows, tok_rows, FRAMES, heads_dev)
    value_clips = by_clips(arranged, 2 * tok_rows, tok_rows, FRAMES, heads_dev)
    text_keys = by_clips(arranged, 3 * tok_rows, text_rows, TEXT, heads_dev)
    text_values = by_clips(arranged, 3 * tok_rows + text_rows, text_rows, TEXT, heads_dev)
    self_clips, self_logs = attend_forward(query_clips, key_clips, value_clips, True)
    self_mix = tokens_layout(self_clips.reshape(row_count, tok_rows, width_dev))[0]
    resid_one = frames + matmul(self_mix, out_self)
    hidden_two = norm_forward(resid_one, norm_params[2], norm_params[3]).astype(jnp.bfloat16)
    cross_q = matmul(hidden_two, query_cross).astype(jnp.bfloat16)
    cross_arranged = heads_layout(cross_q).reshape(row_count, tok_rows, width_dev)
    cross_queries = by_clips(cross_arranged, 0, tok_rows, FRAMES, heads_dev)
    cross_clips, cross_logs = attend_forward(cross_queries, text_keys, text_values, False)
    cross_mix = tokens_layout(cross_clips.reshape(row_count, tok_rows, width_dev))[0]
    resid_two = resid_one + matmul(cross_mix, out_cross)
    hidden_three = norm_forward(resid_two, norm_params[4], norm_params[5]).astype(jnp.bfloat16)
    pre_act = matmul(hidden_three, up_full)
    inner = jax.nn.gelu(pre_act, approximate=False).astype(jnp.bfloat16)
    layer_out = (resid_two + matmul(inner, down_full)).astype(jnp.bfloat16)
    gathered = collect(param_blocks)
    (
        query_self,
        key_self,
        value_self,
        out_self,
        query_cross,
        key_cross,
        value_cross,
        out_cross,
        up_full,
        down_full,
    ) = gathered[:10]
    norm_params = unpack_gains(gathered[10])
    cotan_full = cotangent.astype(jnp.float32)
    down_grad = over_tokens(inner, cotangent)
    grad_inner = by_transposed(cotangent, down_full)
    unused_gelu, gelu_pull = jax.vjp(partial(jax.nn.gelu, approximate=False), pre_act)
    grad_pre = gelu_pull(grad_inner)[0].astype(jnp.bfloat16)
    up_grad = over_tokens(hidden_three, grad_pre)
    grad_three = by_transposed(grad_pre, up_full)
    unused_three, pull_three = jax.vjp(norm_forward, resid_two, norm_params[4], norm_params[5])
    through_three, third_gain_part, third_bias_part = pull_three(grad_three)
    grad_resid_two = cotan_full + through_three
    grad_cross = grad_resid_two.astype(jnp.bfloat16)
    cross_out_grad = over_tokens(cross_mix, grad_cross)
    grad_cross_mix = by_transposed(grad_cross, out_cross).astype(jnp.bfloat16)
    grad_cross_arr = heads_layout(grad_cross_mix).reshape(row_count, tok_rows, width_dev)
    grad_cross_clips = by_clips(grad_cross_arr, 0, tok_rows, FRAMES, heads_dev)
    cq_clips, tk_clips, tv_clips = attend_backward(
        cross_queries, text_keys, text_values, cross_logs, grad_cross_clips, False
    )
    back_cross = jnp.concatenate(
        [
            cq_clips.reshape(row_count, tok_rows, width_dev),
            tk_clips.reshape(row_count, text_rows, width_dev),
            tv_clips.reshape(row_count, text_rows, width_dev),
        ],
        axis=1,
    )
    back_cross = tokens_layout(back_cross)[0]
    grad_cross_q = back_cross[:tok_rows]
    grad_text_k = back_cross[tok_rows : tok_rows + text_rows]
    grad_text_v = back_cross[tok_rows + text_rows :]
    cross_query_part = over_tokens(hidden_two, grad_cross_q)
    cross_key_part = over_tokens(text_states, grad_text_k)
    cross_value_part = over_tokens(text_states, grad_text_v)
    text_grad = by_transposed(grad_text_k, key_cross) + by_transposed(grad_text_v, value_cross)
    grad_two = by_transposed(grad_cross_q, query_cross)
    unused_two, pull_two = jax.vjp(norm_forward, resid_one, norm_params[2], norm_params[3])
    through_two, second_gain_part, second_bias_part = pull_two(grad_two)
    grad_resid_one = grad_resid_two + through_two
    grad_self = grad_resid_one.astype(jnp.bfloat16)
    self_out_grad = over_tokens(self_mix, grad_self)
    grad_self_mix = by_transposed(grad_self, out_self).astype(jnp.bfloat16)
    grad_self_arr = heads_layout(grad_self_mix).reshape(row_count, tok_rows, width_dev)
    grad_self_clips = by_clips(grad_self_arr, 0, tok_rows, FRAMES, heads_dev)
    sq_clips, sk_clips, sv_clips = attend_backward(
        query_clips, key_clips, value_clips, self_logs, grad_self_clips, True
    )
    back_self = jnp.concatenate(
        [
            sq_clips.reshape(row_count, tok_rows, width_dev),
            sk_clips.reshape(row_count, tok_rows, width_dev),
            sv_clips.reshape(row_count, tok_rows, width_dev),
        ],
        axis=1,
    )
    back_self = tokens_layout(back_self)[0]
    grad_self_q = back_self[:tok_rows]
    grad_self_k = back_self[tok_rows : 2 * tok_rows]
    grad_self_v = back_self[2 * tok_rows :]
    self_query_part = over_tokens(hidden_one, grad_self_q)
    self_key_part = over_tokens(hidden_one, grad_self_k)
    self_value_part = over_tokens(hidden_one, grad_self_v)
    grad_one = (
        by_transposed(grad_self_q, query_self)
        + by_transposed(grad_self_k, key_self)
        + by_transposed(grad_self_v, value_self)
    )
    unused_one, pull_one = jax.vjp(norm_forward, frames, norm_params[0], norm_params[1])
    through_one, first_gain_part, first_bias_part = pull_one(grad_one)
    input_grad = grad_resid_one + through_one
    norm_grads = jnp.stack(
        [
            first_gain_part,
            first_bias_part,
            second_gain_part,
            second_bias_part,
            third_gain_part,
            third_bias_part,
        ]
    )
    norm_grads = norm_grads.reshape(6, row_count, col_count, piece_len).transpose(1, 2, 0, 3)
    norm_grads = norm_grads.reshape(row_count, col_count * 6 * piece_len)
    summed = spread(
        (
            self_query_part,
            self_key_part,
            self_value_part,
            self_out_grad,
            cross_query_part,
            cross_key_part,
            cross_value_part,
            cross_out_grad,
            up_grad,
            down_grad,
            norm_grads,
        )
    )
    norm_parts = summed[10].reshape(6, piece_len)
    return (
        layer_out,
        input_grad,
        text_grad,
        summed[0],
        summed[1],
        summed[2],
        summed[3],
        summed[4],
        summed[5],
        summed[6],
        summed[7],
        summed[8],
        summed[9],
        norm_parts[0],
        norm_parts[1],
        norm_parts[2],
        norm_parts[3],
        norm_parts[4],
        norm_parts[5],
    )


NT=(((1,),(1,)),((),())); NN=(((1,),(0,)),((),())); TN=(((0,),(0,)),((),()))
def dg(a,b,dims): return lax.dot_general(a,b,dims,preferred_element_type=jnp.float32)

def attend_kernel(causal,tile,q_ref,k_ref,v_ref,o_ref,lse_ref):
    pair=pl.program_id(0)
    rows=q_ref.shape[0]
    low=lax.broadcasted_iota(jnp.int32,(1,128),1)<HEAD_DIM
    lane=lax.broadcasted_iota(jnp.int32,(1,128),1)
    value=v_ref[...]
    ones=jnp.ones_like(value)
    @pl.when(pair==0)
    def _(): lse_ref[...]=jnp.zeros_like(lse_ref)
    for start in range(0,rows,tile):
        n=min(tile,rows-start)
        q=q_ref[start:start+n,:]*jnp.bfloat16(HEAD_DIM**-0.5)
        mixed=[]; sums=[]
        lse=lse_ref[start:start+n,:]
        for h in range(2):
            mine=low if h==0 else jnp.logical_not(low)
            qh=jnp.where(mine,q,jnp.bfloat16(0))
            vh=jnp.where(mine,value,ones)
            if causal:
                spans=([(0,start)] if start else [])+[(start,n)]
            else: spans=[(0,k_ref.shape[0])]
            scores=[]
            for at,length in spans:
                s=dg(qh,k_ref[at:at+length,:],NT)
                if causal and at==start:
                    ok=lax.broadcasted_iota(jnp.int32,s.shape,0)>=lax.broadcasted_iota(jnp.int32,s.shape,1)
                    s=jnp.where(ok,s,-1e30)
                scores.append(s)
            top=functools.reduce(jnp.maximum,[jnp.max(s,axis=1,keepdims=True) for s in scores])
            out=None
            for (at,length),s in zip(spans,scores):
                p=jnp.exp(s-top).astype(jnp.bfloat16)
                part=dg(p,vh[at:at+length,:],NN)
                out=part if out is None else out+part
            total=out[:,HEAD_DIM:HEAD_DIM+1] if h==0 else out[:,0:1]
            mixed.append(out/total)
            lse=jnp.where(lane==2*pair+h,top+jnp.log(total),lse)
        lse_ref[start:start+n,:]=lse
        o_ref[start:start+n,:]=jnp.where(low,mixed[0],mixed[1]).astype(o_ref.dtype)

def attend(q,k,v,causal,out_dtype,tile=256):
    rows,width=q.shape; keys=k.shape[0]
    return pl.pallas_call(functools.partial(attend_kernel,causal,tile),grid=(width//128,),
        in_specs=[pl.BlockSpec((rows,128),lambda i:(0,i)),pl.BlockSpec((keys,128),lambda i:(0,i)),pl.BlockSpec((keys,128),lambda i:(0,i))],
        out_specs=[pl.BlockSpec((rows,128),lambda i:(0,i)),pl.BlockSpec((rows,128),lambda i:(0,0))],
        out_shape=[jax.ShapeDtypeStruct((rows,width),out_dtype),jax.ShapeDtypeStruct((rows,128),jnp.float32)],
        compiler_params=pltpu.CompilerParams(vmem_limit_bytes=40<<20),
        cost_estimate=pl.CostEstimate(flops=4*rows*keys*width,bytes_accessed=8*rows*width,transcendentals=rows*keys*width//64))(q,k,v)

def feed_kernel(h_ref,cot_ref,res_ref,up_ref,down_ref,out_ref,g_ref,dup_ref,ddown_ref,acc):
    i=pl.program_id(0)
    @pl.when(i==0)
    def _():
        acc[...]=res_ref[...]
        g_ref[...]=jnp.zeros_like(g_ref)
    h=h_ref[...]
    up=up_ref[:,0].reshape(h.shape[1],-1)
    blocks,wide=down_ref.shape[1],down_ref.shape[3]
    pre=dg(h,up,NN)
    cdf=0.5*(1.0+lax.erf(pre*0.7071067811865476))
    inner=(pre*cdf).astype(jnp.bfloat16)
    slope=cdf+pre*(jnp.exp(-0.5*pre*pre)*0.3989422804014327)
    grad=None
    for at in range(blocks):
        columns=slice(at*wide,(at+1)*wide)
        cot=cot_ref[:,columns]
        acc[:,columns]+=dg(inner,down_ref[0,at],NN)
        ddown_ref[:,columns]=dg(inner,cot,TN).astype(ddown_ref.dtype)
        part=dg(cot,down_ref[0,at],NT)
        grad=part if grad is None else grad+part
    gpre=(grad*slope).astype(jnp.bfloat16)
    dup_ref[:,0]=dg(h,gpre,TN).astype(dup_ref.dtype).reshape(dup_ref.shape[0],dup_ref.shape[2],dup_ref.shape[3])
    g_ref[...]+=dg(gpre,up,NT)
    @pl.when(i==pl.num_programs(0)-1)
    def _(): out_ref[...]=acc[...].astype(out_ref.dtype)

def feed(h,cot,res,up,down):
    rows,d=h.shape; chunk=down.shape[2]; strips=up.shape[3]//chunk; ff=down.shape[0]*chunk
    whole=pl.BlockSpec((rows,d),lambda i:(0,0))
    up_spec=pl.BlockSpec((up.shape[0],1,up.shape[2],chunk),lambda i:(0,i//strips,0,i%strips))
    down_spec=pl.BlockSpec((1,)+down.shape[1:],lambda i:(i,0,0,0))
    return pl.pallas_call(feed_kernel,grid=(ff//chunk,),
        in_specs=[whole,whole,whole,up_spec,down_spec],
        out_specs=[whole,whole,up_spec,pl.BlockSpec((chunk,d),lambda i:(i,0))],
        out_shape=[jax.ShapeDtypeStruct((rows,d),jnp.bfloat16),jax.ShapeDtypeStruct((rows,d),jnp.float32),jax.ShapeDtypeStruct(up.shape,jnp.bfloat16),jax.ShapeDtypeStruct((ff,d),jnp.bfloat16)],
        scratch_shapes=[pltpu.VMEM((rows,d),jnp.float32)],
        compiler_params=pltpu.CompilerParams(vmem_limit_bytes=56<<20),
        cost_estimate=pl.CostEstimate(flops=12*rows*d*ff,bytes_accessed=8*d*ff+16*rows*d,transcendentals=2*rows*ff))(h,cot,res,up,down)


MESH = pl.DeviceIdType.MESH
ORDERS = ("xzy", "yzx", "xzy", "yzx", "zxy", "zyx")


class Place:
    def __init__(self):
        row, col = lax.axis_index("row"), lax.axis_index("col")
        self.z, self.y, self.x, self.k = row // 2, row % 2, col // 2, col % 2
        self.along = lax.axis_size("row") // 2

    def device(self, dz=0, y=False, x=False, k=False):
        other_y = 1 - self.y if y else self.y
        other_x = 1 - self.x if x else self.x
        other_k = 1 - self.k if k else self.k
        return ((self.z + dz) * 2 + other_y, other_x * 2 + other_k)

    def across(self, axis):
        return self.device(y=axis == "y", x=axis == "x", k=axis == "k")

    def greet(self):
        barrier = pltpu.get_barrier_semaphore()
        for axis in "xyk":
            pl.semaphore_signal(barrier, inc=1, device_id=self.across(axis), device_id_type=MESH)

        @pl.when(self.z > 0)
        def _():
            pl.semaphore_signal(barrier, inc=1, device_id=self.device(dz=-1), device_id_type=MESH)

        @pl.when(self.z + 1 < self.along)
        def _():
            pl.semaphore_signal(barrier, inc=1, device_id=self.device(dz=1), device_id_type=MESH)

        below = jnp.where(self.z > 0, 1, 0)
        above = jnp.where(self.z + 1 < self.along, 1, 0)
        pl.semaphore_wait(barrier, 3 + below + above)


def when(condition, run):
    if condition is None:
        run()
    else:
        pl.when(condition)(run)


def in_turn(units, lag):
    ready = [(lag * at, at) for at in range(len(units))]
    while ready:
        turn, at = min(ready)
        ready.remove((turn, at))
        if next(units[at], units) is not units:
            ready.append((turn + 1, at))
        yield


class Gather:
    def __init__(self, place, block, full, strip, order, send, recv):
        self.place, self.block, self.full, self.strip = place, block, full, strip
        turn = order.index("z")
        self.before, self.after = order[:turn], order[turn + 1 :]
        self.send, self.recv, self.used, self.sent, self.started = send, recv, 0, 0, []

    def region(self, z, y, x):
        part, start, count = self.strip
        column = (x * 2 + self.place.k) * self.block.shape[-1] + start
        return self.full.at[z, y, part, :, pl.ds(pl.multiple_of(column, 128), count)]

    def held(self, done, z):
        y = slice(None) if "y" in done else self.place.y
        return [self.region(z, y, x) for x in (range(2) if "x" in done else [self.place.x])]

    def pairs(self, done, z, first):
        if first:
            part, start, count = self.strip
            place = self.place
            return [(self.block.at[part, :, pl.ds(start, count)], self.region(place.z, place.y, place.x))]
        return [(region, region) for region in self.held(done, z)]

    def semaphore(self):
        self.used += 2
        return self.used - 2

    def copies(self, device, pairs, semaphore, send=0):
        return [
            pltpu.make_async_remote_copy(
                src_ref=source, dst_ref=target, send_sem=self.send.at[send + at],
                recv_sem=self.recv.at[semaphore + at], device_id=device, device_id_type=MESH)
            for at, (source, target) in enumerate(pairs)
        ]

    def start(self, device, pairs, wide, condition, semaphore):
        send = self.sent
        self.sent += wide

        def make():
            return self.copies(device(), pairs(), semaphore, send)

        when(condition(), lambda: [copy.start() for copy in make()] and None)
        self.started.append((condition, make))
        return condition, make

    def arrive(self, sent):
        condition, make = sent
        when(condition(), lambda: [copy.wait_recv() for copy in make()] and None)

    def stages(self):
        place, along = self.place, self.place.along
        done = []

        def always():
            return None

        def width(axes):
            return 2 if "x" in axes else 1

        for axis in self.before:
            axes = tuple(done)
            sent = self.start(
                lambda axis=axis: place.across(axis), lambda axes=axes: self.pairs(axes, place.z, not axes),
                width(axes), always, self.semaphore())
            yield
            self.arrive(sent)
            done.append(axis)
        first = not done
        axes_z = tuple(done)
        from_left = [self.semaphore() for _ in range(along - 1)]
        from_right = [self.semaphore() for _ in range(along - 1)]

        def pass_on(turn, step):
            axes = axes_z + tuple(self.after[:turn])
            sent = []
            for way in ((-1, 1) if step else (0,)):

                def inside(way=way):
                    z = place.z + way * step
                    return (z >= 0) & (z < along) if way else None

                sent.append(self.start(
                    lambda: place.across(self.after[turn]),
                    lambda way=way: self.pairs(axes, place.z + way * step, not axes and not step),
                    width(axes), inside, self.semaphore()))
            return turn, step, sent

        def step_out(step):
            self.start(
                lambda: place.device(dz=1), lambda: self.pairs(axes_z, place.z - (step - 1), first and step == 1),
                width(axes_z), lambda: (place.z - (step - 1) >= 0) & (place.z + 1 < along), from_left[step - 1])
            self.start(
                lambda: place.device(dz=-1), lambda: self.pairs(axes_z, place.z + (step - 1), first and step == 1),
                width(axes_z), lambda: (place.z + (step - 1) < along) & (place.z > 0), from_right[step - 1])

        def step_in(step):
            for way, semaphore in ((-1, from_left), (1, from_right)):
                z = place.z + way * step
                self.arrive((
                    lambda: (z >= 0) & (z < along),
                    lambda: self.copies(place.across("k"), self.pairs(axes_z, z, False), semaphore[step - 1])))

        step_out(1)
        waiting = [pass_on(0, 0)] if self.after else []
        for step in range(1, along + len(self.after)):
            yield
            if step < along:
                step_in(step)
                if step + 1 < along:
                    step_out(step + 1)
            following = []
            for turn, at, sent in waiting:
                for one in sent:
                    self.arrive(one)
                if turn + 1 < len(self.after):
                    following.append(pass_on(turn + 1, at))
            if self.after and step < along:
                following.append(pass_on(0, step))
            waiting = following
        sent = self.start(
            lambda: place.across("k"), lambda: [(r, r) for r in [self.region(slice(None), slice(None), x) for x in range(2)]],
            2, always, self.semaphore())
        yield
        self.arrive(sent)

    def finish(self):
        for condition, make in self.started:
            when(condition(), lambda make=make: [copy.wait_send() for copy in make()] and None)


class OwnBlocks:
    def __init__(self, place, blocks, fulls, local):
        self.place, self.blocks, self.fulls, self.local = place, blocks, fulls, local

    def copies(self):
        place = self.place
        for at, (block, full) in enumerate(zip(self.blocks, self.fulls)):
            width = block.shape[-1]
            columns = pl.ds(pl.multiple_of((place.x * 2 + place.k) * width, 128), width)
            yield pltpu.make_async_copy(block, full.at[place.z, place.y, :, :, columns], self.local.at[at])

    def start(self):
        for copy in self.copies():
            copy.start()

    def wait(self):
        for copy in self.copies():
            copy.wait()


def gathers_of(place, units, blocks, fulls, send, recv):
    return [
        Gather(place, blocks[which], fulls[which], strip, order, send.at[at], recv.at[at])
        for at, (which, strip, order) in enumerate(units)
    ]


def gather_kernel(units, count, *refs):
    blocks, fulls = refs[:count], refs[count : 2 * count]
    send, recv, local = refs[2 * count :]
    place = Place()
    place.greet()
    own = OwnBlocks(place, blocks, fulls, local)
    own.start()
    gathers = gathers_of(place, units, blocks, fulls, send, recv)
    waited = False
    for unused in in_turn([gather.stages() for gather in gathers], 0.0):
        if not waited:
            own.wait()
            waited = True
    for gather in gathers:
        gather.finish()


def gather_units(blocks, least, orders):
    strips = []
    for which, block in enumerate(blocks):
        wide = min(least, block.shape[-1])
        for part in range(block.shape[0]):
            for start in range(0, block.shape[-1], wide):
                strips.append((which, (part, start, wide)))
    return [strip + (orders[at % len(orders)],) for at, strip in enumerate(strips)]


def gather_plan(blocks, least, orders):
    along, cols = lax.axis_size("row") // 2, lax.axis_size("col")
    units = gather_units(blocks, least, orders)
    fulls = [jax.ShapeDtypeStruct((along, 2) + b.shape[:2] + (cols * b.shape[2],), b.dtype) for b in blocks]
    scratch = [
        pltpu.SemaphoreType.DMA((len(units), 8 * along)),
        pltpu.SemaphoreType.DMA((len(units), 12 * along)),
        pltpu.SemaphoreType.DMA((len(blocks),)),
    ]
    return fulls, units, scratch


def gather_blocks(blocks, collective_id, least):
    fulls, units, scratch = gather_plan(blocks, least, ORDERS)
    count = len(blocks)
    anywhere = pl.BlockSpec(memory_space=pl.ANY)
    return pl.pallas_call(
        functools.partial(gather_kernel, units, count),
        out_shape=fulls,
        in_specs=[anywhere] * count,
        out_specs=[anywhere] * count,
        scratch_shapes=scratch,
        compiler_params=pltpu.CompilerParams(collective_id=collective_id, has_side_effects=True),
        cost_estimate=pl.CostEstimate(flops=0, bytes_accessed=4 * sum(f.size for f in fulls), transcendentals=0),
    )(*blocks)


def add_blocks(total, extra, leading):
    def one(at, unused):
        place = []
        for size in leading[::-1]:
            place.append(at % size)
            at = at // size
        place = tuple(place[::-1])
        total[place] = total[place] + extra[place]
        return unused

    if not leading:
        total[...] = total[...] + extra[...]
        return
    count = 1
    for size in leading:
        count *= size
    lax.fori_loop(0, count, one, 0)


class Scatter:
    def __init__(self, place, grad, out, strip, width, order, slots, send, recv, local):
        self.place, self.grad, self.out, self.strip, self.width = place, grad, out, strip, width
        self.order = order[::-1]
        self.total, self.other_core, self.halves, self.steps = slots
        self.send, self.recv, self.local = send, recv, local
        self.used, self.started = 0, []

    def region(self, x, k):
        part, start, count = self.strip
        column = (x * 2 + k) * self.width + start
        return self.grad.at[:, :, part, :, pl.ds(pl.multiple_of(column, 128), count)]

    def copy(self, device, source, target, semaphore):
        return pltpu.make_async_remote_copy(
            src_ref=source, dst_ref=target, send_sem=self.send.at[semaphore], recv_sem=self.recv.at[semaphore],
            device_id=device, device_id_type=MESH)

    def reserve(self, count):
        self.used += count
        return self.used - count

    def start(self, make, condition=lambda: None):
        when(condition(), lambda: make().start())
        self.started.append((condition, make))

    def stages(self):
        place, along = self.place, self.place.along
        rows, columns = self.total.shape[-2:]
        core = self.reserve(2)

        def own(x):
            return pltpu.make_async_copy(self.region(x, place.k), self.total.at[:, :, x], self.local.at[x])

        def swapped(x):
            return self.copy(
                place.across("k"), self.region(x, 1 - place.k), self.other_core.at[:, :, x], core + x)

        for x in range(2):
            own(x).start()
            self.start(functools.partial(swapped, x))
        yield
        for x in range(2):
            own(x).wait()
            swapped(x).wait_recv()
        add_blocks(self.total, self.other_core, (along, 2, 2))
        left = {"z": slice(None), "y": slice(None), "x": slice(None)}
        at = {"y": place.y, "x": place.x}

        def view(ref, kept=None, **places):
            return ref.at[tuple({**(left if kept is None else kept), **places}[axis] for axis in "zyx")]

        def sizes():
            return tuple(size for axis, size in zip("zyx", (along, 2, 2)) if isinstance(left[axis], slice))

        exchanges = 0
        for axis in self.order:
            if axis == "z":
                shape = tuple(2 for name in "yx" if isinstance(left[name], slice))
                inner = tuple(slice(None) if isinstance(left[name], slice) else 0 for name in "yx")

                def landing(side, step, inner=inner):
                    return self.steps.at[(side, step) + inner]

                base = self.reserve(2 * along)
                right, leftward = range(base, base + along), range(base + along, base + 2 * along)
                for step in range(along):
                    if step:
                        yield
                    for way, names, first in ((1, right, place.z), (-1, leftward, along - 1 - place.z)):
                        goal = along - 1 - step + place.z if way == 1 else step - along + 1 + place.z
                        side = 0 if way == 1 else 1
                        if step:
                            arrived = landing(side, step - 1)

                            def take(arrived=arrived, goal=goal, side=side, step=step, names=names):
                                self.copy(place.across("k"), arrived, arrived, names[step - 1]).wait_recv()
                                add_blocks(view(self.total, z=goal), arrived, shape)

                            pl.when((first >= 1) & (first <= step))(take)
                        if step < along - 1:
                            kept = dict(left)

                            def onward(way=way, step=step, kept=kept, landing=landing, side=side, names=names):
                                goal = along - 1 - step + place.z if way == 1 else step - along + 1 + place.z
                                source = view(self.total, kept, z=jnp.clip(goal, 0, along - 1))
                                return self.copy(place.device(dz=way), source, landing(side, step), names[step])

                            def reached(way=way, step=step):
                                first = place.z if way == 1 else along - 1 - place.z
                                return (first <= step) & (first < along - 1)

                            self.start(onward, reached)
                left["z"] = place.z
            else:
                landing = self.halves[exchanges]
                exchanges += 1
                inner = tuple(slice(None) if isinstance(left[name], slice) and name != axis else 0 for name in "zyx")
                semaphore, kept = self.reserve(1), dict(left)

                def swap(axis=axis, kept=kept, landing=landing, inner=inner, semaphore=semaphore):
                    source = view(self.total, kept, **{axis: 1 - at[axis]})
                    return self.copy(place.across(axis), source, landing.at[inner], semaphore)

                self.start(swap)
                yield
                swap().wait_recv()
                left[axis] = at[axis]
                add_blocks(view(self.total), landing.at[inner], sizes())
        part, start, count = self.strip
        self.out[part, :, start : start + count] = view(self.total)[...].astype(jnp.float32)

    def finish(self):
        for condition, make in self.started:
            when(condition(), lambda make=make: make().wait_send())


def scatter_slots(along, rows, columns, order):
    left = {"z": along, "y": 2, "x": 2}
    whole = (along, 2, 2, rows, columns)
    shapes = [whole, whole]
    steps = None
    for axis in order[::-1]:
        if axis == "z":
            steps = (2, along - 1, left["y"], left["x"], rows, columns)
        left[axis] = 1
        if axis != "z":
            shapes.append((left["z"], left["y"], left["x"], rows, columns))
    return shapes + [steps]


def scatters_of(place, units, grads, outs, send, recv, local, slots):
    scatters = []
    for at, (which, strip, order) in enumerate(units):
        total, other_core, first, second, steps = slots[5 * at : 5 * at + 5]
        scatters.append(
            Scatter(place, grads[which], outs[which], strip, outs[which].shape[-1], order,
                    (total, other_core, (first, second), steps), send.at[at], recv.at[at], local.at[at]))
    return scatters


def scatter_kernel(units, count, *refs):
    grads, outs = refs[:count], refs[count : 2 * count]
    place = Place()
    place.greet()
    scatters = scatters_of(place, units, grads, outs, *refs[2 * count : 2 * count + 3], refs[2 * count + 3 :])
    for unused in in_turn([scatter.stages() for scatter in scatters], 0.5):
        pass
    for scatter in scatters:
        scatter.finish()


def scatter_plan(grads, least, orders):
    along, cols = lax.axis_size("row") // 2, lax.axis_size("col")
    blocks = [jax.ShapeDtypeStruct(g.shape[2:4] + (g.shape[4] // cols,), jnp.float32) for g in grads]
    units = gather_units(blocks, least, orders)
    scratch = [pltpu.SemaphoreType.DMA((len(units), 2 * along + 4))] * 2 + [pltpu.SemaphoreType.DMA((len(units), 2))]
    for which, strip, order in units:
        shapes = scatter_slots(along, blocks[which].shape[1], strip[2], order)
        scratch += [pltpu.VMEM(shape, jnp.bfloat16) for shape in shapes]
    return blocks, units, scratch


def scatter_blocks(grads, collective_id, least):
    blocks, units, scratch = scatter_plan(grads, least, ORDERS)
    count = len(grads)
    anywhere = pl.BlockSpec(memory_space=pl.ANY)
    return pl.pallas_call(
        functools.partial(scatter_kernel, units, count),
        out_shape=blocks,
        in_specs=[anywhere] * count,
        out_specs=[pl.BlockSpec(memory_space=pltpu.VMEM)] * count,
        scratch_shapes=scratch,
        compiler_params=pltpu.CompilerParams(
            collective_id=collective_id, has_side_effects=True, vmem_limit_bytes=60 << 20),
        cost_estimate=pl.CostEstimate(
            flops=sum(g.size for g in grads), bytes_accessed=4 * sum(g.size for g in grads), transcendentals=0),
    )(*grads)


ACROSS = ("yzx", "yzx", "yzx", "yzx", "yxz")


def attend_rows(q, key_ref, value_ref, spans, diagonal, put):
    low = lax.broadcasted_iota(jnp.int32, (1, 128), 1) < HEAD_DIM
    mixed, logs = [], []
    for h in range(2):
        mine = low if h == 0 else jnp.logical_not(low)
        qh = jnp.where(mine, q, jnp.bfloat16(0))
        scores = []
        for at, length in spans:
            s = dg(qh, key_ref[at : at + length, :], NT)
            if at == diagonal:
                allowed = lax.broadcasted_iota(jnp.int32, s.shape, 0) >= lax.broadcasted_iota(jnp.int32, s.shape, 1)
                s = jnp.where(allowed, s, -1e30)
            scores.append(s)
        top = functools.reduce(jnp.maximum, [jnp.max(s, axis=1, keepdims=True) for s in scores])
        out = None
        for (at, length), s in zip(spans, scores):
            p = jnp.exp(s - top).astype(jnp.bfloat16)
            value = value_ref[at : at + length, :]
            part = dg(p, jnp.where(mine, value, jnp.ones_like(value)), NN)
            out = part if out is None else out + part
        total = out[:, HEAD_DIM : HEAD_DIM + 1] if h == 0 else out[:, 0:1]
        mixed.append(out / total)
        logs.append(top + jnp.log(total))
    put(logs)
    return jnp.where(low, mixed[0], mixed[1])


def rows_of(lanes_ref, first):
    picked = lax.broadcasted_iota(jnp.int32, (8, 128), 0) + first == lax.broadcasted_iota(jnp.int32, (8, 128), 1)
    return lax.dot_general(
        picked.astype(jnp.float32), lanes_ref[...], NT, precision=lax.Precision.HIGHEST,
        preferred_element_type=jnp.float32)


def pair_attend_kernel(tile, units, count, events, *refs):
    q_ref, k_ref, v_ref, q_any, k_any, v_any = refs[:6]
    blocks = refs[6 : 6 + count]
    mix_ref, logs_ref, fq_out, fk_out, fv_out = refs[6 + count : 11 + count]
    fulls = refs[11 + count : 11 + 2 * count]
    (near, near_logs, far_q, far_k, far_v, far, far_logs, got, far_rows, got_rows,
     send, recv, local, keep) = refs[11 + 2 * count : 25 + 2 * count]
    gather_send, gather_recv, gather_local = refs[25 + 2 * count :]
    step = pl.program_id(0)
    place = Place()
    own = OwnBlocks(place, blocks, fulls, gather_local)
    gathers = gathers_of(place, units, blocks, fulls, gather_send, gather_recv)
    turns = in_turn([gather.stages() for gather in gathers], 0.25)
    pairs = near.shape[0]
    fars = pairs // 2
    rows = q_ref.shape[0]
    first, second = place.y == 0, place.y == 1
    partner = place.across("y")
    lane = lax.broadcasted_iota(jnp.int32, (1, 128), 1)
    scale = jnp.bfloat16(HEAD_DIM**-0.5)
    plan = ((q_any, far_q, False), (k_any, far_k, True), (v_any, far_v, True))

    def columns(pair):
        return pl.ds(pl.multiple_of(pair * 128, 128), 128)

    def sending(which, j):
        array, landing, by_first = plan[which]
        return pltpu.make_async_remote_copy(
            src_ref=array.at[:, columns(j if by_first else fars + j)], dst_ref=landing.at[j],
            send_sem=send.at[which, j], recv_sem=recv.at[which, j], device_id=partner, device_id_type=MESH)

    def keeping(which, j):
        array, landing, by_first = plan[which]
        return pltpu.make_async_copy(
            array.at[:, columns(fars + j if by_first else j)], landing.at[j], local.at[which, j])

    def mixture_out(j):
        return pltpu.make_async_remote_copy(
            src_ref=far.at[j], dst_ref=got.at[j], send_sem=send.at[3, j], recv_sem=recv.at[3, j],
            device_id=partner, device_id_type=MESH)

    def logs_out():
        return pltpu.make_async_remote_copy(
            src_ref=far_rows, dst_ref=got_rows, send_sem=send.at[4, 0], recv_sem=recv.at[4, 0],
            device_id=partner, device_id_type=MESH)

    def saving(which):
        return pltpu.make_async_copy(plan[which][1], (fq_out, fk_out, fv_out)[which], keep.at[which])

    @pl.when(step == 0)
    def _():
        place.greet()
        own.start()
        near_logs[...] = jnp.zeros_like(near_logs)
        far_logs[...] = jnp.zeros_like(far_logs)
        for j in range(fars):
            for which in range(3):

                @pl.when(first if plan[which][2] else second)
                def _(which=which, j=j):
                    keeping(which, j).start()

    @pl.when((step % 3 == 0) & (step < 3 * fars))
    def _():
        j = step // 3
        for which in range(3):

            @pl.when(first if plan[which][2] else second)
            def _(which=which):
                @pl.when(j > 0)
                def _():
                    sending(which, j - 1).wait_send()

                sending(which, j).start()

    for at, number in enumerate(events):

        @pl.when(step == at)
        def _(at=at, number=number):
            if at == 0:
                own.wait()
            for unused in range(number):
                next(turns, None)

    @pl.when(step < pairs)
    def _():
        for start in range(0, rows, tile):
            n = min(tile, rows - start)

            def put(logs, start=start, n=n):
                kept = near_logs[start : start + n, :]
                for h in range(2):
                    kept = jnp.where(lane == 2 * step + h, logs[h], kept)
                near_logs[start : start + n, :] = kept

            spans = ([(0, start)] if start else []) + [(start, n)]
            near[step, start : start + n, :] = attend_rows(
                q_ref[start : start + n, :] * scale, k_ref, v_ref, spans, start, put)

    @pl.when((step >= pairs) & (step < pairs + fars))
    def _():
        j = step - pairs
        for which in range(3):
            by_first = plan[which][2]

            @pl.when(first if by_first else second)
            def _(which=which):
                keeping(which, j).wait()

            @pl.when(second if by_first else first)
            def _(which=which):
                sending(which, j).wait_recv()

        base = jnp.where(first, 2 * fars, 0)
        for start in range(0, rows, tile):
            n = min(tile, rows - start)

            def put(logs, start=start, n=n):
                kept = far_logs[start : start + n, :]
                for h in range(2):
                    kept = jnp.where(lane == base + 2 * j + h, logs[h], kept)
                far_logs[start : start + n, :] = kept

            far[j, start : start + n, :] = attend_rows(
                far_q[j, start : start + n, :] * scale, far_k.at[j], far_v.at[j], [(0, rows)], None, put
            ).astype(far.dtype)

        @pl.when(first)
        def _():
            mixture_out(j).start()

    @pl.when(step == pairs + fars)
    def _():
        for which in range(3):
            saving(which).start()

        @pl.when(first)
        def _():
            far_rows[...] = rows_of(far_logs, 2 * fars)
            logs_out().start()
            for pair in range(pairs):
                mix_ref[:, pair * 128 : (pair + 1) * 128] = near[pair].astype(mix_ref.dtype)
            logs_ref[...] = near_logs[...]
            logs_out().wait_send()
            for j in range(fars):
                mixture_out(j).wait_send()
            for which in (1, 2):
                sending(which, fars - 1).wait_send()

        @pl.when(second)
        def _():
            logs_out().wait_recv()
            for j in range(fars):
                mixture_out(j).wait_recv()
            sending(0, fars - 1).wait_send()
            spread_out = (lax.broadcasted_iota(jnp.int32, (8, 128), 0) + 2 * fars == lane).astype(jnp.float32)
            theirs = lax.dot_general(
                got_rows[...], spread_out, TN, precision=lax.Precision.HIGHEST, preferred_element_type=jnp.float32)
            logs_far = far_logs[...] + theirs
            logs_near = near_logs[...]
            top = jnp.maximum(logs_near, logs_far)
            total = top + jnp.log(jnp.exp(logs_near - top) + jnp.exp(logs_far - top))
            logs_ref[...] = total
            share = jnp.exp(logs_near - total)
            low = lane < HEAD_DIM
            for pair in range(pairs):
                part = jnp.where(low, share[:, 2 * pair : 2 * pair + 1], share[:, 2 * pair + 1 : 2 * pair + 2])
                other = (far[pair] if pair < fars else got[pair - fars]).astype(jnp.float32)
                mix_ref[:, pair * 128 : (pair + 1) * 128] = (other + (near[pair] - other) * part).astype(mix_ref.dtype)

        for which in range(3):
            saving(which).wait()
        for unused in turns:
            pass
        for gather in gathers:
            gather.finish()


def pair_attend(q, k, v, blocks, collective_id, events, tile=384):
    rows, width = q.shape
    pairs = width // 128
    fars = pairs // 2
    block = pl.BlockSpec((rows, 128), lambda i: (0, jnp.minimum(i, pairs - 1)))
    anywhere = pl.BlockSpec(memory_space=pl.ANY)
    kept = jax.ShapeDtypeStruct((fars, rows, 128), jnp.bfloat16)
    half = pltpu.VMEM((fars, rows, 128), jnp.bfloat16)
    fulls, units, scratch = gather_plan(blocks, 256, ACROSS)
    count = len(blocks)
    result = pl.pallas_call(
        functools.partial(pair_attend_kernel, tile, units, count, events),
        grid=(pairs + fars + 1,),
        in_specs=[block] * 3 + [anywhere] * (3 + count),
        out_specs=[pl.BlockSpec((rows, width), lambda i: (0, 0)), pl.BlockSpec((rows, 128), lambda i: (0, 0))] + [anywhere] * (3 + count),
        out_shape=[
            jax.ShapeDtypeStruct((rows, width), jnp.bfloat16), jax.ShapeDtypeStruct((rows, 128), jnp.float32), kept, kept, kept, *fulls],
        scratch_shapes=[
            pltpu.VMEM((pairs, rows, 128), jnp.float32), pltpu.VMEM((rows, 128), jnp.float32),
            half, half, half, half, pltpu.VMEM((rows, 128), jnp.float32), half,
            pltpu.VMEM((8, rows), jnp.float32), pltpu.VMEM((8, rows), jnp.float32),
            pltpu.SemaphoreType.DMA((5, fars)), pltpu.SemaphoreType.DMA((5, fars)),
            pltpu.SemaphoreType.DMA((3, fars)), pltpu.SemaphoreType.DMA((3,)), *scratch,
        ],
        compiler_params=pltpu.CompilerParams(
            collective_id=collective_id, has_side_effects=True, vmem_limit_bytes=48 << 20),
        cost_estimate=pl.CostEstimate(
            flops=4 * rows * rows * width, bytes_accessed=16 * rows * width, transcendentals=rows * rows * pairs * 2),
    )(q, k, v, q, k, v, *blocks)
    return result[:5], result[5:]


def back_pair(tile, causal, q_ref, k_ref, v_ref, do_ref, stats, acc, put):
    rows, keys = q_ref.shape[0], k_ref.shape[0]
    low = lax.broadcasted_iota(jnp.int32, (1, 128), 1) < HEAD_DIM
    acc[...] = jnp.zeros_like(acc)
    for start in range(0, keys, tile):
        n = min(tile, keys - start)
        k = k_ref[start : start + n, :] * jnp.bfloat16(HEAD_DIM**-0.5)
        v = v_ref[start : start + n, :]
        spans = [(0, rows)]
        if causal:
            spans = [(start, n)] + ([(start + n, rows - start - n)] if start + n < rows else [])
        dks, dvs = [], []
        for h in range(2):
            mine = low if h == 0 else jnp.logical_not(low)
            kh, vh = jnp.where(mine, k, jnp.bfloat16(0)), jnp.where(mine, v, jnp.bfloat16(0))
            dk = dv = None
            for at, length in spans:
                qs, do = q_ref[at : at + length, :], do_ref[at : at + length, :]
                p = jnp.exp(dg(kh, qs, NT) - stats[h : h + 1, at : at + length])
                if causal and at == start:
                    allowed = lax.broadcasted_iota(jnp.int32, p.shape, 0) <= lax.broadcasted_iota(jnp.int32, p.shape, 1)
                    p = jnp.where(allowed, p, 0.0)
                ds = (p * (dg(vh, do, NT) - stats[2 + h : 3 + h, at : at + length])).astype(jnp.bfloat16)
                a, b = dg(p.astype(jnp.bfloat16), do, NN), dg(ds, qs, NN)
                dv = a if dv is None else dv + a
                dk = b if dk is None else dk + b
                acc[at : at + length, :] += dg(ds, kh, TN)
            dks.append(dk)
            dvs.append(dv)
        put(start, n, jnp.where(low, dks[0], dks[1]) * HEAD_DIM**-0.5, jnp.where(low, dvs[0], dvs[1]))


def pair_stats(pair, mix_ref, do_ref, logs_ref):
    lane = lax.broadcasted_iota(jnp.int32, (8, 128), 1)
    line = lax.broadcasted_iota(jnp.int32, (8, 128), 0)
    picked = ((line < 2) & (line + 2 * pair == lane)).astype(jnp.float32)
    halves = (((line == 2) & (lane < HEAD_DIM)) | ((line == 3) & (lane >= HEAD_DIM))).astype(jnp.float32)
    products = mix_ref[...].astype(jnp.float32) * do_ref[...].astype(jnp.float32)
    logs = lax.dot_general(
        picked, logs_ref[...], NT, precision=lax.Precision.HIGHEST, preferred_element_type=jnp.float32)
    return logs + lax.dot_general(
        halves, products, NT, precision=lax.Precision.HIGHEST, preferred_element_type=jnp.float32)


def cross_back_kernel(q_ref, k_ref, v_ref, do_ref, mix_ref, logs_ref, dq_ref, dk_ref, dv_ref, acc, stats):
    stats[...] = pair_stats(pl.program_id(0), mix_ref, do_ref, logs_ref)

    def put(start, n, dk, dv):
        dk_ref[start : start + n, :] = dk.astype(dk_ref.dtype)
        dv_ref[start : start + n, :] = dv.astype(dv_ref.dtype)

    back_pair(k_ref.shape[0], False, q_ref, k_ref, v_ref, do_ref, stats, acc, put)
    dq_ref[...] = acc[...].astype(dq_ref.dtype)


def cross_back(q, k, v, do, mix, logs):
    rows, width = q.shape
    keys = k.shape[0]
    long, short = pl.BlockSpec((rows, 128), lambda i: (0, i)), pl.BlockSpec((keys, 128), lambda i: (0, i))
    return pl.pallas_call(
        cross_back_kernel,
        grid=(width // 128,),
        in_specs=[long, short, short, long, long, pl.BlockSpec((rows, 128), lambda i: (0, 0))],
        out_specs=[long, short, short],
        out_shape=[jax.ShapeDtypeStruct(a.shape, jnp.bfloat16) for a in (q, k, v)],
        scratch_shapes=[pltpu.VMEM((rows, 128), jnp.float32), pltpu.VMEM((8, rows), jnp.float32)],
        compiler_params=pltpu.CompilerParams(vmem_limit_bytes=40 << 20),
        cost_estimate=pl.CostEstimate(
            flops=10 * rows * keys * width, bytes_accessed=10 * rows * width, transcendentals=rows * keys * width // HEAD_DIM),
    )(q, k, v, do, mix, logs)


def pair_back_kernel(tile, far_tile, units, count, events, *refs):
    q_ref, k_ref, v_ref, do_ref, mix_ref, logs_ref, do_any, fq_any, fk_any, fv_any = refs[:10]
    grads, (dq_ref, dk_ref, dv_ref) = refs[10 : 10 + count], refs[10 + count : 13 + count]
    sums = refs[13 + count : 13 + 2 * count]
    (near, acc, stats, far_stats, used_stats, far_q, far_k, far_v, far_do, far_dq, far_dk, far_dv, got_q, got_k, got_v,
     send, recv, local, do_local) = refs[13 + 2 * count : 32 + 2 * count]
    scatter_refs = refs[32 + 2 * count :]
    step = pl.program_id(0)
    place = Place()
    pairs = near.shape[1]
    fars = pairs // 2
    first, second = place.y == 0, place.y == 1
    partner = place.across("y")

    def columns(pair):
        return pl.ds(pl.multiple_of(pair * 128, 128), 128)

    def remote(source, target, which, j):
        return pltpu.make_async_remote_copy(
            src_ref=source, dst_ref=target, send_sem=send.at[which, j], recv_sem=recv.at[which, j],
            device_id=partner, device_id_type=MESH)

    def grad_over(j):
        return remote(do_any.at[:, columns(fars + j)], far_do.at[j], 0, j)

    def grad_kept(j):
        return pltpu.make_async_copy(do_any.at[:, columns(j)], far_do.at[j], do_local.at[j])

    def stats_over():
        return remote(stats.at[pl.ds(fars, fars)], far_stats, 4, 0)

    def back_over(which, j):
        source, target = ((far_dq, got_q), (far_dk, got_k), (far_dv, got_v))[which]
        return remote(source.at[j], target.at[j], 1 + which, j)

    def far_in(which):
        source, target = ((fq_any, far_q), (fk_any, far_k), (fv_any, far_v))[which]
        return pltpu.make_async_copy(source, target, local.at[which])

    scatters = scatters_of(place, units, grads, sums, *scatter_refs[:3], scatter_refs[3:])
    turns = in_turn([scatter.stages() for scatter in scatters], 0.5)

    @pl.when(step == 0)
    def _():
        place.greet()
        for which in range(3):
            far_in(which).start()
        for j in range(fars):

            @pl.when(second)
            def _(j=j):
                grad_over(j).start()

            @pl.when(second)
            def _(j=j):
                grad_kept(j).start()

    for at, number in enumerate(events):

        @pl.when(step == at)
        def _(number=number):
            for unused in range(number):
                next(turns, None)

    @pl.when((step == fars) & second)
    def _():
        stats_over().start()

    @pl.when(step < pairs)
    def _():
        pair = lax.rem(step + fars, pairs)
        stats[pair] = pair_stats(pair, mix_ref, do_ref, logs_ref)

        def put(start, n, dk, dv):
            near[1, pair, start : start + n, :] = dk
            near[2, pair, start : start + n, :] = dv

        back_pair(tile, True, q_ref, k_ref, v_ref, do_ref, stats.at[pair], acc, put)
        near[0, pair] = acc[...]

    @pl.when((step >= pairs) & (step < pairs + fars))
    def _():
        j = step - pairs

        @pl.when(j == 0)
        def _():
            for which in range(3):
                far_in(which).wait()

            @pl.when(first)
            def _():
                stats_over().wait_recv()

        @pl.when(first)
        def _():
            grad_over(j).wait_recv()
            used_stats[...] = far_stats[j]

        @pl.when(second)
        def _():
            grad_kept(j).wait()
            used_stats[...] = stats[j]

        def put(start, n, dk, dv):
            far_dk[j, start : start + n, :] = dk.astype(far_dk.dtype)
            far_dv[j, start : start + n, :] = dv.astype(far_dv.dtype)

        back_pair(far_tile, False, far_q.at[j], far_k.at[j], far_v.at[j], far_do.at[j], used_stats, acc, put)
        far_dq[j] = acc[...].astype(far_dq.dtype)

        @pl.when(first)
        def _():
            back_over(0, j).start()

        @pl.when(second)
        def _():
            back_over(1, j).start()
            back_over(2, j).start()

    @pl.when(step >= pairs + fars)
    def _():
        pair = step - pairs - fars
        lower = pair < fars
        j = lax.rem(pair, fars)

        def write(ref, which, other):
            total = near[which, pair]
            if other is not None:
                total = total + other[j].astype(jnp.float32)
            ref[...] = total.astype(ref.dtype)

        @pl.when(first & lower)
        def _():
            for which in (1, 2):
                back_over(which, j).wait_recv()
            write(dq_ref, 0, None)
            write(dk_ref, 1, got_k)
            write(dv_ref, 2, got_v)

        @pl.when(first & jnp.logical_not(lower))
        def _():
            write(dq_ref, 0, None)
            write(dk_ref, 1, far_dk)
            write(dv_ref, 2, far_dv)

        @pl.when(second & lower)
        def _():
            write(dq_ref, 0, far_dq)
            write(dk_ref, 1, None)
            write(dv_ref, 2, None)

        @pl.when(second & jnp.logical_not(lower))
        def _():
            back_over(0, j).wait_recv()
            write(dq_ref, 0, got_q)
            write(dk_ref, 1, None)
            write(dv_ref, 2, None)

    @pl.when(step == 2 * pairs + fars - 1)
    def _():
        for unused in turns:
            pass
        for scatter in scatters:
            scatter.finish()

        @pl.when(first)
        def _():
            for j in range(fars):
                back_over(0, j).wait_send()

        @pl.when(second)
        def _():
            stats_over().wait_send()
            for j in range(fars):
                grad_over(j).wait_send()
                for which in (1, 2):
                    back_over(which, j).wait_send()


def pair_back(q, k, v, do, mix, logs, far, grads, collective_id, events, tile=384, far_tile=256):
    rows, width = q.shape
    pairs = width // 128
    fars = pairs // 2
    blocks, units, scratch = scatter_plan(grads, 256, ORDERS)
    count = len(grads)
    block = pl.BlockSpec((rows, 128), lambda i: (0, lax.rem(jnp.minimum(i, pairs - 1) + fars, pairs)))
    joined = pl.BlockSpec((rows, 128), lambda i: (0, jnp.maximum(i - pairs - fars, 0)))
    anywhere = pl.BlockSpec(memory_space=pl.ANY)
    half = pltpu.VMEM((fars, rows, 128), jnp.bfloat16)
    out = jax.ShapeDtypeStruct((rows, width), jnp.bfloat16)
    result = pl.pallas_call(
        functools.partial(pair_back_kernel, tile, far_tile, units, count, events),
        grid=(2 * pairs + fars,),
        in_specs=[block] * 5 + [pl.BlockSpec((rows, 128), lambda i: (0, 0))] + [anywhere] * (4 + count),
        out_specs=[joined] * 3 + [pl.BlockSpec(memory_space=pltpu.VMEM)] * count,
        out_shape=[out] * 3 + blocks,
        scratch_shapes=[
            pltpu.VMEM((3, pairs, rows, 128), jnp.float32), pltpu.VMEM((rows, 128), jnp.float32),
            pltpu.VMEM((pairs, 8, rows), jnp.float32), pltpu.VMEM((fars, 8, rows), jnp.float32),
            pltpu.VMEM((8, rows), jnp.float32), *[half] * 10,
            pltpu.SemaphoreType.DMA((5, fars)), pltpu.SemaphoreType.DMA((5, fars)),
            pltpu.SemaphoreType.DMA((3,)), pltpu.SemaphoreType.DMA((fars,)), *scratch,
        ],
        compiler_params=pltpu.CompilerParams(
            collective_id=collective_id, has_side_effects=True, vmem_limit_bytes=62 << 20),
        cost_estimate=pl.CostEstimate(
            flops=10 * rows * rows * width, bytes_accessed=16 * rows * width, transcendentals=rows * rows * pairs * 2),
    )(q, k, v, do, mix, logs, do, *far, *grads)
    return result[:3], result[3:]


def fast(
    frames_in, text_states, self_query, self_key, self_value, self_output, cross_query, cross_key, cross_value, cross_output,
    up_weight, down_weight, first_gain, first_bias, second_gain, second_bias, third_gain, third_bias, cotangent,
):
    row = lax.axis_index("row")
    rows, width = frames_in.shape
    half = width // 2
    piece = first_gain.shape[0]
    block_rows, block_cols = self_query.shape
    back = row % 2
    pairs = lax.axis_size("row") // 2
    forth_perm = [(2 * i, 2 * i + 1) for i in range(pairs)]
    back_perm = [(2 * i + 1, 2 * i) for i in range(pairs)]
    swap = forth_perm + back_perm

    def forth(array):
        return lax.ppermute(array, "row", forth_perm)

    def home(array):
        return lax.ppermute(array, "row", back_perm)

    def by_side(first, second):
        return jnp.where(back == 0, first, second)

    gains = jnp.zeros((1, 16, 128), jnp.bfloat16)
    gains = gains.at[0, :6, :piece].set(
        jnp.stack([first_gain, first_bias, second_gain, second_bias, third_gain, third_bias])
    )

    everyone = ("row", "col")
    places = (lax.axis_size("row"), lax.axis_size("col"))
    up_blocks = lax.all_gather(up_weight, everyone).reshape(*places, *up_weight.shape)
    down_blocks = lax.all_gather(down_weight, everyone).reshape(*places, *down_weight.shape)

    def small(block):
        return block.reshape(1, block_rows, block_cols)

    def flat(array):
        return array.reshape(-1, array.shape[-1])

    early = gather_blocks(
        [small(self_query), small(self_key), small(self_value), gains], 1, 128)
    query_self, key_self, value_self = [flat(w) for w in early[:3]]
    norm_params = early[3].reshape(pairs * 2, 16, -1, 128)[:, :6, :, :piece].transpose(1, 0, 2, 3)
    norm_params = norm_params.reshape(6, width).astype(jnp.float32)

    frames = frames_in.astype(jnp.float32)
    hidden_one = norm_forward(frames, norm_params[0], norm_params[1]).astype(jnp.bfloat16)
    self_k = matmul(hidden_one, key_self).astype(jnp.bfloat16)
    self_v = matmul(hidden_one, value_self).astype(jnp.bfloat16)
    self_q = matmul(hidden_one, query_self).astype(jnp.bfloat16)
    (self_mix, log_lanes, far_q, far_k, far_v), late = pair_attend(
        self_q, self_k, self_v, [small(w) for w in (self_output, cross_query, cross_key, cross_value, cross_output)],
        5, [3] * 12)
    out_self, query_cross, key_cross, value_cross, out_cross = [flat(w) for w in late]
    resid_one = frames + matmul(self_mix, out_self)
    hidden_two = norm_forward(resid_one, norm_params[2], norm_params[3]).astype(jnp.bfloat16)
    cross_q = matmul(hidden_two, query_cross).astype(jnp.bfloat16)
    other_text = lax.ppermute(text_states, "row", swap)
    clip_text = by_side(
        jnp.concatenate([text_states, other_text]), jnp.concatenate([other_text, text_states])
    )
    text_k = matmul(clip_text, key_cross).astype(jnp.bfloat16)
    text_v = matmul(clip_text, value_cross).astype(jnp.bfloat16)
    cross_mix, cross_logs = attend(cross_q, text_k, text_v, False, jnp.bfloat16)
    resid_two = resid_one + matmul(cross_mix, out_cross)
    hidden_three = norm_forward(resid_two, norm_params[4], norm_params[5]).astype(jnp.bfloat16)
    layer_out, grad_three, up_grad, down_grad = feed(hidden_three, cotangent, resid_two, up_blocks, down_blocks)
    up_sum = lax.psum_scatter(up_grad.reshape(-1, *up_weight.shape), everyone, scatter_dimension=0).astype(jnp.float32)

    cotan_full = cotangent.astype(jnp.float32)
    unused_three, pull_three = jax.vjp(norm_forward, resid_two, norm_params[4], norm_params[5])
    through_three, third_gain_part, third_bias_part = pull_three(grad_three)
    grad_resid_two = cotan_full + through_three
    grad_cross = grad_resid_two.astype(jnp.bfloat16)
    cross_out_grad = over_tokens(cross_mix, grad_cross)
    grad_cross_mix = by_transposed(grad_cross, out_cross).astype(jnp.bfloat16)
    grad_cross_q, text_k_part, text_v_part = cross_back(cross_q, text_k, text_v, grad_cross_mix, cross_mix, cross_logs)
    text_rows = text_states.shape[0]
    text_parts = jnp.concatenate([text_k_part, text_v_part], axis=1)
    given = lax.ppermute(by_side(text_parts[text_rows:], text_parts[:text_rows]), "row", swap)
    kept = by_side(text_parts[:text_rows], text_parts[text_rows:])
    text_parts = (kept.astype(jnp.float32) + given.astype(jnp.float32)).astype(jnp.bfloat16)
    grad_text_k, grad_text_v = text_parts[:, :width], text_parts[:, width:]
    cross_query_part = over_tokens(hidden_two, grad_cross_q)
    cross_key_part = over_tokens(text_states, grad_text_k)
    cross_value_part = over_tokens(text_states, grad_text_v)
    text_grad = by_transposed(grad_text_k, key_cross) + by_transposed(grad_text_v, value_cross)
    grad_two = by_transposed(grad_cross_q, query_cross)
    unused_two, pull_two = jax.vjp(norm_forward, resid_one, norm_params[2], norm_params[3])
    through_two, second_gain_part, second_bias_part = pull_two(grad_two)
    grad_resid_one = grad_resid_two + through_two
    grad_self = grad_resid_one.astype(jnp.bfloat16)
    self_out_grad = over_tokens(self_mix, grad_self)
    grad_self_mix = by_transposed(grad_self, out_self).astype(jnp.bfloat16)

    def by_place(grad, parts):
        return grad.astype(jnp.bfloat16).reshape(pairs, 2, parts, -1, grad.shape[-1])

    (grad_self_q, grad_self_k, grad_self_v), early_sums = pair_back(
        self_q, self_k, self_v, grad_self_mix, self_mix, log_lanes, (far_q, far_k, far_v),
        [by_place(g, 1) for g in (self_out_grad, cross_query_part, cross_key_part, cross_value_part, cross_out_grad)]
        + [by_place(down_grad, down_weight.shape[0] // block_rows)], 4, [5] * 12)
    self_query_part = over_tokens(hidden_one, grad_self_q)
    self_key_part = over_tokens(hidden_one, grad_self_k)
    self_value_part = over_tokens(hidden_one, grad_self_v)
    grad_one = (
        by_transposed(grad_self_q, query_self)
        + by_transposed(grad_self_k, key_self)
        + by_transposed(grad_self_v, value_self)
    )
    unused_one, pull_one = jax.vjp(norm_forward, frames, norm_params[0], norm_params[1])
    through_one, first_gain_part, first_bias_part = pull_one(grad_one)
    input_grad = grad_resid_one + through_one
    norm_grads = jnp.stack(
        [first_gain_part, first_bias_part, second_gain_part, second_bias_part, third_gain_part, third_bias_part]
    )
    norm_grads = norm_grads.reshape(6, 2 * pairs, -1, piece).transpose(1, 0, 2, 3)
    norm_grads = jnp.pad(norm_grads, ((0, 0), (0, 10), (0, 0), (0, 128 - piece)))

    late_sums = scatter_blocks(
        [by_place(g, 1) for g in (self_query_part, self_key_part, self_value_part)]
        + [by_place(norm_grads.reshape(2 * pairs * 16, -1), 1)], 3, 128)
    norm_parts = late_sums[3][0, :6, :piece]
    sums = [*late_sums[:3], *early_sums]
    sums = [total.reshape(-1, total.shape[-1]) for total in sums]
    return (layer_out, input_grad, text_grad, *sums[:-1], up_sum, sums[-1], *norm_parts)


def local(*arrays):
    frames_in, self_query = arrays[0], arrays[2]
    halves = 2 * frames_in.shape[0] == FRAMES and lax.axis_size("row") % 2 == 0
    if halves and lax.axis_size("col") % 2 == 0 and self_query.shape[1] % 256 == 0 and self_query.shape[0] % 128 == 0:
        return fast(*arrays)
    return general(*arrays)


def solution(mesh):
    placed = (
        P(("col", "row"), None),
        P(("col", "row"), None),
        P("row", "col"),
        P("row", "col"),
        P("row", "col"),
        P("row", "col"),
        P("row", "col"),
        P("row", "col"),
        P("row", "col"),
        P("row", "col"),
        P("row", "col"),
        P("row", "col"),
        P(("row", "col")),
        P(("row", "col")),
        P(("row", "col")),
        P(("row", "col")),
        P(("row", "col")),
        P(("row", "col")),
        P(("col", "row"), None),
    )
    return jax.shard_map(
        local,
        mesh=mesh,
        in_specs=placed,
        out_specs=(
            P(("col", "row"), None),
            P(("col", "row"), None),
            P(("col", "row"), None),
            P("row", "col"),
            P("row", "col"),
            P("row", "col"),
            P("row", "col"),
            P("row", "col"),
            P("row", "col"),
            P("row", "col"),
            P("row", "col"),
            P("row", "col"),
            P("row", "col"),
            P(("row", "col")),
            P(("row", "col")),
            P(("row", "col")),
            P(("row", "col")),
            P(("row", "col")),
            P(("row", "col")),
        ),
        check_vma=False,
    )
```

```python
import functools
from functools import partial

import jax
import jax.numpy as jnp
from jax import lax
from jax.experimental import pallas as pl
from jax.experimental.pallas import tpu as pltpu
from jax.sharding import PartitionSpec as P

HEADS = 16
HEAD_DIM = 64
FRAMES = 1500
TEXT = 64


def norm_forward(values, norm_gain, norm_bias):
    center = values - jnp.mean(values, axis=-1, keepdims=True)
    variance = jnp.mean(center * center, axis=-1, keepdims=True)
    return center * lax.rsqrt(variance + 1e-05) * norm_gain + norm_bias


def matmul(left, right):
    return jnp.dot(left, right, preferred_element_type=jnp.float32)


def by_transposed(left, right):
    return lax.dot_general(
        left, right, (((1,), (1,)), ((), ())), preferred_element_type=jnp.float32
    )


def over_tokens(left, right):
    return lax.dot_general(
        left, right, (((0,), (0,)), ((), ())), preferred_element_type=jnp.float32
    )


def collect(blocks):
    partly = (
        lax.all_gather(blocks[0], "col", axis=1, tiled=True),
        lax.all_gather(blocks[1], "col", axis=1, tiled=True),
        lax.all_gather(blocks[2], "col", axis=1, tiled=True),
        lax.all_gather(blocks[3], "col", axis=1, tiled=True),
        lax.all_gather(blocks[4], "col", axis=1, tiled=True),
        lax.all_gather(blocks[5], "col", axis=1, tiled=True),
        lax.all_gather(blocks[6], "col", axis=1, tiled=True),
        lax.all_gather(blocks[7], "col", axis=1, tiled=True),
        lax.all_gather(blocks[8], "col", axis=1, tiled=True),
        lax.all_gather(blocks[9], "col", axis=1, tiled=True),
        lax.all_gather(blocks[10], "col", axis=1, tiled=True),
    )
    return (
        lax.all_gather(partly[0], "row", axis=0, tiled=True),
        lax.all_gather(partly[1], "row", axis=0, tiled=True),
        lax.all_gather(partly[2], "row", axis=0, tiled=True),
        lax.all_gather(partly[3], "row", axis=0, tiled=True),
        lax.all_gather(partly[4], "row", axis=0, tiled=True),
        lax.all_gather(partly[5], "row", axis=0, tiled=True),
        lax.all_gather(partly[6], "row", axis=0, tiled=True),
        lax.all_gather(partly[7], "row", axis=0, tiled=True),
        lax.all_gather(partly[8], "row", axis=0, tiled=True),
        lax.all_gather(partly[9], "row", axis=0, tiled=True),
        lax.all_gather(partly[10], "row", axis=0, tiled=True),
    )


def spread(grads):
    partly = (
        lax.psum_scatter(
            grads[0].astype(jnp.bfloat16), "row", scatter_dimension=0, tiled=True
        ).astype(jnp.float32),
        lax.psum_scatter(
            grads[1].astype(jnp.bfloat16), "row", scatter_dimension=0, tiled=True
        ).astype(jnp.float32),
        lax.psum_scatter(
            grads[2].astype(jnp.bfloat16), "row", scatter_dimension=0, tiled=True
        ).astype(jnp.float32),
        lax.psum_scatter(
            grads[3].astype(jnp.bfloat16), "row", scatter_dimension=0, tiled=True
        ).astype(jnp.float32),
        lax.psum_scatter(
            grads[4].astype(jnp.bfloat16), "row", scatter_dimension=0, tiled=True
        ).astype(jnp.float32),
        lax.psum_scatter(
            grads[5].astype(jnp.bfloat16), "row", scatter_dimension=0, tiled=True
        ).astype(jnp.float32),
        lax.psum_scatter(
            grads[6].astype(jnp.bfloat16), "row", scatter_dimension=0, tiled=True
        ).astype(jnp.float32),
        lax.psum_scatter(
            grads[7].astype(jnp.bfloat16), "row", scatter_dimension=0, tiled=True
        ).astype(jnp.float32),
        lax.psum_scatter(
            grads[8].astype(jnp.bfloat16), "row", scatter_dimension=0, tiled=True
        ).astype(jnp.float32),
        lax.psum_scatter(
            grads[9].astype(jnp.bfloat16), "row", scatter_dimension=0, tiled=True
        ).astype(jnp.float32),
        lax.psum_scatter(
            grads[10].astype(jnp.bfloat16), "row", scatter_dimension=0, tiled=True
        ).astype(jnp.float32),
    )
    return (
        lax.psum_scatter(
            partly[0].astype(jnp.bfloat16), "col", scatter_dimension=1, tiled=True
        ).astype(jnp.float32),
        lax.psum_scatter(
            partly[1].astype(jnp.bfloat16), "col", scatter_dimension=1, tiled=True
        ).astype(jnp.float32),
        lax.psum_scatter(
            partly[2].astype(jnp.bfloat16), "col", scatter_dimension=1, tiled=True
        ).astype(jnp.float32),
        lax.psum_scatter(
            partly[3].astype(jnp.bfloat16), "col", scatter_dimension=1, tiled=True
        ).astype(jnp.float32),
        lax.psum_scatter(
            partly[4].astype(jnp.bfloat16), "col", scatter_dimension=1, tiled=True
        ).astype(jnp.float32),
        lax.psum_scatter(
            partly[5].astype(jnp.bfloat16), "col", scatter_dimension=1, tiled=True
        ).astype(jnp.float32),
        lax.psum_scatter(
            partly[6].astype(jnp.bfloat16), "col", scatter_dimension=1, tiled=True
        ).astype(jnp.float32),
        lax.psum_scatter(
            partly[7].astype(jnp.bfloat16), "col", scatter_dimension=1, tiled=True
        ).astype(jnp.float32),
        lax.psum_scatter(
            partly[8].astype(jnp.bfloat16), "col", scatter_dimension=1, tiled=True
        ).astype(jnp.float32),
        lax.psum_scatter(
            partly[9].astype(jnp.bfloat16), "col", scatter_dimension=1, tiled=True
        ).astype(jnp.float32),
        lax.psum_scatter(
            partly[10].astype(jnp.bfloat16), "col", scatter_dimension=1, tiled=True
        ).astype(jnp.float32),
    )


def heads_layout(stacked):
    return lax.all_to_all(stacked, "row", split_axis=1, concat_axis=0, tiled=True)


def tokens_layout(stacked):
    return lax.all_to_all(stacked, "row", split_axis=0, concat_axis=2, tiled=True)


def by_clips(arranged, start, count, length, heads_dev):
    section = arranged[:, start : start + count]
    return section.reshape(-1, length, heads_dev, HEAD_DIM)


def causal_scores(query_clip, key_clip, causal):
    scores = jnp.einsum(
        "qhd,khd->hqk", query_clip, key_clip, preferred_element_type=jnp.float32
    ) * HEAD_DIM ** (-0.5)
    if causal:
        allowed = jnp.arange(scores.shape[1])[:, None] >= jnp.arange(scores.shape[2])[None, :]
        scores = jnp.where(allowed, scores, -1e30)
    return scores


def attend_forward(query_clips, key_clips, value_clips, causal):

    def one_clip(operands):
        query_clip, key_clip, value_clip = operands
        scores = causal_scores(query_clip, key_clip, causal)
        highest = jnp.max(scores, axis=-1, keepdims=True)
        powers = jnp.exp(scores - highest)
        totals = jnp.sum(powers, axis=-1, keepdims=True)
        weights_low = (powers / totals).astype(jnp.bfloat16)
        mixture = jnp.einsum(
            "hqk,khd->qhd", weights_low, value_clip, preferred_element_type=jnp.float32
        )
        return (mixture.astype(jnp.bfloat16), (highest + jnp.log(totals))[..., 0])

    return lax.map(one_clip, (query_clips, key_clips, value_clips))


def attend_backward(query_clips, key_clips, value_clips, log_sums, grad_clips, causal):

    def one_clip(operands):
        query_clip, key_clip, value_clip, log_clip, grad_clip = operands
        scores = causal_scores(query_clip, key_clip, causal)
        probs_full = jnp.exp(scores - log_clip[..., None])
        grad_probs = jnp.einsum(
            "qhd,khd->hqk", grad_clip, value_clip, preferred_element_type=jnp.float32
        )
        grad_value = jnp.einsum(
            "hqk,qhd->khd",
            probs_full.astype(jnp.bfloat16),
            grad_clip,
            preferred_element_type=jnp.float32,
        )
        centered = grad_probs - jnp.sum(probs_full * grad_probs, axis=-1, keepdims=True)
        grad_scores = (probs_full * centered).astype(jnp.bfloat16)
        grad_query = jnp.einsum(
            "hqk,khd->qhd", grad_scores, key_clip, preferred_element_type=jnp.float32
        ) * HEAD_DIM ** (-0.5)
        grad_key = jnp.einsum(
            "hqk,qhd->khd", grad_scores, query_clip, preferred_element_type=jnp.float32
        ) * HEAD_DIM ** (-0.5)
        return (
            grad_query.astype(jnp.bfloat16),
            grad_key.astype(jnp.bfloat16),
            grad_value.astype(jnp.bfloat16),
        )

    return lax.map(one_clip, (query_clips, key_clips, value_clips, log_sums, grad_clips))


def general(
    frames_in,
    text_states,
    self_query,
    self_key,
    self_value,
    self_output,
    cross_query,
    cross_key,
    cross_value,
    cross_output,
    up_weight,
    down_weight,
    first_gain,
    first_bias,
    second_gain,
    second_bias,
    third_gain,
    third_bias,
    cotangent,
):
    row_count = lax.axis_size("row")
    col_count = lax.axis_size("col")
    heads_dev = HEADS // row_count
    width_dev = heads_dev * HEAD_DIM
    tok_rows = frames_in.shape[0]
    text_rows = text_states.shape[0]
    piece_len = first_gain.shape[0]
    gain_block = jnp.stack(
        [first_gain, first_bias, second_gain, second_bias, third_gain, third_bias]
    ).reshape(1, 6 * piece_len)
    param_blocks = (
        self_query,
        self_key,
        self_value,
        self_output,
        cross_query,
        cross_key,
        cross_value,
        cross_output,
        up_weight,
        down_weight,
        gain_block,
    )

    def unpack_gains(gathered_gains):
        arranged = gathered_gains.reshape(row_count, col_count, 6, piece_len).transpose(2, 0, 1, 3)
        return arranged.reshape(6, row_count * col_count * piece_len).astype(jnp.float32)

    gathered = collect(param_blocks)
    (
        query_self,
        key_self,
        value_self,
        out_self,
        query_cross,
        key_cross,
        value_cross,
        out_cross,
        up_full,
        down_full,
    ) = gathered[:10]
    norm_params = unpack_gains(gathered[10])
    frames = frames_in.astype(jnp.float32)
    hidden_one = norm_forward(frames, norm_params[0], norm_params[1]).astype(jnp.bfloat16)
    self_q = matmul(hidden_one, query_self).astype(jnp.bfloat16)
    self_k = matmul(hidden_one, key_self).astype(jnp.bfloat16)
    self_v = matmul(hidden_one, value_self).astype(jnp.bfloat16)
    text_k = matmul(text_states, key_cross).astype(jnp.bfloat16)
    text_v = matmul(text_states, value_cross).astype(jnp.bfloat16)
    sent_rows = 3 * tok_rows + 2 * text_rows
    arranged = heads_layout(jnp.concatenate([self_q, self_k, self_v, text_k, text_v], axis=0))
    arranged = arranged.reshape(row_count, sent_rows, width_dev)
    query_clips = by_clips(arranged, 0, tok_rows, FRAMES, heads_dev)
    key_clips = by_clips(arranged, tok_rows, tok_rows, FRAMES, heads_dev)
    value_clips = by_clips(arranged, 2 * tok_rows, tok_rows, FRAMES, heads_dev)
    text_keys = by_clips(arranged, 3 * tok_rows, text_rows, TEXT, heads_dev)
    text_values = by_clips(arranged, 3 * tok_rows + text_rows, text_rows, TEXT, heads_dev)
    self_clips, self_logs = attend_forward(query_clips, key_clips, value_clips, True)
    self_mix = tokens_layout(self_clips.reshape(row_count, tok_rows, width_dev))[0]
    resid_one = frames + matmul(self_mix, out_self)
    hidden_two = norm_forward(resid_one, norm_params[2], norm_params[3]).astype(jnp.bfloat16)
    cross_q = matmul(hidden_two, query_cross).astype(jnp.bfloat16)
    cross_arranged = heads_layout(cross_q).reshape(row_count, tok_rows, width_dev)
    cross_queries = by_clips(cross_arranged, 0, tok_rows, FRAMES, heads_dev)
    cross_clips, cross_logs = attend_forward(cross_queries, text_keys, text_values, False)
    cross_mix = tokens_layout(cross_clips.reshape(row_count, tok_rows, width_dev))[0]
    resid_two = resid_one + matmul(cross_mix, out_cross)
    hidden_three = norm_forward(resid_two, norm_params[4], norm_params[5]).astype(jnp.bfloat16)
    pre_act = matmul(hidden_three, up_full)
    inner = jax.nn.gelu(pre_act, approximate=False).astype(jnp.bfloat16)
    layer_out = (resid_two + matmul(inner, down_full)).astype(jnp.bfloat16)
    gathered = collect(param_blocks)
    (
        query_self,
        key_self,
        value_self,
        out_self,
        query_cross,
        key_cross,
        value_cross,
        out_cross,
        up_full,
        down_full,
    ) = gathered[:10]
    norm_params = unpack_gains(gathered[10])
    cotan_full = cotangent.astype(jnp.float32)
    down_grad = over_tokens(inner, cotangent)
    grad_inner = by_transposed(cotangent, down_full)
    unused_gelu, gelu_pull = jax.vjp(partial(jax.nn.gelu, approximate=False), pre_act)
    grad_pre = gelu_pull(grad_inner)[0].astype(jnp.bfloat16)
    up_grad = over_tokens(hidden_three, grad_pre)
    grad_three = by_transposed(grad_pre, up_full)
    unused_three, pull_three = jax.vjp(norm_forward, resid_two, norm_params[4], norm_params[5])
    through_three, third_gain_part, third_bias_part = pull_three(grad_three)
    grad_resid_two = cotan_full + through_three
    grad_cross = grad_resid_two.astype(jnp.bfloat16)
    cross_out_grad = over_tokens(cross_mix, grad_cross)
    grad_cross_mix = by_transposed(grad_cross, out_cross).astype(jnp.bfloat16)
    grad_cross_arr = heads_layout(grad_cross_mix).reshape(row_count, tok_rows, width_dev)
    grad_cross_clips = by_clips(grad_cross_arr, 0, tok_rows, FRAMES, heads_dev)
    cq_clips, tk_clips, tv_clips = attend_backward(
        cross_queries, text_keys, text_values, cross_logs, grad_cross_clips, False
    )
    back_cross = jnp.concatenate(
        [
            cq_clips.reshape(row_count, tok_rows, width_dev),
            tk_clips.reshape(row_count, text_rows, width_dev),
            tv_clips.reshape(row_count, text_rows, width_dev),
        ],
        axis=1,
    )
    back_cross = tokens_layout(back_cross)[0]
    grad_cross_q = back_cross[:tok_rows]
    grad_text_k = back_cross[tok_rows : tok_rows + text_rows]
    grad_text_v = back_cross[tok_rows + text_rows :]
    cross_query_part = over_tokens(hidden_two, grad_cross_q)
    cross_key_part = over_tokens(text_states, grad_text_k)
    cross_value_part = over_tokens(text_states, grad_text_v)
    text_grad = by_transposed(grad_text_k, key_cross) + by_transposed(grad_text_v, value_cross)
    grad_two = by_transposed(grad_cross_q, query_cross)
    unused_two, pull_two = jax.vjp(norm_forward, resid_one, norm_params[2], norm_params[3])
    through_two, second_gain_part, second_bias_part = pull_two(grad_two)
    grad_resid_one = grad_resid_two + through_two
    grad_self = grad_resid_one.astype(jnp.bfloat16)
    self_out_grad = over_tokens(self_mix, grad_self)
    grad_self_mix = by_transposed(grad_self, out_self).astype(jnp.bfloat16)
    grad_self_arr = heads_layout(grad_self_mix).reshape(row_count, tok_rows, width_dev)
    grad_self_clips = by_clips(grad_self_arr, 0, tok_rows, FRAMES, heads_dev)
    sq_clips, sk_clips, sv_clips = attend_backward(
        query_clips, key_clips, value_clips, self_logs, grad_self_clips, True
    )
    back_self = jnp.concatenate(
        [
            sq_clips.reshape(row_count, tok_rows, width_dev),
            sk_clips.reshape(row_count, tok_rows, width_dev),
            sv_clips.reshape(row_count, tok_rows, width_dev),
        ],
        axis=1,
    )
    back_self = tokens_layout(back_self)[0]
    grad_self_q = back_self[:tok_rows]
    grad_self_k = back_self[tok_rows : 2 * tok_rows]
    grad_self_v = back_self[2 * tok_rows :]
    self_query_part = over_tokens(hidden_one, grad_self_q)
    self_key_part = over_tokens(hidden_one, grad_self_k)
    self_value_part = over_tokens(hidden_one, grad_self_v)
    grad_one = (
        by_transposed(grad_self_q, query_self)
        + by_transposed(grad_self_k, key_self)
        + by_transposed(grad_self_v, value_self)
    )
    unused_one, pull_one = jax.vjp(norm_forward, frames, norm_params[0], norm_params[1])
    through_one, first_gain_part, first_bias_part = pull_one(grad_one)
    input_grad = grad_resid_one + through_one
    norm_grads = jnp.stack(
        [
            first_gain_part,
            first_bias_part,
            second_gain_part,
            second_bias_part,
            third_gain_part,
            third_bias_part,
        ]
    )
    norm_grads = norm_grads.reshape(6, row_count, col_count, piece_len).transpose(1, 2, 0, 3)
    norm_grads = norm_grads.reshape(row_count, col_count * 6 * piece_len)
    summed = spread(
        (
            self_query_part,
            self_key_part,
            self_value_part,
            self_out_grad,
            cross_query_part,
            cross_key_part,
            cross_value_part,
            cross_out_grad,
            up_grad,
            down_grad,
            norm_grads,
        )
    )
    norm_parts = summed[10].reshape(6, piece_len)
    return (
        layer_out,
        input_grad,
        text_grad,
        summed[0],
        summed[1],
        summed[2],
        summed[3],
        summed[4],
        summed[5],
        summed[6],
        summed[7],
        summed[8],
        summed[9],
        norm_parts[0],
        norm_parts[1],
        norm_parts[2],
        norm_parts[3],
        norm_parts[4],
        norm_parts[5],
    )


NT=(((1,),(1,)),((),())); NN=(((1,),(0,)),((),())); TN=(((0,),(0,)),((),()))
def dg(a,b,dims): return lax.dot_general(a,b,dims,preferred_element_type=jnp.float32)

def feed_kernel(h_ref,cot_ref,res_ref,up_ref,down_ref,out_ref,g_ref,dup_ref,ddown_ref,acc):
    i=pl.program_id(0)
    @pl.when(i==0)
    def _():
        acc[...]=res_ref[...]
        g_ref[...]=jnp.zeros_like(g_ref)
    h=h_ref[...]
    up=up_ref[:,0].reshape(h.shape[1],-1)
    blocks,wide=down_ref.shape[1],down_ref.shape[3]
    pre=dg(h,up,NN)
    cdf=0.5*(1.0+lax.erf(pre*0.7071067811865476))
    inner=(pre*cdf).astype(jnp.bfloat16)
    slope=cdf+pre*(jnp.exp(-0.5*pre*pre)*0.3989422804014327)
    grad=None
    for at in range(blocks):
        columns=slice(at*wide,(at+1)*wide)
        cot=cot_ref[:,columns]
        acc[:,columns]+=dg(inner,down_ref[0,at],NN)
        ddown_ref[:,columns]=dg(inner,cot,TN).astype(ddown_ref.dtype)
        part=dg(cot,down_ref[0,at],NT)
        grad=part if grad is None else grad+part
    gpre=(grad*slope).astype(jnp.bfloat16)
    dup_ref[:,0]=dg(h,gpre,TN).astype(dup_ref.dtype).reshape(dup_ref.shape[0],dup_ref.shape[2],dup_ref.shape[3])
    g_ref[...]+=dg(gpre,up,NT)
    @pl.when(i==pl.num_programs(0)-1)
    def _(): out_ref[...]=acc[...].astype(out_ref.dtype)

def feed(h,cot,res,up,down):
    rows,d=h.shape; chunk=down.shape[2]; strips=up.shape[3]//chunk; ff=down.shape[0]*chunk
    whole=pl.BlockSpec((rows,d),lambda i:(0,0))
    up_spec=pl.BlockSpec((up.shape[0],1,up.shape[2],chunk),lambda i:(0,i//strips,0,i%strips))
    down_spec=pl.BlockSpec((1,)+down.shape[1:],lambda i:(i,0,0,0))
    return pl.pallas_call(feed_kernel,grid=(ff//chunk,),
        in_specs=[whole,whole,whole,up_spec,down_spec],
        out_specs=[whole,whole,up_spec,pl.BlockSpec((chunk,d),lambda i:(i,0))],
        out_shape=[jax.ShapeDtypeStruct((rows,d),jnp.bfloat16),jax.ShapeDtypeStruct((rows,d),jnp.float32),jax.ShapeDtypeStruct(up.shape,jnp.bfloat16),jax.ShapeDtypeStruct((ff,d),jnp.bfloat16)],
        scratch_shapes=[pltpu.VMEM((rows,d),jnp.float32)],
        compiler_params=pltpu.CompilerParams(vmem_limit_bytes=56<<20),
        cost_estimate=pl.CostEstimate(flops=12*rows*d*ff,bytes_accessed=8*d*ff+16*rows*d,transcendentals=2*rows*ff))(h,cot,res,up,down)


MESH = pl.DeviceIdType.MESH
ORDERS = ("xzy", "yzx", "xzy", "yzx", "zxy", "zyx")


class Place:
    def __init__(self):
        row, col = lax.axis_index("row"), lax.axis_index("col")
        self.z, self.y, self.x, self.k = row // 2, row % 2, col // 2, col % 2
        self.along = lax.axis_size("row") // 2

    def device(self, dz=0, y=False, x=False, k=False):
        other_y = 1 - self.y if y else self.y
        other_x = 1 - self.x if x else self.x
        other_k = 1 - self.k if k else self.k
        return ((self.z + dz) * 2 + other_y, other_x * 2 + other_k)

    def across(self, axis):
        return self.device(y=axis == "y", x=axis == "x", k=axis == "k")

    def greet(self):
        barrier = pltpu.get_barrier_semaphore()
        for axis in "xyk":
            pl.semaphore_signal(barrier, inc=1, device_id=self.across(axis), device_id_type=MESH)

        @pl.when(self.z > 0)
        def _():
            pl.semaphore_signal(barrier, inc=1, device_id=self.device(dz=-1), device_id_type=MESH)

        @pl.when(self.z + 1 < self.along)
        def _():
            pl.semaphore_signal(barrier, inc=1, device_id=self.device(dz=1), device_id_type=MESH)

        below = jnp.where(self.z > 0, 1, 0)
        above = jnp.where(self.z + 1 < self.along, 1, 0)
        pl.semaphore_wait(barrier, 3 + below + above)


def when(condition, run):
    if condition is None:
        run()
    else:
        pl.when(condition)(run)


def in_turn(units, lag):
    ready = [(lag * at, at) for at in range(len(units))]
    while ready:
        turn, at = min(ready)
        ready.remove((turn, at))
        if next(units[at], units) is not units:
            ready.append((turn + 1, at))
        yield


class Gather:
    def __init__(self, place, block, full, strip, order, send, recv):
        self.place, self.block, self.full, self.strip = place, block, full, strip
        turn = order.index("z")
        self.before, self.after = order[:turn], order[turn + 1 :]
        self.send, self.recv, self.used, self.sent, self.started = send, recv, 0, 0, []

    def region(self, z, y, x):
        part, start, count = self.strip
        column = (x * 2 + self.place.k) * self.block.shape[-1] + start
        return self.full.at[z, y, part, :, pl.ds(pl.multiple_of(column, 128), count)]

    def held(self, done, z):
        y = slice(None) if "y" in done else self.place.y
        return [self.region(z, y, x) for x in (range(2) if "x" in done else [self.place.x])]

    def pairs(self, done, z, first):
        if first:
            part, start, count = self.strip
            place = self.place
            return [(self.block.at[part, :, pl.ds(start, count)], self.region(place.z, place.y, place.x))]
        return [(region, region) for region in self.held(done, z)]

    def semaphore(self):
        self.used += 2
        return self.used - 2

    def copies(self, device, pairs, semaphore, send=0):
        return [
            pltpu.make_async_remote_copy(
                src_ref=source, dst_ref=target, send_sem=self.send.at[send + at],
                recv_sem=self.recv.at[semaphore + at], device_id=device, device_id_type=MESH)
            for at, (source, target) in enumerate(pairs)
        ]

    def start(self, device, pairs, wide, condition, semaphore):
        send = self.sent
        self.sent += wide

        def make():
            return self.copies(device(), pairs(), semaphore, send)

        when(condition(), lambda: [copy.start() for copy in make()] and None)
        self.started.append((condition, make))
        return condition, make

    def arrive(self, sent):
        condition, make = sent
        when(condition(), lambda: [copy.wait_recv() for copy in make()] and None)

    def stages(self):
        place, along = self.place, self.place.along
        done = []

        def always():
            return None

        def width(axes):
            return 2 if "x" in axes else 1

        for axis in self.before:
            axes = tuple(done)
            sent = self.start(
                lambda axis=axis: place.across(axis), lambda axes=axes: self.pairs(axes, place.z, not axes),
                width(axes), always, self.semaphore())
            yield
            self.arrive(sent)
            done.append(axis)
        first = not done
        axes_z = tuple(done)
        from_left = [self.semaphore() for _ in range(along - 1)]
        from_right = [self.semaphore() for _ in range(along - 1)]

        def pass_on(turn, step):
            axes = axes_z + tuple(self.after[:turn])
            sent = []
            for way in ((-1, 1) if step else (0,)):

                def inside(way=way):
                    z = place.z + way * step
                    return (z >= 0) & (z < along) if way else None

                sent.append(self.start(
                    lambda: place.across(self.after[turn]),
                    lambda way=way: self.pairs(axes, place.z + way * step, not axes and not step),
                    width(axes), inside, self.semaphore()))
            return turn, step, sent

        def step_out(step):
            self.start(
                lambda: place.device(dz=1), lambda: self.pairs(axes_z, place.z - (step - 1), first and step == 1),
                width(axes_z), lambda: (place.z - (step - 1) >= 0) & (place.z + 1 < along), from_left[step - 1])
            self.start(
                lambda: place.device(dz=-1), lambda: self.pairs(axes_z, place.z + (step - 1), first and step == 1),
                width(axes_z), lambda: (place.z + (step - 1) < along) & (place.z > 0), from_right[step - 1])

        def step_in(step):
            for way, semaphore in ((-1, from_left), (1, from_right)):
                z = place.z + way * step
                self.arrive((
                    lambda: (z >= 0) & (z < along),
                    lambda: self.copies(place.across("k"), self.pairs(axes_z, z, False), semaphore[step - 1])))

        step_out(1)
        waiting = [pass_on(0, 0)] if self.after else []
        for step in range(1, along + len(self.after)):
            yield
            if step < along:
                step_in(step)
                if step + 1 < along:
                    step_out(step + 1)
            following = []
            for turn, at, sent in waiting:
                for one in sent:
                    self.arrive(one)
                if turn + 1 < len(self.after):
                    following.append(pass_on(turn + 1, at))
            if self.after and step < along:
                following.append(pass_on(0, step))
            waiting = following
        sent = self.start(
            lambda: place.across("k"), lambda: [(r, r) for r in [self.region(slice(None), slice(None), x) for x in range(2)]],
            2, always, self.semaphore())
        yield
        self.arrive(sent)

    def finish(self):
        for condition, make in self.started:
            when(condition(), lambda make=make: [copy.wait_send() for copy in make()] and None)


class OwnBlocks:
    def __init__(self, place, blocks, fulls, local):
        self.place, self.blocks, self.fulls, self.local = place, blocks, fulls, local

    def copies(self):
        place = self.place
        for at, (block, full) in enumerate(zip(self.blocks, self.fulls)):
            width = block.shape[-1]
            columns = pl.ds(pl.multiple_of((place.x * 2 + place.k) * width, 128), width)
            yield pltpu.make_async_copy(block, full.at[place.z, place.y, :, :, columns], self.local.at[at])

    def start(self):
        for copy in self.copies():
            copy.start()

    def wait(self):
        for copy in self.copies():
            copy.wait()


def gathers_of(place, units, blocks, fulls, send, recv):
    return [
        Gather(place, blocks[which], fulls[which], strip, order, send.at[at], recv.at[at])
        for at, (which, strip, order) in enumerate(units)
    ]


def gather_kernel(units, count, *refs):
    blocks, fulls = refs[:count], refs[count : 2 * count]
    send, recv, local = refs[2 * count :]
    place = Place()
    place.greet()
    own = OwnBlocks(place, blocks, fulls, local)
    own.start()
    gathers = gathers_of(place, units, blocks, fulls, send, recv)
    waited = False
    for unused in in_turn([gather.stages() for gather in gathers], 0.0):
        if not waited:
            own.wait()
            waited = True
    for gather in gathers:
        gather.finish()


def gather_units(blocks, least, orders):
    strips = []
    for which, block in enumerate(blocks):
        wide = min(least, block.shape[-1])
        for part in range(block.shape[0]):
            for start in range(0, block.shape[-1], wide):
                strips.append((which, (part, start, wide)))
    return [strip + (orders[at % len(orders)],) for at, strip in enumerate(strips)]


def gather_plan(blocks, least, orders):
    along, cols = lax.axis_size("row") // 2, lax.axis_size("col")
    units = gather_units(blocks, least, orders)
    fulls = [jax.ShapeDtypeStruct((along, 2) + b.shape[:2] + (cols * b.shape[2],), b.dtype) for b in blocks]
    scratch = [
        pltpu.SemaphoreType.DMA((len(units), 8 * along)),
        pltpu.SemaphoreType.DMA((len(units), 12 * along)),
        pltpu.SemaphoreType.DMA((len(blocks),)),
    ]
    return fulls, units, scratch


def gather_blocks(blocks, collective_id, least):
    fulls, units, scratch = gather_plan(blocks, least, ORDERS)
    count = len(blocks)
    anywhere = pl.BlockSpec(memory_space=pl.ANY)
    return pl.pallas_call(
        functools.partial(gather_kernel, units, count),
        out_shape=fulls,
        in_specs=[anywhere] * count,
        out_specs=[anywhere] * count,
        scratch_shapes=scratch,
        compiler_params=pltpu.CompilerParams(collective_id=collective_id, has_side_effects=True),
        cost_estimate=pl.CostEstimate(flops=0, bytes_accessed=4 * sum(f.size for f in fulls), transcendentals=0),
    )(*blocks)


def add_blocks(total, extra, leading):
    def one(at, unused):
        place = []
        for size in leading[::-1]:
            place.append(at % size)
            at = at // size
        place = tuple(place[::-1])
        total[place] = total[place] + extra[place]
        return unused

    if not leading:
        total[...] = total[...] + extra[...]
        return
    count = 1
    for size in leading:
        count *= size
    lax.fori_loop(0, count, one, 0)


class Scatter:
    def __init__(self, place, grad, out, strip, width, order, slots, send, recv, local):
        self.place, self.grad, self.out, self.strip, self.width = place, grad, out, strip, width
        self.order = order[::-1]
        self.total, self.other_core, self.halves, self.steps = slots
        self.send, self.recv, self.local = send, recv, local
        self.used, self.started = 0, []

    def region(self, x, k):
        part, start, count = self.strip
        column = (x * 2 + k) * self.width + start
        return self.grad.at[:, :, part, :, pl.ds(pl.multiple_of(column, 128), count)]

    def copy(self, device, source, target, semaphore):
        return pltpu.make_async_remote_copy(
            src_ref=source, dst_ref=target, send_sem=self.send.at[semaphore], recv_sem=self.recv.at[semaphore],
            device_id=device, device_id_type=MESH)

    def reserve(self, count):
        self.used += count
        return self.used - count

    def start(self, make, condition=lambda: None):
        when(condition(), lambda: make().start())
        self.started.append((condition, make))

    def stages(self):
        place, along = self.place, self.place.along
        rows, columns = self.total.shape[-2:]
        core = self.reserve(2)

        def own(x):
            return pltpu.make_async_copy(self.region(x, place.k), self.total.at[:, :, x], self.local.at[x])

        def swapped(x):
            return self.copy(
                place.across("k"), self.region(x, 1 - place.k), self.other_core.at[:, :, x], core + x)

        for x in range(2):
            own(x).start()
            self.start(functools.partial(swapped, x))
        yield
        for x in range(2):
            own(x).wait()
            swapped(x).wait_recv()
        add_blocks(self.total, self.other_core, (along, 2, 2))
        left = {"z": slice(None), "y": slice(None), "x": slice(None)}
        at = {"y": place.y, "x": place.x}

        def view(ref, kept=None, **places):
            return ref.at[tuple({**(left if kept is None else kept), **places}[axis] for axis in "zyx")]

        def sizes():
            return tuple(size for axis, size in zip("zyx", (along, 2, 2)) if isinstance(left[axis], slice))

        exchanges = 0
        for axis in self.order:
            if axis == "z":
                shape = tuple(2 for name in "yx" if isinstance(left[name], slice))
                inner = tuple(slice(None) if isinstance(left[name], slice) else 0 for name in "yx")

                def landing(side, step, inner=inner):
                    return self.steps.at[(side, step) + inner]

                base = self.reserve(2 * along)
                right, leftward = range(base, base + along), range(base + along, base + 2 * along)
                for step in range(along):
                    if step:
                        yield
                    for way, names, first in ((1, right, place.z), (-1, leftward, along - 1 - place.z)):
                        goal = along - 1 - step + place.z if way == 1 else step - along + 1 + place.z
                        side = 0 if way == 1 else 1
                        if step:
                            arrived = landing(side, step - 1)

                            def take(arrived=arrived, goal=goal, side=side, step=step, names=names):
                                self.copy(place.across("k"), arrived, arrived, names[step - 1]).wait_recv()
                                add_blocks(view(self.total, z=goal), arrived, shape)

                            pl.when((first >= 1) & (first <= step))(take)
                        if step < along - 1:
                            kept = dict(left)

                            def onward(way=way, step=step, kept=kept, landing=landing, side=side, names=names):
                                goal = along - 1 - step + place.z if way == 1 else step - along + 1 + place.z
                                source = view(self.total, kept, z=jnp.clip(goal, 0, along - 1))
                                return self.copy(place.device(dz=way), source, landing(side, step), names[step])

                            def reached(way=way, step=step):
                                first = place.z if way == 1 else along - 1 - place.z
                                return (first <= step) & (first < along - 1)

                            self.start(onward, reached)
                left["z"] = place.z
            else:
                landing = self.halves[exchanges]
                exchanges += 1
                inner = tuple(slice(None) if isinstance(left[name], slice) and name != axis else 0 for name in "zyx")
                semaphore, kept = self.reserve(1), dict(left)

                def swap(axis=axis, kept=kept, landing=landing, inner=inner, semaphore=semaphore):
                    source = view(self.total, kept, **{axis: 1 - at[axis]})
                    return self.copy(place.across(axis), source, landing.at[inner], semaphore)

                self.start(swap)
                yield
                swap().wait_recv()
                left[axis] = at[axis]
                add_blocks(view(self.total), landing.at[inner], sizes())
        part, start, count = self.strip
        self.out[part, :, start : start + count] = view(self.total)[...].astype(jnp.float32)

    def finish(self):
        for condition, make in self.started:
            when(condition(), lambda make=make: make().wait_send())


def scatter_slots(along, rows, columns, order):
    left = {"z": along, "y": 2, "x": 2}
    whole = (along, 2, 2, rows, columns)
    shapes = [whole, whole]
    steps = None
    for axis in order[::-1]:
        if axis == "z":
            steps = (2, along - 1, left["y"], left["x"], rows, columns)
        left[axis] = 1
        if axis != "z":
            shapes.append((left["z"], left["y"], left["x"], rows, columns))
    return shapes + [steps]


def scatters_of(place, units, grads, outs, send, recv, local, slots):
    scatters = []
    for at, (which, strip, order) in enumerate(units):
        total, other_core, first, second, steps = slots[5 * at : 5 * at + 5]
        scatters.append(
            Scatter(place, grads[which], outs[which], strip, outs[which].shape[-1], order,
                    (total, other_core, (first, second), steps), send.at[at], recv.at[at], local.at[at]))
    return scatters


def scatter_kernel(units, count, *refs):
    grads, outs = refs[:count], refs[count : 2 * count]
    place = Place()
    place.greet()
    scatters = scatters_of(place, units, grads, outs, *refs[2 * count : 2 * count + 3], refs[2 * count + 3 :])
    for unused in in_turn([scatter.stages() for scatter in scatters], 0.25):
        pass
    for scatter in scatters:
        scatter.finish()


def scatter_plan(grads, least, orders):
    along, cols = lax.axis_size("row") // 2, lax.axis_size("col")
    blocks = [jax.ShapeDtypeStruct(g.shape[2:4] + (g.shape[4] // cols,), jnp.float32) for g in grads]
    units = gather_units(blocks, least, orders)
    scratch = [pltpu.SemaphoreType.DMA((len(units), 2 * along + 4))] * 2 + [pltpu.SemaphoreType.DMA((len(units), 2))]
    for which, strip, order in units:
        shapes = scatter_slots(along, blocks[which].shape[1], strip[2], order)
        scratch += [pltpu.VMEM(shape, jnp.bfloat16) for shape in shapes]
    return blocks, units, scratch


def scatter_blocks(grads, collective_id, least):
    blocks, units, scratch = scatter_plan(grads, least, ("xyz", "yxz", "zxy", "zyx", "xzy", "yzx"))
    count = len(grads)
    anywhere = pl.BlockSpec(memory_space=pl.ANY)
    return pl.pallas_call(
        functools.partial(scatter_kernel, units, count),
        out_shape=blocks,
        in_specs=[anywhere] * count,
        out_specs=[pl.BlockSpec(memory_space=pltpu.VMEM)] * count,
        scratch_shapes=scratch,
        compiler_params=pltpu.CompilerParams(
            collective_id=collective_id, has_side_effects=True, vmem_limit_bytes=60 << 20),
        cost_estimate=pl.CostEstimate(
            flops=sum(g.size for g in grads), bytes_accessed=4 * sum(g.size for g in grads), transcendentals=0),
    )(*grads)


ACROSS = ("yzx", "yzx", "yzx", "yzx", "yxz")


def attend_rows(q, key_ref, value_ref, spans, diagonal, put):
    low = lax.broadcasted_iota(jnp.int32, (1, 128), 1) < HEAD_DIM
    mixed, logs = [], []
    for h in range(2):
        mine = low if h == 0 else jnp.logical_not(low)
        qh = jnp.where(mine, q, jnp.bfloat16(0))
        scores = []
        for at, length in spans:
            s = dg(qh, key_ref[at : at + length, :], NT)
            if at == diagonal:
                allowed = lax.broadcasted_iota(jnp.int32, s.shape, 0) >= lax.broadcasted_iota(jnp.int32, s.shape, 1)
                s = jnp.where(allowed, s, -1e30)
            scores.append(s)
        top = functools.reduce(jnp.maximum, [jnp.max(s, axis=1, keepdims=True) for s in scores])
        out = None
        for (at, length), s in zip(spans, scores):
            p = jnp.exp(s - top).astype(jnp.bfloat16)
            value = value_ref[at : at + length, :]
            part = dg(p, jnp.where(mine, value, jnp.ones_like(value)), NN)
            out = part if out is None else out + part
        total = out[:, HEAD_DIM : HEAD_DIM + 1] if h == 0 else out[:, 0:1]
        mixed.append(out / total)
        logs.append(top + jnp.log(total))
    put(logs)
    return jnp.where(low, mixed[0], mixed[1])


def rows_of(lanes_ref, first):
    picked = lax.broadcasted_iota(jnp.int32, (8, 128), 0) + first == lax.broadcasted_iota(jnp.int32, (8, 128), 1)
    return lax.dot_general(
        picked.astype(jnp.float32), lanes_ref[...], NT, precision=lax.Precision.HIGHEST,
        preferred_element_type=jnp.float32)


def pair_attend_kernel(tile, units, count, events, *refs):
    q_ref, k_ref, v_ref, q_any, k_any, v_any = refs[:6]
    blocks = refs[6 : 6 + count]
    mix_ref, logs_ref, fq_out, fk_out, fv_out = refs[6 + count : 11 + count]
    fulls = refs[11 + count : 11 + 2 * count]
    (near, near_logs, far_q, far_k, far_v, far, far_logs, got, far_rows, got_rows,
     send, recv, local, keep) = refs[11 + 2 * count : 25 + 2 * count]
    gather_send, gather_recv, gather_local = refs[25 + 2 * count :]
    step = pl.program_id(0)
    place = Place()
    own = OwnBlocks(place, blocks, fulls, gather_local)
    gathers = gathers_of(place, units, blocks, fulls, gather_send, gather_recv)
    turns = in_turn([gather.stages() for gather in gathers], 0.25)
    pairs = near.shape[0]
    fars = pairs // 2
    rows = q_ref.shape[0]
    first, second = place.y == 0, place.y == 1
    partner = place.across("y")
    lane = lax.broadcasted_iota(jnp.int32, (1, 128), 1)
    scale = jnp.bfloat16(HEAD_DIM**-0.5)
    plan = ((q_any, far_q, False), (k_any, far_k, True), (v_any, far_v, True))

    def columns(pair):
        return pl.ds(pl.multiple_of(pair * 128, 128), 128)

    def sending(which, j):
        array, landing, by_first = plan[which]
        return pltpu.make_async_remote_copy(
            src_ref=array.at[:, columns(j if by_first else fars + j)], dst_ref=landing.at[j],
            send_sem=send.at[which, j], recv_sem=recv.at[which, j], device_id=partner, device_id_type=MESH)

    def keeping(which, j):
        array, landing, by_first = plan[which]
        return pltpu.make_async_copy(
            array.at[:, columns(fars + j if by_first else j)], landing.at[j], local.at[which, j])

    def mixture_out(j):
        return pltpu.make_async_remote_copy(
            src_ref=far.at[j], dst_ref=got.at[j], send_sem=send.at[3, j], recv_sem=recv.at[3, j],
            device_id=partner, device_id_type=MESH)

    def logs_out():
        return pltpu.make_async_remote_copy(
            src_ref=far_rows, dst_ref=got_rows, send_sem=send.at[4, 0], recv_sem=recv.at[4, 0],
            device_id=partner, device_id_type=MESH)

    def saving(which):
        return pltpu.make_async_copy(plan[which][1], (fq_out, fk_out, fv_out)[which], keep.at[which])

    @pl.when(step == 0)
    def _():
        place.greet()
        own.start()
        near_logs[...] = jnp.zeros_like(near_logs)
        far_logs[...] = jnp.zeros_like(far_logs)
        for j in range(fars):
            for which in range(3):

                @pl.when(first if plan[which][2] else second)
                def _(which=which, j=j):
                    keeping(which, j).start()

    @pl.when((step % 3 == 0) & (step < 3 * fars))
    def _():
        j = step // 3
        for which in range(3):

            @pl.when(first if plan[which][2] else second)
            def _(which=which):
                @pl.when(j > 0)
                def _():
                    sending(which, j - 1).wait_send()

                sending(which, j).start()

    for at, number in enumerate(events):

        @pl.when(step == at)
        def _(at=at, number=number):
            if at == 0:
                own.wait()
            for unused in range(number):
                next(turns, None)

    @pl.when(step < pairs)
    def _():
        for start in range(0, rows, tile):
            n = min(tile, rows - start)

            def put(logs, start=start, n=n):
                kept = near_logs[start : start + n, :]
                for h in range(2):
                    kept = jnp.where(lane == 2 * step + h, logs[h], kept)
                near_logs[start : start + n, :] = kept

            spans = ([(0, start)] if start else []) + [(start, n)]
            near[step, start : start + n, :] = attend_rows(
                q_ref[start : start + n, :] * scale, k_ref, v_ref, spans, start, put)

    @pl.when((step >= pairs) & (step < pairs + fars))
    def _():
        j = step - pairs
        for which in range(3):
            by_first = plan[which][2]

            @pl.when(first if by_first else second)
            def _(which=which):
                keeping(which, j).wait()

            @pl.when(second if by_first else first)
            def _(which=which):
                sending(which, j).wait_recv()

        base = jnp.where(first, 2 * fars, 0)
        for start in range(0, rows, tile):
            n = min(tile, rows - start)

            def put(logs, start=start, n=n):
                kept = far_logs[start : start + n, :]
                for h in range(2):
                    kept = jnp.where(lane == base + 2 * j + h, logs[h], kept)
                far_logs[start : start + n, :] = kept

            far[j, start : start + n, :] = attend_rows(
                far_q[j, start : start + n, :] * scale, far_k.at[j], far_v.at[j], [(0, rows)], None, put
            ).astype(far.dtype)

        @pl.when(first)
        def _():
            mixture_out(j).start()

    @pl.when(step == pairs + fars)
    def _():
        for which in range(3):
            saving(which).start()

        @pl.when(first)
        def _():
            far_rows[...] = rows_of(far_logs, 2 * fars)
            logs_out().start()
            for pair in range(pairs):
                mix_ref[:, pair * 128 : (pair + 1) * 128] = near[pair].astype(mix_ref.dtype)
            logs_ref[...] = near_logs[...]
            logs_out().wait_send()
            for j in range(fars):
                mixture_out(j).wait_send()
            for which in (1, 2):
                sending(which, fars - 1).wait_send()

        @pl.when(second)
        def _():
            logs_out().wait_recv()
            for j in range(fars):
                mixture_out(j).wait_recv()
            sending(0, fars - 1).wait_send()
            spread_out = (lax.broadcasted_iota(jnp.int32, (8, 128), 0) + 2 * fars == lane).astype(jnp.float32)
            theirs = lax.dot_general(
                got_rows[...], spread_out, TN, precision=lax.Precision.HIGHEST, preferred_element_type=jnp.float32)
            logs_far = far_logs[...] + theirs
            logs_near = near_logs[...]
            top = jnp.maximum(logs_near, logs_far)
            total = top + jnp.log(jnp.exp(logs_near - top) + jnp.exp(logs_far - top))
            logs_ref[...] = total
            share = jnp.exp(logs_near - total)
            low = lane < HEAD_DIM
            for pair in range(pairs):
                part = jnp.where(low, share[:, 2 * pair : 2 * pair + 1], share[:, 2 * pair + 1 : 2 * pair + 2])
                other = (far[pair] if pair < fars else got[pair - fars]).astype(jnp.float32)
                mix_ref[:, pair * 128 : (pair + 1) * 128] = (other + (near[pair] - other) * part).astype(mix_ref.dtype)

        for which in range(3):
            saving(which).wait()
        for unused in turns:
            pass
        for gather in gathers:
            gather.finish()


def pair_attend(q, k, v, blocks, collective_id, events, tile=384):
    rows, width = q.shape
    pairs = width // 128
    fars = pairs // 2
    block = pl.BlockSpec((rows, 128), lambda i: (0, jnp.minimum(i, pairs - 1)))
    anywhere = pl.BlockSpec(memory_space=pl.ANY)
    kept = jax.ShapeDtypeStruct((fars, rows, 128), jnp.bfloat16)
    half = pltpu.VMEM((fars, rows, 128), jnp.bfloat16)
    fulls, units, scratch = gather_plan(blocks, 256, ACROSS)
    count = len(blocks)
    result = pl.pallas_call(
        functools.partial(pair_attend_kernel, tile, units, count, events),
        grid=(pairs + fars + 1,),
        in_specs=[block] * 3 + [anywhere] * (3 + count),
        out_specs=[pl.BlockSpec((rows, width), lambda i: (0, 0)), pl.BlockSpec((rows, 128), lambda i: (0, 0))] + [anywhere] * (3 + count),
        out_shape=[
            jax.ShapeDtypeStruct((rows, width), jnp.bfloat16), jax.ShapeDtypeStruct((rows, 128), jnp.float32), kept, kept, kept, *fulls],
        scratch_shapes=[
            pltpu.VMEM((pairs, rows, 128), jnp.float32), pltpu.VMEM((rows, 128), jnp.float32),
            half, half, half, half, pltpu.VMEM((rows, 128), jnp.float32), half,
            pltpu.VMEM((8, rows), jnp.float32), pltpu.VMEM((8, rows), jnp.float32),
            pltpu.SemaphoreType.DMA((5, fars)), pltpu.SemaphoreType.DMA((5, fars)),
            pltpu.SemaphoreType.DMA((3, fars)), pltpu.SemaphoreType.DMA((3,)), *scratch,
        ],
        compiler_params=pltpu.CompilerParams(
            collective_id=collective_id, has_side_effects=True, vmem_limit_bytes=48 << 20),
        cost_estimate=pl.CostEstimate(
            flops=4 * rows * rows * width, bytes_accessed=16 * rows * width, transcendentals=rows * rows * pairs * 2),
    )(q, k, v, q, k, v, *blocks)
    return result[:5], result[5:]


def back_pair(tile, causal, q_ref, k_ref, v_ref, do_ref, stats, acc, put):
    rows, keys = q_ref.shape[0], k_ref.shape[0]
    low = lax.broadcasted_iota(jnp.int32, (1, 128), 1) < HEAD_DIM
    acc[...] = jnp.zeros_like(acc)
    for start in range(0, keys, tile):
        n = min(tile, keys - start)
        k = k_ref[start : start + n, :] * jnp.bfloat16(HEAD_DIM**-0.5)
        v = v_ref[start : start + n, :]
        spans = [(0, rows)]
        if causal:
            spans = [(start, n)] + ([(start + n, rows - start - n)] if start + n < rows else [])
        dks, dvs = [], []
        for h in range(2):
            mine = low if h == 0 else jnp.logical_not(low)
            kh, vh = jnp.where(mine, k, jnp.bfloat16(0)), jnp.where(mine, v, jnp.bfloat16(0))
            dk = dv = None
            for at, length in spans:
                qs, do = q_ref[at : at + length, :], do_ref[at : at + length, :]
                p = jnp.exp(dg(kh, qs, NT) - stats[h : h + 1, at : at + length])
                if causal and at == start:
                    allowed = lax.broadcasted_iota(jnp.int32, p.shape, 0) <= lax.broadcasted_iota(jnp.int32, p.shape, 1)
                    p = jnp.where(allowed, p, 0.0)
                ds = (p * (dg(vh, do, NT) - stats[2 + h : 3 + h, at : at + length])).astype(jnp.bfloat16)
                a, b = dg(p.astype(jnp.bfloat16), do, NN), dg(ds, qs, NN)
                dv = a if dv is None else dv + a
                dk = b if dk is None else dk + b
                acc[at : at + length, :] += dg(ds, kh, TN)
            dks.append(dk)
            dvs.append(dv)
        put(start, n, jnp.where(low, dks[0], dks[1]) * HEAD_DIM**-0.5, jnp.where(low, dvs[0], dvs[1]))


def pair_stats(pair, mix_ref, do_ref, logs_ref):
    lane = lax.broadcasted_iota(jnp.int32, (8, 128), 1)
    line = lax.broadcasted_iota(jnp.int32, (8, 128), 0)
    picked = ((line < 2) & (line + 2 * pair == lane)).astype(jnp.float32)
    halves = (((line == 2) & (lane < HEAD_DIM)) | ((line == 3) & (lane >= HEAD_DIM))).astype(jnp.float32)
    products = mix_ref[...].astype(jnp.float32) * do_ref[...].astype(jnp.float32)
    logs = lax.dot_general(
        picked, logs_ref[...], NT, precision=lax.Precision.HIGH, preferred_element_type=jnp.float32)
    return logs + lax.dot_general(
        halves, products, NT, precision=lax.Precision.HIGH, preferred_element_type=jnp.float32)


def both_heads(array):
    low = lax.broadcasted_iota(jnp.int32, (1, 128), 1) < HEAD_DIM
    zero = jnp.zeros_like(array)
    return jnp.concatenate([jnp.where(low, array, zero), jnp.where(low, zero, array)], axis=0)


def one_head_each(array):
    low = lax.broadcasted_iota(jnp.int32, (1, 128), 1) < HEAD_DIM
    half = array.shape[0] // 2
    return jnp.where(low, array[:half], array[half:])


def cross_kernel(q_ref, k_ref, v_ref, mix_ref, logs_ref):
    pair = pl.program_id(0)
    keys = k_ref.shape[0]
    lane = lax.broadcasted_iota(jnp.int32, (1, 128), 1)
    lower = lax.broadcasted_iota(jnp.int32, (1, 2 * keys), 1) < keys

    @pl.when(pair == 0)
    def _():
        logs_ref[...] = jnp.zeros_like(logs_ref)

    scores = dg(q_ref[...] * jnp.bfloat16(HEAD_DIM**-0.5), both_heads(k_ref[...]), NT)
    tops = [
        jnp.max(jnp.where(lower if h == 0 else jnp.logical_not(lower), scores, -1e30), axis=1, keepdims=True) for h in range(2)
    ]
    powers = jnp.exp(scores - jnp.where(lower, tops[0], tops[1])).astype(jnp.bfloat16)
    values = both_heads(v_ref[...])
    ones = both_heads(jnp.ones(v_ref.shape, v_ref.dtype))
    out = dg(powers, jnp.concatenate([values, ones], axis=1), NN)
    totals = out[:, 128:]
    mix_ref[...] = (out[:, :128] / totals).astype(mix_ref.dtype)
    sums = jnp.log(totals)
    logs = logs_ref[...]
    for h in range(2):
        logs = jnp.where(lane == 2 * pair + h, tops[h] + sums[:, h * HEAD_DIM : h * HEAD_DIM + 1], logs)
    logs_ref[...] = logs


def cross(q, k, v):
    rows, width = q.shape
    keys = k.shape[0]
    long, short = pl.BlockSpec((rows, 128), lambda i: (0, i)), pl.BlockSpec((keys, 128), lambda i: (0, i))
    return pl.pallas_call(
        cross_kernel,
        grid=(width // 128,),
        in_specs=[long, short, short],
        out_specs=[long, pl.BlockSpec((rows, 128), lambda i: (0, 0))],
        out_shape=[jax.ShapeDtypeStruct((rows, width), jnp.bfloat16), jax.ShapeDtypeStruct((rows, 128), jnp.float32)],
        compiler_params=pltpu.CompilerParams(vmem_limit_bytes=40 << 20),
        cost_estimate=pl.CostEstimate(
            flops=4 * rows * keys * width, bytes_accessed=6 * rows * width, transcendentals=rows * keys * width // HEAD_DIM),
    )(q, k, v)


def cross_back_kernel(q_ref, k_ref, v_ref, do_ref, mix_ref, logs_ref, dq_ref, dk_ref, dv_ref):
    keys = k_ref.shape[0]
    stats = pair_stats(pl.program_id(0), mix_ref, do_ref, logs_ref)
    upper = lax.broadcasted_iota(jnp.int32, (2 * keys, 1), 0) < keys
    k, v, do = both_heads(k_ref[...] * jnp.bfloat16(HEAD_DIM**-0.5)), both_heads(v_ref[...]), do_ref[...]
    p = jnp.exp(dg(k, q_ref[...], NT) - jnp.where(upper, stats[0:1, :], stats[1:2, :]))
    ds = (p * (dg(v, do, NT) - jnp.where(upper, stats[2:3, :], stats[3:4, :]))).astype(jnp.bfloat16)
    dv_ref[...] = one_head_each(dg(p.astype(jnp.bfloat16), do, NN)).astype(dv_ref.dtype)
    dk_ref[...] = (one_head_each(dg(ds, q_ref[...], NN)) * HEAD_DIM**-0.5).astype(dk_ref.dtype)
    dq_ref[...] = dg(ds, k, TN).astype(dq_ref.dtype)


def cross_back(q, k, v, do, mix, logs):
    rows, width = q.shape
    keys = k.shape[0]
    long, short = pl.BlockSpec((rows, 128), lambda i: (0, i)), pl.BlockSpec((keys, 128), lambda i: (0, i))
    return pl.pallas_call(
        cross_back_kernel,
        grid=(width // 128,),
        in_specs=[long, short, short, long, long, pl.BlockSpec((rows, 128), lambda i: (0, 0))],
        out_specs=[long, short, short],
        out_shape=[jax.ShapeDtypeStruct(a.shape, jnp.bfloat16) for a in (q, k, v)],
        compiler_params=pltpu.CompilerParams(vmem_limit_bytes=40 << 20),
        cost_estimate=pl.CostEstimate(
            flops=10 * rows * keys * width, bytes_accessed=10 * rows * width, transcendentals=rows * keys * width // HEAD_DIM),
    )(q, k, v, do, mix, logs)


def pair_back_kernel(tile, far_tile, units, count, events, *refs):
    q_ref, k_ref, v_ref, do_ref, mix_ref, logs_ref, do_any, fq_any, fk_any, fv_any = refs[:10]
    grads, (dq_ref, dk_ref, dv_ref) = refs[10 : 10 + count], refs[10 + count : 13 + count]
    sums = refs[13 + count : 13 + 2 * count]
    (near, acc, stats, far_stats, used_stats, far_q, far_k, far_v, far_do, far_dq, far_dk, far_dv, got_q, got_k, got_v,
     send, recv, local, do_local) = refs[13 + 2 * count : 32 + 2 * count]
    scatter_refs = refs[32 + 2 * count :]
    step = pl.program_id(0)
    place = Place()
    pairs = near.shape[1]
    fars = pairs // 2
    first, second = place.y == 0, place.y == 1
    partner = place.across("y")

    def columns(pair):
        return pl.ds(pl.multiple_of(pair * 128, 128), 128)

    def remote(source, target, which, j):
        return pltpu.make_async_remote_copy(
            src_ref=source, dst_ref=target, send_sem=send.at[which, j], recv_sem=recv.at[which, j],
            device_id=partner, device_id_type=MESH)

    def grad_over(j):
        return remote(do_any.at[:, columns(fars + j)], far_do.at[j], 0, j)

    def grad_kept(j):
        return pltpu.make_async_copy(do_any.at[:, columns(j)], far_do.at[j], do_local.at[j])

    def stats_over():
        return remote(stats.at[pl.ds(fars, fars)], far_stats, 4, 0)

    def back_over(which, j):
        source, target = ((far_dq, got_q), (far_dk, got_k), (far_dv, got_v))[which]
        return remote(source.at[j], target.at[j], 1 + which, j)

    def far_in(which):
        source, target = ((fq_any, far_q), (fk_any, far_k), (fv_any, far_v))[which]
        return pltpu.make_async_copy(source, target, local.at[which])

    scatters = scatters_of(place, units, grads, sums, *scatter_refs[:3], scatter_refs[3:])
    turns = in_turn([scatter.stages() for scatter in scatters], 0.5)

    @pl.when(step == 0)
    def _():
        place.greet()
        for which in range(3):
            far_in(which).start()
        for j in range(fars):

            @pl.when(second)
            def _(j=j):
                grad_over(j).start()

            @pl.when(second)
            def _(j=j):
                grad_kept(j).start()

    for at, number in enumerate(events):

        @pl.when(step == at)
        def _(number=number):
            for unused in range(number):
                next(turns, None)

    @pl.when((step == fars) & second)
    def _():
        stats_over().start()

    @pl.when(step < pairs)
    def _():
        pair = lax.rem(step + fars, pairs)
        stats[pair] = pair_stats(pair, mix_ref, do_ref, logs_ref)

        def put(start, n, dk, dv):
            near[1, pair, start : start + n, :] = dk
            near[2, pair, start : start + n, :] = dv

        back_pair(tile, True, q_ref, k_ref, v_ref, do_ref, stats.at[pair], acc, put)
        near[0, pair] = acc[...]

    @pl.when((step >= pairs) & (step < pairs + fars))
    def _():
        j = step - pairs

        @pl.when(j == 0)
        def _():
            for which in range(3):
                far_in(which).wait()

            @pl.when(first)
            def _():
                stats_over().wait_recv()

        @pl.when(first)
        def _():
            grad_over(j).wait_recv()
            used_stats[...] = far_stats[j]

        @pl.when(second)
        def _():
            grad_kept(j).wait()
            used_stats[...] = stats[j]

        def put(start, n, dk, dv):
            far_dk[j, start : start + n, :] = dk.astype(far_dk.dtype)
            far_dv[j, start : start + n, :] = dv.astype(far_dv.dtype)

        back_pair(far_tile, False, far_q.at[j], far_k.at[j], far_v.at[j], far_do.at[j], used_stats, acc, put)
        far_dq[j] = acc[...].astype(far_dq.dtype)

        @pl.when(first)
        def _():
            back_over(0, j).start()

        @pl.when(second)
        def _():
            back_over(1, j).start()
            back_over(2, j).start()

    @pl.when(step >= pairs + fars)
    def _():
        pair = step - pairs - fars
        lower = pair < fars
        j = lax.rem(pair, fars)

        def write(ref, which, other):
            total = near[which, pair]
            if other is not None:
                total = total + other[j].astype(jnp.float32)
            ref[...] = total.astype(ref.dtype)

        @pl.when(first & lower)
        def _():
            for which in (1, 2):
                back_over(which, j).wait_recv()
            write(dq_ref, 0, None)
            write(dk_ref, 1, got_k)
            write(dv_ref, 2, got_v)

        @pl.when(first & jnp.logical_not(lower))
        def _():
            write(dq_ref, 0, None)
            write(dk_ref, 1, far_dk)
            write(dv_ref, 2, far_dv)

        @pl.when(second & lower)
        def _():
            write(dq_ref, 0, far_dq)
            write(dk_ref, 1, None)
            write(dv_ref, 2, None)

        @pl.when(second & jnp.logical_not(lower))
        def _():
            back_over(0, j).wait_recv()
            write(dq_ref, 0, got_q)
            write(dk_ref, 1, None)
            write(dv_ref, 2, None)

    @pl.when(step == 2 * pairs + fars - 1)
    def _():
        for unused in turns:
            pass
        for scatter in scatters:
            scatter.finish()

        @pl.when(first)
        def _():
            for j in range(fars):
                back_over(0, j).wait_send()

        @pl.when(second)
        def _():
            stats_over().wait_send()
            for j in range(fars):
                grad_over(j).wait_send()
                for which in (1, 2):
                    back_over(which, j).wait_send()


def pair_back(q, k, v, do, mix, logs, far, grads, collective_id, events, tile=384, far_tile=256):
    rows, width = q.shape
    pairs = width // 128
    fars = pairs // 2
    blocks, units, scratch = scatter_plan(grads, 256, ORDERS)
    count = len(grads)
    block = pl.BlockSpec((rows, 128), lambda i: (0, lax.rem(jnp.minimum(i, pairs - 1) + fars, pairs)))
    joined = pl.BlockSpec((rows, 128), lambda i: (0, jnp.maximum(i - pairs - fars, 0)))
    anywhere = pl.BlockSpec(memory_space=pl.ANY)
    half = pltpu.VMEM((fars, rows, 128), jnp.bfloat16)
    out = jax.ShapeDtypeStruct((rows, width), jnp.bfloat16)
    result = pl.pallas_call(
        functools.partial(pair_back_kernel, tile, far_tile, units, count, events),
        grid=(2 * pairs + fars,),
        in_specs=[block] * 5 + [pl.BlockSpec((rows, 128), lambda i: (0, 0))] + [anywhere] * (4 + count),
        out_specs=[joined] * 3 + [pl.BlockSpec(memory_space=pltpu.VMEM)] * count,
        out_shape=[out] * 3 + blocks,
        scratch_shapes=[
            pltpu.VMEM((3, pairs, rows, 128), jnp.float32), pltpu.VMEM((rows, 128), jnp.float32),
            pltpu.VMEM((pairs, 8, rows), jnp.float32), pltpu.VMEM((fars, 8, rows), jnp.float32),
            pltpu.VMEM((8, rows), jnp.float32), *[half] * 10,
            pltpu.SemaphoreType.DMA((5, fars)), pltpu.SemaphoreType.DMA((5, fars)),
            pltpu.SemaphoreType.DMA((3,)), pltpu.SemaphoreType.DMA((fars,)), *scratch,
        ],
        compiler_params=pltpu.CompilerParams(
            collective_id=collective_id, has_side_effects=True, vmem_limit_bytes=62 << 20),
        cost_estimate=pl.CostEstimate(
            flops=10 * rows * rows * width, bytes_accessed=16 * rows * width, transcendentals=rows * rows * pairs * 2),
    )(q, k, v, do, mix, logs, do, *far, *grads)
    return result[:3], result[3:]


def fast(
    frames_in, text_states, self_query, self_key, self_value, self_output, cross_query, cross_key, cross_value, cross_output,
    up_weight, down_weight, first_gain, first_bias, second_gain, second_bias, third_gain, third_bias, cotangent,
):
    row = lax.axis_index("row")
    rows, width = frames_in.shape
    half = width // 2
    piece = first_gain.shape[0]
    block_rows, block_cols = self_query.shape
    back = row % 2
    pairs = lax.axis_size("row") // 2
    forth_perm = [(2 * i, 2 * i + 1) for i in range(pairs)]
    back_perm = [(2 * i + 1, 2 * i) for i in range(pairs)]
    swap = forth_perm + back_perm

    def forth(array):
        return lax.ppermute(array, "row", forth_perm)

    def home(array):
        return lax.ppermute(array, "row", back_perm)

    def by_side(first, second):
        return jnp.where(back == 0, first, second)

    gains = jnp.zeros((1, 16, 128), jnp.bfloat16)
    gains = gains.at[0, :6, :piece].set(
        jnp.stack([first_gain, first_bias, second_gain, second_bias, third_gain, third_bias])
    )

    everyone = ("row", "col")
    places = (lax.axis_size("row"), lax.axis_size("col"))
    up_blocks = lax.all_gather(up_weight, everyone).reshape(*places, *up_weight.shape)
    down_blocks = lax.all_gather(down_weight, everyone).reshape(*places, *down_weight.shape)

    def small(block):
        return block.reshape(1, block_rows, block_cols)

    def flat(array):
        return array.reshape(-1, array.shape[-1])

    early = gather_blocks(
        [small(self_query), small(self_key), small(self_value), gains], 1, 128)
    query_self, key_self, value_self = [flat(w) for w in early[:3]]
    norm_params = early[3].reshape(pairs * 2, 16, -1, 128)[:, :6, :, :piece].transpose(1, 0, 2, 3)
    norm_params = norm_params.reshape(6, width).astype(jnp.float32)

    frames = frames_in.astype(jnp.float32)
    hidden_one = norm_forward(frames, norm_params[0], norm_params[1]).astype(jnp.bfloat16)
    self_k = matmul(hidden_one, key_self).astype(jnp.bfloat16)
    self_v = matmul(hidden_one, value_self).astype(jnp.bfloat16)
    self_q = matmul(hidden_one, query_self).astype(jnp.bfloat16)
    (self_mix, log_lanes, far_q, far_k, far_v), late = pair_attend(
        self_q, self_k, self_v, [small(w) for w in (self_output, cross_query, cross_key, cross_value, cross_output)],
        5, [3] * 12)
    out_self, query_cross, key_cross, value_cross, out_cross = [flat(w) for w in late]
    resid_one = frames + matmul(self_mix, out_self)
    hidden_two = norm_forward(resid_one, norm_params[2], norm_params[3]).astype(jnp.bfloat16)
    cross_q = matmul(hidden_two, query_cross).astype(jnp.bfloat16)
    other_text = lax.ppermute(text_states, "row", swap)
    clip_text = by_side(
        jnp.concatenate([text_states, other_text]), jnp.concatenate([other_text, text_states])
    )
    text_k = matmul(clip_text, key_cross).astype(jnp.bfloat16)
    text_v = matmul(clip_text, value_cross).astype(jnp.bfloat16)
    cross_mix, cross_logs = cross(cross_q, text_k, text_v)
    resid_two = resid_one + matmul(cross_mix, out_cross)
    hidden_three = norm_forward(resid_two, norm_params[4], norm_params[5]).astype(jnp.bfloat16)
    layer_out, grad_three, up_grad, down_grad = feed(hidden_three, cotangent, resid_two, up_blocks, down_blocks)
    up_sum = lax.psum_scatter(up_grad.reshape(-1, *up_weight.shape), everyone, scatter_dimension=0).astype(jnp.float32)

    cotan_full = cotangent.astype(jnp.float32)
    unused_three, pull_three = jax.vjp(norm_forward, resid_two, norm_params[4], norm_params[5])
    through_three, third_gain_part, third_bias_part = pull_three(grad_three)
    grad_resid_two = cotan_full + through_three
    grad_cross = grad_resid_two.astype(jnp.bfloat16)
    cross_out_grad = over_tokens(cross_mix, grad_cross)
    grad_cross_mix = by_transposed(grad_cross, out_cross).astype(jnp.bfloat16)
    grad_cross_q, text_k_part, text_v_part = cross_back(cross_q, text_k, text_v, grad_cross_mix, cross_mix, cross_logs)
    text_rows = text_states.shape[0]
    text_parts = jnp.concatenate([text_k_part, text_v_part], axis=1)
    given = lax.ppermute(by_side(text_parts[text_rows:], text_parts[:text_rows]), "row", swap)
    kept = by_side(text_parts[:text_rows], text_parts[text_rows:])
    text_parts = (kept.astype(jnp.float32) + given.astype(jnp.float32)).astype(jnp.bfloat16)
    grad_text_k, grad_text_v = text_parts[:, :width], text_parts[:, width:]
    cross_query_part = over_tokens(hidden_two, grad_cross_q)
    cross_key_part = over_tokens(text_states, grad_text_k)
    cross_value_part = over_tokens(text_states, grad_text_v)
    text_grad = by_transposed(grad_text_k, key_cross) + by_transposed(grad_text_v, value_cross)
    grad_two = by_transposed(grad_cross_q, query_cross)
    unused_two, pull_two = jax.vjp(norm_forward, resid_one, norm_params[2], norm_params[3])
    through_two, second_gain_part, second_bias_part = pull_two(grad_two)
    grad_resid_one = grad_resid_two + through_two
    grad_self = grad_resid_one.astype(jnp.bfloat16)
    self_out_grad = over_tokens(self_mix, grad_self)
    grad_self_mix = by_transposed(grad_self, out_self).astype(jnp.bfloat16)

    def by_place(grad, parts):
        return grad.astype(jnp.bfloat16).reshape(pairs, 2, parts, -1, grad.shape[-1])

    (grad_self_q, grad_self_k, grad_self_v), early_sums = pair_back(
        self_q, self_k, self_v, grad_self_mix, self_mix, log_lanes, (far_q, far_k, far_v),
        [by_place(g, 1) for g in (self_out_grad, cross_query_part, cross_key_part, cross_value_part, cross_out_grad)]
        + [by_place(down_grad, down_weight.shape[0] // block_rows)], 4, [5] * 12)
    self_query_part = over_tokens(hidden_one, grad_self_q)
    self_key_part = over_tokens(hidden_one, grad_self_k)
    self_value_part = over_tokens(hidden_one, grad_self_v)
    grad_one = (
        by_transposed(grad_self_q, query_self)
        + by_transposed(grad_self_k, key_self)
        + by_transposed(grad_self_v, value_self)
    )
    unused_one, pull_one = jax.vjp(norm_forward, frames, norm_params[0], norm_params[1])
    through_one, first_gain_part, first_bias_part = pull_one(grad_one)
    input_grad = grad_resid_one + through_one
    norm_grads = jnp.stack(
        [first_gain_part, first_bias_part, second_gain_part, second_bias_part, third_gain_part, third_bias_part]
    )
    norm_grads = norm_grads.reshape(6, 2 * pairs, -1, piece).transpose(1, 0, 2, 3)
    norm_grads = jnp.pad(norm_grads, ((0, 0), (0, 10), (0, 0), (0, 128 - piece)))

    late_sums = scatter_blocks(
        [by_place(g, 1) for g in (self_query_part, self_key_part, self_value_part)]
        + [by_place(norm_grads.reshape(2 * pairs * 16, -1), 1)], 3, 128)
    norm_parts = late_sums[3][0, :6, :piece]
    sums = [*late_sums[:3], *early_sums]
    sums = [total.reshape(-1, total.shape[-1]) for total in sums]
    return (layer_out, input_grad, text_grad, *sums[:-1], up_sum, sums[-1], *norm_parts)


def local(*arrays):
    frames_in, self_query = arrays[0], arrays[2]
    halves = 2 * frames_in.shape[0] == FRAMES and lax.axis_size("row") % 2 == 0
    if halves and lax.axis_size("col") % 2 == 0 and self_query.shape[1] % 256 == 0 and self_query.shape[0] % 128 == 0:
        return fast(*arrays)
    return general(*arrays)


def solution(mesh):
    placed = (
        P(("col", "row"), None),
        P(("col", "row"), None),
        P("row", "col"),
        P("row", "col"),
        P("row", "col"),
        P("row", "col"),
        P("row", "col"),
        P("row", "col"),
        P("row", "col"),
        P("row", "col"),
        P("row", "col"),
        P("row", "col"),
        P(("row", "col")),
        P(("row", "col")),
        P(("row", "col")),
        P(("row", "col")),
        P(("row", "col")),
        P(("row", "col")),
        P(("col", "row"), None),
    )
    return jax.shard_map(
        local,
        mesh=mesh,
        in_specs=placed,
        out_specs=(
            P(("col", "row"), None),
            P(("col", "row"), None),
            P(("col", "row"), None),
            P("row", "col"),
            P("row", "col"),
            P("row", "col"),
            P("row", "col"),
            P("row", "col"),
            P("row", "col"),
            P("row", "col"),
            P("row", "col"),
            P("row", "col"),
            P("row", "col"),
            P(("row", "col")),
            P(("row", "col")),
            P(("row", "col")),
            P(("row", "col")),
            P(("row", "col")),
            P(("row", "col")),
        ),
        check_vma=False,
    )
```

```python
import functools
from functools import partial

import jax
import jax.numpy as jnp
from jax import lax
from jax.experimental import pallas as pl
from jax.experimental.pallas import tpu as pltpu
from jax.sharding import PartitionSpec as P

HEADS = 16
HEAD_DIM = 64
FRAMES = 1500
TEXT = 64


def norm_forward(values, norm_gain, norm_bias):
    center = values - jnp.mean(values, axis=-1, keepdims=True)
    variance = jnp.mean(center * center, axis=-1, keepdims=True)
    return center * lax.rsqrt(variance + 1e-05) * norm_gain + norm_bias


def matmul(left, right):
    return jnp.dot(left, right, preferred_element_type=jnp.float32)


def by_transposed(left, right):
    return lax.dot_general(
        left, right, (((1,), (1,)), ((), ())), preferred_element_type=jnp.float32
    )


def over_tokens(left, right):
    return lax.dot_general(
        left, right, (((0,), (0,)), ((), ())), preferred_element_type=jnp.float32
    )


def collect(blocks):
    partly = (
        lax.all_gather(blocks[0], "col", axis=1, tiled=True),
        lax.all_gather(blocks[1], "col", axis=1, tiled=True),
        lax.all_gather(blocks[2], "col", axis=1, tiled=True),
        lax.all_gather(blocks[3], "col", axis=1, tiled=True),
        lax.all_gather(blocks[4], "col", axis=1, tiled=True),
        lax.all_gather(blocks[5], "col", axis=1, tiled=True),
        lax.all_gather(blocks[6], "col", axis=1, tiled=True),
        lax.all_gather(blocks[7], "col", axis=1, tiled=True),
        lax.all_gather(blocks[8], "col", axis=1, tiled=True),
        lax.all_gather(blocks[9], "col", axis=1, tiled=True),
        lax.all_gather(blocks[10], "col", axis=1, tiled=True),
    )
    return (
        lax.all_gather(partly[0], "row", axis=0, tiled=True),
        lax.all_gather(partly[1], "row", axis=0, tiled=True),
        lax.all_gather(partly[2], "row", axis=0, tiled=True),
        lax.all_gather(partly[3], "row", axis=0, tiled=True),
        lax.all_gather(partly[4], "row", axis=0, tiled=True),
        lax.all_gather(partly[5], "row", axis=0, tiled=True),
        lax.all_gather(partly[6], "row", axis=0, tiled=True),
        lax.all_gather(partly[7], "row", axis=0, tiled=True),
        lax.all_gather(partly[8], "row", axis=0, tiled=True),
        lax.all_gather(partly[9], "row", axis=0, tiled=True),
        lax.all_gather(partly[10], "row", axis=0, tiled=True),
    )


def spread(grads):
    partly = (
        lax.psum_scatter(
            grads[0].astype(jnp.bfloat16), "row", scatter_dimension=0, tiled=True
        ).astype(jnp.float32),
        lax.psum_scatter(
            grads[1].astype(jnp.bfloat16), "row", scatter_dimension=0, tiled=True
        ).astype(jnp.float32),
        lax.psum_scatter(
            grads[2].astype(jnp.bfloat16), "row", scatter_dimension=0, tiled=True
        ).astype(jnp.float32),
        lax.psum_scatter(
            grads[3].astype(jnp.bfloat16), "row", scatter_dimension=0, tiled=True
        ).astype(jnp.float32),
        lax.psum_scatter(
            grads[4].astype(jnp.bfloat16), "row", scatter_dimension=0, tiled=True
        ).astype(jnp.float32),
        lax.psum_scatter(
            grads[5].astype(jnp.bfloat16), "row", scatter_dimension=0, tiled=True
        ).astype(jnp.float32),
        lax.psum_scatter(
            grads[6].astype(jnp.bfloat16), "row", scatter_dimension=0, tiled=True
        ).astype(jnp.float32),
        lax.psum_scatter(
            grads[7].astype(jnp.bfloat16), "row", scatter_dimension=0, tiled=True
        ).astype(jnp.float32),
        lax.psum_scatter(
            grads[8].astype(jnp.bfloat16), "row", scatter_dimension=0, tiled=True
        ).astype(jnp.float32),
        lax.psum_scatter(
            grads[9].astype(jnp.bfloat16), "row", scatter_dimension=0, tiled=True
        ).astype(jnp.float32),
        lax.psum_scatter(
            grads[10].astype(jnp.bfloat16), "row", scatter_dimension=0, tiled=True
        ).astype(jnp.float32),
    )
    return (
        lax.psum_scatter(
            partly[0].astype(jnp.bfloat16), "col", scatter_dimension=1, tiled=True
        ).astype(jnp.float32),
        lax.psum_scatter(
            partly[1].astype(jnp.bfloat16), "col", scatter_dimension=1, tiled=True
        ).astype(jnp.float32),
        lax.psum_scatter(
            partly[2].astype(jnp.bfloat16), "col", scatter_dimension=1, tiled=True
        ).astype(jnp.float32),
        lax.psum_scatter(
            partly[3].astype(jnp.bfloat16), "col", scatter_dimension=1, tiled=True
        ).astype(jnp.float32),
        lax.psum_scatter(
            partly[4].astype(jnp.bfloat16), "col", scatter_dimension=1, tiled=True
        ).astype(jnp.float32),
        lax.psum_scatter(
            partly[5].astype(jnp.bfloat16), "col", scatter_dimension=1, tiled=True
        ).astype(jnp.float32),
        lax.psum_scatter(
            partly[6].astype(jnp.bfloat16), "col", scatter_dimension=1, tiled=True
        ).astype(jnp.float32),
        lax.psum_scatter(
            partly[7].astype(jnp.bfloat16), "col", scatter_dimension=1, tiled=True
        ).astype(jnp.float32),
        lax.psum_scatter(
            partly[8].astype(jnp.bfloat16), "col", scatter_dimension=1, tiled=True
        ).astype(jnp.float32),
        lax.psum_scatter(
            partly[9].astype(jnp.bfloat16), "col", scatter_dimension=1, tiled=True
        ).astype(jnp.float32),
        lax.psum_scatter(
            partly[10].astype(jnp.bfloat16), "col", scatter_dimension=1, tiled=True
        ).astype(jnp.float32),
    )


def heads_layout(stacked):
    return lax.all_to_all(stacked, "row", split_axis=1, concat_axis=0, tiled=True)


def tokens_layout(stacked):
    return lax.all_to_all(stacked, "row", split_axis=0, concat_axis=2, tiled=True)


def by_clips(arranged, start, count, length, heads_dev):
    section = arranged[:, start : start + count]
    return section.reshape(-1, length, heads_dev, HEAD_DIM)


def causal_scores(query_clip, key_clip, causal):
    scores = jnp.einsum(
        "qhd,khd->hqk", query_clip, key_clip, preferred_element_type=jnp.float32
    ) * HEAD_DIM ** (-0.5)
    if causal:
        allowed = jnp.arange(scores.shape[1])[:, None] >= jnp.arange(scores.shape[2])[None, :]
        scores = jnp.where(allowed, scores, -1e30)
    return scores


def attend_forward(query_clips, key_clips, value_clips, causal):

    def one_clip(operands):
        query_clip, key_clip, value_clip = operands
        scores = causal_scores(query_clip, key_clip, causal)
        highest = jnp.max(scores, axis=-1, keepdims=True)
        powers = jnp.exp(scores - highest)
        totals = jnp.sum(powers, axis=-1, keepdims=True)
        weights_low = (powers / totals).astype(jnp.bfloat16)
        mixture = jnp.einsum(
            "hqk,khd->qhd", weights_low, value_clip, preferred_element_type=jnp.float32
        )
        return (mixture.astype(jnp.bfloat16), (highest + jnp.log(totals))[..., 0])

    return lax.map(one_clip, (query_clips, key_clips, value_clips))


def attend_backward(query_clips, key_clips, value_clips, log_sums, grad_clips, causal):

    def one_clip(operands):
        query_clip, key_clip, value_clip, log_clip, grad_clip = operands
        scores = causal_scores(query_clip, key_clip, causal)
        probs_full = jnp.exp(scores - log_clip[..., None])
        grad_probs = jnp.einsum(
            "qhd,khd->hqk", grad_clip, value_clip, preferred_element_type=jnp.float32
        )
        grad_value = jnp.einsum(
            "hqk,qhd->khd",
            probs_full.astype(jnp.bfloat16),
            grad_clip,
            preferred_element_type=jnp.float32,
        )
        centered = grad_probs - jnp.sum(probs_full * grad_probs, axis=-1, keepdims=True)
        grad_scores = (probs_full * centered).astype(jnp.bfloat16)
        grad_query = jnp.einsum(
            "hqk,khd->qhd", grad_scores, key_clip, preferred_element_type=jnp.float32
        ) * HEAD_DIM ** (-0.5)
        grad_key = jnp.einsum(
            "hqk,qhd->khd", grad_scores, query_clip, preferred_element_type=jnp.float32
        ) * HEAD_DIM ** (-0.5)
        return (
            grad_query.astype(jnp.bfloat16),
            grad_key.astype(jnp.bfloat16),
            grad_value.astype(jnp.bfloat16),
        )

    return lax.map(one_clip, (query_clips, key_clips, value_clips, log_sums, grad_clips))


def general(
    frames_in,
    text_states,
    self_query,
    self_key,
    self_value,
    self_output,
    cross_query,
    cross_key,
    cross_value,
    cross_output,
    up_weight,
    down_weight,
    first_gain,
    first_bias,
    second_gain,
    second_bias,
    third_gain,
    third_bias,
    cotangent,
):
    row_count = lax.axis_size("row")
    col_count = lax.axis_size("col")
    heads_dev = HEADS // row_count
    width_dev = heads_dev * HEAD_DIM
    tok_rows = frames_in.shape[0]
    text_rows = text_states.shape[0]
    piece_len = first_gain.shape[0]
    gain_block = jnp.stack(
        [first_gain, first_bias, second_gain, second_bias, third_gain, third_bias]
    ).reshape(1, 6 * piece_len)
    param_blocks = (
        self_query,
        self_key,
        self_value,
        self_output,
        cross_query,
        cross_key,
        cross_value,
        cross_output,
        up_weight,
        down_weight,
        gain_block,
    )

    def unpack_gains(gathered_gains):
        arranged = gathered_gains.reshape(row_count, col_count, 6, piece_len).transpose(2, 0, 1, 3)
        return arranged.reshape(6, row_count * col_count * piece_len).astype(jnp.float32)

    gathered = collect(param_blocks)
    (
        query_self,
        key_self,
        value_self,
        out_self,
        query_cross,
        key_cross,
        value_cross,
        out_cross,
        up_full,
        down_full,
    ) = gathered[:10]
    norm_params = unpack_gains(gathered[10])
    frames = frames_in.astype(jnp.float32)
    hidden_one = norm_forward(frames, norm_params[0], norm_params[1]).astype(jnp.bfloat16)
    self_q = matmul(hidden_one, query_self).astype(jnp.bfloat16)
    self_k = matmul(hidden_one, key_self).astype(jnp.bfloat16)
    self_v = matmul(hidden_one, value_self).astype(jnp.bfloat16)
    text_k = matmul(text_states, key_cross).astype(jnp.bfloat16)
    text_v = matmul(text_states, value_cross).astype(jnp.bfloat16)
    sent_rows = 3 * tok_rows + 2 * text_rows
    arranged = heads_layout(jnp.concatenate([self_q, self_k, self_v, text_k, text_v], axis=0))
    arranged = arranged.reshape(row_count, sent_rows, width_dev)
    query_clips = by_clips(arranged, 0, tok_rows, FRAMES, heads_dev)
    key_clips = by_clips(arranged, tok_rows, tok_rows, FRAMES, heads_dev)
    value_clips = by_clips(arranged, 2 * tok_rows, tok_rows, FRAMES, heads_dev)
    text_keys = by_clips(arranged, 3 * tok_rows, text_rows, TEXT, heads_dev)
    text_values = by_clips(arranged, 3 * tok_rows + text_rows, text_rows, TEXT, heads_dev)
    self_clips, self_logs = attend_forward(query_clips, key_clips, value_clips, True)
    self_mix = tokens_layout(self_clips.reshape(row_count, tok_rows, width_dev))[0]
    resid_one = frames + matmul(self_mix, out_self)
    hidden_two = norm_forward(resid_one, norm_params[2], norm_params[3]).astype(jnp.bfloat16)
    cross_q = matmul(hidden_two, query_cross).astype(jnp.bfloat16)
    cross_arranged = heads_layout(cross_q).reshape(row_count, tok_rows, width_dev)
    cross_queries = by_clips(cross_arranged, 0, tok_rows, FRAMES, heads_dev)
    cross_clips, cross_logs = attend_forward(cross_queries, text_keys, text_values, False)
    cross_mix = tokens_layout(cross_clips.reshape(row_count, tok_rows, width_dev))[0]
    resid_two = resid_one + matmul(cross_mix, out_cross)
    hidden_three = norm_forward(resid_two, norm_params[4], norm_params[5]).astype(jnp.bfloat16)
    pre_act = matmul(hidden_three, up_full)
    inner = jax.nn.gelu(pre_act, approximate=False).astype(jnp.bfloat16)
    layer_out = (resid_two + matmul(inner, down_full)).astype(jnp.bfloat16)
    gathered = collect(param_blocks)
    (
        query_self,
        key_self,
        value_self,
        out_self,
        query_cross,
        key_cross,
        value_cross,
        out_cross,
        up_full,
        down_full,
    ) = gathered[:10]
    norm_params = unpack_gains(gathered[10])
    cotan_full = cotangent.astype(jnp.float32)
    down_grad = over_tokens(inner, cotangent)
    grad_inner = by_transposed(cotangent, down_full)
    unused_gelu, gelu_pull = jax.vjp(partial(jax.nn.gelu, approximate=False), pre_act)
    grad_pre = gelu_pull(grad_inner)[0].astype(jnp.bfloat16)
    up_grad = over_tokens(hidden_three, grad_pre)
    grad_three = by_transposed(grad_pre, up_full)
    unused_three, pull_three = jax.vjp(norm_forward, resid_two, norm_params[4], norm_params[5])
    through_three, third_gain_part, third_bias_part = pull_three(grad_three)
    grad_resid_two = cotan_full + through_three
    grad_cross = grad_resid_two.astype(jnp.bfloat16)
    cross_out_grad = over_tokens(cross_mix, grad_cross)
    grad_cross_mix = by_transposed(grad_cross, out_cross).astype(jnp.bfloat16)
    grad_cross_arr = heads_layout(grad_cross_mix).reshape(row_count, tok_rows, width_dev)
    grad_cross_clips = by_clips(grad_cross_arr, 0, tok_rows, FRAMES, heads_dev)
    cq_clips, tk_clips, tv_clips = attend_backward(
        cross_queries, text_keys, text_values, cross_logs, grad_cross_clips, False
    )
    back_cross = jnp.concatenate(
        [
            cq_clips.reshape(row_count, tok_rows, width_dev),
            tk_clips.reshape(row_count, text_rows, width_dev),
            tv_clips.reshape(row_count, text_rows, width_dev),
        ],
        axis=1,
    )
    back_cross = tokens_layout(back_cross)[0]
    grad_cross_q = back_cross[:tok_rows]
    grad_text_k = back_cross[tok_rows : tok_rows + text_rows]
    grad_text_v = back_cross[tok_rows + text_rows :]
    cross_query_part = over_tokens(hidden_two, grad_cross_q)
    cross_key_part = over_tokens(text_states, grad_text_k)
    cross_value_part = over_tokens(text_states, grad_text_v)
    text_grad = by_transposed(grad_text_k, key_cross) + by_transposed(grad_text_v, value_cross)
    grad_two = by_transposed(grad_cross_q, query_cross)
    unused_two, pull_two = jax.vjp(norm_forward, resid_one, norm_params[2], norm_params[3])
    through_two, second_gain_part, second_bias_part = pull_two(grad_two)
    grad_resid_one = grad_resid_two + through_two
    grad_self = grad_resid_one.astype(jnp.bfloat16)
    self_out_grad = over_tokens(self_mix, grad_self)
    grad_self_mix = by_transposed(grad_self, out_self).astype(jnp.bfloat16)
    grad_self_arr = heads_layout(grad_self_mix).reshape(row_count, tok_rows, width_dev)
    grad_self_clips = by_clips(grad_self_arr, 0, tok_rows, FRAMES, heads_dev)
    sq_clips, sk_clips, sv_clips = attend_backward(
        query_clips, key_clips, value_clips, self_logs, grad_self_clips, True
    )
    back_self = jnp.concatenate(
        [
            sq_clips.reshape(row_count, tok_rows, width_dev),
            sk_clips.reshape(row_count, tok_rows, width_dev),
            sv_clips.reshape(row_count, tok_rows, width_dev),
        ],
        axis=1,
    )
    back_self = tokens_layout(back_self)[0]
    grad_self_q = back_self[:tok_rows]
    grad_self_k = back_self[tok_rows : 2 * tok_rows]
    grad_self_v = back_self[2 * tok_rows :]
    self_query_part = over_tokens(hidden_one, grad_self_q)
    self_key_part = over_tokens(hidden_one, grad_self_k)
    self_value_part = over_tokens(hidden_one, grad_self_v)
    grad_one = (
        by_transposed(grad_self_q, query_self)
        + by_transposed(grad_self_k, key_self)
        + by_transposed(grad_self_v, value_self)
    )
    unused_one, pull_one = jax.vjp(norm_forward, frames, norm_params[0], norm_params[1])
    through_one, first_gain_part, first_bias_part = pull_one(grad_one)
    input_grad = grad_resid_one + through_one
    norm_grads = jnp.stack(
        [
            first_gain_part,
            first_bias_part,
            second_gain_part,
            second_bias_part,
            third_gain_part,
            third_bias_part,
        ]
    )
    norm_grads = norm_grads.reshape(6, row_count, col_count, piece_len).transpose(1, 2, 0, 3)
    norm_grads = norm_grads.reshape(row_count, col_count * 6 * piece_len)
    summed = spread(
        (
            self_query_part,
            self_key_part,
            self_value_part,
            self_out_grad,
            cross_query_part,
            cross_key_part,
            cross_value_part,
            cross_out_grad,
            up_grad,
            down_grad,
            norm_grads,
        )
    )
    norm_parts = summed[10].reshape(6, piece_len)
    return (
        layer_out,
        input_grad,
        text_grad,
        summed[0],
        summed[1],
        summed[2],
        summed[3],
        summed[4],
        summed[5],
        summed[6],
        summed[7],
        summed[8],
        summed[9],
        norm_parts[0],
        norm_parts[1],
        norm_parts[2],
        norm_parts[3],
        norm_parts[4],
        norm_parts[5],
    )


NT=(((1,),(1,)),((),())); NN=(((1,),(0,)),((),())); TN=(((0,),(0,)),((),()))
def dg(a,b,dims): return lax.dot_general(a,b,dims,preferred_element_type=jnp.float32)

def feed_kernel(h_ref,cot_ref,res_ref,up_ref,down_ref,out_ref,g_ref,dup_ref,ddown_ref,ddown_blocks_ref,acc):
    i=pl.program_id(0)
    @pl.when(i==0)
    def _():
        acc[...]=res_ref[...]
        g_ref[...]=jnp.zeros_like(g_ref)
    h=h_ref[...]
    up=up_ref[:,0].reshape(h.shape[1],-1)
    blocks,wide=down_ref.shape[1],down_ref.shape[3]
    pre=dg(h,up,NN)
    cdf=0.5*(1.0+lax.erf(pre*0.7071067811865476))
    inner=(pre*cdf).astype(jnp.bfloat16)
    slope=cdf+pre*(jnp.exp(-0.5*pre*pre)*0.3989422804014327)
    grad=None
    for at in range(blocks):
        columns=slice(at*wide,(at+1)*wide)
        cot=cot_ref[:,columns]
        acc[:,columns]+=dg(inner,down_ref[0,at],NN)
        ddown=dg(inner,cot,TN).astype(ddown_ref.dtype)
        split=ddown_ref.shape[1]
        ddown_ref[0,:,columns]=ddown[:split]
        ddown_blocks_ref[0,at]=ddown[split:]
        part=dg(cot,down_ref[0,at],NT)
        grad=part if grad is None else grad+part
    gpre=(grad*slope).astype(jnp.bfloat16)
    dup_ref[:,0]=dg(h,gpre,TN).astype(dup_ref.dtype).reshape(dup_ref.shape[0],dup_ref.shape[2],dup_ref.shape[3])
    g_ref[...]+=dg(gpre,up,NT)
    @pl.when(i==pl.num_programs(0)-1)
    def _(): out_ref[...]=acc[...].astype(out_ref.dtype)

def feed(h,cot,res,up,down):
    rows,d=h.shape; chunk=down.shape[2]; strips=up.shape[3]//chunk; ff=down.shape[0]*chunk; split=chunk//2
    whole=pl.BlockSpec((rows,d),lambda i:(0,0))
    up_spec=pl.BlockSpec((up.shape[0],1,up.shape[2],chunk),lambda i:(0,i//strips,0,i%strips))
    down_spec=pl.BlockSpec((1,)+down.shape[1:],lambda i:(i,0,0,0))
    return pl.pallas_call(feed_kernel,grid=(ff//chunk,),
        in_specs=[whole,whole,whole,up_spec,down_spec],
        out_specs=[whole,whole,up_spec,pl.BlockSpec((1,split,d),lambda i:(i,0,0)),pl.BlockSpec((1,down.shape[1],chunk-split,down.shape[3]),lambda i:(i,0,0,0))],
        out_shape=[jax.ShapeDtypeStruct((rows,d),jnp.bfloat16),jax.ShapeDtypeStruct((rows,d),jnp.float32),jax.ShapeDtypeStruct(up.shape,jnp.bfloat16),jax.ShapeDtypeStruct((down.shape[0],split,d),jnp.bfloat16),jax.ShapeDtypeStruct((*down.shape[:2],chunk-split,down.shape[3]),jnp.bfloat16)],
        scratch_shapes=[pltpu.VMEM((rows,d),jnp.float32)],
        compiler_params=pltpu.CompilerParams(vmem_limit_bytes=56<<20),
        cost_estimate=pl.CostEstimate(flops=12*rows*d*ff,bytes_accessed=8*d*ff+16*rows*d,transcendentals=2*rows*ff))(h,cot,res,up,down)


MESH = pl.DeviceIdType.MESH
ORDERS = ("xzy", "yzx", "xzy", "yzx", "zxy", "zyx")


class Place:
    def __init__(self):
        row, col = lax.axis_index("row"), lax.axis_index("col")
        self.z, self.y, self.x, self.k = row // 2, row % 2, col // 2, col % 2
        self.along = lax.axis_size("row") // 2

    def device(self, dz=0, y=False, x=False, k=False):
        other_y = 1 - self.y if y else self.y
        other_x = 1 - self.x if x else self.x
        other_k = 1 - self.k if k else self.k
        return ((self.z + dz) * 2 + other_y, other_x * 2 + other_k)

    def across(self, axis):
        return self.device(y=axis == "y", x=axis == "x", k=axis == "k")

    def greet(self):
        barrier = pltpu.get_barrier_semaphore()
        for axis in "xyk":
            pl.semaphore_signal(barrier, inc=1, device_id=self.across(axis), device_id_type=MESH)

        @pl.when(self.z > 0)
        def _():
            pl.semaphore_signal(barrier, inc=1, device_id=self.device(dz=-1), device_id_type=MESH)

        @pl.when(self.z + 1 < self.along)
        def _():
            pl.semaphore_signal(barrier, inc=1, device_id=self.device(dz=1), device_id_type=MESH)

        below = jnp.where(self.z > 0, 1, 0)
        above = jnp.where(self.z + 1 < self.along, 1, 0)
        pl.semaphore_wait(barrier, 3 + below + above)


def when(condition, run):
    if condition is None:
        run()
    else:
        pl.when(condition)(run)


def in_turn(units, lag):
    ready = [(lag * at, at) for at in range(len(units))]
    while ready:
        turn, at = min(ready)
        ready.remove((turn, at))
        if next(units[at], units) is not units:
            ready.append((turn + 1, at))
        yield


class Gather:
    def __init__(self, place, block, full, strip, order, send, recv):
        self.place, self.block, self.full, self.strip = place, block, full, strip
        turn = order.index("z")
        self.before, self.after = order[:turn], order[turn + 1 :]
        self.send, self.recv, self.used, self.sent, self.started = send, recv, 0, 0, []

    def region(self, z, y, x):
        part, start, count = self.strip
        column = (x * 2 + self.place.k) * self.block.shape[-1] + start
        return self.full.at[z, y, part, :, pl.ds(pl.multiple_of(column, 128), count)]

    def held(self, done, z):
        y = slice(None) if "y" in done else self.place.y
        return [self.region(z, y, x) for x in (range(2) if "x" in done else [self.place.x])]

    def pairs(self, done, z, first):
        if first:
            part, start, count = self.strip
            place = self.place
            return [(self.block.at[part, :, pl.ds(start, count)], self.region(place.z, place.y, place.x))]
        return [(region, region) for region in self.held(done, z)]

    def semaphore(self):
        self.used += 2
        return self.used - 2

    def copies(self, device, pairs, semaphore, send=0):
        return [
            pltpu.make_async_remote_copy(
                src_ref=source, dst_ref=target, send_sem=self.send.at[send + at],
                recv_sem=self.recv.at[semaphore + at], device_id=device, device_id_type=MESH)
            for at, (source, target) in enumerate(pairs)
        ]

    def start(self, device, pairs, wide, condition, semaphore):
        send = self.sent
        self.sent += wide

        def make():
            return self.copies(device(), pairs(), semaphore, send)

        when(condition(), lambda: [copy.start() for copy in make()] and None)
        self.started.append((condition, make))
        return condition, make

    def arrive(self, sent):
        condition, make = sent
        when(condition(), lambda: [copy.wait_recv() for copy in make()] and None)

    def stages(self):
        place, along = self.place, self.place.along
        done = []

        def always():
            return None

        def width(axes):
            return 2 if "x" in axes else 1

        for axis in self.before:
            axes = tuple(done)
            sent = self.start(
                lambda axis=axis: place.across(axis), lambda axes=axes: self.pairs(axes, place.z, not axes),
                width(axes), always, self.semaphore())
            yield
            self.arrive(sent)
            done.append(axis)
        first = not done
        axes_z = tuple(done)
        from_left = [self.semaphore() for _ in range(along - 1)]
        from_right = [self.semaphore() for _ in range(along - 1)]

        def pass_on(turn, step):
            axes = axes_z + tuple(self.after[:turn])
            sent = []
            for way in ((-1, 1) if step else (0,)):

                def inside(way=way):
                    z = place.z + way * step
                    return (z >= 0) & (z < along) if way else None

                sent.append(self.start(
                    lambda: place.across(self.after[turn]),
                    lambda way=way: self.pairs(axes, place.z + way * step, not axes and not step),
                    width(axes), inside, self.semaphore()))
            return turn, step, sent

        def step_out(step):
            self.start(
                lambda: place.device(dz=1), lambda: self.pairs(axes_z, place.z - (step - 1), first and step == 1),
                width(axes_z), lambda: (place.z - (step - 1) >= 0) & (place.z + 1 < along), from_left[step - 1])
            self.start(
                lambda: place.device(dz=-1), lambda: self.pairs(axes_z, place.z + (step - 1), first and step == 1),
                width(axes_z), lambda: (place.z + (step - 1) < along) & (place.z > 0), from_right[step - 1])

        def step_in(step):
            for way, semaphore in ((-1, from_left), (1, from_right)):
                z = place.z + way * step
                self.arrive((
                    lambda: (z >= 0) & (z < along),
                    lambda: self.copies(place.across("k"), self.pairs(axes_z, z, False), semaphore[step - 1])))

        step_out(1)
        waiting = [pass_on(0, 0)] if self.after else []
        for step in range(1, along + len(self.after)):
            yield
            if step < along:
                step_in(step)
                if step + 1 < along:
                    step_out(step + 1)
            following = []
            for turn, at, sent in waiting:
                for one in sent:
                    self.arrive(one)
                if turn + 1 < len(self.after):
                    following.append(pass_on(turn + 1, at))
            if self.after and step < along:
                following.append(pass_on(0, step))
            waiting = following
        sent = self.start(
            lambda: place.across("k"), lambda: [(r, r) for r in [self.region(slice(None), slice(None), x) for x in range(2)]],
            2, always, self.semaphore())
        yield
        self.arrive(sent)

    def finish(self):
        for condition, make in self.started:
            when(condition(), lambda make=make: [copy.wait_send() for copy in make()] and None)


class OwnBlocks:
    def __init__(self, place, blocks, fulls, local):
        self.place, self.blocks, self.fulls, self.local = place, blocks, fulls, local

    def copies(self):
        place = self.place
        for at, (block, full) in enumerate(zip(self.blocks, self.fulls)):
            width = block.shape[-1]
            columns = pl.ds(pl.multiple_of((place.x * 2 + place.k) * width, 128), width)
            yield pltpu.make_async_copy(block, full.at[place.z, place.y, :, :, columns], self.local.at[at])

    def start(self):
        for copy in self.copies():
            copy.start()

    def wait(self):
        for copy in self.copies():
            copy.wait()


def gathers_of(place, units, blocks, fulls, send, recv):
    return [
        Gather(place, blocks[which], fulls[which], strip, order, send.at[at], recv.at[at])
        for at, (which, strip, order) in enumerate(units)
    ]


def gather_kernel(units, count, *refs):
    blocks, fulls = refs[:count], refs[count : 2 * count]
    send, recv, local = refs[2 * count :]
    place = Place()
    place.greet()
    own = OwnBlocks(place, blocks, fulls, local)
    own.start()
    gathers = gathers_of(place, units, blocks, fulls, send, recv)
    waited = False
    for unused in in_turn([gather.stages() for gather in gathers], 0.0):
        if not waited:
            own.wait()
            waited = True
    for gather in gathers:
        gather.finish()


def gather_units(blocks, least, orders):
    strips = []
    for which, block in enumerate(blocks):
        wide = min(least, block.shape[-1])
        for part in range(block.shape[0]):
            for start in range(0, block.shape[-1], wide):
                strips.append((which, (part, start, wide)))
    return [strip + (orders[at % len(orders)],) for at, strip in enumerate(strips)]


def gather_plan(blocks, least, orders):
    along, cols = lax.axis_size("row") // 2, lax.axis_size("col")
    units = gather_units(blocks, least, orders)
    fulls = [jax.ShapeDtypeStruct((along, 2) + b.shape[:2] + (cols * b.shape[2],), b.dtype) for b in blocks]
    scratch = [
        pltpu.SemaphoreType.DMA((len(units), 8 * along)),
        pltpu.SemaphoreType.DMA((len(units), 12 * along)),
        pltpu.SemaphoreType.DMA((len(blocks),)),
    ]
    return fulls, units, scratch


def gather_blocks(blocks, collective_id, least):
    fulls, units, scratch = gather_plan(blocks, least, ORDERS)
    count = len(blocks)
    anywhere = pl.BlockSpec(memory_space=pl.ANY)
    return pl.pallas_call(
        functools.partial(gather_kernel, units, count),
        out_shape=fulls,
        in_specs=[anywhere] * count,
        out_specs=[anywhere] * count,
        scratch_shapes=scratch,
        compiler_params=pltpu.CompilerParams(collective_id=collective_id, has_side_effects=True),
        cost_estimate=pl.CostEstimate(flops=0, bytes_accessed=4 * sum(f.size for f in fulls), transcendentals=0),
    )(*blocks)


def add_blocks(total, extra, leading):
    def one(at, unused):
        place = []
        for size in leading[::-1]:
            place.append(at % size)
            at = at // size
        place = tuple(place[::-1])
        total[place] = total[place] + extra[place]
        return unused

    if not leading:
        total[...] = total[...] + extra[...]
        return
    count = 1
    for size in leading:
        count *= size
    lax.fori_loop(0, count, one, 0)


class Scatter:
    def __init__(self, place, grad, out, strip, width, order, slots, send, recv, local):
        self.place, self.grad, self.out, self.strip, self.width = place, grad, out, strip, width
        self.order = order[::-1]
        self.total, self.other_core, self.halves, self.steps = slots
        self.send, self.recv, self.local = send, recv, local
        self.used, self.started = 0, []

    def region(self, x, k):
        part, start, count = self.strip
        column = (x * 2 + k) * self.width + start
        return self.grad.at[:, :, part, :, pl.ds(pl.multiple_of(column, 128), count)]

    def copy(self, device, source, target, semaphore):
        return pltpu.make_async_remote_copy(
            src_ref=source, dst_ref=target, send_sem=self.send.at[semaphore], recv_sem=self.recv.at[semaphore],
            device_id=device, device_id_type=MESH)

    def reserve(self, count):
        self.used += count
        return self.used - count

    def start(self, make, condition=lambda: None):
        when(condition(), lambda: make().start())
        self.started.append((condition, make))

    def stages(self):
        place, along = self.place, self.place.along
        rows, columns = self.total.shape[-2:]
        core = self.reserve(2)

        def own(x):
            return pltpu.make_async_copy(self.region(x, place.k), self.total.at[:, :, x], self.local.at[x])

        def swapped(x):
            return self.copy(
                place.across("k"), self.region(x, 1 - place.k), self.other_core.at[:, :, x], core + x)

        for x in range(2):
            own(x).start()
            self.start(functools.partial(swapped, x))
        yield
        for x in range(2):
            own(x).wait()
            swapped(x).wait_recv()
        add_blocks(self.total, self.other_core, (along, 2, 2))
        left = {"z": slice(None), "y": slice(None), "x": slice(None)}
        at = {"y": place.y, "x": place.x}

        def view(ref, kept=None, **places):
            return ref.at[tuple({**(left if kept is None else kept), **places}[axis] for axis in "zyx")]

        def sizes():
            return tuple(size for axis, size in zip("zyx", (along, 2, 2)) if isinstance(left[axis], slice))

        exchanges = 0
        for axis in self.order:
            if axis == "z":
                shape = tuple(2 for name in "yx" if isinstance(left[name], slice))
                inner = tuple(slice(None) if isinstance(left[name], slice) else 0 for name in "yx")

                def landing(side, step, inner=inner):
                    return self.steps.at[(side, step) + inner]

                base = self.reserve(2 * along)
                right, leftward = range(base, base + along), range(base + along, base + 2 * along)
                for step in range(along):
                    if step:
                        yield
                    for way, names, first in ((1, right, place.z), (-1, leftward, along - 1 - place.z)):
                        goal = along - 1 - step + place.z if way == 1 else step - along + 1 + place.z
                        side = 0 if way == 1 else 1
                        if step:
                            arrived = landing(side, step - 1)

                            def take(arrived=arrived, goal=goal, side=side, step=step, names=names):
                                self.copy(place.across("k"), arrived, arrived, names[step - 1]).wait_recv()
                                add_blocks(view(self.total, z=goal), arrived, shape)

                            pl.when((first >= 1) & (first <= step))(take)
                        if step < along - 1:
                            kept = dict(left)

                            def onward(way=way, step=step, kept=kept, landing=landing, side=side, names=names):
                                goal = along - 1 - step + place.z if way == 1 else step - along + 1 + place.z
                                source = view(self.total, kept, z=jnp.clip(goal, 0, along - 1))
                                return self.copy(place.device(dz=way), source, landing(side, step), names[step])

                            def reached(way=way, step=step):
                                first = place.z if way == 1 else along - 1 - place.z
                                return (first <= step) & (first < along - 1)

                            self.start(onward, reached)
                left["z"] = place.z
            else:
                landing = self.halves[exchanges]
                exchanges += 1
                inner = tuple(slice(None) if isinstance(left[name], slice) and name != axis else 0 for name in "zyx")
                semaphore, kept = self.reserve(1), dict(left)

                def swap(axis=axis, kept=kept, landing=landing, inner=inner, semaphore=semaphore):
                    source = view(self.total, kept, **{axis: 1 - at[axis]})
                    return self.copy(place.across(axis), source, landing.at[inner], semaphore)

                self.start(swap)
                yield
                swap().wait_recv()
                left[axis] = at[axis]
                add_blocks(view(self.total), landing.at[inner], sizes())
        part, start, count = self.strip
        self.out[part, :, start : start + count] = view(self.total)[...].astype(jnp.float32)

    def finish(self):
        for condition, make in self.started:
            when(condition(), lambda make=make: make().wait_send())


def scatter_slots(along, rows, columns, order):
    left = {"z": along, "y": 2, "x": 2}
    whole = (along, 2, 2, rows, columns)
    shapes = [whole, whole]
    steps = None
    for axis in order[::-1]:
        if axis == "z":
            steps = (2, along - 1, left["y"], left["x"], rows, columns)
        left[axis] = 1
        if axis != "z":
            shapes.append((left["z"], left["y"], left["x"], rows, columns))
    return shapes + [steps]


def scatters_of(place, units, grads, outs, send, recv, local, slots):
    scatters = []
    for at, (which, strip, order) in enumerate(units):
        total, other_core, first, second, steps = slots[5 * at : 5 * at + 5]
        scatters.append(
            Scatter(place, grads[which], outs[which], strip, outs[which].shape[-1], order,
                    (total, other_core, (first, second), steps), send.at[at], recv.at[at], local.at[at]))
    return scatters


def scatter_kernel(units, count, *refs):
    grads, outs = refs[:count], refs[count : 2 * count]
    place = Place()
    place.greet()
    scatters = scatters_of(place, units, grads, outs, *refs[2 * count : 2 * count + 3], refs[2 * count + 3 :])
    for unused in in_turn([scatter.stages() for scatter in scatters], 0.25):
        pass
    for scatter in scatters:
        scatter.finish()


def scatter_plan(grads, least, orders):
    along, cols = lax.axis_size("row") // 2, lax.axis_size("col")
    blocks = [jax.ShapeDtypeStruct(g.shape[2:4] + (g.shape[4] // cols,), jnp.float32) for g in grads]
    units = gather_units(blocks, least, orders)
    scratch = [pltpu.SemaphoreType.DMA((len(units), 2 * along + 4))] * 2 + [pltpu.SemaphoreType.DMA((len(units), 2))]
    for which, strip, order in units:
        shapes = scatter_slots(along, blocks[which].shape[1], strip[2], order)
        scratch += [pltpu.VMEM(shape, jnp.bfloat16) for shape in shapes]
    return blocks, units, scratch


def scatter_blocks(grads, collective_id, least):
    blocks, units, scratch = scatter_plan(grads, least, ("xyz", "yxz", "zxy", "zyx", "xzy", "yzx"))
    count = len(grads)
    anywhere = pl.BlockSpec(memory_space=pl.ANY)
    return pl.pallas_call(
        functools.partial(scatter_kernel, units, count),
        out_shape=blocks,
        in_specs=[anywhere] * count,
        out_specs=[pl.BlockSpec(memory_space=pltpu.VMEM)] * count,
        scratch_shapes=scratch,
        compiler_params=pltpu.CompilerParams(
            collective_id=collective_id, has_side_effects=True, vmem_limit_bytes=60 << 20),
        cost_estimate=pl.CostEstimate(
            flops=sum(g.size for g in grads), bytes_accessed=4 * sum(g.size for g in grads), transcendentals=0),
    )(*grads)


ACROSS = ("yzx", "yzx", "yzx", "yzx", "yxz")


def attend_rows(q, key_ref, value_ref, spans, diagonal, put):
    low = lax.broadcasted_iota(jnp.int32, (1, 128), 1) < HEAD_DIM
    mixed, logs = [], []
    for h in range(2):
        mine = low if h == 0 else jnp.logical_not(low)
        qh = jnp.where(mine, q, jnp.bfloat16(0))
        scores = []
        for at, length in spans:
            s = dg(qh, key_ref[at : at + length, :], NT)
            if at == diagonal:
                allowed = lax.broadcasted_iota(jnp.int32, s.shape, 0) >= lax.broadcasted_iota(jnp.int32, s.shape, 1)
                s = jnp.where(allowed, s, -1e30)
            scores.append(s)
        top = functools.reduce(jnp.maximum, [jnp.max(s, axis=1, keepdims=True) for s in scores])
        out = None
        for (at, length), s in zip(spans, scores):
            p = jnp.exp(s - top).astype(jnp.bfloat16)
            value = value_ref[at : at + length, :]
            part = dg(p, jnp.where(mine, value, jnp.ones_like(value)), NN)
            out = part if out is None else out + part
        total = out[:, HEAD_DIM : HEAD_DIM + 1] if h == 0 else out[:, 0:1]
        mixed.append(out / total)
        logs.append(top + jnp.log(total))
    put(logs)
    return jnp.where(low, mixed[0], mixed[1])


def rows_of(lanes_ref, first):
    picked = lax.broadcasted_iota(jnp.int32, (8, 128), 0) + first == lax.broadcasted_iota(jnp.int32, (8, 128), 1)
    return lax.dot_general(
        picked.astype(jnp.float32), lanes_ref[...], NT, precision=lax.Precision.HIGHEST,
        preferred_element_type=jnp.float32)


def pair_attend_kernel(tile, units, count, events, *refs):
    q_ref, k_ref, v_ref, q_any, k_any, v_any = refs[:6]
    blocks = refs[6 : 6 + count]
    mix_ref, logs_ref, fq_out, fk_out, fv_out = refs[6 + count : 11 + count]
    fulls = refs[11 + count : 11 + 2 * count]
    (near, near_logs, far_q, far_k, far_v, far, far_logs, got, far_rows, got_rows,
     send, recv, local, keep) = refs[11 + 2 * count : 25 + 2 * count]
    gather_send, gather_recv, gather_local = refs[25 + 2 * count :]
    step = pl.program_id(0)
    place = Place()
    own = OwnBlocks(place, blocks, fulls, gather_local)
    gathers = gathers_of(place, units, blocks, fulls, gather_send, gather_recv)
    turns = in_turn([gather.stages() for gather in gathers], 0.25)
    pairs = near.shape[0]
    fars = pairs // 2
    rows = q_ref.shape[0]
    first, second = place.y == 0, place.y == 1
    partner = place.across("y")
    lane = lax.broadcasted_iota(jnp.int32, (1, 128), 1)
    scale = jnp.bfloat16(HEAD_DIM**-0.5)
    plan = ((q_any, far_q, False), (k_any, far_k, True), (v_any, far_v, True))

    def columns(pair):
        return pl.ds(pl.multiple_of(pair * 128, 128), 128)

    def sending(which, j):
        array, landing, by_first = plan[which]
        return pltpu.make_async_remote_copy(
            src_ref=array.at[:, columns(j if by_first else fars + j)], dst_ref=landing.at[j],
            send_sem=send.at[which, j], recv_sem=recv.at[which, j], device_id=partner, device_id_type=MESH)

    def keeping(which, j):
        array, landing, by_first = plan[which]
        return pltpu.make_async_copy(
            array.at[:, columns(fars + j if by_first else j)], landing.at[j], local.at[which, j])

    def mixture_out(j):
        return pltpu.make_async_remote_copy(
            src_ref=far.at[j], dst_ref=got.at[j], send_sem=send.at[3, j], recv_sem=recv.at[3, j],
            device_id=partner, device_id_type=MESH)

    def logs_out():
        return pltpu.make_async_remote_copy(
            src_ref=far_rows, dst_ref=got_rows, send_sem=send.at[4, 0], recv_sem=recv.at[4, 0],
            device_id=partner, device_id_type=MESH)

    def saving(which):
        return pltpu.make_async_copy(plan[which][1], (fq_out, fk_out, fv_out)[which], keep.at[which])

    @pl.when(step == 0)
    def _():
        place.greet()
        own.start()
        near_logs[...] = jnp.zeros_like(near_logs)
        far_logs[...] = jnp.zeros_like(far_logs)
        for j in range(fars):
            for which in range(3):

                @pl.when(first if plan[which][2] else second)
                def _(which=which, j=j):
                    keeping(which, j).start()

    @pl.when((step % 3 == 0) & (step < 3 * fars))
    def _():
        j = step // 3
        for which in range(3):

            @pl.when(first if plan[which][2] else second)
            def _(which=which):
                @pl.when(j > 0)
                def _():
                    sending(which, j - 1).wait_send()

                sending(which, j).start()

    for at, number in enumerate(events):

        @pl.when(step == at)
        def _(at=at, number=number):
            if at == 0:
                own.wait()
            for unused in range(number):
                next(turns, None)

    @pl.when(step < pairs)
    def _():
        for start in range(0, rows, tile):
            n = min(tile, rows - start)

            def put(logs, start=start, n=n):
                kept = near_logs[start : start + n, :]
                for h in range(2):
                    kept = jnp.where(lane == 2 * step + h, logs[h], kept)
                near_logs[start : start + n, :] = kept

            spans = ([(0, start)] if start else []) + [(start, n)]
            near[step, start : start + n, :] = attend_rows(
                q_ref[start : start + n, :] * scale, k_ref, v_ref, spans, start, put)

    @pl.when((step >= pairs) & (step < pairs + fars))
    def _():
        j = step - pairs
        for which in range(3):
            by_first = plan[which][2]

            @pl.when(first if by_first else second)
            def _(which=which):
                keeping(which, j).wait()

            @pl.when(second if by_first else first)
            def _(which=which):
                sending(which, j).wait_recv()

        base = jnp.where(first, 2 * fars, 0)
        for start in range(0, rows, tile):
            n = min(tile, rows - start)

            def put(logs, start=start, n=n):
                kept = far_logs[start : start + n, :]
                for h in range(2):
                    kept = jnp.where(lane == base + 2 * j + h, logs[h], kept)
                far_logs[start : start + n, :] = kept

            far[j, start : start + n, :] = attend_rows(
                far_q[j, start : start + n, :] * scale, far_k.at[j], far_v.at[j], [(0, rows)], None, put
            ).astype(far.dtype)

        @pl.when(first)
        def _():
            mixture_out(j).start()

    @pl.when(step == pairs + fars)
    def _():
        for which in range(3):
            saving(which).start()

        @pl.when(first)
        def _():
            far_rows[...] = rows_of(far_logs, 2 * fars)
            logs_out().start()
            for pair in range(pairs):
                mix_ref[:, pair * 128 : (pair + 1) * 128] = near[pair].astype(mix_ref.dtype)
            logs_ref[...] = near_logs[...]
            logs_out().wait_send()
            for j in range(fars):
                mixture_out(j).wait_send()
            for which in (1, 2):
                sending(which, fars - 1).wait_send()

        @pl.when(second)
        def _():
            logs_out().wait_recv()
            for j in range(fars):
                mixture_out(j).wait_recv()
            sending(0, fars - 1).wait_send()
            spread_out = (lax.broadcasted_iota(jnp.int32, (8, 128), 0) + 2 * fars == lane).astype(jnp.float32)
            theirs = lax.dot_general(
                got_rows[...], spread_out, TN, precision=lax.Precision.HIGHEST, preferred_element_type=jnp.float32)
            logs_far = far_logs[...] + theirs
            logs_near = near_logs[...]
            top = jnp.maximum(logs_near, logs_far)
            total = top + jnp.log(jnp.exp(logs_near - top) + jnp.exp(logs_far - top))
            logs_ref[...] = total
            share = jnp.exp(logs_near - total)
            low = lane < HEAD_DIM
            for pair in range(pairs):
                part = jnp.where(low, share[:, 2 * pair : 2 * pair + 1], share[:, 2 * pair + 1 : 2 * pair + 2])
                other = (far[pair] if pair < fars else got[pair - fars]).astype(jnp.float32)
                mix_ref[:, pair * 128 : (pair + 1) * 128] = (other + (near[pair] - other) * part).astype(mix_ref.dtype)

        for which in range(3):
            saving(which).wait()
        for unused in turns:
            pass
        for gather in gathers:
            gather.finish()


def pair_attend(q, k, v, blocks, collective_id, events, tile=384):
    rows, width = q.shape
    pairs = width // 128
    fars = pairs // 2
    block = pl.BlockSpec((rows, 128), lambda i: (0, jnp.minimum(i, pairs - 1)))
    anywhere = pl.BlockSpec(memory_space=pl.ANY)
    kept = jax.ShapeDtypeStruct((fars, rows, 128), jnp.bfloat16)
    half = pltpu.VMEM((fars, rows, 128), jnp.bfloat16)
    fulls, units, scratch = gather_plan(blocks, 256, ACROSS)
    count = len(blocks)
    result = pl.pallas_call(
        functools.partial(pair_attend_kernel, tile, units, count, events),
        grid=(pairs + fars + 1,),
        in_specs=[block] * 3 + [anywhere] * (3 + count),
        out_specs=[pl.BlockSpec((rows, width), lambda i: (0, 0)), pl.BlockSpec((rows, 128), lambda i: (0, 0))] + [anywhere] * (3 + count),
        out_shape=[
            jax.ShapeDtypeStruct((rows, width), jnp.bfloat16), jax.ShapeDtypeStruct((rows, 128), jnp.float32), kept, kept, kept, *fulls],
        scratch_shapes=[
            pltpu.VMEM((pairs, rows, 128), jnp.float32), pltpu.VMEM((rows, 128), jnp.float32),
            half, half, half, half, pltpu.VMEM((rows, 128), jnp.float32), half,
            pltpu.VMEM((8, rows), jnp.float32), pltpu.VMEM((8, rows), jnp.float32),
            pltpu.SemaphoreType.DMA((5, fars)), pltpu.SemaphoreType.DMA((5, fars)),
            pltpu.SemaphoreType.DMA((3, fars)), pltpu.SemaphoreType.DMA((3,)), *scratch,
        ],
        compiler_params=pltpu.CompilerParams(
            collective_id=collective_id, has_side_effects=True, vmem_limit_bytes=48 << 20),
        cost_estimate=pl.CostEstimate(
            flops=4 * rows * rows * width, bytes_accessed=16 * rows * width, transcendentals=rows * rows * pairs * 2),
    )(q, k, v, q, k, v, *blocks)
    return result[:5], result[5:]


def back_pair(tile, causal, q_ref, k_ref, v_ref, do_ref, stats, acc, put):
    rows, keys = q_ref.shape[0], k_ref.shape[0]
    low = lax.broadcasted_iota(jnp.int32, (1, 128), 1) < HEAD_DIM
    acc[...] = jnp.zeros_like(acc)
    for start in range(0, keys, tile):
        n = min(tile, keys - start)
        k = k_ref[start : start + n, :] * jnp.bfloat16(HEAD_DIM**-0.5)
        v = v_ref[start : start + n, :]
        spans = [(0, rows)]
        if causal:
            spans = [(start, n)] + ([(start + n, rows - start - n)] if start + n < rows else [])
        dks, dvs = [], []
        for h in range(2):
            mine = low if h == 0 else jnp.logical_not(low)
            kh, vh = jnp.where(mine, k, jnp.bfloat16(0)), jnp.where(mine, v, jnp.bfloat16(0))
            dk = dv = None
            for at, length in spans:
                qs, do = q_ref[at : at + length, :], do_ref[at : at + length, :]
                p = jnp.exp(dg(kh, qs, NT) - stats[h : h + 1, at : at + length])
                if causal and at == start:
                    allowed = lax.broadcasted_iota(jnp.int32, p.shape, 0) <= lax.broadcasted_iota(jnp.int32, p.shape, 1)
                    p = jnp.where(allowed, p, 0.0)
                ds = (p * (dg(vh, do, NT) - stats[2 + h : 3 + h, at : at + length])).astype(jnp.bfloat16)
                a, b = dg(p.astype(jnp.bfloat16), do, NN), dg(ds, qs, NN)
                dv = a if dv is None else dv + a
                dk = b if dk is None else dk + b
                acc[at : at + length, :] += dg(ds, kh, TN)
            dks.append(dk)
            dvs.append(dv)
        put(start, n, jnp.where(low, dks[0], dks[1]) * HEAD_DIM**-0.5, jnp.where(low, dvs[0], dvs[1]))


def pair_stats(pair, mix_ref, do_ref, logs_ref):
    lane = lax.broadcasted_iota(jnp.int32, (8, 128), 1)
    line = lax.broadcasted_iota(jnp.int32, (8, 128), 0)
    picked = ((line < 2) & (line + 2 * pair == lane)).astype(jnp.float32)
    halves = (((line == 2) & (lane < HEAD_DIM)) | ((line == 3) & (lane >= HEAD_DIM))).astype(jnp.float32)
    products = mix_ref[...].astype(jnp.float32) * do_ref[...].astype(jnp.float32)
    logs = lax.dot_general(
        picked, logs_ref[...], NT, precision=lax.Precision.HIGH, preferred_element_type=jnp.float32)
    return logs + lax.dot_general(
        halves, products, NT, precision=lax.Precision.HIGH, preferred_element_type=jnp.float32)


def both_heads(array):
    low = lax.broadcasted_iota(jnp.int32, (1, 128), 1) < HEAD_DIM
    zero = jnp.zeros_like(array)
    return jnp.concatenate([jnp.where(low, array, zero), jnp.where(low, zero, array)], axis=0)


def one_head_each(array):
    low = lax.broadcasted_iota(jnp.int32, (1, 128), 1) < HEAD_DIM
    half = array.shape[0] // 2
    return jnp.where(low, array[:half], array[half:])


def cross_kernel(q_ref, k_ref, v_ref, mix_ref, logs_ref):
    pair = pl.program_id(0)
    keys = k_ref.shape[0]
    lane = lax.broadcasted_iota(jnp.int32, (1, 128), 1)
    lower = lax.broadcasted_iota(jnp.int32, (1, 2 * keys), 1) < keys

    @pl.when(pair == 0)
    def _():
        logs_ref[...] = jnp.zeros_like(logs_ref)

    scores = dg(q_ref[...] * jnp.bfloat16(HEAD_DIM**-0.5), both_heads(k_ref[...]), NT)
    tops = [
        jnp.max(jnp.where(lower if h == 0 else jnp.logical_not(lower), scores, -1e30), axis=1, keepdims=True) for h in range(2)
    ]
    powers = jnp.exp(scores - jnp.where(lower, tops[0], tops[1])).astype(jnp.bfloat16)
    values = both_heads(v_ref[...])
    ones = both_heads(jnp.ones(v_ref.shape, v_ref.dtype))
    out = dg(powers, jnp.concatenate([values, ones], axis=1), NN)
    totals = out[:, 128:]
    mix_ref[...] = (out[:, :128] / totals).astype(mix_ref.dtype)
    sums = jnp.log(totals)
    logs = logs_ref[...]
    for h in range(2):
        logs = jnp.where(lane == 2 * pair + h, tops[h] + sums[:, h * HEAD_DIM : h * HEAD_DIM + 1], logs)
    logs_ref[...] = logs


def cross(q, k, v):
    rows, width = q.shape
    keys = k.shape[0]
    long, short = pl.BlockSpec((rows, 128), lambda i: (0, i)), pl.BlockSpec((keys, 128), lambda i: (0, i))
    return pl.pallas_call(
        cross_kernel,
        grid=(width // 128,),
        in_specs=[long, short, short],
        out_specs=[long, pl.BlockSpec((rows, 128), lambda i: (0, 0))],
        out_shape=[jax.ShapeDtypeStruct((rows, width), jnp.bfloat16), jax.ShapeDtypeStruct((rows, 128), jnp.float32)],
        compiler_params=pltpu.CompilerParams(vmem_limit_bytes=40 << 20),
        cost_estimate=pl.CostEstimate(
            flops=4 * rows * keys * width, bytes_accessed=6 * rows * width, transcendentals=rows * keys * width // HEAD_DIM),
    )(q, k, v)


def cross_back_kernel(q_ref, k_ref, v_ref, do_ref, mix_ref, logs_ref, dq_ref, dk_ref, dv_ref):
    keys = k_ref.shape[0]
    stats = pair_stats(pl.program_id(0), mix_ref, do_ref, logs_ref)
    upper = lax.broadcasted_iota(jnp.int32, (2 * keys, 1), 0) < keys
    k, v, do = both_heads(k_ref[...] * jnp.bfloat16(HEAD_DIM**-0.5)), both_heads(v_ref[...]), do_ref[...]
    p = jnp.exp(dg(k, q_ref[...], NT) - jnp.where(upper, stats[0:1, :], stats[1:2, :]))
    ds = (p * (dg(v, do, NT) - jnp.where(upper, stats[2:3, :], stats[3:4, :]))).astype(jnp.bfloat16)
    dv_ref[...] = one_head_each(dg(p.astype(jnp.bfloat16), do, NN)).astype(dv_ref.dtype)
    dk_ref[...] = (one_head_each(dg(ds, q_ref[...], NN)) * HEAD_DIM**-0.5).astype(dk_ref.dtype)
    dq_ref[...] = dg(ds, k, TN).astype(dq_ref.dtype)


def cross_back(q, k, v, do, mix, logs):
    rows, width = q.shape
    keys = k.shape[0]
    long, short = pl.BlockSpec((rows, 128), lambda i: (0, i)), pl.BlockSpec((keys, 128), lambda i: (0, i))
    return pl.pallas_call(
        cross_back_kernel,
        grid=(width // 128,),
        in_specs=[long, short, short, long, long, pl.BlockSpec((rows, 128), lambda i: (0, 0))],
        out_specs=[long, short, short],
        out_shape=[jax.ShapeDtypeStruct(a.shape, jnp.bfloat16) for a in (q, k, v)],
        compiler_params=pltpu.CompilerParams(vmem_limit_bytes=40 << 20),
        cost_estimate=pl.CostEstimate(
            flops=10 * rows * keys * width, bytes_accessed=10 * rows * width, transcendentals=rows * keys * width // HEAD_DIM),
    )(q, k, v, do, mix, logs)


def pair_back_kernel(tile, far_tile, units, count, events, *refs):
    q_ref, k_ref, v_ref, do_ref, mix_ref, logs_ref, do_any, fq_any, fk_any, fv_any = refs[:10]
    grads, (dq_ref, dk_ref, dv_ref) = refs[10 : 10 + count], refs[10 + count : 13 + count]
    sums = refs[13 + count : 13 + 2 * count]
    (near, acc, stats, far_stats, used_stats, far_q, far_k, far_v, far_do, far_dq, far_dk, far_dv, got_q, got_k, got_v,
     send, recv, local, do_local) = refs[13 + 2 * count : 32 + 2 * count]
    scatter_refs = refs[32 + 2 * count :]
    step = pl.program_id(0)
    place = Place()
    pairs = near.shape[1]
    fars = pairs // 2
    first, second = place.y == 0, place.y == 1
    partner = place.across("y")

    def columns(pair):
        return pl.ds(pl.multiple_of(pair * 128, 128), 128)

    def remote(source, target, which, j):
        return pltpu.make_async_remote_copy(
            src_ref=source, dst_ref=target, send_sem=send.at[which, j], recv_sem=recv.at[which, j],
            device_id=partner, device_id_type=MESH)

    def grad_over(j):
        return remote(do_any.at[:, columns(fars + j)], far_do.at[j], 0, j)

    def grad_kept(j):
        return pltpu.make_async_copy(do_any.at[:, columns(j)], far_do.at[j], do_local.at[j])

    def stats_over():
        return remote(stats.at[pl.ds(fars, fars)], far_stats, 4, 0)

    def back_over(which, j):
        source, target = ((far_dq, got_q), (far_dk, got_k), (far_dv, got_v))[which]
        return remote(source.at[j], target.at[j], 1 + which, j)

    def far_in(which):
        source, target = ((fq_any, far_q), (fk_any, far_k), (fv_any, far_v))[which]
        return pltpu.make_async_copy(source, target, local.at[which])

    scatters = scatters_of(place, units, grads, sums, *scatter_refs[:3], scatter_refs[3:])
    turns = in_turn([scatter.stages() for scatter in scatters], 0.5)

    @pl.when(step == 0)
    def _():
        place.greet()
        for which in range(3):
            far_in(which).start()
        for j in range(fars):

            @pl.when(second)
            def _(j=j):
                grad_over(j).start()

            @pl.when(second)
            def _(j=j):
                grad_kept(j).start()

    for at, number in enumerate(events):

        @pl.when(step == at)
        def _(number=number):
            for unused in range(number):
                next(turns, None)

    @pl.when((step == fars) & second)
    def _():
        stats_over().start()

    @pl.when(step < pairs)
    def _():
        pair = lax.rem(step + fars, pairs)
        stats[pair] = pair_stats(pair, mix_ref, do_ref, logs_ref)

        def put(start, n, dk, dv):
            near[1, pair, start : start + n, :] = dk
            near[2, pair, start : start + n, :] = dv

        back_pair(tile, True, q_ref, k_ref, v_ref, do_ref, stats.at[pair], acc, put)
        near[0, pair] = acc[...]

    @pl.when((step >= pairs) & (step < pairs + fars))
    def _():
        j = step - pairs

        @pl.when(j == 0)
        def _():
            for which in range(3):
                far_in(which).wait()

            @pl.when(first)
            def _():
                stats_over().wait_recv()

        @pl.when(first)
        def _():
            grad_over(j).wait_recv()
            used_stats[...] = far_stats[j]

        @pl.when(second)
        def _():
            grad_kept(j).wait()
            used_stats[...] = stats[j]

        def put(start, n, dk, dv):
            far_dk[j, start : start + n, :] = dk.astype(far_dk.dtype)
            far_dv[j, start : start + n, :] = dv.astype(far_dv.dtype)

        back_pair(far_tile, False, far_q.at[j], far_k.at[j], far_v.at[j], far_do.at[j], used_stats, acc, put)
        far_dq[j] = acc[...].astype(far_dq.dtype)

        @pl.when(first)
        def _():
            back_over(0, j).start()

        @pl.when(second)
        def _():
            back_over(1, j).start()
            back_over(2, j).start()

    @pl.when(step >= pairs + fars)
    def _():
        pair = step - pairs - fars
        lower = pair < fars
        j = lax.rem(pair, fars)

        def write(ref, which, other):
            total = near[which, pair]
            if other is not None:
                total = total + other[j].astype(jnp.float32)
            ref[...] = total.astype(ref.dtype)

        @pl.when(first & lower)
        def _():
            for which in (1, 2):
                back_over(which, j).wait_recv()
            write(dq_ref, 0, None)
            write(dk_ref, 1, got_k)
            write(dv_ref, 2, got_v)

        @pl.when(first & jnp.logical_not(lower))
        def _():
            write(dq_ref, 0, None)
            write(dk_ref, 1, far_dk)
            write(dv_ref, 2, far_dv)

        @pl.when(second & lower)
        def _():
            write(dq_ref, 0, far_dq)
            write(dk_ref, 1, None)
            write(dv_ref, 2, None)

        @pl.when(second & jnp.logical_not(lower))
        def _():
            back_over(0, j).wait_recv()
            write(dq_ref, 0, got_q)
            write(dk_ref, 1, None)
            write(dv_ref, 2, None)

    @pl.when(step == 2 * pairs + fars - 1)
    def _():
        for unused in turns:
            pass
        for scatter in scatters:
            scatter.finish()

        @pl.when(first)
        def _():
            for j in range(fars):
                back_over(0, j).wait_send()

        @pl.when(second)
        def _():
            stats_over().wait_send()
            for j in range(fars):
                grad_over(j).wait_send()
                for which in (1, 2):
                    back_over(which, j).wait_send()


def pair_back(q, k, v, do, mix, logs, far, grads, collective_id, events, tile=384, far_tile=256):
    rows, width = q.shape
    pairs = width // 128
    fars = pairs // 2
    blocks, units, scratch = scatter_plan(grads, 256, ORDERS)
    count = len(grads)
    block = pl.BlockSpec((rows, 128), lambda i: (0, lax.rem(jnp.minimum(i, pairs - 1) + fars, pairs)))
    joined = pl.BlockSpec((rows, 128), lambda i: (0, jnp.maximum(i - pairs - fars, 0)))
    anywhere = pl.BlockSpec(memory_space=pl.ANY)
    half = pltpu.VMEM((fars, rows, 128), jnp.bfloat16)
    out = jax.ShapeDtypeStruct((rows, width), jnp.bfloat16)
    result = pl.pallas_call(
        functools.partial(pair_back_kernel, tile, far_tile, units, count, events),
        grid=(2 * pairs + fars,),
        in_specs=[block] * 5 + [pl.BlockSpec((rows, 128), lambda i: (0, 0))] + [anywhere] * (4 + count),
        out_specs=[joined] * 3 + [pl.BlockSpec(memory_space=pltpu.VMEM)] * count,
        out_shape=[out] * 3 + blocks,
        scratch_shapes=[
            pltpu.VMEM((3, pairs, rows, 128), jnp.float32), pltpu.VMEM((rows, 128), jnp.float32),
            pltpu.VMEM((pairs, 8, rows), jnp.float32), pltpu.VMEM((fars, 8, rows), jnp.float32),
            pltpu.VMEM((8, rows), jnp.float32), *[half] * 10,
            pltpu.SemaphoreType.DMA((5, fars)), pltpu.SemaphoreType.DMA((5, fars)),
            pltpu.SemaphoreType.DMA((3,)), pltpu.SemaphoreType.DMA((fars,)), *scratch,
        ],
        compiler_params=pltpu.CompilerParams(
            collective_id=collective_id, has_side_effects=True, vmem_limit_bytes=62 << 20),
        cost_estimate=pl.CostEstimate(
            flops=10 * rows * rows * width, bytes_accessed=16 * rows * width, transcendentals=rows * rows * pairs * 2),
    )(q, k, v, do, mix, logs, do, *far, *grads)
    return result[:3], result[3:]


def fast(
    frames_in, text_states, self_query, self_key, self_value, self_output, cross_query, cross_key, cross_value, cross_output,
    up_weight, down_weight, first_gain, first_bias, second_gain, second_bias, third_gain, third_bias, cotangent,
):
    row = lax.axis_index("row")
    rows, width = frames_in.shape
    half = width // 2
    piece = first_gain.shape[0]
    block_rows, block_cols = self_query.shape
    back = row % 2
    pairs = lax.axis_size("row") // 2
    forth_perm = [(2 * i, 2 * i + 1) for i in range(pairs)]
    back_perm = [(2 * i + 1, 2 * i) for i in range(pairs)]
    swap = forth_perm + back_perm

    def forth(array):
        return lax.ppermute(array, "row", forth_perm)

    def home(array):
        return lax.ppermute(array, "row", back_perm)

    def by_side(first, second):
        return jnp.where(back == 0, first, second)

    gains = jnp.zeros((1, 16, 128), jnp.bfloat16)
    gains = gains.at[0, :6, :piece].set(
        jnp.stack([first_gain, first_bias, second_gain, second_bias, third_gain, third_bias])
    )

    everyone = ("row", "col")
    places = (lax.axis_size("row"), lax.axis_size("col"))
    up_blocks = lax.all_gather(up_weight, everyone).reshape(*places, *up_weight.shape)
    down_blocks = lax.all_gather(down_weight, everyone).reshape(*places, *down_weight.shape)

    out_cross = lax.all_gather(cross_output, everyone).reshape(*places, *cross_output.shape)
    out_cross = out_cross.transpose(0, 2, 1, 3).reshape(width, width)

    def small(block):
        return block.reshape(1, block_rows, block_cols)

    def flat(array):
        return array.reshape(-1, array.shape[-1])

    early = gather_blocks(
        [small(self_query), small(self_key), small(self_value), gains], 1, 128)
    query_self, key_self, value_self = [flat(w) for w in early[:3]]
    norm_params = early[3].reshape(pairs * 2, 16, -1, 128)[:, :6, :, :piece].transpose(1, 0, 2, 3)
    norm_params = norm_params.reshape(6, width).astype(jnp.float32)

    frames = frames_in.astype(jnp.float32)
    hidden_one = norm_forward(frames, norm_params[0], norm_params[1]).astype(jnp.bfloat16)
    self_k = matmul(hidden_one, key_self).astype(jnp.bfloat16)
    self_v = matmul(hidden_one, value_self).astype(jnp.bfloat16)
    self_q = matmul(hidden_one, query_self).astype(jnp.bfloat16)
    (self_mix, log_lanes, far_q, far_k, far_v), late = pair_attend(
        self_q, self_k, self_v, [small(w) for w in (self_output, cross_query, cross_key, cross_value)], 5, [3] * 12)
    out_self, query_cross, key_cross, value_cross = [flat(w) for w in late]
    resid_one = frames + matmul(self_mix, out_self)
    hidden_two = norm_forward(resid_one, norm_params[2], norm_params[3]).astype(jnp.bfloat16)
    cross_q = matmul(hidden_two, query_cross).astype(jnp.bfloat16)
    other_text = lax.ppermute(text_states, "row", swap)
    clip_text = by_side(
        jnp.concatenate([text_states, other_text]), jnp.concatenate([other_text, text_states])
    )
    text_k = matmul(clip_text, key_cross).astype(jnp.bfloat16)
    text_v = matmul(clip_text, value_cross).astype(jnp.bfloat16)
    cross_mix, cross_logs = cross(cross_q, text_k, text_v)
    resid_two = resid_one + matmul(cross_mix, out_cross)
    hidden_three = norm_forward(resid_two, norm_params[4], norm_params[5]).astype(jnp.bfloat16)
    layer_out, grad_three, up_grad, down_grad, down_grad_blocks = feed(hidden_three, cotangent, resid_two, up_blocks, down_blocks)
    up_sum, down_sum = [
        lax.psum_scatter(g.reshape(-1, *g.shape[2:]), everyone, scatter_dimension=0).astype(jnp.float32)
        for g in (up_grad, down_grad_blocks)
    ]

    cotan_full = cotangent.astype(jnp.float32)
    unused_three, pull_three = jax.vjp(norm_forward, resid_two, norm_params[4], norm_params[5])
    through_three, third_gain_part, third_bias_part = pull_three(grad_three)
    grad_resid_two = cotan_full + through_three
    grad_cross = grad_resid_two.astype(jnp.bfloat16)
    cross_out_grad = over_tokens(cross_mix, grad_cross)
    grad_cross_mix = by_transposed(grad_cross, out_cross).astype(jnp.bfloat16)
    grad_cross_q, text_k_part, text_v_part = cross_back(cross_q, text_k, text_v, grad_cross_mix, cross_mix, cross_logs)
    text_rows = text_states.shape[0]
    text_parts = jnp.concatenate([text_k_part, text_v_part], axis=1)
    given = lax.ppermute(by_side(text_parts[text_rows:], text_parts[:text_rows]), "row", swap)
    kept = by_side(text_parts[:text_rows], text_parts[text_rows:])
    text_parts = (kept.astype(jnp.float32) + given.astype(jnp.float32)).astype(jnp.bfloat16)
    grad_text_k, grad_text_v = text_parts[:, :width], text_parts[:, width:]
    cross_query_part = over_tokens(hidden_two, grad_cross_q)
    cross_key_part = over_tokens(text_states, grad_text_k)
    cross_value_part = over_tokens(text_states, grad_text_v)
    text_grad = by_transposed(grad_text_k, key_cross) + by_transposed(grad_text_v, value_cross)
    grad_two = by_transposed(grad_cross_q, query_cross)
    unused_two, pull_two = jax.vjp(norm_forward, resid_one, norm_params[2], norm_params[3])
    through_two, second_gain_part, second_bias_part = pull_two(grad_two)
    grad_resid_one = grad_resid_two + through_two
    grad_self = grad_resid_one.astype(jnp.bfloat16)
    self_out_grad = over_tokens(self_mix, grad_self)
    grad_self_mix = by_transposed(grad_self, out_self).astype(jnp.bfloat16)

    def by_place(grad, parts):
        return grad.astype(jnp.bfloat16).reshape(pairs, 2, parts, -1, grad.shape[-1])

    (grad_self_q, grad_self_k, grad_self_v), early_sums = pair_back(
        self_q, self_k, self_v, grad_self_mix, self_mix, log_lanes, (far_q, far_k, far_v),
        [by_place(g, 1) for g in (self_out_grad, cross_query_part, cross_key_part, cross_value_part, cross_out_grad)]
        + [by_place(down_grad, down_grad.shape[1] // block_rows)], 4, [5] * 12)
    self_query_part = over_tokens(hidden_one, grad_self_q)
    self_key_part = over_tokens(hidden_one, grad_self_k)
    self_value_part = over_tokens(hidden_one, grad_self_v)
    grad_one = (
        by_transposed(grad_self_q, query_self)
        + by_transposed(grad_self_k, key_self)
        + by_transposed(grad_self_v, value_self)
    )
    unused_one, pull_one = jax.vjp(norm_forward, frames, norm_params[0], norm_params[1])
    through_one, first_gain_part, first_bias_part = pull_one(grad_one)
    input_grad = grad_resid_one + through_one
    norm_grads = jnp.stack(
        [first_gain_part, first_bias_part, second_gain_part, second_bias_part, third_gain_part, third_bias_part]
    )
    norm_grads = norm_grads.reshape(6, 2 * pairs, -1, piece).transpose(1, 0, 2, 3)
    norm_grads = jnp.pad(norm_grads, ((0, 0), (0, 10), (0, 0), (0, 128 - piece)))

    late_sums = scatter_blocks(
        [by_place(g, 1) for g in (self_query_part, self_key_part, self_value_part)]
        + [by_place(norm_grads.reshape(2 * pairs * 16, -1), 1)], 3, 128)
    norm_parts = late_sums[3][0, :6, :piece]
    sums = [*late_sums[:3], *early_sums]
    sums = [total.reshape(-1, total.shape[-1]) for total in sums]
    return (layer_out, input_grad, text_grad, *sums[:-1], up_sum, jnp.concatenate([sums[-1], down_sum]), *norm_parts)


def local(*arrays):
    frames_in, self_query = arrays[0], arrays[2]
    halves = 2 * frames_in.shape[0] == FRAMES and lax.axis_size("row") % 2 == 0
    if halves and lax.axis_size("col") % 2 == 0 and self_query.shape[1] % 256 == 0 and self_query.shape[0] % 128 == 0:
        return fast(*arrays)
    return general(*arrays)


def solution(mesh):
    placed = (
        P(("col", "row"), None),
        P(("col", "row"), None),
        P("row", "col"),
        P("row", "col"),
        P("row", "col"),
        P("row", "col"),
        P("row", "col"),
        P("row", "col"),
        P("row", "col"),
        P("row", "col"),
        P("row", "col"),
        P("row", "col"),
        P(("row", "col")),
        P(("row", "col")),
        P(("row", "col")),
        P(("row", "col")),
        P(("row", "col")),
        P(("row", "col")),
        P(("col", "row"), None),
    )
    return jax.shard_map(
        local,
        mesh=mesh,
        in_specs=placed,
        out_specs=(
            P(("col", "row"), None),
            P(("col", "row"), None),
            P(("col", "row"), None),
            P("row", "col"),
            P("row", "col"),
            P("row", "col"),
            P("row", "col"),
            P("row", "col"),
            P("row", "col"),
            P("row", "col"),
            P("row", "col"),
            P("row", "col"),
            P("row", "col"),
            P(("row", "col")),
            P(("row", "col")),
            P(("row", "col")),
            P(("row", "col")),
            P(("row", "col")),
            P(("row", "col")),
        ),
        check_vma=False,
    )
```

```python
import functools
from functools import partial

import jax
import jax.numpy as jnp
from jax import lax
from jax.experimental import pallas as pl
from jax.experimental.pallas import tpu as pltpu
from jax.sharding import PartitionSpec as P

HEADS = 16
HEAD_DIM = 64
FRAMES = 1500
TEXT = 64


def norm_forward(values, norm_gain, norm_bias):
    center = values - jnp.mean(values, axis=-1, keepdims=True)
    variance = jnp.mean(center * center, axis=-1, keepdims=True)
    return center * lax.rsqrt(variance + 1e-05) * norm_gain + norm_bias


def matmul(left, right):
    return jnp.dot(left, right, preferred_element_type=jnp.float32)


def by_transposed(left, right):
    return lax.dot_general(
        left, right, (((1,), (1,)), ((), ())), preferred_element_type=jnp.float32
    )


def over_tokens(left, right):
    return lax.dot_general(
        left, right, (((0,), (0,)), ((), ())), preferred_element_type=jnp.float32
    )


def collect(blocks):
    partly = (
        lax.all_gather(blocks[0], "col", axis=1, tiled=True),
        lax.all_gather(blocks[1], "col", axis=1, tiled=True),
        lax.all_gather(blocks[2], "col", axis=1, tiled=True),
        lax.all_gather(blocks[3], "col", axis=1, tiled=True),
        lax.all_gather(blocks[4], "col", axis=1, tiled=True),
        lax.all_gather(blocks[5], "col", axis=1, tiled=True),
        lax.all_gather(blocks[6], "col", axis=1, tiled=True),
        lax.all_gather(blocks[7], "col", axis=1, tiled=True),
        lax.all_gather(blocks[8], "col", axis=1, tiled=True),
        lax.all_gather(blocks[9], "col", axis=1, tiled=True),
        lax.all_gather(blocks[10], "col", axis=1, tiled=True),
    )
    return (
        lax.all_gather(partly[0], "row", axis=0, tiled=True),
        lax.all_gather(partly[1], "row", axis=0, tiled=True),
        lax.all_gather(partly[2], "row", axis=0, tiled=True),
        lax.all_gather(partly[3], "row", axis=0, tiled=True),
        lax.all_gather(partly[4], "row", axis=0, tiled=True),
        lax.all_gather(partly[5], "row", axis=0, tiled=True),
        lax.all_gather(partly[6], "row", axis=0, tiled=True),
        lax.all_gather(partly[7], "row", axis=0, tiled=True),
        lax.all_gather(partly[8], "row", axis=0, tiled=True),
        lax.all_gather(partly[9], "row", axis=0, tiled=True),
        lax.all_gather(partly[10], "row", axis=0, tiled=True),
    )


def spread(grads):
    partly = (
        lax.psum_scatter(
            grads[0].astype(jnp.bfloat16), "row", scatter_dimension=0, tiled=True
        ).astype(jnp.float32),
        lax.psum_scatter(
            grads[1].astype(jnp.bfloat16), "row", scatter_dimension=0, tiled=True
        ).astype(jnp.float32),
        lax.psum_scatter(
            grads[2].astype(jnp.bfloat16), "row", scatter_dimension=0, tiled=True
        ).astype(jnp.float32),
        lax.psum_scatter(
            grads[3].astype(jnp.bfloat16), "row", scatter_dimension=0, tiled=True
        ).astype(jnp.float32),
        lax.psum_scatter(
            grads[4].astype(jnp.bfloat16), "row", scatter_dimension=0, tiled=True
        ).astype(jnp.float32),
        lax.psum_scatter(
            grads[5].astype(jnp.bfloat16), "row", scatter_dimension=0, tiled=True
        ).astype(jnp.float32),
        lax.psum_scatter(
            grads[6].astype(jnp.bfloat16), "row", scatter_dimension=0, tiled=True
        ).astype(jnp.float32),
        lax.psum_scatter(
            grads[7].astype(jnp.bfloat16), "row", scatter_dimension=0, tiled=True
        ).astype(jnp.float32),
        lax.psum_scatter(
            grads[8].astype(jnp.bfloat16), "row", scatter_dimension=0, tiled=True
        ).astype(jnp.float32),
        lax.psum_scatter(
            grads[9].astype(jnp.bfloat16), "row", scatter_dimension=0, tiled=True
        ).astype(jnp.float32),
        lax.psum_scatter(
            grads[10].astype(jnp.bfloat16), "row", scatter_dimension=0, tiled=True
        ).astype(jnp.float32),
    )
    return (
        lax.psum_scatter(
            partly[0].astype(jnp.bfloat16), "col", scatter_dimension=1, tiled=True
        ).astype(jnp.float32),
        lax.psum_scatter(
            partly[1].astype(jnp.bfloat16), "col", scatter_dimension=1, tiled=True
        ).astype(jnp.float32),
        lax.psum_scatter(
            partly[2].astype(jnp.bfloat16), "col", scatter_dimension=1, tiled=True
        ).astype(jnp.float32),
        lax.psum_scatter(
            partly[3].astype(jnp.bfloat16), "col", scatter_dimension=1, tiled=True
        ).astype(jnp.float32),
        lax.psum_scatter(
            partly[4].astype(jnp.bfloat16), "col", scatter_dimension=1, tiled=True
        ).astype(jnp.float32),
        lax.psum_scatter(
            partly[5].astype(jnp.bfloat16), "col", scatter_dimension=1, tiled=True
        ).astype(jnp.float32),
        lax.psum_scatter(
            partly[6].astype(jnp.bfloat16), "col", scatter_dimension=1, tiled=True
        ).astype(jnp.float32),
        lax.psum_scatter(
            partly[7].astype(jnp.bfloat16), "col", scatter_dimension=1, tiled=True
        ).astype(jnp.float32),
        lax.psum_scatter(
            partly[8].astype(jnp.bfloat16), "col", scatter_dimension=1, tiled=True
        ).astype(jnp.float32),
        lax.psum_scatter(
            partly[9].astype(jnp.bfloat16), "col", scatter_dimension=1, tiled=True
        ).astype(jnp.float32),
        lax.psum_scatter(
            partly[10].astype(jnp.bfloat16), "col", scatter_dimension=1, tiled=True
        ).astype(jnp.float32),
    )


def heads_layout(stacked):
    return lax.all_to_all(stacked, "row", split_axis=1, concat_axis=0, tiled=True)


def tokens_layout(stacked):
    return lax.all_to_all(stacked, "row", split_axis=0, concat_axis=2, tiled=True)


def by_clips(arranged, start, count, length, heads_dev):
    section = arranged[:, start : start + count]
    return section.reshape(-1, length, heads_dev, HEAD_DIM)


def causal_scores(query_clip, key_clip, causal):
    scores = jnp.einsum(
        "qhd,khd->hqk", query_clip, key_clip, preferred_element_type=jnp.float32
    ) * HEAD_DIM ** (-0.5)
    if causal:
        allowed = jnp.arange(scores.shape[1])[:, None] >= jnp.arange(scores.shape[2])[None, :]
        scores = jnp.where(allowed, scores, -1e30)
    return scores


def attend_forward(query_clips, key_clips, value_clips, causal):

    def one_clip(operands):
        query_clip, key_clip, value_clip = operands
        scores = causal_scores(query_clip, key_clip, causal)
        highest = jnp.max(scores, axis=-1, keepdims=True)
        powers = jnp.exp(scores - highest)
        totals = jnp.sum(powers, axis=-1, keepdims=True)
        weights_low = (powers / totals).astype(jnp.bfloat16)
        mixture = jnp.einsum(
            "hqk,khd->qhd", weights_low, value_clip, preferred_element_type=jnp.float32
        )
        return (mixture.astype(jnp.bfloat16), (highest + jnp.log(totals))[..., 0])

    return lax.map(one_clip, (query_clips, key_clips, value_clips))


def attend_backward(query_clips, key_clips, value_clips, log_sums, grad_clips, causal):

    def one_clip(operands):
        query_clip, key_clip, value_clip, log_clip, grad_clip = operands
        scores = causal_scores(query_clip, key_clip, causal)
        probs_full = jnp.exp(scores - log_clip[..., None])
        grad_probs = jnp.einsum(
            "qhd,khd->hqk", grad_clip, value_clip, preferred_element_type=jnp.float32
        )
        grad_value = jnp.einsum(
            "hqk,qhd->khd",
            probs_full.astype(jnp.bfloat16),
            grad_clip,
            preferred_element_type=jnp.float32,
        )
        centered = grad_probs - jnp.sum(probs_full * grad_probs, axis=-1, keepdims=True)
        grad_scores = (probs_full * centered).astype(jnp.bfloat16)
        grad_query = jnp.einsum(
            "hqk,khd->qhd", grad_scores, key_clip, preferred_element_type=jnp.float32
        ) * HEAD_DIM ** (-0.5)
        grad_key = jnp.einsum(
            "hqk,qhd->khd", grad_scores, query_clip, preferred_element_type=jnp.float32
        ) * HEAD_DIM ** (-0.5)
        return (
            grad_query.astype(jnp.bfloat16),
            grad_key.astype(jnp.bfloat16),
            grad_value.astype(jnp.bfloat16),
        )

    return lax.map(one_clip, (query_clips, key_clips, value_clips, log_sums, grad_clips))


def general(
    frames_in,
    text_states,
    self_query,
    self_key,
    self_value,
    self_output,
    cross_query,
    cross_key,
    cross_value,
    cross_output,
    up_weight,
    down_weight,
    first_gain,
    first_bias,
    second_gain,
    second_bias,
    third_gain,
    third_bias,
    cotangent,
):
    row_count = lax.axis_size("row")
    col_count = lax.axis_size("col")
    heads_dev = HEADS // row_count
    width_dev = heads_dev * HEAD_DIM
    tok_rows = frames_in.shape[0]
    text_rows = text_states.shape[0]
    piece_len = first_gain.shape[0]
    gain_block = jnp.stack(
        [first_gain, first_bias, second_gain, second_bias, third_gain, third_bias]
    ).reshape(1, 6 * piece_len)
    param_blocks = (
        self_query,
        self_key,
        self_value,
        self_output,
        cross_query,
        cross_key,
        cross_value,
        cross_output,
        up_weight,
        down_weight,
        gain_block,
    )

    def unpack_gains(gathered_gains):
        arranged = gathered_gains.reshape(row_count, col_count, 6, piece_len).transpose(2, 0, 1, 3)
        return arranged.reshape(6, row_count * col_count * piece_len).astype(jnp.float32)

    gathered = collect(param_blocks)
    (
        query_self,
        key_self,
        value_self,
        out_self,
        query_cross,
        key_cross,
        value_cross,
        out_cross,
        up_full,
        down_full,
    ) = gathered[:10]
    norm_params = unpack_gains(gathered[10])
    frames = frames_in.astype(jnp.float32)
    hidden_one = norm_forward(frames, norm_params[0], norm_params[1]).astype(jnp.bfloat16)
    self_q = matmul(hidden_one, query_self).astype(jnp.bfloat16)
    self_k = matmul(hidden_one, key_self).astype(jnp.bfloat16)
    self_v = matmul(hidden_one, value_self).astype(jnp.bfloat16)
    text_k = matmul(text_states, key_cross).astype(jnp.bfloat16)
    text_v = matmul(text_states, value_cross).astype(jnp.bfloat16)
    sent_rows = 3 * tok_rows + 2 * text_rows
    arranged = heads_layout(jnp.concatenate([self_q, self_k, self_v, text_k, text_v], axis=0))
    arranged = arranged.reshape(row_count, sent_rows, width_dev)
    query_clips = by_clips(arranged, 0, tok_rows, FRAMES, heads_dev)
    key_clips = by_clips(arranged, tok_rows, tok_rows, FRAMES, heads_dev)
    value_clips = by_clips(arranged, 2 * tok_rows, tok_rows, FRAMES, heads_dev)
    text_keys = by_clips(arranged, 3 * tok_rows, text_rows, TEXT, heads_dev)
    text_values = by_clips(arranged, 3 * tok_rows + text_rows, text_rows, TEXT, heads_dev)
    self_clips, self_logs = attend_forward(query_clips, key_clips, value_clips, True)
    self_mix = tokens_layout(self_clips.reshape(row_count, tok_rows, width_dev))[0]
    resid_one = frames + matmul(self_mix, out_self)
    hidden_two = norm_forward(resid_one, norm_params[2], norm_params[3]).astype(jnp.bfloat16)
    cross_q = matmul(hidden_two, query_cross).astype(jnp.bfloat16)
    cross_arranged = heads_layout(cross_q).reshape(row_count, tok_rows, width_dev)
    cross_queries = by_clips(cross_arranged, 0, tok_rows, FRAMES, heads_dev)
    cross_clips, cross_logs = attend_forward(cross_queries, text_keys, text_values, False)
    cross_mix = tokens_layout(cross_clips.reshape(row_count, tok_rows, width_dev))[0]
    resid_two = resid_one + matmul(cross_mix, out_cross)
    hidden_three = norm_forward(resid_two, norm_params[4], norm_params[5]).astype(jnp.bfloat16)
    pre_act = matmul(hidden_three, up_full)
    inner = jax.nn.gelu(pre_act, approximate=False).astype(jnp.bfloat16)
    layer_out = (resid_two + matmul(inner, down_full)).astype(jnp.bfloat16)
    gathered = collect(param_blocks)
    (
        query_self,
        key_self,
        value_self,
        out_self,
        query_cross,
        key_cross,
        value_cross,
        out_cross,
        up_full,
        down_full,
    ) = gathered[:10]
    norm_params = unpack_gains(gathered[10])
    cotan_full = cotangent.astype(jnp.float32)
    down_grad = over_tokens(inner, cotangent)
    grad_inner = by_transposed(cotangent, down_full)
    unused_gelu, gelu_pull = jax.vjp(partial(jax.nn.gelu, approximate=False), pre_act)
    grad_pre = gelu_pull(grad_inner)[0].astype(jnp.bfloat16)
    up_grad = over_tokens(hidden_three, grad_pre)
    grad_three = by_transposed(grad_pre, up_full)
    unused_three, pull_three = jax.vjp(norm_forward, resid_two, norm_params[4], norm_params[5])
    through_three, third_gain_part, third_bias_part = pull_three(grad_three)
    grad_resid_two = cotan_full + through_three
    grad_cross = grad_resid_two.astype(jnp.bfloat16)
    cross_out_grad = over_tokens(cross_mix, grad_cross)
    grad_cross_mix = by_transposed(grad_cross, out_cross).astype(jnp.bfloat16)
    grad_cross_arr = heads_layout(grad_cross_mix).reshape(row_count, tok_rows, width_dev)
    grad_cross_clips = by_clips(grad_cross_arr, 0, tok_rows, FRAMES, heads_dev)
    cq_clips, tk_clips, tv_clips = attend_backward(
        cross_queries, text_keys, text_values, cross_logs, grad_cross_clips, False
    )
    back_cross = jnp.concatenate(
        [
            cq_clips.reshape(row_count, tok_rows, width_dev),
            tk_clips.reshape(row_count, text_rows, width_dev),
            tv_clips.reshape(row_count, text_rows, width_dev),
        ],
        axis=1,
    )
    back_cross = tokens_layout(back_cross)[0]
    grad_cross_q = back_cross[:tok_rows]
    grad_text_k = back_cross[tok_rows : tok_rows + text_rows]
    grad_text_v = back_cross[tok_rows + text_rows :]
    cross_query_part = over_tokens(hidden_two, grad_cross_q)
    cross_key_part = over_tokens(text_states, grad_text_k)
    cross_value_part = over_tokens(text_states, grad_text_v)
    text_grad = by_transposed(grad_text_k, key_cross) + by_transposed(grad_text_v, value_cross)
    grad_two = by_transposed(grad_cross_q, query_cross)
    unused_two, pull_two = jax.vjp(norm_forward, resid_one, norm_params[2], norm_params[3])
    through_two, second_gain_part, second_bias_part = pull_two(grad_two)
    grad_resid_one = grad_resid_two + through_two
    grad_self = grad_resid_one.astype(jnp.bfloat16)
    self_out_grad = over_tokens(self_mix, grad_self)
    grad_self_mix = by_transposed(grad_self, out_self).astype(jnp.bfloat16)
    grad_self_arr = heads_layout(grad_self_mix).reshape(row_count, tok_rows, width_dev)
    grad_self_clips = by_clips(grad_self_arr, 0, tok_rows, FRAMES, heads_dev)
    sq_clips, sk_clips, sv_clips = attend_backward(
        query_clips, key_clips, value_clips, self_logs, grad_self_clips, True
    )
    back_self = jnp.concatenate(
        [
            sq_clips.reshape(row_count, tok_rows, width_dev),
            sk_clips.reshape(row_count, tok_rows, width_dev),
            sv_clips.reshape(row_count, tok_rows, width_dev),
        ],
        axis=1,
    )
    back_self = tokens_layout(back_self)[0]
    grad_self_q = back_self[:tok_rows]
    grad_self_k = back_self[tok_rows : 2 * tok_rows]
    grad_self_v = back_self[2 * tok_rows :]
    self_query_part = over_tokens(hidden_one, grad_self_q)
    self_key_part = over_tokens(hidden_one, grad_self_k)
    self_value_part = over_tokens(hidden_one, grad_self_v)
    grad_one = (
        by_transposed(grad_self_q, query_self)
        + by_transposed(grad_self_k, key_self)
        + by_transposed(grad_self_v, value_self)
    )
    unused_one, pull_one = jax.vjp(norm_forward, frames, norm_params[0], norm_params[1])
    through_one, first_gain_part, first_bias_part = pull_one(grad_one)
    input_grad = grad_resid_one + through_one
    norm_grads = jnp.stack(
        [
            first_gain_part,
            first_bias_part,
            second_gain_part,
            second_bias_part,
            third_gain_part,
            third_bias_part,
        ]
    )
    norm_grads = norm_grads.reshape(6, row_count, col_count, piece_len).transpose(1, 2, 0, 3)
    norm_grads = norm_grads.reshape(row_count, col_count * 6 * piece_len)
    summed = spread(
        (
            self_query_part,
            self_key_part,
            self_value_part,
            self_out_grad,
            cross_query_part,
            cross_key_part,
            cross_value_part,
            cross_out_grad,
            up_grad,
            down_grad,
            norm_grads,
        )
    )
    norm_parts = summed[10].reshape(6, piece_len)
    return (
        layer_out,
        input_grad,
        text_grad,
        summed[0],
        summed[1],
        summed[2],
        summed[3],
        summed[4],
        summed[5],
        summed[6],
        summed[7],
        summed[8],
        summed[9],
        norm_parts[0],
        norm_parts[1],
        norm_parts[2],
        norm_parts[3],
        norm_parts[4],
        norm_parts[5],
    )


NT=(((1,),(1,)),((),())); NN=(((1,),(0,)),((),())); TN=(((0,),(0,)),((),()))
def dg(a,b,dims): return lax.dot_general(a,b,dims,preferred_element_type=jnp.float32)

def feed_kernel(h_ref,cot_ref,res_ref,up_ref,down_ref,out_ref,g_ref,dup_ref,ddown_ref,acc):
    i=pl.program_id(0)
    @pl.when(i==0)
    def _():
        acc[...]=res_ref[...]
        g_ref[...]=jnp.zeros_like(g_ref)
    h=h_ref[...]
    up=up_ref[:,0].reshape(h.shape[1],-1)
    blocks,wide=down_ref.shape[1],down_ref.shape[3]
    pre=dg(h,up,NN)
    cdf=0.5*(1.0+lax.erf(pre*0.7071067811865476))
    inner=(pre*cdf).astype(jnp.bfloat16)
    slope=cdf+pre*(jnp.exp(-0.5*pre*pre)*0.3989422804014327)
    grad=None
    for at in range(blocks):
        columns=slice(at*wide,(at+1)*wide)
        cot=cot_ref[:,columns]
        acc[:,columns]+=dg(inner,down_ref[0,at],NN)
        ddown_ref[:,columns]=dg(inner,cot,TN).astype(ddown_ref.dtype)
        part=dg(cot,down_ref[0,at],NT)
        grad=part if grad is None else grad+part
    gpre=(grad*slope).astype(jnp.bfloat16)
    dup_ref[:,0]=dg(h,gpre,TN).astype(dup_ref.dtype).reshape(dup_ref.shape[0],dup_ref.shape[2],dup_ref.shape[3])
    g_ref[...]+=dg(gpre,up,NT)
    @pl.when(i==pl.num_programs(0)-1)
    def _(): out_ref[...]=acc[...].astype(out_ref.dtype)

def feed(h,cot,res,up,down):
    rows,d=h.shape; chunk=down.shape[2]; strips=up.shape[3]//chunk; ff=down.shape[0]*chunk
    whole=pl.BlockSpec((rows,d),lambda i:(0,0))
    up_spec=pl.BlockSpec((up.shape[0],1,up.shape[2],chunk),lambda i:(0,i//strips,0,i%strips))
    down_spec=pl.BlockSpec((1,)+down.shape[1:],lambda i:(i,0,0,0))
    return pl.pallas_call(feed_kernel,grid=(ff//chunk,),
        in_specs=[whole,whole,whole,up_spec,down_spec],
        out_specs=[whole,whole,up_spec,pl.BlockSpec((chunk,d),lambda i:(i,0))],
        out_shape=[jax.ShapeDtypeStruct((rows,d),jnp.bfloat16),jax.ShapeDtypeStruct((rows,d),jnp.float32),jax.ShapeDtypeStruct(up.shape,jnp.bfloat16),jax.ShapeDtypeStruct((ff,d),jnp.bfloat16)],
        scratch_shapes=[pltpu.VMEM((rows,d),jnp.float32)],
        compiler_params=pltpu.CompilerParams(vmem_limit_bytes=56<<20),
        cost_estimate=pl.CostEstimate(flops=12*rows*d*ff,bytes_accessed=8*d*ff+16*rows*d,transcendentals=2*rows*ff))(h,cot,res,up,down)


MESH = pl.DeviceIdType.MESH
ORDERS = ("xzy", "yzx", "xzy", "yzx", "zxy", "zyx")


class Place:
    def __init__(self):
        row, col = lax.axis_index("row"), lax.axis_index("col")
        self.z, self.y, self.x, self.k = row // 2, row % 2, col // 2, col % 2
        self.along = lax.axis_size("row") // 2

    def device(self, dz=0, y=False, x=False, k=False):
        other_y = 1 - self.y if y else self.y
        other_x = 1 - self.x if x else self.x
        other_k = 1 - self.k if k else self.k
        return ((self.z + dz) * 2 + other_y, other_x * 2 + other_k)

    def across(self, axis):
        return self.device(y=axis == "y", x=axis == "x", k=axis == "k")

    def greet(self):
        barrier = pltpu.get_barrier_semaphore()
        for axis in "xyk":
            pl.semaphore_signal(barrier, inc=1, device_id=self.across(axis), device_id_type=MESH)

        @pl.when(self.z > 0)
        def _():
            pl.semaphore_signal(barrier, inc=1, device_id=self.device(dz=-1), device_id_type=MESH)

        @pl.when(self.z + 1 < self.along)
        def _():
            pl.semaphore_signal(barrier, inc=1, device_id=self.device(dz=1), device_id_type=MESH)

        below = jnp.where(self.z > 0, 1, 0)
        above = jnp.where(self.z + 1 < self.along, 1, 0)
        pl.semaphore_wait(barrier, 3 + below + above)


def when(condition, run):
    if condition is None:
        run()
    else:
        pl.when(condition)(run)


def in_turn(units, lag):
    ready = [(lag * at, at) for at in range(len(units))]
    while ready:
        turn, at = min(ready)
        ready.remove((turn, at))
        if next(units[at], units) is not units:
            ready.append((turn + 1, at))
        yield


class Gather:
    def __init__(self, place, block, full, strip, order, send, recv):
        self.place, self.block, self.full, self.strip = place, block, full, strip
        turn = order.index("z")
        self.before, self.after = order[:turn], order[turn + 1 :]
        self.send, self.recv, self.used, self.sent, self.started = send, recv, 0, 0, []

    def region(self, z, y, x):
        part, start, count = self.strip
        column = (x * 2 + self.place.k) * self.block.shape[-1] + start
        return self.full.at[z, y, part, :, pl.ds(pl.multiple_of(column, 128), count)]

    def held(self, done, z):
        y = slice(None) if "y" in done else self.place.y
        return [self.region(z, y, x) for x in (range(2) if "x" in done else [self.place.x])]

    def pairs(self, done, z, first):
        if first:
            part, start, count = self.strip
            place = self.place
            return [(self.block.at[part, :, pl.ds(start, count)], self.region(place.z, place.y, place.x))]
        return [(region, region) for region in self.held(done, z)]

    def semaphore(self):
        self.used += 2
        return self.used - 2

    def copies(self, device, pairs, semaphore, send=0):
        return [
            pltpu.make_async_remote_copy(
                src_ref=source, dst_ref=target, send_sem=self.send.at[send + at],
                recv_sem=self.recv.at[semaphore + at], device_id=device, device_id_type=MESH)
            for at, (source, target) in enumerate(pairs)
        ]

    def start(self, device, pairs, wide, condition, semaphore):
        send = self.sent
        self.sent += wide

        def make():
            return self.copies(device(), pairs(), semaphore, send)

        when(condition(), lambda: [copy.start() for copy in make()] and None)
        self.started.append((condition, make))
        return condition, make

    def arrive(self, sent):
        condition, make = sent
        when(condition(), lambda: [copy.wait_recv() for copy in make()] and None)

    def stages(self):
        place, along = self.place, self.place.along
        done = []

        def always():
            return None

        def width(axes):
            return 2 if "x" in axes else 1

        for axis in self.before:
            axes = tuple(done)
            sent = self.start(
                lambda axis=axis: place.across(axis), lambda axes=axes: self.pairs(axes, place.z, not axes),
                width(axes), always, self.semaphore())
            yield
            self.arrive(sent)
            done.append(axis)
        first = not done
        axes_z = tuple(done)
        from_left = [self.semaphore() for _ in range(along - 1)]
        from_right = [self.semaphore() for _ in range(along - 1)]

        def pass_on(turn, step):
            axes = axes_z + tuple(self.after[:turn])
            sent = []
            for way in ((-1, 1) if step else (0,)):

                def inside(way=way):
                    z = place.z + way * step
                    return (z >= 0) & (z < along) if way else None

                sent.append(self.start(
                    lambda: place.across(self.after[turn]),
                    lambda way=way: self.pairs(axes, place.z + way * step, not axes and not step),
                    width(axes), inside, self.semaphore()))
            return turn, step, sent

        def step_out(step):
            self.start(
                lambda: place.device(dz=1), lambda: self.pairs(axes_z, place.z - (step - 1), first and step == 1),
                width(axes_z), lambda: (place.z - (step - 1) >= 0) & (place.z + 1 < along), from_left[step - 1])
            self.start(
                lambda: place.device(dz=-1), lambda: self.pairs(axes_z, place.z + (step - 1), first and step == 1),
                width(axes_z), lambda: (place.z + (step - 1) < along) & (place.z > 0), from_right[step - 1])

        def step_in(step):
            for way, semaphore in ((-1, from_left), (1, from_right)):
                z = place.z + way * step
                self.arrive((
                    lambda: (z >= 0) & (z < along),
                    lambda: self.copies(place.across("k"), self.pairs(axes_z, z, False), semaphore[step - 1])))

        step_out(1)
        waiting = [pass_on(0, 0)] if self.after else []
        for step in range(1, along + len(self.after)):
            yield
            if step < along:
                step_in(step)
                if step + 1 < along:
                    step_out(step + 1)
            following = []
            for turn, at, sent in waiting:
                for one in sent:
                    self.arrive(one)
                if turn + 1 < len(self.after):
                    following.append(pass_on(turn + 1, at))
            if self.after and step < along:
                following.append(pass_on(0, step))
            waiting = following
        sent = self.start(
            lambda: place.across("k"), lambda: [(r, r) for r in [self.region(slice(None), slice(None), x) for x in range(2)]],
            2, always, self.semaphore())
        yield
        self.arrive(sent)

    def finish(self):
        for condition, make in self.started:
            when(condition(), lambda make=make: [copy.wait_send() for copy in make()] and None)


class OwnBlocks:
    def __init__(self, place, blocks, fulls, local):
        self.place, self.blocks, self.fulls, self.local = place, blocks, fulls, local

    def copies(self):
        place = self.place
        for at, (block, full) in enumerate(zip(self.blocks, self.fulls)):
            width = block.shape[-1]
            columns = pl.ds(pl.multiple_of((place.x * 2 + place.k) * width, 128), width)
            yield pltpu.make_async_copy(block, full.at[place.z, place.y, :, :, columns], self.local.at[at])

    def start(self):
        for copy in self.copies():
            copy.start()

    def wait(self):
        for copy in self.copies():
            copy.wait()


def gathers_of(place, units, blocks, fulls, send, recv):
    return [
        Gather(place, blocks[which], fulls[which], strip, order, send.at[at], recv.at[at])
        for at, (which, strip, order) in enumerate(units)
    ]


def gather_kernel(units, count, *refs):
    blocks, fulls = refs[:count], refs[count : 2 * count]
    send, recv, local = refs[2 * count :]
    place = Place()
    place.greet()
    own = OwnBlocks(place, blocks, fulls, local)
    own.start()
    gathers = gathers_of(place, units, blocks, fulls, send, recv)
    waited = False
    for unused in in_turn([gather.stages() for gather in gathers], 0.0):
        if not waited:
            own.wait()
            waited = True
    for gather in gathers:
        gather.finish()


def gather_units(blocks, least, orders):
    strips = []
    for which, block in enumerate(blocks):
        wide = min(least, block.shape[-1])
        for part in range(block.shape[0]):
            for start in range(0, block.shape[-1], wide):
                strips.append((which, (part, start, wide)))
    return [strip + (orders[at % len(orders)],) for at, strip in enumerate(strips)]


def gather_plan(blocks, least, orders):
    along, cols = lax.axis_size("row") // 2, lax.axis_size("col")
    units = gather_units(blocks, least, orders)
    fulls = [jax.ShapeDtypeStruct((along, 2) + b.shape[:2] + (cols * b.shape[2],), b.dtype) for b in blocks]
    scratch = [
        pltpu.SemaphoreType.DMA((len(units), 8 * along)),
        pltpu.SemaphoreType.DMA((len(units), 12 * along)),
        pltpu.SemaphoreType.DMA((len(blocks),)),
    ]
    return fulls, units, scratch


def gather_blocks(blocks, collective_id, least):
    fulls, units, scratch = gather_plan(blocks, least, ORDERS)
    count = len(blocks)
    anywhere = pl.BlockSpec(memory_space=pl.ANY)
    return pl.pallas_call(
        functools.partial(gather_kernel, units, count),
        out_shape=fulls,
        in_specs=[anywhere] * count,
        out_specs=[anywhere] * count,
        scratch_shapes=scratch,
        compiler_params=pltpu.CompilerParams(collective_id=collective_id, has_side_effects=True),
        cost_estimate=pl.CostEstimate(flops=0, bytes_accessed=4 * sum(f.size for f in fulls), transcendentals=0),
    )(*blocks)


SCATTER_ORDERS = ("xyz", "yxz", "zxy", "zyx", "xzy", "yzx")


def add_blocks(total, extra, leading):
    def one(at, unused):
        place = []
        for size in leading[::-1]:
            place.append(at % size)
            at = at // size
        place = tuple(place[::-1])
        total[place] = total[place] + extra[place]
        return unused

    if not leading:
        total[...] = total[...] + extra[...]
        return
    count = 1
    for size in leading:
        count *= size
    lax.fori_loop(0, count, one, 0)


class Scatter:
    def __init__(self, place, grad, out, strip, width, order, slots, send, recv, local):
        self.place, self.grad, self.out, self.strip, self.width = place, grad, out, strip, width
        self.order = order[::-1]
        self.total, self.other_core, self.halves, self.steps = slots
        self.send, self.recv, self.local = send, recv, local
        self.used, self.started = 0, []

    def region(self, x, k):
        part, start, count = self.strip
        column = (x * 2 + k) * self.width + start
        return self.grad.at[:, :, part, :, pl.ds(pl.multiple_of(column, 128), count)]

    def copy(self, device, source, target, semaphore):
        return pltpu.make_async_remote_copy(
            src_ref=source, dst_ref=target, send_sem=self.send.at[semaphore], recv_sem=self.recv.at[semaphore],
            device_id=device, device_id_type=MESH)

    def reserve(self, count):
        self.used += count
        return self.used - count

    def start(self, make, condition=lambda: None):
        when(condition(), lambda: make().start())
        self.started.append((condition, make))

    def stages(self):
        place, along = self.place, self.place.along
        rows, columns = self.total.shape[-2:]
        core = self.reserve(2)

        def own(x):
            return pltpu.make_async_copy(self.region(x, place.k), self.total.at[:, :, x], self.local.at[x])

        def swapped(x):
            return self.copy(
                place.across("k"), self.region(x, 1 - place.k), self.other_core.at[:, :, x], core + x)

        for x in range(2):
            own(x).start()
            self.start(functools.partial(swapped, x))
        yield
        for x in range(2):
            own(x).wait()
            swapped(x).wait_recv()
        add_blocks(self.total, self.other_core, (along, 2, 2))
        left = {"z": slice(None), "y": slice(None), "x": slice(None)}
        at = {"y": place.y, "x": place.x}

        def view(ref, kept=None, **places):
            return ref.at[tuple({**(left if kept is None else kept), **places}[axis] for axis in "zyx")]

        def sizes():
            return tuple(size for axis, size in zip("zyx", (along, 2, 2)) if isinstance(left[axis], slice))

        exchanges = 0
        for axis in self.order:
            if axis == "z":
                shape = tuple(2 for name in "yx" if isinstance(left[name], slice))
                inner = tuple(slice(None) if isinstance(left[name], slice) else 0 for name in "yx")

                def landing(side, step, inner=inner):
                    return self.steps.at[(side, step) + inner]

                base = self.reserve(2 * along)
                right, leftward = range(base, base + along), range(base + along, base + 2 * along)
                for step in range(along):
                    if step:
                        yield
                    for way, names, first in ((1, right, place.z), (-1, leftward, along - 1 - place.z)):
                        goal = along - 1 - step + place.z if way == 1 else step - along + 1 + place.z
                        side = 0 if way == 1 else 1
                        if step:
                            arrived = landing(side, step - 1)

                            def take(arrived=arrived, goal=goal, side=side, step=step, names=names):
                                self.copy(place.across("k"), arrived, arrived, names[step - 1]).wait_recv()
                                add_blocks(view(self.total, z=goal), arrived, shape)

                            pl.when((first >= 1) & (first <= step))(take)
                        if step < along - 1:
                            kept = dict(left)

                            def onward(way=way, step=step, kept=kept, landing=landing, side=side, names=names):
                                goal = along - 1 - step + place.z if way == 1 else step - along + 1 + place.z
                                source = view(self.total, kept, z=jnp.clip(goal, 0, along - 1))
                                return self.copy(place.device(dz=way), source, landing(side, step), names[step])

                            def reached(way=way, step=step):
                                first = place.z if way == 1 else along - 1 - place.z
                                return (first <= step) & (first < along - 1)

                            self.start(onward, reached)
                left["z"] = place.z
            else:
                landing = self.halves[exchanges]
                exchanges += 1
                inner = tuple(slice(None) if isinstance(left[name], slice) and name != axis else 0 for name in "zyx")
                semaphore, kept = self.reserve(1), dict(left)

                def swap(axis=axis, kept=kept, landing=landing, inner=inner, semaphore=semaphore):
                    source = view(self.total, kept, **{axis: 1 - at[axis]})
                    return self.copy(place.across(axis), source, landing.at[inner], semaphore)

                self.start(swap)
                yield
                swap().wait_recv()
                left[axis] = at[axis]
                add_blocks(view(self.total), landing.at[inner], sizes())
        part, start, count = self.strip
        self.out[part, :, start : start + count] = view(self.total)[...].astype(jnp.float32)

    def finish(self):
        for condition, make in self.started:
            when(condition(), lambda make=make: make().wait_send())


def scatter_slots(along, rows, columns, order):
    left = {"z": along, "y": 2, "x": 2}
    whole = (along, 2, 2, rows, columns)
    shapes = [whole, whole]
    steps = None
    for axis in order[::-1]:
        if axis == "z":
            steps = (2, along - 1, left["y"], left["x"], rows, columns)
        left[axis] = 1
        if axis != "z":
            shapes.append((left["z"], left["y"], left["x"], rows, columns))
    return shapes + [steps]


def scatters_of(place, units, grads, outs, send, recv, local, slots):
    scatters = []
    for at, (which, strip, order) in enumerate(units):
        total, other_core, first, second, steps = slots[5 * at : 5 * at + 5]
        scatters.append(
            Scatter(place, grads[which], outs[which], strip, outs[which].shape[-1], order,
                    (total, other_core, (first, second), steps), send.at[at], recv.at[at], local.at[at]))
    return scatters


def scatter_kernel(units, count, *refs):
    grads, outs = refs[:count], refs[count : 2 * count]
    place = Place()
    place.greet()
    scatters = scatters_of(place, units, grads, outs, *refs[2 * count : 2 * count + 3], refs[2 * count + 3 :])
    for unused in in_turn([scatter.stages() for scatter in scatters], 0.25):
        pass
    for scatter in scatters:
        scatter.finish()


def scatter_plan(grads, least, orders):
    along, cols = lax.axis_size("row") // 2, lax.axis_size("col")
    blocks = [jax.ShapeDtypeStruct(g.shape[2:4] + (g.shape[4] // cols,), jnp.float32) for g in grads]
    units = gather_units(blocks, least, orders)
    scratch = [pltpu.SemaphoreType.DMA((len(units), 2 * along + 4))] * 2 + [pltpu.SemaphoreType.DMA((len(units), 2))]
    for which, strip, order in units:
        shapes = scatter_slots(along, blocks[which].shape[1], strip[2], order)
        scratch += [pltpu.VMEM(shape, jnp.bfloat16) for shape in shapes]
    return blocks, units, scratch


def scatter_blocks(grads, collective_id, least):
    blocks, units, scratch = scatter_plan(grads, least, SCATTER_ORDERS)
    count = len(grads)
    anywhere = pl.BlockSpec(memory_space=pl.ANY)
    return pl.pallas_call(
        functools.partial(scatter_kernel, units, count),
        out_shape=blocks,
        in_specs=[anywhere] * count,
        out_specs=[pl.BlockSpec(memory_space=pltpu.VMEM)] * count,
        scratch_shapes=scratch,
        compiler_params=pltpu.CompilerParams(
            collective_id=collective_id, has_side_effects=True, vmem_limit_bytes=60 << 20),
        cost_estimate=pl.CostEstimate(
            flops=sum(g.size for g in grads), bytes_accessed=4 * sum(g.size for g in grads), transcendentals=0),
    )(*grads)


ACROSS = ("yzx", "yzx", "yzx", "yzx", "yxz")


def attend_rows(q, key_ref, value_ref, spans, diagonal, put):
    low = lax.broadcasted_iota(jnp.int32, (1, 128), 1) < HEAD_DIM
    mixed, logs = [], []
    for h in range(2):
        mine = low if h == 0 else jnp.logical_not(low)
        qh = jnp.where(mine, q, jnp.bfloat16(0))
        scores = []
        for at, length in spans:
            s = dg(qh, key_ref[at : at + length, :], NT)
            if at == diagonal:
                allowed = lax.broadcasted_iota(jnp.int32, s.shape, 0) >= lax.broadcasted_iota(jnp.int32, s.shape, 1)
                s = jnp.where(allowed, s, -1e30)
            scores.append(s)
        top = functools.reduce(jnp.maximum, [jnp.max(s, axis=1, keepdims=True) for s in scores])
        out = None
        for (at, length), s in zip(spans, scores):
            p = jnp.exp(s - top).astype(jnp.bfloat16)
            value = value_ref[at : at + length, :]
            part = dg(p, jnp.where(mine, value, jnp.ones_like(value)), NN)
            out = part if out is None else out + part
        total = out[:, HEAD_DIM : HEAD_DIM + 1] if h == 0 else out[:, 0:1]
        mixed.append(out / total)
        logs.append(top + jnp.log(total))
    put(logs)
    return jnp.where(low, mixed[0], mixed[1])


def rows_of(lanes_ref, first):
    picked = lax.broadcasted_iota(jnp.int32, (8, 128), 0) + first == lax.broadcasted_iota(jnp.int32, (8, 128), 1)
    return lax.dot_general(
        picked.astype(jnp.float32), lanes_ref[...], NT, precision=lax.Precision.HIGHEST,
        preferred_element_type=jnp.float32)


def pair_attend_kernel(tile, units, count, events, *refs):
    q_ref, k_ref, v_ref, q_any, k_any, v_any = refs[:6]
    blocks = refs[6 : 6 + count]
    mix_ref, logs_ref, fq_out, fk_out, fv_out = refs[6 + count : 11 + count]
    fulls = refs[11 + count : 11 + 2 * count]
    (near, near_logs, far_q, far_k, far_v, far, far_logs, got, far_rows, got_rows,
     send, recv, local, keep) = refs[11 + 2 * count : 25 + 2 * count]
    gather_send, gather_recv, gather_local = refs[25 + 2 * count :]
    step = pl.program_id(0)
    place = Place()
    own = OwnBlocks(place, blocks, fulls, gather_local)
    gathers = gathers_of(place, units, blocks, fulls, gather_send, gather_recv)
    turns = in_turn([gather.stages() for gather in gathers], 0.25)
    pairs = near.shape[0]
    fars = pairs // 2
    rows = q_ref.shape[0]
    first, second = place.y == 0, place.y == 1
    partner = place.across("y")
    lane = lax.broadcasted_iota(jnp.int32, (1, 128), 1)
    scale = jnp.bfloat16(HEAD_DIM**-0.5)
    plan = ((q_any, far_q, False), (k_any, far_k, True), (v_any, far_v, True))

    def columns(pair):
        return pl.ds(pl.multiple_of(pair * 128, 128), 128)

    def sending(which, j):
        array, landing, by_first = plan[which]
        return pltpu.make_async_remote_copy(
            src_ref=array.at[:, columns(j if by_first else fars + j)], dst_ref=landing.at[j],
            send_sem=send.at[which, j], recv_sem=recv.at[which, j], device_id=partner, device_id_type=MESH)

    def keeping(which, j):
        array, landing, by_first = plan[which]
        return pltpu.make_async_copy(
            array.at[:, columns(fars + j if by_first else j)], landing.at[j], local.at[which, j])

    def mixture_out(j):
        return pltpu.make_async_remote_copy(
            src_ref=far.at[j], dst_ref=got.at[j], send_sem=send.at[3, j], recv_sem=recv.at[3, j],
            device_id=partner, device_id_type=MESH)

    def logs_out():
        return pltpu.make_async_remote_copy(
            src_ref=far_rows, dst_ref=got_rows, send_sem=send.at[4, 0], recv_sem=recv.at[4, 0],
            device_id=partner, device_id_type=MESH)

    def saving(which):
        return pltpu.make_async_copy(plan[which][1], (fq_out, fk_out, fv_out)[which], keep.at[which])

    @pl.when(step == 0)
    def _():
        place.greet()
        own.start()
        near_logs[...] = jnp.zeros_like(near_logs)
        far_logs[...] = jnp.zeros_like(far_logs)
        for j in range(fars):
            for which in range(3):

                @pl.when(first if plan[which][2] else second)
                def _(which=which, j=j):
                    keeping(which, j).start()

    @pl.when((step % 3 == 0) & (step < 3 * fars))
    def _():
        j = step // 3
        for which in range(3):

            @pl.when(first if plan[which][2] else second)
            def _(which=which):
                @pl.when(j > 0)
                def _():
                    sending(which, j - 1).wait_send()

                sending(which, j).start()

    for at, number in enumerate(events):

        @pl.when(step == at)
        def _(at=at, number=number):
            if at == 0:
                own.wait()
            for unused in range(number):
                next(turns, None)

    @pl.when(step < pairs)
    def _():
        for start in range(0, rows, tile):
            n = min(tile, rows - start)

            def put(logs, start=start, n=n):
                kept = near_logs[start : start + n, :]
                for h in range(2):
                    kept = jnp.where(lane == 2 * step + h, logs[h], kept)
                near_logs[start : start + n, :] = kept

            spans = ([(0, start)] if start else []) + [(start, n)]
            near[step, start : start + n, :] = attend_rows(
                q_ref[start : start + n, :] * scale, k_ref, v_ref, spans, start, put)

    @pl.when((step >= pairs) & (step < pairs + fars))
    def _():
        j = step - pairs
        for which in range(3):
            by_first = plan[which][2]

            @pl.when(first if by_first else second)
            def _(which=which):
                keeping(which, j).wait()

            @pl.when(second if by_first else first)
            def _(which=which):
                sending(which, j).wait_recv()

        base = jnp.where(first, 2 * fars, 0)
        for start in range(0, rows, tile):
            n = min(tile, rows - start)

            def put(logs, start=start, n=n):
                kept = far_logs[start : start + n, :]
                for h in range(2):
                    kept = jnp.where(lane == base + 2 * j + h, logs[h], kept)
                far_logs[start : start + n, :] = kept

            far[j, start : start + n, :] = attend_rows(
                far_q[j, start : start + n, :] * scale, far_k.at[j], far_v.at[j], [(0, rows)], None, put
            ).astype(far.dtype)

        @pl.when(first)
        def _():
            mixture_out(j).start()

    @pl.when(step == pairs + fars)
    def _():
        for which in range(3):
            saving(which).start()

        @pl.when(first)
        def _():
            far_rows[...] = rows_of(far_logs, 2 * fars)
            logs_out().start()
            for pair in range(pairs):
                mix_ref[:, pair * 128 : (pair + 1) * 128] = near[pair].astype(mix_ref.dtype)
            logs_ref[...] = near_logs[...]
            logs_out().wait_send()
            for j in range(fars):
                mixture_out(j).wait_send()
            for which in (1, 2):
                sending(which, fars - 1).wait_send()

        @pl.when(second)
        def _():
            logs_out().wait_recv()
            for j in range(fars):
                mixture_out(j).wait_recv()
            sending(0, fars - 1).wait_send()
            spread_out = (lax.broadcasted_iota(jnp.int32, (8, 128), 0) + 2 * fars == lane).astype(jnp.float32)
            theirs = lax.dot_general(
                got_rows[...], spread_out, TN, precision=lax.Precision.HIGHEST, preferred_element_type=jnp.float32)
            logs_far = far_logs[...] + theirs
            logs_near = near_logs[...]
            top = jnp.maximum(logs_near, logs_far)
            total = top + jnp.log(jnp.exp(logs_near - top) + jnp.exp(logs_far - top))
            logs_ref[...] = total
            share = jnp.exp(logs_near - total)
            low = lane < HEAD_DIM
            for pair in range(pairs):
                part = jnp.where(low, share[:, 2 * pair : 2 * pair + 1], share[:, 2 * pair + 1 : 2 * pair + 2])
                other = (far[pair] if pair < fars else got[pair - fars]).astype(jnp.float32)
                mix_ref[:, pair * 128 : (pair + 1) * 128] = (other + (near[pair] - other) * part).astype(mix_ref.dtype)

        for which in range(3):
            saving(which).wait()
        for unused in turns:
            pass
        for gather in gathers:
            gather.finish()


def pair_attend(q, k, v, blocks, collective_id, events, tile=384):
    rows, width = q.shape
    pairs = width // 128
    fars = pairs // 2
    block = pl.BlockSpec((rows, 128), lambda i: (0, jnp.minimum(i, pairs - 1)))
    anywhere = pl.BlockSpec(memory_space=pl.ANY)
    kept = jax.ShapeDtypeStruct((fars, rows, 128), jnp.bfloat16)
    half = pltpu.VMEM((fars, rows, 128), jnp.bfloat16)
    fulls, units, scratch = gather_plan(blocks, 256, ACROSS)
    count = len(blocks)
    result = pl.pallas_call(
        functools.partial(pair_attend_kernel, tile, units, count, events),
        grid=(pairs + fars + 1,),
        in_specs=[block] * 3 + [anywhere] * (3 + count),
        out_specs=[pl.BlockSpec((rows, width), lambda i: (0, 0)), pl.BlockSpec((rows, 128), lambda i: (0, 0))] + [anywhere] * (3 + count),
        out_shape=[
            jax.ShapeDtypeStruct((rows, width), jnp.bfloat16), jax.ShapeDtypeStruct((rows, 128), jnp.float32), kept, kept, kept, *fulls],
        scratch_shapes=[
            pltpu.VMEM((pairs, rows, 128), jnp.float32), pltpu.VMEM((rows, 128), jnp.float32),
            half, half, half, half, pltpu.VMEM((rows, 128), jnp.float32), half,
            pltpu.VMEM((8, rows), jnp.float32), pltpu.VMEM((8, rows), jnp.float32),
            pltpu.SemaphoreType.DMA((5, fars)), pltpu.SemaphoreType.DMA((5, fars)),
            pltpu.SemaphoreType.DMA((3, fars)), pltpu.SemaphoreType.DMA((3,)), *scratch,
        ],
        compiler_params=pltpu.CompilerParams(
            collective_id=collective_id, has_side_effects=True, vmem_limit_bytes=48 << 20),
        cost_estimate=pl.CostEstimate(
            flops=4 * rows * rows * width, bytes_accessed=16 * rows * width, transcendentals=rows * rows * pairs * 2),
    )(q, k, v, q, k, v, *blocks)
    return result[:5], result[5:]


def back_pair(tile, causal, q_ref, k_ref, v_ref, do_ref, stats, acc, put):
    rows, keys = q_ref.shape[0], k_ref.shape[0]
    low = lax.broadcasted_iota(jnp.int32, (1, 128), 1) < HEAD_DIM
    acc[...] = jnp.zeros_like(acc)
    for start in range(0, keys, tile):
        n = min(tile, keys - start)
        k = k_ref[start : start + n, :] * jnp.bfloat16(HEAD_DIM**-0.5)
        v = v_ref[start : start + n, :]
        spans = [(0, rows)]
        if causal:
            spans = [(start, n)] + ([(start + n, rows - start - n)] if start + n < rows else [])
        dks, dvs = [], []
        for h in range(2):
            mine = low if h == 0 else jnp.logical_not(low)
            kh, vh = jnp.where(mine, k, jnp.bfloat16(0)), jnp.where(mine, v, jnp.bfloat16(0))
            dk = dv = None
            for at, length in spans:
                qs, do = q_ref[at : at + length, :], do_ref[at : at + length, :]
                p = jnp.exp(dg(kh, qs, NT) - stats[h : h + 1, at : at + length])
                if causal and at == start:
                    allowed = lax.broadcasted_iota(jnp.int32, p.shape, 0) <= lax.broadcasted_iota(jnp.int32, p.shape, 1)
                    p = jnp.where(allowed, p, 0.0)
                ds = (p * (dg(vh, do, NT) - stats[2 + h : 3 + h, at : at + length])).astype(jnp.bfloat16)
                a, b = dg(p.astype(jnp.bfloat16), do, NN), dg(ds, qs, NN)
                dv = a if dv is None else dv + a
                dk = b if dk is None else dk + b
                acc[at : at + length, :] += dg(ds, kh, TN)
            dks.append(dk)
            dvs.append(dv)
        put(start, n, jnp.where(low, dks[0], dks[1]) * HEAD_DIM**-0.5, jnp.where(low, dvs[0], dvs[1]))


def pair_stats(pair, mix_ref, do_ref, logs_ref):
    lane = lax.broadcasted_iota(jnp.int32, (8, 128), 1)
    line = lax.broadcasted_iota(jnp.int32, (8, 128), 0)
    picked = ((line < 2) & (line + 2 * pair == lane)).astype(jnp.float32)
    halves = (((line == 2) & (lane < HEAD_DIM)) | ((line == 3) & (lane >= HEAD_DIM))).astype(jnp.float32)
    products = mix_ref[...].astype(jnp.float32) * do_ref[...].astype(jnp.float32)
    logs = lax.dot_general(
        picked, logs_ref[...], NT, precision=lax.Precision.HIGH, preferred_element_type=jnp.float32)
    return logs + lax.dot_general(
        halves, products, NT, precision=lax.Precision.HIGH, preferred_element_type=jnp.float32)


def both_heads(array):
    low = lax.broadcasted_iota(jnp.int32, (1, 128), 1) < HEAD_DIM
    zero = jnp.zeros_like(array)
    return jnp.concatenate([jnp.where(low, array, zero), jnp.where(low, zero, array)], axis=0)


def one_head_each(array):
    low = lax.broadcasted_iota(jnp.int32, (1, 128), 1) < HEAD_DIM
    half = array.shape[0] // 2
    return jnp.where(low, array[:half], array[half:])


def cross_kernel(q_ref, k_ref, v_ref, mix_ref, logs_ref):
    pair = pl.program_id(0)
    keys = k_ref.shape[0]
    lane = lax.broadcasted_iota(jnp.int32, (1, 128), 1)
    lower = lax.broadcasted_iota(jnp.int32, (1, 2 * keys), 1) < keys

    @pl.when(pair == 0)
    def _():
        logs_ref[...] = jnp.zeros_like(logs_ref)

    scores = dg(q_ref[...] * jnp.bfloat16(HEAD_DIM**-0.5), both_heads(k_ref[...]), NT)
    tops = [
        jnp.max(jnp.where(lower if h == 0 else jnp.logical_not(lower), scores, -1e30), axis=1, keepdims=True) for h in range(2)
    ]
    powers = jnp.exp(scores - jnp.where(lower, tops[0], tops[1])).astype(jnp.bfloat16)
    values = both_heads(v_ref[...])
    ones = both_heads(jnp.ones(v_ref.shape, v_ref.dtype))
    out = dg(powers, jnp.concatenate([values, ones], axis=1), NN)
    totals = out[:, 128:]
    mix_ref[...] = (out[:, :128] / totals).astype(mix_ref.dtype)
    sums = jnp.log(totals)
    logs = logs_ref[...]
    for h in range(2):
        logs = jnp.where(lane == 2 * pair + h, tops[h] + sums[:, h * HEAD_DIM : h * HEAD_DIM + 1], logs)
    logs_ref[...] = logs


def cross(q, k, v):
    rows, width = q.shape
    keys = k.shape[0]
    long, short = pl.BlockSpec((rows, 128), lambda i: (0, i)), pl.BlockSpec((keys, 128), lambda i: (0, i))
    return pl.pallas_call(
        cross_kernel,
        grid=(width // 128,),
        in_specs=[long, short, short],
        out_specs=[long, pl.BlockSpec((rows, 128), lambda i: (0, 0))],
        out_shape=[jax.ShapeDtypeStruct((rows, width), jnp.bfloat16), jax.ShapeDtypeStruct((rows, 128), jnp.float32)],
        compiler_params=pltpu.CompilerParams(vmem_limit_bytes=40 << 20),
        cost_estimate=pl.CostEstimate(
            flops=4 * rows * keys * width, bytes_accessed=6 * rows * width, transcendentals=rows * keys * width // HEAD_DIM),
    )(q, k, v)


def cross_back_kernel(q_ref, k_ref, v_ref, do_ref, mix_ref, logs_ref, dq_ref, dk_ref, dv_ref):
    keys = k_ref.shape[0]
    stats = pair_stats(pl.program_id(0), mix_ref, do_ref, logs_ref)
    upper = lax.broadcasted_iota(jnp.int32, (2 * keys, 1), 0) < keys
    k, v, do = both_heads(k_ref[...] * jnp.bfloat16(HEAD_DIM**-0.5)), both_heads(v_ref[...]), do_ref[...]
    p = jnp.exp(dg(k, q_ref[...], NT) - jnp.where(upper, stats[0:1, :], stats[1:2, :]))
    ds = (p * (dg(v, do, NT) - jnp.where(upper, stats[2:3, :], stats[3:4, :]))).astype(jnp.bfloat16)
    dv_ref[...] = one_head_each(dg(p.astype(jnp.bfloat16), do, NN)).astype(dv_ref.dtype)
    dk_ref[...] = (one_head_each(dg(ds, q_ref[...], NN)) * HEAD_DIM**-0.5).astype(dk_ref.dtype)
    dq_ref[...] = dg(ds, k, TN).astype(dq_ref.dtype)


def cross_back(q, k, v, do, mix, logs):
    rows, width = q.shape
    keys = k.shape[0]
    long, short = pl.BlockSpec((rows, 128), lambda i: (0, i)), pl.BlockSpec((keys, 128), lambda i: (0, i))
    return pl.pallas_call(
        cross_back_kernel,
        grid=(width // 128,),
        in_specs=[long, short, short, long, long, pl.BlockSpec((rows, 128), lambda i: (0, 0))],
        out_specs=[long, short, short],
        out_shape=[jax.ShapeDtypeStruct(a.shape, jnp.bfloat16) for a in (q, k, v)],
        compiler_params=pltpu.CompilerParams(vmem_limit_bytes=40 << 20),
        cost_estimate=pl.CostEstimate(
            flops=10 * rows * keys * width, bytes_accessed=10 * rows * width, transcendentals=rows * keys * width // HEAD_DIM),
    )(q, k, v, do, mix, logs)


def pair_back_kernel(tile, far_tile, units, count, events, *refs):
    q_ref, k_ref, v_ref, do_ref, mix_ref, logs_ref, do_any, fq_any, fk_any, fv_any = refs[:10]
    grads, (dq_ref, dk_ref, dv_ref) = refs[10 : 10 + count], refs[10 + count : 13 + count]
    sums = refs[13 + count : 13 + 2 * count]
    (near, acc, stats, far_stats, used_stats, far_q, far_k, far_v, far_do, far_dq, far_dk, far_dv, got_q, got_k, got_v,
     send, recv, local, do_local) = refs[13 + 2 * count : 32 + 2 * count]
    scatter_refs = refs[32 + 2 * count :]
    step = pl.program_id(0)
    place = Place()
    pairs = near.shape[1]
    fars = pairs // 2
    first, second = place.y == 0, place.y == 1
    partner = place.across("y")

    def columns(pair):
        return pl.ds(pl.multiple_of(pair * 128, 128), 128)

    def remote(source, target, which, j):
        return pltpu.make_async_remote_copy(
            src_ref=source, dst_ref=target, send_sem=send.at[which, j], recv_sem=recv.at[which, j],
            device_id=partner, device_id_type=MESH)

    def grad_over(j):
        return remote(do_any.at[:, columns(fars + j)], far_do.at[j], 0, j)

    def grad_kept(j):
        return pltpu.make_async_copy(do_any.at[:, columns(j)], far_do.at[j], do_local.at[j])

    def stats_over():
        return remote(stats.at[pl.ds(fars, fars)], far_stats, 4, 0)

    def back_over(which, j):
        source, target = ((far_dq, got_q), (far_dk, got_k), (far_dv, got_v))[which]
        return remote(source.at[j], target.at[j], 1 + which, j)

    def far_in(which):
        source, target = ((fq_any, far_q), (fk_any, far_k), (fv_any, far_v))[which]
        return pltpu.make_async_copy(source, target, local.at[which])

    scatters = scatters_of(place, units, grads, sums, *scatter_refs[:3], scatter_refs[3:])
    turns = in_turn([scatter.stages() for scatter in scatters], 0.25)

    @pl.when(step == 0)
    def _():
        place.greet()
        for which in range(3):
            far_in(which).start()
        for j in range(fars):

            @pl.when(second)
            def _(j=j):
                grad_over(j).start()

            @pl.when(second)
            def _(j=j):
                grad_kept(j).start()

    for at, number in enumerate(events):

        @pl.when(step == at)
        def _(number=number):
            for unused in range(number):
                next(turns, None)

    @pl.when((step == fars) & second)
    def _():
        stats_over().start()

    @pl.when(step < pairs)
    def _():
        pair = lax.rem(step + fars, pairs)
        stats[pair] = pair_stats(pair, mix_ref, do_ref, logs_ref)

        def put(start, n, dk, dv):
            near[1, pair, start : start + n, :] = dk
            near[2, pair, start : start + n, :] = dv

        back_pair(tile, True, q_ref, k_ref, v_ref, do_ref, stats.at[pair], acc, put)
        near[0, pair] = acc[...]

    @pl.when((step >= pairs) & (step < pairs + fars))
    def _():
        j = step - pairs

        @pl.when(j == 0)
        def _():
            for which in range(3):
                far_in(which).wait()

            @pl.when(first)
            def _():
                stats_over().wait_recv()

        @pl.when(first)
        def _():
            grad_over(j).wait_recv()
            used_stats[...] = far_stats[j]

        @pl.when(second)
        def _():
            grad_kept(j).wait()
            used_stats[...] = stats[j]

        def put(start, n, dk, dv):
            far_dk[j, start : start + n, :] = dk.astype(far_dk.dtype)
            far_dv[j, start : start + n, :] = dv.astype(far_dv.dtype)

        back_pair(far_tile, False, far_q.at[j], far_k.at[j], far_v.at[j], far_do.at[j], used_stats, acc, put)
        far_dq[j] = acc[...].astype(far_dq.dtype)

        @pl.when(first)
        def _():
            back_over(0, j).start()

        @pl.when(second)
        def _():
            back_over(1, j).start()
            back_over(2, j).start()

    @pl.when(step >= pairs + fars)
    def _():
        pair = step - pairs - fars
        lower = pair < fars
        j = lax.rem(pair, fars)

        def write(ref, which, other):
            total = near[which, pair]
            if other is not None:
                total = total + other[j].astype(jnp.float32)
            ref[...] = total.astype(ref.dtype)

        @pl.when(first & lower)
        def _():
            for which in (1, 2):
                back_over(which, j).wait_recv()
            write(dq_ref, 0, None)
            write(dk_ref, 1, got_k)
            write(dv_ref, 2, got_v)

        @pl.when(first & jnp.logical_not(lower))
        def _():
            write(dq_ref, 0, None)
            write(dk_ref, 1, far_dk)
            write(dv_ref, 2, far_dv)

        @pl.when(second & lower)
        def _():
            write(dq_ref, 0, far_dq)
            write(dk_ref, 1, None)
            write(dv_ref, 2, None)

        @pl.when(second & jnp.logical_not(lower))
        def _():
            back_over(0, j).wait_recv()
            write(dq_ref, 0, got_q)
            write(dk_ref, 1, None)
            write(dv_ref, 2, None)

    @pl.when(step == 2 * pairs + fars - 1)
    def _():
        for unused in turns:
            pass
        for scatter in scatters:
            scatter.finish()

        @pl.when(first)
        def _():
            for j in range(fars):
                back_over(0, j).wait_send()

        @pl.when(second)
        def _():
            stats_over().wait_send()
            for j in range(fars):
                grad_over(j).wait_send()
                for which in (1, 2):
                    back_over(which, j).wait_send()


def pair_back(q, k, v, do, mix, logs, far, grads, collective_id, events, tile=384, far_tile=256):
    rows, width = q.shape
    pairs = width // 128
    fars = pairs // 2
    blocks, units, scratch = scatter_plan(grads, 256, SCATTER_ORDERS)
    count = len(grads)
    block = pl.BlockSpec((rows, 128), lambda i: (0, lax.rem(jnp.minimum(i, pairs - 1) + fars, pairs)))
    joined = pl.BlockSpec((rows, 128), lambda i: (0, jnp.maximum(i - pairs - fars, 0)))
    anywhere = pl.BlockSpec(memory_space=pl.ANY)
    half = pltpu.VMEM((fars, rows, 128), jnp.bfloat16)
    out = jax.ShapeDtypeStruct((rows, width), jnp.bfloat16)
    result = pl.pallas_call(
        functools.partial(pair_back_kernel, tile, far_tile, units, count, events),
        grid=(2 * pairs + fars,),
        in_specs=[block] * 5 + [pl.BlockSpec((rows, 128), lambda i: (0, 0))] + [anywhere] * (4 + count),
        out_specs=[joined] * 3 + [pl.BlockSpec(memory_space=pltpu.VMEM)] * count,
        out_shape=[out] * 3 + blocks,
        scratch_shapes=[
            pltpu.VMEM((3, pairs, rows, 128), jnp.float32), pltpu.VMEM((rows, 128), jnp.float32),
            pltpu.VMEM((pairs, 8, rows), jnp.float32), pltpu.VMEM((fars, 8, rows), jnp.float32),
            pltpu.VMEM((8, rows), jnp.float32), *[half] * 10,
            pltpu.SemaphoreType.DMA((5, fars)), pltpu.SemaphoreType.DMA((5, fars)),
            pltpu.SemaphoreType.DMA((3,)), pltpu.SemaphoreType.DMA((fars,)), *scratch,
        ],
        compiler_params=pltpu.CompilerParams(
            collective_id=collective_id, has_side_effects=True, vmem_limit_bytes=62 << 20),
        cost_estimate=pl.CostEstimate(
            flops=10 * rows * rows * width, bytes_accessed=16 * rows * width, transcendentals=rows * rows * pairs * 2),
    )(q, k, v, do, mix, logs, do, *far, *grads)
    return result[:3], result[3:]


def fast(
    frames_in, text_states, self_query, self_key, self_value, self_output, cross_query, cross_key, cross_value, cross_output,
    up_weight, down_weight, first_gain, first_bias, second_gain, second_bias, third_gain, third_bias, cotangent,
):
    row = lax.axis_index("row")
    rows, width = frames_in.shape
    half = width // 2
    piece = first_gain.shape[0]
    block_rows, block_cols = self_query.shape
    back = row % 2
    pairs = lax.axis_size("row") // 2
    forth_perm = [(2 * i, 2 * i + 1) for i in range(pairs)]
    back_perm = [(2 * i + 1, 2 * i) for i in range(pairs)]
    swap = forth_perm + back_perm

    def forth(array):
        return lax.ppermute(array, "row", forth_perm)

    def home(array):
        return lax.ppermute(array, "row", back_perm)

    def by_side(first, second):
        return jnp.where(back == 0, first, second)

    gains = jnp.zeros((1, 16, 128), jnp.bfloat16)
    gains = gains.at[0, :6, :piece].set(
        jnp.stack([first_gain, first_bias, second_gain, second_bias, third_gain, third_bias])
    )

    everyone = ("row", "col")
    places = (lax.axis_size("row"), lax.axis_size("col"))
    up_blocks = lax.all_gather(up_weight, everyone).reshape(*places, *up_weight.shape)
    down_blocks = lax.all_gather(down_weight, everyone).reshape(*places, *down_weight.shape)

    def small(block):
        return block.reshape(1, block_rows, block_cols)

    def flat(array):
        return array.reshape(-1, array.shape[-1])

    early = gather_blocks(
        [small(self_query), small(self_key), small(self_value), gains], 1, 128)
    query_self, key_self, value_self = [flat(w) for w in early[:3]]
    norm_params = early[3].reshape(pairs * 2, 16, -1, 128)[:, :6, :, :piece].transpose(1, 0, 2, 3)
    norm_params = norm_params.reshape(6, width).astype(jnp.float32)

    frames = frames_in.astype(jnp.float32)
    hidden_one = norm_forward(frames, norm_params[0], norm_params[1]).astype(jnp.bfloat16)
    self_k = matmul(hidden_one, key_self).astype(jnp.bfloat16)
    self_v = matmul(hidden_one, value_self).astype(jnp.bfloat16)
    self_q = matmul(hidden_one, query_self).astype(jnp.bfloat16)
    (self_mix, log_lanes, far_q, far_k, far_v), late = pair_attend(
        self_q, self_k, self_v, [small(w) for w in (self_output, cross_query, cross_key, cross_value, cross_output)],
        5, [3] * 12)
    out_self, query_cross, key_cross, value_cross, out_cross = [flat(w) for w in late]
    resid_one = frames + matmul(self_mix, out_self)
    hidden_two = norm_forward(resid_one, norm_params[2], norm_params[3]).astype(jnp.bfloat16)
    cross_q = matmul(hidden_two, query_cross).astype(jnp.bfloat16)
    other_text = lax.ppermute(text_states, "row", swap)
    clip_text = by_side(
        jnp.concatenate([text_states, other_text]), jnp.concatenate([other_text, text_states])
    )
    text_k = matmul(clip_text, key_cross).astype(jnp.bfloat16)
    text_v = matmul(clip_text, value_cross).astype(jnp.bfloat16)
    cross_mix, cross_logs = cross(cross_q, text_k, text_v)
    resid_two = resid_one + matmul(cross_mix, out_cross)
    hidden_three = norm_forward(resid_two, norm_params[4], norm_params[5]).astype(jnp.bfloat16)
    layer_out, grad_three, up_grad, down_grad = feed(hidden_three, cotangent, resid_two, up_blocks, down_blocks)
    up_sum = lax.psum_scatter(up_grad.reshape(-1, *up_weight.shape), everyone, scatter_dimension=0).astype(jnp.float32)

    cotan_full = cotangent.astype(jnp.float32)
    unused_three, pull_three = jax.vjp(norm_forward, resid_two, norm_params[4], norm_params[5])
    through_three, third_gain_part, third_bias_part = pull_three(grad_three)
    grad_resid_two = cotan_full + through_three
    grad_cross = grad_resid_two.astype(jnp.bfloat16)
    cross_out_grad = over_tokens(cross_mix, grad_cross)
    grad_cross_mix = by_transposed(grad_cross, out_cross).astype(jnp.bfloat16)
    grad_cross_q, text_k_part, text_v_part = cross_back(cross_q, text_k, text_v, grad_cross_mix, cross_mix, cross_logs)
    text_rows = text_states.shape[0]
    text_parts = jnp.concatenate([text_k_part, text_v_part], axis=1)
    given = lax.ppermute(by_side(text_parts[text_rows:], text_parts[:text_rows]), "row", swap)
    kept = by_side(text_parts[:text_rows], text_parts[text_rows:])
    text_parts = (kept.astype(jnp.float32) + given.astype(jnp.float32)).astype(jnp.bfloat16)
    grad_text_k, grad_text_v = text_parts[:, :width], text_parts[:, width:]
    cross_query_part = over_tokens(hidden_two, grad_cross_q)
    cross_key_part = over_tokens(text_states, grad_text_k)
    cross_value_part = over_tokens(text_states, grad_text_v)
    text_grad = by_transposed(grad_text_k, key_cross) + by_transposed(grad_text_v, value_cross)
    grad_two = by_transposed(grad_cross_q, query_cross)
    unused_two, pull_two = jax.vjp(norm_forward, resid_one, norm_params[2], norm_params[3])
    through_two, second_gain_part, second_bias_part = pull_two(grad_two)
    grad_resid_one = grad_resid_two + through_two
    grad_self = grad_resid_one.astype(jnp.bfloat16)
    self_out_grad = over_tokens(self_mix, grad_self)
    grad_self_mix = by_transposed(grad_self, out_self).astype(jnp.bfloat16)

    def by_place(grad, parts):
        return grad.astype(jnp.bfloat16).reshape(pairs, 2, parts, -1, grad.shape[-1])

    (grad_self_q, grad_self_k, grad_self_v), early_sums = pair_back(
        self_q, self_k, self_v, grad_self_mix, self_mix, log_lanes, (far_q, far_k, far_v),
        [by_place(g, 1) for g in (self_out_grad, cross_query_part, cross_key_part, cross_value_part, cross_out_grad)]
        + [by_place(down_grad, down_weight.shape[0] // block_rows)], 4, [5] * 12)
    self_query_part = over_tokens(hidden_one, grad_self_q)
    self_key_part = over_tokens(hidden_one, grad_self_k)
    self_value_part = over_tokens(hidden_one, grad_self_v)
    grad_one = (
        by_transposed(grad_self_q, query_self)
        + by_transposed(grad_self_k, key_self)
        + by_transposed(grad_self_v, value_self)
    )
    unused_one, pull_one = jax.vjp(norm_forward, frames, norm_params[0], norm_params[1])
    through_one, first_gain_part, first_bias_part = pull_one(grad_one)
    input_grad = grad_resid_one + through_one
    norm_grads = jnp.stack(
        [first_gain_part, first_bias_part, second_gain_part, second_bias_part, third_gain_part, third_bias_part]
    )
    norm_grads = norm_grads.reshape(6, 2 * pairs, -1, piece).transpose(1, 0, 2, 3)
    norm_grads = jnp.pad(norm_grads, ((0, 0), (0, 10), (0, 0), (0, 128 - piece)))

    late_sums = scatter_blocks(
        [by_place(g, 1) for g in (self_query_part, self_key_part, self_value_part)]
        + [by_place(norm_grads.reshape(2 * pairs * 16, -1), 1)], 3, 128)
    norm_parts = late_sums[3][0, :6, :piece]
    sums = [*late_sums[:3], *early_sums]
    sums = [total.reshape(-1, total.shape[-1]) for total in sums]
    return (layer_out, input_grad, text_grad, *sums[:-1], up_sum, sums[-1], *norm_parts)


def local(*arrays):
    frames_in, self_query = arrays[0], arrays[2]
    halves = 2 * frames_in.shape[0] == FRAMES and lax.axis_size("row") % 2 == 0
    if halves and lax.axis_size("col") % 2 == 0 and self_query.shape[1] % 256 == 0 and self_query.shape[0] % 128 == 0:
        return fast(*arrays)
    return general(*arrays)


def solution(mesh):
    placed = (
        P(("col", "row"), None),
        P(("col", "row"), None),
        P("row", "col"),
        P("row", "col"),
        P("row", "col"),
        P("row", "col"),
        P("row", "col"),
        P("row", "col"),
        P("row", "col"),
        P("row", "col"),
        P("row", "col"),
        P("row", "col"),
        P(("row", "col")),
        P(("row", "col")),
        P(("row", "col")),
        P(("row", "col")),
        P(("row", "col")),
        P(("row", "col")),
        P(("col", "row"), None),
    )
    return jax.shard_map(
        local,
        mesh=mesh,
        in_specs=placed,
        out_specs=(
            P(("col", "row"), None),
            P(("col", "row"), None),
            P(("col", "row"), None),
            P("row", "col"),
            P("row", "col"),
            P("row", "col"),
            P("row", "col"),
            P("row", "col"),
            P("row", "col"),
            P("row", "col"),
            P("row", "col"),
            P("row", "col"),
            P("row", "col"),
            P(("row", "col")),
            P(("row", "col")),
            P(("row", "col")),
            P(("row", "col")),
            P(("row", "col")),
            P(("row", "col")),
        ),
        check_vma=False,
    )
```

```python
import functools
from functools import partial

import jax
import jax.numpy as jnp
from jax import lax
from jax.experimental import pallas as pl
from jax.experimental.pallas import tpu as pltpu
from jax.sharding import PartitionSpec as P

HEADS = 16
HEAD_DIM = 64
FRAMES = 1500
TEXT = 64


def norm_forward(values, norm_gain, norm_bias):
    center = values - jnp.mean(values, axis=-1, keepdims=True)
    variance = jnp.mean(center * center, axis=-1, keepdims=True)
    return center * lax.rsqrt(variance + 1e-05) * norm_gain + norm_bias


def matmul(left, right):
    return jnp.dot(left, right, preferred_element_type=jnp.float32)


def by_transposed(left, right):
    return lax.dot_general(
        left, right, (((1,), (1,)), ((), ())), preferred_element_type=jnp.float32
    )


def over_tokens(left, right):
    return lax.dot_general(
        left, right, (((0,), (0,)), ((), ())), preferred_element_type=jnp.float32
    )


def collect(blocks):
    partly = (
        lax.all_gather(blocks[0], "col", axis=1, tiled=True),
        lax.all_gather(blocks[1], "col", axis=1, tiled=True),
        lax.all_gather(blocks[2], "col", axis=1, tiled=True),
        lax.all_gather(blocks[3], "col", axis=1, tiled=True),
        lax.all_gather(blocks[4], "col", axis=1, tiled=True),
        lax.all_gather(blocks[5], "col", axis=1, tiled=True),
        lax.all_gather(blocks[6], "col", axis=1, tiled=True),
        lax.all_gather(blocks[7], "col", axis=1, tiled=True),
        lax.all_gather(blocks[8], "col", axis=1, tiled=True),
        lax.all_gather(blocks[9], "col", axis=1, tiled=True),
        lax.all_gather(blocks[10], "col", axis=1, tiled=True),
    )
    return (
        lax.all_gather(partly[0], "row", axis=0, tiled=True),
        lax.all_gather(partly[1], "row", axis=0, tiled=True),
        lax.all_gather(partly[2], "row", axis=0, tiled=True),
        lax.all_gather(partly[3], "row", axis=0, tiled=True),
        lax.all_gather(partly[4], "row", axis=0, tiled=True),
        lax.all_gather(partly[5], "row", axis=0, tiled=True),
        lax.all_gather(partly[6], "row", axis=0, tiled=True),
        lax.all_gather(partly[7], "row", axis=0, tiled=True),
        lax.all_gather(partly[8], "row", axis=0, tiled=True),
        lax.all_gather(partly[9], "row", axis=0, tiled=True),
        lax.all_gather(partly[10], "row", axis=0, tiled=True),
    )


def spread(grads):
    partly = (
        lax.psum_scatter(
            grads[0].astype(jnp.bfloat16), "row", scatter_dimension=0, tiled=True
        ).astype(jnp.float32),
        lax.psum_scatter(
            grads[1].astype(jnp.bfloat16), "row", scatter_dimension=0, tiled=True
        ).astype(jnp.float32),
        lax.psum_scatter(
            grads[2].astype(jnp.bfloat16), "row", scatter_dimension=0, tiled=True
        ).astype(jnp.float32),
        lax.psum_scatter(
            grads[3].astype(jnp.bfloat16), "row", scatter_dimension=0, tiled=True
        ).astype(jnp.float32),
        lax.psum_scatter(
            grads[4].astype(jnp.bfloat16), "row", scatter_dimension=0, tiled=True
        ).astype(jnp.float32),
        lax.psum_scatter(
            grads[5].astype(jnp.bfloat16), "row", scatter_dimension=0, tiled=True
        ).astype(jnp.float32),
        lax.psum_scatter(
            grads[6].astype(jnp.bfloat16), "row", scatter_dimension=0, tiled=True
        ).astype(jnp.float32),
        lax.psum_scatter(
            grads[7].astype(jnp.bfloat16), "row", scatter_dimension=0, tiled=True
        ).astype(jnp.float32),
        lax.psum_scatter(
            grads[8].astype(jnp.bfloat16), "row", scatter_dimension=0, tiled=True
        ).astype(jnp.float32),
        lax.psum_scatter(
            grads[9].astype(jnp.bfloat16), "row", scatter_dimension=0, tiled=True
        ).astype(jnp.float32),
        lax.psum_scatter(
            grads[10].astype(jnp.bfloat16), "row", scatter_dimension=0, tiled=True
        ).astype(jnp.float32),
    )
    return (
        lax.psum_scatter(
            partly[0].astype(jnp.bfloat16), "col", scatter_dimension=1, tiled=True
        ).astype(jnp.float32),
        lax.psum_scatter(
            partly[1].astype(jnp.bfloat16), "col", scatter_dimension=1, tiled=True
        ).astype(jnp.float32),
        lax.psum_scatter(
            partly[2].astype(jnp.bfloat16), "col", scatter_dimension=1, tiled=True
        ).astype(jnp.float32),
        lax.psum_scatter(
            partly[3].astype(jnp.bfloat16), "col", scatter_dimension=1, tiled=True
        ).astype(jnp.float32),
        lax.psum_scatter(
            partly[4].astype(jnp.bfloat16), "col", scatter_dimension=1, tiled=True
        ).astype(jnp.float32),
        lax.psum_scatter(
            partly[5].astype(jnp.bfloat16), "col", scatter_dimension=1, tiled=True
        ).astype(jnp.float32),
        lax.psum_scatter(
            partly[6].astype(jnp.bfloat16), "col", scatter_dimension=1, tiled=True
        ).astype(jnp.float32),
        lax.psum_scatter(
            partly[7].astype(jnp.bfloat16), "col", scatter_dimension=1, tiled=True
        ).astype(jnp.float32),
        lax.psum_scatter(
            partly[8].astype(jnp.bfloat16), "col", scatter_dimension=1, tiled=True
        ).astype(jnp.float32),
        lax.psum_scatter(
            partly[9].astype(jnp.bfloat16), "col", scatter_dimension=1, tiled=True
        ).astype(jnp.float32),
        lax.psum_scatter(
            partly[10].astype(jnp.bfloat16), "col", scatter_dimension=1, tiled=True
        ).astype(jnp.float32),
    )


def heads_layout(stacked):
    return lax.all_to_all(stacked, "row", split_axis=1, concat_axis=0, tiled=True)


def tokens_layout(stacked):
    return lax.all_to_all(stacked, "row", split_axis=0, concat_axis=2, tiled=True)


def by_clips(arranged, start, count, length, heads_dev):
    section = arranged[:, start : start + count]
    return section.reshape(-1, length, heads_dev, HEAD_DIM)


def causal_scores(query_clip, key_clip, causal):
    scores = jnp.einsum(
        "qhd,khd->hqk", query_clip, key_clip, preferred_element_type=jnp.float32
    ) * HEAD_DIM ** (-0.5)
    if causal:
        allowed = jnp.arange(scores.shape[1])[:, None] >= jnp.arange(scores.shape[2])[None, :]
        scores = jnp.where(allowed, scores, -1e30)
    return scores


def attend_forward(query_clips, key_clips, value_clips, causal):

    def one_clip(operands):
        query_clip, key_clip, value_clip = operands
        scores = causal_scores(query_clip, key_clip, causal)
        highest = jnp.max(scores, axis=-1, keepdims=True)
        powers = jnp.exp(scores - highest)
        totals = jnp.sum(powers, axis=-1, keepdims=True)
        weights_low = (powers / totals).astype(jnp.bfloat16)
        mixture = jnp.einsum(
            "hqk,khd->qhd", weights_low, value_clip, preferred_element_type=jnp.float32
        )
        return (mixture.astype(jnp.bfloat16), (highest + jnp.log(totals))[..., 0])

    return lax.map(one_clip, (query_clips, key_clips, value_clips))


def attend_backward(query_clips, key_clips, value_clips, log_sums, grad_clips, causal):

    def one_clip(operands):
        query_clip, key_clip, value_clip, log_clip, grad_clip = operands
        scores = causal_scores(query_clip, key_clip, causal)
        probs_full = jnp.exp(scores - log_clip[..., None])
        grad_probs = jnp.einsum(
            "qhd,khd->hqk", grad_clip, value_clip, preferred_element_type=jnp.float32
        )
        grad_value = jnp.einsum(
            "hqk,qhd->khd",
            probs_full.astype(jnp.bfloat16),
            grad_clip,
            preferred_element_type=jnp.float32,
        )
        centered = grad_probs - jnp.sum(probs_full * grad_probs, axis=-1, keepdims=True)
        grad_scores = (probs_full * centered).astype(jnp.bfloat16)
        grad_query = jnp.einsum(
            "hqk,khd->qhd", grad_scores, key_clip, preferred_element_type=jnp.float32
        ) * HEAD_DIM ** (-0.5)
        grad_key = jnp.einsum(
            "hqk,qhd->khd", grad_scores, query_clip, preferred_element_type=jnp.float32
        ) * HEAD_DIM ** (-0.5)
        return (
            grad_query.astype(jnp.bfloat16),
            grad_key.astype(jnp.bfloat16),
            grad_value.astype(jnp.bfloat16),
        )

    return lax.map(one_clip, (query_clips, key_clips, value_clips, log_sums, grad_clips))


def general(
    frames_in,
    text_states,
    self_query,
    self_key,
    self_value,
    self_output,
    cross_query,
    cross_key,
    cross_value,
    cross_output,
    up_weight,
    down_weight,
    first_gain,
    first_bias,
    second_gain,
    second_bias,
    third_gain,
    third_bias,
    cotangent,
):
    row_count = lax.axis_size("row")
    col_count = lax.axis_size("col")
    heads_dev = HEADS // row_count
    width_dev = heads_dev * HEAD_DIM
    tok_rows = frames_in.shape[0]
    text_rows = text_states.shape[0]
    piece_len = first_gain.shape[0]
    gain_block = jnp.stack(
        [first_gain, first_bias, second_gain, second_bias, third_gain, third_bias]
    ).reshape(1, 6 * piece_len)
    param_blocks = (
        self_query,
        self_key,
        self_value,
        self_output,
        cross_query,
        cross_key,
        cross_value,
        cross_output,
        up_weight,
        down_weight,
        gain_block,
    )

    def unpack_gains(gathered_gains):
        arranged = gathered_gains.reshape(row_count, col_count, 6, piece_len).transpose(2, 0, 1, 3)
        return arranged.reshape(6, row_count * col_count * piece_len).astype(jnp.float32)

    gathered = collect(param_blocks)
    (
        query_self,
        key_self,
        value_self,
        out_self,
        query_cross,
        key_cross,
        value_cross,
        out_cross,
        up_full,
        down_full,
    ) = gathered[:10]
    norm_params = unpack_gains(gathered[10])
    frames = frames_in.astype(jnp.float32)
    hidden_one = norm_forward(frames, norm_params[0], norm_params[1]).astype(jnp.bfloat16)
    self_q = matmul(hidden_one, query_self).astype(jnp.bfloat16)
    self_k = matmul(hidden_one, key_self).astype(jnp.bfloat16)
    self_v = matmul(hidden_one, value_self).astype(jnp.bfloat16)
    text_k = matmul(text_states, key_cross).astype(jnp.bfloat16)
    text_v = matmul(text_states, value_cross).astype(jnp.bfloat16)
    sent_rows = 3 * tok_rows + 2 * text_rows
    arranged = heads_layout(jnp.concatenate([self_q, self_k, self_v, text_k, text_v], axis=0))
    arranged = arranged.reshape(row_count, sent_rows, width_dev)
    query_clips = by_clips(arranged, 0, tok_rows, FRAMES, heads_dev)
    key_clips = by_clips(arranged, tok_rows, tok_rows, FRAMES, heads_dev)
    value_clips = by_clips(arranged, 2 * tok_rows, tok_rows, FRAMES, heads_dev)
    text_keys = by_clips(arranged, 3 * tok_rows, text_rows, TEXT, heads_dev)
    text_values = by_clips(arranged, 3 * tok_rows + text_rows, text_rows, TEXT, heads_dev)
    self_clips, self_logs = attend_forward(query_clips, key_clips, value_clips, True)
    self_mix = tokens_layout(self_clips.reshape(row_count, tok_rows, width_dev))[0]
    resid_one = frames + matmul(self_mix, out_self)
    hidden_two = norm_forward(resid_one, norm_params[2], norm_params[3]).astype(jnp.bfloat16)
    cross_q = matmul(hidden_two, query_cross).astype(jnp.bfloat16)
    cross_arranged = heads_layout(cross_q).reshape(row_count, tok_rows, width_dev)
    cross_queries = by_clips(cross_arranged, 0, tok_rows, FRAMES, heads_dev)
    cross_clips, cross_logs = attend_forward(cross_queries, text_keys, text_values, False)
    cross_mix = tokens_layout(cross_clips.reshape(row_count, tok_rows, width_dev))[0]
    resid_two = resid_one + matmul(cross_mix, out_cross)
    hidden_three = norm_forward(resid_two, norm_params[4], norm_params[5]).astype(jnp.bfloat16)
    pre_act = matmul(hidden_three, up_full)
    inner = jax.nn.gelu(pre_act, approximate=False).astype(jnp.bfloat16)
    layer_out = (resid_two + matmul(inner, down_full)).astype(jnp.bfloat16)
    gathered = collect(param_blocks)
    (
        query_self,
        key_self,
        value_self,
        out_self,
        query_cross,
        key_cross,
        value_cross,
        out_cross,
        up_full,
        down_full,
    ) = gathered[:10]
    norm_params = unpack_gains(gathered[10])
    cotan_full = cotangent.astype(jnp.float32)
    down_grad = over_tokens(inner, cotangent)
    grad_inner = by_transposed(cotangent, down_full)
    unused_gelu, gelu_pull = jax.vjp(partial(jax.nn.gelu, approximate=False), pre_act)
    grad_pre = gelu_pull(grad_inner)[0].astype(jnp.bfloat16)
    up_grad = over_tokens(hidden_three, grad_pre)
    grad_three = by_transposed(grad_pre, up_full)
    unused_three, pull_three = jax.vjp(norm_forward, resid_two, norm_params[4], norm_params[5])
    through_three, third_gain_part, third_bias_part = pull_three(grad_three)
    grad_resid_two = cotan_full + through_three
    grad_cross = grad_resid_two.astype(jnp.bfloat16)
    cross_out_grad = over_tokens(cross_mix, grad_cross)
    grad_cross_mix = by_transposed(grad_cross, out_cross).astype(jnp.bfloat16)
    grad_cross_arr = heads_layout(grad_cross_mix).reshape(row_count, tok_rows, width_dev)
    grad_cross_clips = by_clips(grad_cross_arr, 0, tok_rows, FRAMES, heads_dev)
    cq_clips, tk_clips, tv_clips = attend_backward(
        cross_queries, text_keys, text_values, cross_logs, grad_cross_clips, False
    )
    back_cross = jnp.concatenate(
        [
            cq_clips.reshape(row_count, tok_rows, width_dev),
            tk_clips.reshape(row_count, text_rows, width_dev),
            tv_clips.reshape(row_count, text_rows, width_dev),
        ],
        axis=1,
    )
    back_cross = tokens_layout(back_cross)[0]
    grad_cross_q = back_cross[:tok_rows]
    grad_text_k = back_cross[tok_rows : tok_rows + text_rows]
    grad_text_v = back_cross[tok_rows + text_rows :]
    cross_query_part = over_tokens(hidden_two, grad_cross_q)
    cross_key_part = over_tokens(text_states, grad_text_k)
    cross_value_part = over_tokens(text_states, grad_text_v)
    text_grad = by_transposed(grad_text_k, key_cross) + by_transposed(grad_text_v, value_cross)
    grad_two = by_transposed(grad_cross_q, query_cross)
    unused_two, pull_two = jax.vjp(norm_forward, resid_one, norm_params[2], norm_params[3])
    through_two, second_gain_part, second_bias_part = pull_two(grad_two)
    grad_resid_one = grad_resid_two + through_two
    grad_self = grad_resid_one.astype(jnp.bfloat16)
    self_out_grad = over_tokens(self_mix, grad_self)
    grad_self_mix = by_transposed(grad_self, out_self).astype(jnp.bfloat16)
    grad_self_arr = heads_layout(grad_self_mix).reshape(row_count, tok_rows, width_dev)
    grad_self_clips = by_clips(grad_self_arr, 0, tok_rows, FRAMES, heads_dev)
    sq_clips, sk_clips, sv_clips = attend_backward(
        query_clips, key_clips, value_clips, self_logs, grad_self_clips, True
    )
    back_self = jnp.concatenate(
        [
            sq_clips.reshape(row_count, tok_rows, width_dev),
            sk_clips.reshape(row_count, tok_rows, width_dev),
            sv_clips.reshape(row_count, tok_rows, width_dev),
        ],
        axis=1,
    )
    back_self = tokens_layout(back_self)[0]
    grad_self_q = back_self[:tok_rows]
    grad_self_k = back_self[tok_rows : 2 * tok_rows]
    grad_self_v = back_self[2 * tok_rows :]
    self_query_part = over_tokens(hidden_one, grad_self_q)
    self_key_part = over_tokens(hidden_one, grad_self_k)
    self_value_part = over_tokens(hidden_one, grad_self_v)
    grad_one = (
        by_transposed(grad_self_q, query_self)
        + by_transposed(grad_self_k, key_self)
        + by_transposed(grad_self_v, value_self)
    )
    unused_one, pull_one = jax.vjp(norm_forward, frames, norm_params[0], norm_params[1])
    through_one, first_gain_part, first_bias_part = pull_one(grad_one)
    input_grad = grad_resid_one + through_one
    norm_grads = jnp.stack(
        [
            first_gain_part,
            first_bias_part,
            second_gain_part,
            second_bias_part,
            third_gain_part,
            third_bias_part,
        ]
    )
    norm_grads = norm_grads.reshape(6, row_count, col_count, piece_len).transpose(1, 2, 0, 3)
    norm_grads = norm_grads.reshape(row_count, col_count * 6 * piece_len)
    summed = spread(
        (
            self_query_part,
            self_key_part,
            self_value_part,
            self_out_grad,
            cross_query_part,
            cross_key_part,
            cross_value_part,
            cross_out_grad,
            up_grad,
            down_grad,
            norm_grads,
        )
    )
    norm_parts = summed[10].reshape(6, piece_len)
    return (
        layer_out,
        input_grad,
        text_grad,
        summed[0],
        summed[1],
        summed[2],
        summed[3],
        summed[4],
        summed[5],
        summed[6],
        summed[7],
        summed[8],
        summed[9],
        norm_parts[0],
        norm_parts[1],
        norm_parts[2],
        norm_parts[3],
        norm_parts[4],
        norm_parts[5],
    )


NT=(((1,),(1,)),((),())); NN=(((1,),(0,)),((),())); TN=(((0,),(0,)),((),()))
def dg(a,b,dims): return lax.dot_general(a,b,dims,preferred_element_type=jnp.float32)

def feed_kernel(h_ref,cot_ref,res_ref,up_ref,down_ref,out_ref,g_ref,dup_ref,ddown_ref,acc):
    i=pl.program_id(0)
    @pl.when(i==0)
    def _():
        acc[...]=res_ref[...]
        g_ref[...]=jnp.zeros_like(g_ref)
    h=h_ref[...]
    up=up_ref[:,0].reshape(h.shape[1],-1)
    blocks,wide=down_ref.shape[1],down_ref.shape[3]
    pre=dg(h,up,NN)
    cdf=0.5*(1.0+lax.erf(pre*0.7071067811865476))
    inner=(pre*cdf).astype(jnp.bfloat16)
    slope=cdf+pre*(jnp.exp(-0.5*pre*pre)*0.3989422804014327)
    grad=None
    for at in range(blocks):
        columns=slice(at*wide,(at+1)*wide)
        cot=cot_ref[:,columns]
        acc[:,columns]+=dg(inner,down_ref[0,at],NN)
        ddown_ref[:,columns]=dg(inner,cot,TN).astype(ddown_ref.dtype)
        part=dg(cot,down_ref[0,at],NT)
        grad=part if grad is None else grad+part
    gpre=(grad*slope).astype(jnp.bfloat16)
    dup_ref[:,0]=dg(h,gpre,TN).astype(dup_ref.dtype).reshape(dup_ref.shape[0],dup_ref.shape[2],dup_ref.shape[3])
    g_ref[...]+=dg(gpre,up,NT)
    @pl.when(i==pl.num_programs(0)-1)
    def _(): out_ref[...]=acc[...].astype(out_ref.dtype)

def feed(h,cot,res,up,down):
    rows,d=h.shape; chunk=down.shape[2]; strips=up.shape[3]//chunk; ff=down.shape[0]*chunk
    whole=pl.BlockSpec((rows,d),lambda i:(0,0))
    up_spec=pl.BlockSpec((up.shape[0],1,up.shape[2],chunk),lambda i:(0,i//strips,0,i%strips))
    down_spec=pl.BlockSpec((1,)+down.shape[1:],lambda i:(i,0,0,0))
    return pl.pallas_call(feed_kernel,grid=(ff//chunk,),
        in_specs=[whole,whole,whole,up_spec,down_spec],
        out_specs=[whole,whole,up_spec,pl.BlockSpec((chunk,d),lambda i:(i,0))],
        out_shape=[jax.ShapeDtypeStruct((rows,d),jnp.bfloat16),jax.ShapeDtypeStruct((rows,d),jnp.float32),jax.ShapeDtypeStruct(up.shape,jnp.bfloat16),jax.ShapeDtypeStruct((ff,d),jnp.bfloat16)],
        scratch_shapes=[pltpu.VMEM((rows,d),jnp.float32)],
        compiler_params=pltpu.CompilerParams(vmem_limit_bytes=56<<20),
        cost_estimate=pl.CostEstimate(flops=12*rows*d*ff,bytes_accessed=8*d*ff+16*rows*d,transcendentals=2*rows*ff))(h,cot,res,up,down)


MESH = pl.DeviceIdType.MESH
ORDERS = ("xzy", "yzx", "xzy", "yzx", "zxy", "zyx")


class Place:
    def __init__(self):
        row, col = lax.axis_index("row"), lax.axis_index("col")
        self.z, self.y, self.x, self.k = row // 2, row % 2, col // 2, col % 2
        self.along = lax.axis_size("row") // 2

    def device(self, dz=0, y=False, x=False, k=False):
        other_y = 1 - self.y if y else self.y
        other_x = 1 - self.x if x else self.x
        other_k = 1 - self.k if k else self.k
        return ((self.z + dz) * 2 + other_y, other_x * 2 + other_k)

    def across(self, axis):
        return self.device(y=axis == "y", x=axis == "x", k=axis == "k")

    def greet(self):
        barrier = pltpu.get_barrier_semaphore()
        for axis in "xyk":
            pl.semaphore_signal(barrier, inc=1, device_id=self.across(axis), device_id_type=MESH)

        @pl.when(self.z > 0)
        def _():
            pl.semaphore_signal(barrier, inc=1, device_id=self.device(dz=-1), device_id_type=MESH)

        @pl.when(self.z + 1 < self.along)
        def _():
            pl.semaphore_signal(barrier, inc=1, device_id=self.device(dz=1), device_id_type=MESH)

        below = jnp.where(self.z > 0, 1, 0)
        above = jnp.where(self.z + 1 < self.along, 1, 0)
        pl.semaphore_wait(barrier, 3 + below + above)


def when(condition, run):
    if condition is None:
        run()
    else:
        pl.when(condition)(run)


def in_turn(units, lag):
    ready = [(lag * at, at) for at in range(len(units))]
    while ready:
        turn, at = min(ready)
        ready.remove((turn, at))
        if next(units[at], units) is not units:
            ready.append((turn + 1, at))
        yield


class Gather:
    def __init__(self, place, block, full, strip, order, send, recv):
        self.place, self.block, self.full, self.strip = place, block, full, strip
        turn = order.index("z")
        self.before, self.after = order[:turn], order[turn + 1 :]
        self.send, self.recv, self.used, self.sent, self.started = send, recv, 0, 0, []

    def region(self, z, y, x):
        part, start, count = self.strip
        column = (x * 2 + self.place.k) * self.block.shape[-1] + start
        return self.full.at[z, y, part, :, pl.ds(pl.multiple_of(column, 128), count)]

    def held(self, done, z):
        y = slice(None) if "y" in done else self.place.y
        return [self.region(z, y, x) for x in (range(2) if "x" in done else [self.place.x])]

    def pairs(self, done, z, first):
        if first:
            part, start, count = self.strip
            place = self.place
            return [(self.block.at[part, :, pl.ds(start, count)], self.region(place.z, place.y, place.x))]
        return [(region, region) for region in self.held(done, z)]

    def semaphore(self):
        self.used += 2
        return self.used - 2

    def copies(self, device, pairs, semaphore, send=0):
        return [
            pltpu.make_async_remote_copy(
                src_ref=source, dst_ref=target, send_sem=self.send.at[send + at],
                recv_sem=self.recv.at[semaphore + at], device_id=device, device_id_type=MESH)
            for at, (source, target) in enumerate(pairs)
        ]

    def start(self, device, pairs, wide, condition, semaphore):
        send = self.sent
        self.sent += wide

        def make():
            return self.copies(device(), pairs(), semaphore, send)

        when(condition(), lambda: [copy.start() for copy in make()] and None)
        self.started.append((condition, make))
        return condition, make

    def arrive(self, sent):
        condition, make = sent
        when(condition(), lambda: [copy.wait_recv() for copy in make()] and None)

    def stages(self):
        place, along = self.place, self.place.along
        done = []

        def always():
            return None

        def width(axes):
            return 2 if "x" in axes else 1

        for axis in self.before:
            axes = tuple(done)
            sent = self.start(
                lambda axis=axis: place.across(axis), lambda axes=axes: self.pairs(axes, place.z, not axes),
                width(axes), always, self.semaphore())
            yield
            self.arrive(sent)
            done.append(axis)
        first = not done
        axes_z = tuple(done)
        from_left = [self.semaphore() for _ in range(along - 1)]
        from_right = [self.semaphore() for _ in range(along - 1)]

        def pass_on(turn, step):
            axes = axes_z + tuple(self.after[:turn])
            sent = []
            for way in ((-1, 1) if step else (0,)):

                def inside(way=way):
                    z = place.z + way * step
                    return (z >= 0) & (z < along) if way else None

                sent.append(self.start(
                    lambda: place.across(self.after[turn]),
                    lambda way=way: self.pairs(axes, place.z + way * step, not axes and not step),
                    width(axes), inside, self.semaphore()))
            return turn, step, sent

        def step_out(step):
            self.start(
                lambda: place.device(dz=1), lambda: self.pairs(axes_z, place.z - (step - 1), first and step == 1),
                width(axes_z), lambda: (place.z - (step - 1) >= 0) & (place.z + 1 < along), from_left[step - 1])
            self.start(
                lambda: place.device(dz=-1), lambda: self.pairs(axes_z, place.z + (step - 1), first and step == 1),
                width(axes_z), lambda: (place.z + (step - 1) < along) & (place.z > 0), from_right[step - 1])

        def step_in(step):
            for way, semaphore in ((-1, from_left), (1, from_right)):
                z = place.z + way * step
                self.arrive((
                    lambda: (z >= 0) & (z < along),
                    lambda: self.copies(place.across("k"), self.pairs(axes_z, z, False), semaphore[step - 1])))

        step_out(1)
        waiting = [pass_on(0, 0)] if self.after else []
        for step in range(1, along + len(self.after)):
            yield
            if step < along:
                step_in(step)
                if step + 1 < along:
                    step_out(step + 1)
            following = []
            for turn, at, sent in waiting:
                for one in sent:
                    self.arrive(one)
                if turn + 1 < len(self.after):
                    following.append(pass_on(turn + 1, at))
            if self.after and step < along:
                following.append(pass_on(0, step))
            waiting = following
        sent = self.start(
            lambda: place.across("k"), lambda: [(r, r) for r in [self.region(slice(None), slice(None), x) for x in range(2)]],
            2, always, self.semaphore())
        yield
        self.arrive(sent)

    def finish(self):
        for condition, make in self.started:
            when(condition(), lambda make=make: [copy.wait_send() for copy in make()] and None)


class OwnBlocks:
    def __init__(self, place, blocks, fulls, local):
        self.place, self.blocks, self.fulls, self.local = place, blocks, fulls, local

    def copies(self):
        place = self.place
        for at, (block, full) in enumerate(zip(self.blocks, self.fulls)):
            width = block.shape[-1]
            columns = pl.ds(pl.multiple_of((place.x * 2 + place.k) * width, 128), width)
            yield pltpu.make_async_copy(block, full.at[place.z, place.y, :, :, columns], self.local.at[at])

    def start(self):
        for copy in self.copies():
            copy.start()

    def wait(self):
        for copy in self.copies():
            copy.wait()


def gathers_of(place, units, blocks, fulls, send, recv):
    return [
        Gather(place, blocks[which], fulls[which], strip, order, send.at[at], recv.at[at])
        for at, (which, strip, order) in enumerate(units)
    ]


def gather_kernel(units, count, *refs):
    blocks, fulls = refs[:count], refs[count : 2 * count]
    send, recv, local = refs[2 * count :]
    place = Place()
    place.greet()
    own = OwnBlocks(place, blocks, fulls, local)
    own.start()
    gathers = gathers_of(place, units, blocks, fulls, send, recv)
    waited = False
    for unused in in_turn([gather.stages() for gather in gathers], 0.0):
        if not waited:
            own.wait()
            waited = True
    for gather in gathers:
        gather.finish()


def gather_units(blocks, least, orders):
    strips = []
    for which, block in enumerate(blocks):
        wide = min(least, block.shape[-1])
        for part in range(block.shape[0]):
            for start in range(0, block.shape[-1], wide):
                strips.append((which, (part, start, wide)))
    return [strip + (orders[at % len(orders)],) for at, strip in enumerate(strips)]


def gather_plan(blocks, least, orders):
    along, cols = lax.axis_size("row") // 2, lax.axis_size("col")
    units = gather_units(blocks, least, orders)
    fulls = [jax.ShapeDtypeStruct((along, 2) + b.shape[:2] + (cols * b.shape[2],), b.dtype) for b in blocks]
    scratch = [
        pltpu.SemaphoreType.DMA((len(units), 8 * along)),
        pltpu.SemaphoreType.DMA((len(units), 12 * along)),
        pltpu.SemaphoreType.DMA((len(blocks),)),
    ]
    return fulls, units, scratch


def gather_blocks(blocks, collective_id, least):
    fulls, units, scratch = gather_plan(blocks, least, ORDERS)
    count = len(blocks)
    anywhere = pl.BlockSpec(memory_space=pl.ANY)
    return pl.pallas_call(
        functools.partial(gather_kernel, units, count),
        out_shape=fulls,
        in_specs=[anywhere] * count,
        out_specs=[anywhere] * count,
        scratch_shapes=scratch,
        compiler_params=pltpu.CompilerParams(collective_id=collective_id, has_side_effects=True),
        cost_estimate=pl.CostEstimate(flops=0, bytes_accessed=4 * sum(f.size for f in fulls), transcendentals=0),
    )(*blocks)


SCATTER_ORDERS = ("xyz", "yxz", "zxy", "zyx", "xzy", "yzx")


def add_blocks(total, extra, leading):
    def one(at, unused):
        place = []
        for size in leading[::-1]:
            place.append(at % size)
            at = at // size
        place = tuple(place[::-1])
        total[place] = total[place] + extra[place]
        return unused

    if not leading:
        total[...] = total[...] + extra[...]
        return
    count = 1
    for size in leading:
        count *= size
    lax.fori_loop(0, count, one, 0)


class Scatter:
    def __init__(self, place, grad, out, strip, width, order, slots, send, recv, local):
        self.place, self.grad, self.out, self.strip, self.width = place, grad, out, strip, width
        self.order = order[::-1]
        self.total, self.other_core, self.halves, self.steps = slots
        self.send, self.recv, self.local = send, recv, local
        self.used, self.started = 0, []

    def region(self, x, k):
        part, start, count = self.strip
        column = (x * 2 + k) * self.width + start
        return self.grad.at[:, :, part, :, pl.ds(pl.multiple_of(column, 128), count)]

    def copy(self, device, source, target, semaphore):
        return pltpu.make_async_remote_copy(
            src_ref=source, dst_ref=target, send_sem=self.send.at[semaphore], recv_sem=self.recv.at[semaphore],
            device_id=device, device_id_type=MESH)

    def reserve(self, count):
        self.used += count
        return self.used - count

    def start(self, make, condition=lambda: None):
        when(condition(), lambda: make().start())
        self.started.append((condition, make))

    def stages(self):
        place, along = self.place, self.place.along
        rows, columns = self.total.shape[-2:]
        core = self.reserve(2)

        def own(x):
            return pltpu.make_async_copy(self.region(x, place.k), self.total.at[:, :, x], self.local.at[x])

        def swapped(x):
            return self.copy(
                place.across("k"), self.region(x, 1 - place.k), self.other_core.at[:, :, x], core + x)

        for x in range(2):
            own(x).start()
            self.start(functools.partial(swapped, x))
        yield
        for x in range(2):
            own(x).wait()
            swapped(x).wait_recv()
        add_blocks(self.total, self.other_core, (along, 2, 2))
        left = {"z": slice(None), "y": slice(None), "x": slice(None)}
        at = {"y": place.y, "x": place.x}

        def view(ref, kept=None, **places):
            return ref.at[tuple({**(left if kept is None else kept), **places}[axis] for axis in "zyx")]

        def sizes():
            return tuple(size for axis, size in zip("zyx", (along, 2, 2)) if isinstance(left[axis], slice))

        exchanges = 0
        for axis in self.order:
            if axis == "z":
                shape = tuple(2 for name in "yx" if isinstance(left[name], slice))
                inner = tuple(slice(None) if isinstance(left[name], slice) else 0 for name in "yx")

                def landing(side, step, inner=inner):
                    return self.steps.at[(side, step) + inner]

                base = self.reserve(2 * along)
                right, leftward = range(base, base + along), range(base + along, base + 2 * along)
                for step in range(along):
                    if step:
                        yield
                    for way, names, first in ((1, right, place.z), (-1, leftward, along - 1 - place.z)):
                        goal = along - 1 - step + place.z if way == 1 else step - along + 1 + place.z
                        side = 0 if way == 1 else 1
                        if step:
                            arrived = landing(side, step - 1)

                            def take(arrived=arrived, goal=goal, side=side, step=step, names=names):
                                self.copy(place.across("k"), arrived, arrived, names[step - 1]).wait_recv()
                                add_blocks(view(self.total, z=goal), arrived, shape)

                            pl.when((first >= 1) & (first <= step))(take)
                        if step < along - 1:
                            kept = dict(left)

                            def onward(way=way, step=step, kept=kept, landing=landing, side=side, names=names):
                                goal = along - 1 - step + place.z if way == 1 else step - along + 1 + place.z
                                source = view(self.total, kept, z=jnp.clip(goal, 0, along - 1))
                                return self.copy(place.device(dz=way), source, landing(side, step), names[step])

                            def reached(way=way, step=step):
                                first = place.z if way == 1 else along - 1 - place.z
                                return (first <= step) & (first < along - 1)

                            self.start(onward, reached)
                left["z"] = place.z
            else:
                landing = self.halves[exchanges]
                exchanges += 1
                inner = tuple(slice(None) if isinstance(left[name], slice) and name != axis else 0 for name in "zyx")
                semaphore, kept = self.reserve(1), dict(left)

                def swap(axis=axis, kept=kept, landing=landing, inner=inner, semaphore=semaphore):
                    source = view(self.total, kept, **{axis: 1 - at[axis]})
                    return self.copy(place.across(axis), source, landing.at[inner], semaphore)

                self.start(swap)
                yield
                swap().wait_recv()
                left[axis] = at[axis]
                add_blocks(view(self.total), landing.at[inner], sizes())
        part, start, count = self.strip
        self.out[part, :, start : start + count] = view(self.total)[...].astype(jnp.float32)

    def finish(self):
        for condition, make in self.started:
            when(condition(), lambda make=make: make().wait_send())


def scatter_slots(along, rows, columns, order):
    left = {"z": along, "y": 2, "x": 2}
    whole = (along, 2, 2, rows, columns)
    shapes = [whole, whole]
    steps = None
    for axis in order[::-1]:
        if axis == "z":
            steps = (2, along - 1, left["y"], left["x"], rows, columns)
        left[axis] = 1
        if axis != "z":
            shapes.append((left["z"], left["y"], left["x"], rows, columns))
    return shapes + [steps]


def scatters_of(place, units, grads, outs, send, recv, local, slots):
    scatters = []
    for at, (which, strip, order) in enumerate(units):
        total, other_core, first, second, steps = slots[5 * at : 5 * at + 5]
        scatters.append(
            Scatter(place, grads[which], outs[which], strip, outs[which].shape[-1], order,
                    (total, other_core, (first, second), steps), send.at[at], recv.at[at], local.at[at]))
    return scatters


def scatter_kernel(units, count, *refs):
    grads, outs = refs[:count], refs[count : 2 * count]
    place = Place()
    place.greet()
    scatters = scatters_of(place, units, grads, outs, *refs[2 * count : 2 * count + 3], refs[2 * count + 3 :])
    for unused in in_turn([scatter.stages() for scatter in scatters], 0.25):
        pass
    for scatter in scatters:
        scatter.finish()


def scatter_plan(grads, least, orders):
    along, cols = lax.axis_size("row") // 2, lax.axis_size("col")
    blocks = [jax.ShapeDtypeStruct(g.shape[2:4] + (g.shape[4] // cols,), jnp.float32) for g in grads]
    units = gather_units(blocks, least, orders)
    scratch = [pltpu.SemaphoreType.DMA((len(units), 2 * along + 4))] * 2 + [pltpu.SemaphoreType.DMA((len(units), 2))]
    for which, strip, order in units:
        shapes = scatter_slots(along, blocks[which].shape[1], strip[2], order)
        scratch += [pltpu.VMEM(shape, jnp.bfloat16) for shape in shapes]
    return blocks, units, scratch


def scatter_blocks(grads, collective_id, least):
    blocks, units, scratch = scatter_plan(grads, least, SCATTER_ORDERS)
    count = len(grads)
    anywhere = pl.BlockSpec(memory_space=pl.ANY)
    return pl.pallas_call(
        functools.partial(scatter_kernel, units, count),
        out_shape=blocks,
        in_specs=[anywhere] * count,
        out_specs=[pl.BlockSpec(memory_space=pltpu.VMEM)] * count,
        scratch_shapes=scratch,
        compiler_params=pltpu.CompilerParams(
            collective_id=collective_id, has_side_effects=True, vmem_limit_bytes=60 << 20),
        cost_estimate=pl.CostEstimate(
            flops=sum(g.size for g in grads), bytes_accessed=4 * sum(g.size for g in grads), transcendentals=0),
    )(*grads)


ACROSS = ("yzx", "yzx", "yzx", "yzx", "yxz")


def attend_rows(q, key_ref, value_ref, spans, diagonal, put):
    low = lax.broadcasted_iota(jnp.int32, (1, 128), 1) < HEAD_DIM
    mixed, logs = [], []
    for h in range(2):
        mine = low if h == 0 else jnp.logical_not(low)
        qh = jnp.where(mine, q, jnp.bfloat16(0))
        scores = []
        for at, length in spans:
            s = dg(qh, key_ref[at : at + length, :], NT)
            if at == diagonal:
                allowed = lax.broadcasted_iota(jnp.int32, s.shape, 0) >= lax.broadcasted_iota(jnp.int32, s.shape, 1)
                s = jnp.where(allowed, s, -1e30)
            scores.append(s)
        top = functools.reduce(jnp.maximum, [jnp.max(s, axis=1, keepdims=True) for s in scores])
        out = None
        for (at, length), s in zip(spans, scores):
            p = jnp.exp(s - top).astype(jnp.bfloat16)
            value = value_ref[at : at + length, :]
            part = dg(p, jnp.where(mine, value, jnp.ones_like(value)), NN)
            out = part if out is None else out + part
        total = out[:, HEAD_DIM : HEAD_DIM + 1] if h == 0 else out[:, 0:1]
        mixed.append(out / total)
        logs.append(top + jnp.log(total))
    put(logs)
    return jnp.where(low, mixed[0], mixed[1])


def rows_of(lanes_ref, first):
    picked = lax.broadcasted_iota(jnp.int32, (8, 128), 0) + first == lax.broadcasted_iota(jnp.int32, (8, 128), 1)
    return lax.dot_general(
        picked.astype(jnp.float32), lanes_ref[...], NT, precision=lax.Precision.HIGHEST,
        preferred_element_type=jnp.float32)


def pair_attend_kernel(tile, units, count, events, *refs):
    q_ref, k_ref, v_ref, q_any, k_any, v_any = refs[:6]
    blocks = refs[6 : 6 + count]
    mix_ref, logs_ref, fq_out, fk_out, fv_out = refs[6 + count : 11 + count]
    fulls = refs[11 + count : 11 + 2 * count]
    (near, near_logs, far_q, far_k, far_v, far, far_logs, got, far_rows, got_rows,
     send, recv, local, keep) = refs[11 + 2 * count : 25 + 2 * count]
    gather_send, gather_recv, gather_local = refs[25 + 2 * count :]
    step = pl.program_id(0)
    place = Place()
    own = OwnBlocks(place, blocks, fulls, gather_local)
    gathers = gathers_of(place, units, blocks, fulls, gather_send, gather_recv)
    turns = in_turn([gather.stages() for gather in gathers], 0.25)
    pairs = near.shape[0]
    fars = pairs // 2
    rows = q_ref.shape[0]
    first, second = place.y == 0, place.y == 1
    partner = place.across("y")
    lane = lax.broadcasted_iota(jnp.int32, (1, 128), 1)
    scale = jnp.bfloat16(HEAD_DIM**-0.5)
    plan = ((q_any, far_q, False), (k_any, far_k, True), (v_any, far_v, True))

    def columns(pair):
        return pl.ds(pl.multiple_of(pair * 128, 128), 128)

    def sending(which, j):
        array, landing, by_first = plan[which]
        return pltpu.make_async_remote_copy(
            src_ref=array.at[:, columns(j if by_first else fars + j)], dst_ref=landing.at[j],
            send_sem=send.at[which, j], recv_sem=recv.at[which, j], device_id=partner, device_id_type=MESH)

    def keeping(which, j):
        array, landing, by_first = plan[which]
        return pltpu.make_async_copy(
            array.at[:, columns(fars + j if by_first else j)], landing.at[j], local.at[which, j])

    def mixture_out(j):
        return pltpu.make_async_remote_copy(
            src_ref=far.at[j], dst_ref=got.at[j], send_sem=send.at[3, j], recv_sem=recv.at[3, j],
            device_id=partner, device_id_type=MESH)

    def logs_out():
        return pltpu.make_async_remote_copy(
            src_ref=far_rows, dst_ref=got_rows, send_sem=send.at[4, 0], recv_sem=recv.at[4, 0],
            device_id=partner, device_id_type=MESH)

    def saving(which):
        return pltpu.make_async_copy(plan[which][1], (fq_out, fk_out, fv_out)[which], keep.at[which])

    @pl.when(step == 0)
    def _():
        place.greet()
        own.start()
        near_logs[...] = jnp.zeros_like(near_logs)
        far_logs[...] = jnp.zeros_like(far_logs)
        for j in range(fars):
            for which in range(3):

                @pl.when(first if plan[which][2] else second)
                def _(which=which, j=j):
                    keeping(which, j).start()

    @pl.when((step % 3 == 0) & (step < 3 * fars))
    def _():
        j = step // 3
        for which in range(3):

            @pl.when(first if plan[which][2] else second)
            def _(which=which):
                @pl.when(j > 0)
                def _():
                    sending(which, j - 1).wait_send()

                sending(which, j).start()

    for at, number in enumerate(events):

        @pl.when(step == at)
        def _(at=at, number=number):
            if at == 0:
                own.wait()
            for unused in range(number):
                next(turns, None)

    @pl.when(step < pairs)
    def _():
        for start in range(0, rows, tile):
            n = min(tile, rows - start)

            def put(logs, start=start, n=n):
                kept = near_logs[start : start + n, :]
                for h in range(2):
                    kept = jnp.where(lane == 2 * step + h, logs[h], kept)
                near_logs[start : start + n, :] = kept

            spans = ([(0, start)] if start else []) + [(start, n)]
            near[step, start : start + n, :] = attend_rows(
                q_ref[start : start + n, :] * scale, k_ref, v_ref, spans, start, put)

    @pl.when((step >= pairs) & (step < pairs + fars))
    def _():
        j = step - pairs
        for which in range(3):
            by_first = plan[which][2]

            @pl.when(first if by_first else second)
            def _(which=which):
                keeping(which, j).wait()

            @pl.when(second if by_first else first)
            def _(which=which):
                sending(which, j).wait_recv()

        base = jnp.where(first, 2 * fars, 0)
        for start in range(0, rows, tile):
            n = min(tile, rows - start)

            def put(logs, start=start, n=n):
                kept = far_logs[start : start + n, :]
                for h in range(2):
                    kept = jnp.where(lane == base + 2 * j + h, logs[h], kept)
                far_logs[start : start + n, :] = kept

            far[j, start : start + n, :] = attend_rows(
                far_q[j, start : start + n, :] * scale, far_k.at[j], far_v.at[j], [(0, rows)], None, put
            ).astype(far.dtype)

        @pl.when(first)
        def _():
            mixture_out(j).start()

    @pl.when(step == pairs + fars)
    def _():
        for which in range(3):
            saving(which).start()

        @pl.when(first)
        def _():
            far_rows[...] = rows_of(far_logs, 2 * fars)
            logs_out().start()
            for pair in range(pairs):
                mix_ref[:, pair * 128 : (pair + 1) * 128] = near[pair].astype(mix_ref.dtype)
            logs_ref[...] = near_logs[...]
            logs_out().wait_send()
            for j in range(fars):
                mixture_out(j).wait_send()
            for which in (1, 2):
                sending(which, fars - 1).wait_send()

        @pl.when(second)
        def _():
            logs_out().wait_recv()
            for j in range(fars):
                mixture_out(j).wait_recv()
            sending(0, fars - 1).wait_send()
            spread_out = (lax.broadcasted_iota(jnp.int32, (8, 128), 0) + 2 * fars == lane).astype(jnp.float32)
            theirs = lax.dot_general(
                got_rows[...], spread_out, TN, precision=lax.Precision.HIGHEST, preferred_element_type=jnp.float32)
            logs_far = far_logs[...] + theirs
            logs_near = near_logs[...]
            top = jnp.maximum(logs_near, logs_far)
            total = top + jnp.log(jnp.exp(logs_near - top) + jnp.exp(logs_far - top))
            logs_ref[...] = total
            share = jnp.exp(logs_near - total)
            low = lane < HEAD_DIM
            for pair in range(pairs):
                part = jnp.where(low, share[:, 2 * pair : 2 * pair + 1], share[:, 2 * pair + 1 : 2 * pair + 2])
                other = (far[pair] if pair < fars else got[pair - fars]).astype(jnp.float32)
                mix_ref[:, pair * 128 : (pair + 1) * 128] = (other + (near[pair] - other) * part).astype(mix_ref.dtype)

        for which in range(3):
            saving(which).wait()
        for unused in turns:
            pass
        for gather in gathers:
            gather.finish()


def pair_attend(q, k, v, blocks, collective_id, events, tile=384):
    rows, width = q.shape
    pairs = width // 128
    fars = pairs // 2
    block = pl.BlockSpec((rows, 128), lambda i: (0, jnp.minimum(i, pairs - 1)))
    anywhere = pl.BlockSpec(memory_space=pl.ANY)
    kept = jax.ShapeDtypeStruct((fars, rows, 128), jnp.bfloat16)
    half = pltpu.VMEM((fars, rows, 128), jnp.bfloat16)
    fulls, units, scratch = gather_plan(blocks, 256, ACROSS)
    count = len(blocks)
    result = pl.pallas_call(
        functools.partial(pair_attend_kernel, tile, units, count, events),
        grid=(pairs + fars + 1,),
        in_specs=[block] * 3 + [anywhere] * (3 + count),
        out_specs=[pl.BlockSpec((rows, width), lambda i: (0, 0)), pl.BlockSpec((rows, 128), lambda i: (0, 0))] + [anywhere] * (3 + count),
        out_shape=[
            jax.ShapeDtypeStruct((rows, width), jnp.bfloat16), jax.ShapeDtypeStruct((rows, 128), jnp.float32), kept, kept, kept, *fulls],
        scratch_shapes=[
            pltpu.VMEM((pairs, rows, 128), jnp.float32), pltpu.VMEM((rows, 128), jnp.float32),
            half, half, half, half, pltpu.VMEM((rows, 128), jnp.float32), half,
            pltpu.VMEM((8, rows), jnp.float32), pltpu.VMEM((8, rows), jnp.float32),
            pltpu.SemaphoreType.DMA((5, fars)), pltpu.SemaphoreType.DMA((5, fars)),
            pltpu.SemaphoreType.DMA((3, fars)), pltpu.SemaphoreType.DMA((3,)), *scratch,
        ],
        compiler_params=pltpu.CompilerParams(
            collective_id=collective_id, has_side_effects=True, vmem_limit_bytes=48 << 20),
        cost_estimate=pl.CostEstimate(
            flops=4 * rows * rows * width, bytes_accessed=16 * rows * width, transcendentals=rows * rows * pairs * 2),
    )(q, k, v, q, k, v, *blocks)
    return result[:5], result[5:]


def back_pair(tile, causal, q_ref, k_ref, v_ref, do_ref, stats, acc, put):
    rows, keys = q_ref.shape[0], k_ref.shape[0]
    low = lax.broadcasted_iota(jnp.int32, (1, 128), 1) < HEAD_DIM
    acc[...] = jnp.zeros_like(acc)
    for start in range(0, keys, tile):
        n = min(tile, keys - start)
        k = k_ref[start : start + n, :] * jnp.bfloat16(HEAD_DIM**-0.5)
        v = v_ref[start : start + n, :]
        spans = [(0, rows)]
        if causal:
            spans = [(start, n)] + ([(start + n, rows - start - n)] if start + n < rows else [])
        dks, dvs = [], []
        for h in range(2):
            mine = low if h == 0 else jnp.logical_not(low)
            kh, vh = jnp.where(mine, k, jnp.bfloat16(0)), jnp.where(mine, v, jnp.bfloat16(0))
            dk = dv = None
            for at, length in spans:
                qs, do = q_ref[at : at + length, :], do_ref[at : at + length, :]
                p = jnp.exp(dg(kh, qs, NT) - stats[h : h + 1, at : at + length])
                if causal and at == start:
                    allowed = lax.broadcasted_iota(jnp.int32, p.shape, 0) <= lax.broadcasted_iota(jnp.int32, p.shape, 1)
                    p = jnp.where(allowed, p, 0.0)
                ds = (p * (dg(vh, do, NT) - stats[2 + h : 3 + h, at : at + length])).astype(jnp.bfloat16)
                a, b = dg(p.astype(jnp.bfloat16), do, NN), dg(ds, qs, NN)
                dv = a if dv is None else dv + a
                dk = b if dk is None else dk + b
                acc[at : at + length, :] += dg(ds, kh, TN)
            dks.append(dk)
            dvs.append(dv)
        put(start, n, jnp.where(low, dks[0], dks[1]) * HEAD_DIM**-0.5, jnp.where(low, dvs[0], dvs[1]))


def pair_stats(pair, mix_ref, do_ref, logs_ref):
    lane = lax.broadcasted_iota(jnp.int32, (8, 128), 1)
    line = lax.broadcasted_iota(jnp.int32, (8, 128), 0)
    picked = ((line < 2) & (line + 2 * pair == lane)).astype(jnp.float32)
    halves = (((line == 2) & (lane < HEAD_DIM)) | ((line == 3) & (lane >= HEAD_DIM))).astype(jnp.float32)
    products = mix_ref[...].astype(jnp.float32) * do_ref[...].astype(jnp.float32)
    logs = lax.dot_general(
        picked, logs_ref[...], NT, precision=lax.Precision.HIGH, preferred_element_type=jnp.float32)
    return logs + lax.dot_general(
        halves, products, NT, precision=lax.Precision.HIGH, preferred_element_type=jnp.float32)


def both_heads(array):
    low = lax.broadcasted_iota(jnp.int32, (1, 128), 1) < HEAD_DIM
    zero = jnp.zeros_like(array)
    return jnp.concatenate([jnp.where(low, array, zero), jnp.where(low, zero, array)], axis=0)


def one_head_each(array):
    low = lax.broadcasted_iota(jnp.int32, (1, 128), 1) < HEAD_DIM
    half = array.shape[0] // 2
    return jnp.where(low, array[:half], array[half:])


def cross_kernel(q_ref, k_ref, v_ref, mix_ref, logs_ref):
    pair = pl.program_id(0)
    keys = k_ref.shape[0]
    lane = lax.broadcasted_iota(jnp.int32, (1, 128), 1)
    lower = lax.broadcasted_iota(jnp.int32, (1, 2 * keys), 1) < keys

    @pl.when(pair == 0)
    def _():
        logs_ref[...] = jnp.zeros_like(logs_ref)

    scores = dg(q_ref[...] * jnp.bfloat16(HEAD_DIM**-0.5), both_heads(k_ref[...]), NT)
    tops = [
        jnp.max(jnp.where(lower if h == 0 else jnp.logical_not(lower), scores, -1e30), axis=1, keepdims=True) for h in range(2)
    ]
    powers = jnp.exp(scores - jnp.where(lower, tops[0], tops[1])).astype(jnp.bfloat16)
    values = both_heads(v_ref[...])
    ones = both_heads(jnp.ones(v_ref.shape, v_ref.dtype))
    out = dg(powers, jnp.concatenate([values, ones], axis=1), NN)
    totals = out[:, 128:]
    mix_ref[...] = (out[:, :128] / totals).astype(mix_ref.dtype)
    sums = jnp.log(totals)
    logs = logs_ref[...]
    for h in range(2):
        logs = jnp.where(lane == 2 * pair + h, tops[h] + sums[:, h * HEAD_DIM : h * HEAD_DIM + 1], logs)
    logs_ref[...] = logs


def cross(q, k, v):
    rows, width = q.shape
    keys = k.shape[0]
    long, short = pl.BlockSpec((rows, 128), lambda i: (0, i)), pl.BlockSpec((keys, 128), lambda i: (0, i))
    return pl.pallas_call(
        cross_kernel,
        grid=(width // 128,),
        in_specs=[long, short, short],
        out_specs=[long, pl.BlockSpec((rows, 128), lambda i: (0, 0))],
        out_shape=[jax.ShapeDtypeStruct((rows, width), jnp.bfloat16), jax.ShapeDtypeStruct((rows, 128), jnp.float32)],
        compiler_params=pltpu.CompilerParams(vmem_limit_bytes=40 << 20),
        cost_estimate=pl.CostEstimate(
            flops=4 * rows * keys * width, bytes_accessed=6 * rows * width, transcendentals=rows * keys * width // HEAD_DIM),
    )(q, k, v)


def cross_back_kernel(q_ref, k_ref, v_ref, do_ref, mix_ref, logs_ref, dq_ref, dk_ref, dv_ref):
    keys = k_ref.shape[0]
    stats = pair_stats(pl.program_id(0), mix_ref, do_ref, logs_ref)
    upper = lax.broadcasted_iota(jnp.int32, (2 * keys, 1), 0) < keys
    k, v, do = both_heads(k_ref[...] * jnp.bfloat16(HEAD_DIM**-0.5)), both_heads(v_ref[...]), do_ref[...]
    p = jnp.exp(dg(k, q_ref[...], NT) - jnp.where(upper, stats[0:1, :], stats[1:2, :]))
    ds = (p * (dg(v, do, NT) - jnp.where(upper, stats[2:3, :], stats[3:4, :]))).astype(jnp.bfloat16)
    dv_ref[...] = one_head_each(dg(p.astype(jnp.bfloat16), do, NN)).astype(dv_ref.dtype)
    dk_ref[...] = (one_head_each(dg(ds, q_ref[...], NN)) * HEAD_DIM**-0.5).astype(dk_ref.dtype)
    dq_ref[...] = dg(ds, k, TN).astype(dq_ref.dtype)


def cross_back(q, k, v, do, mix, logs):
    rows, width = q.shape
    keys = k.shape[0]
    long, short = pl.BlockSpec((rows, 128), lambda i: (0, i)), pl.BlockSpec((keys, 128), lambda i: (0, i))
    return pl.pallas_call(
        cross_back_kernel,
        grid=(width // 128,),
        in_specs=[long, short, short, long, long, pl.BlockSpec((rows, 128), lambda i: (0, 0))],
        out_specs=[long, short, short],
        out_shape=[jax.ShapeDtypeStruct(a.shape, jnp.bfloat16) for a in (q, k, v)],
        compiler_params=pltpu.CompilerParams(vmem_limit_bytes=40 << 20),
        cost_estimate=pl.CostEstimate(
            flops=10 * rows * keys * width, bytes_accessed=10 * rows * width, transcendentals=rows * keys * width // HEAD_DIM),
    )(q, k, v, do, mix, logs)


def pair_back_kernel(tile, far_tile, units, count, events, *refs):
    q_ref, k_ref, v_ref, do_ref, mix_ref, logs_ref, do_any, fq_any, fk_any, fv_any = refs[:10]
    grads, (dq_ref, dk_ref, dv_ref) = refs[10 : 10 + count], refs[10 + count : 13 + count]
    sums = refs[13 + count : 13 + 2 * count]
    (near, acc, stats, far_stats, used_stats, far_q, far_k, far_v, far_do, far_dq, far_dk, far_dv, got_q, got_k, got_v,
     send, recv, local, do_local) = refs[13 + 2 * count : 32 + 2 * count]
    scatter_refs = refs[32 + 2 * count :]
    step = pl.program_id(0)
    place = Place()
    pairs = near.shape[1]
    fars = pairs // 2
    first, second = place.y == 0, place.y == 1
    partner = place.across("y")

    def columns(pair):
        return pl.ds(pl.multiple_of(pair * 128, 128), 128)

    def remote(source, target, which, j):
        return pltpu.make_async_remote_copy(
            src_ref=source, dst_ref=target, send_sem=send.at[which, j], recv_sem=recv.at[which, j],
            device_id=partner, device_id_type=MESH)

    def grad_over(j):
        return remote(do_any.at[:, columns(fars + j)], far_do.at[j], 0, j)

    def grad_kept(j):
        return pltpu.make_async_copy(do_any.at[:, columns(j)], far_do.at[j], do_local.at[j])

    def stats_over():
        return remote(stats.at[pl.ds(fars, fars)], far_stats, 4, 0)

    def back_over(which, j):
        source, target = ((far_dq, got_q), (far_dk, got_k), (far_dv, got_v))[which]
        return remote(source.at[j], target.at[j], 1 + which, j)

    def far_in(which):
        source, target = ((fq_any, far_q), (fk_any, far_k), (fv_any, far_v))[which]
        return pltpu.make_async_copy(source, target, local.at[which])

    scatters = scatters_of(place, units, grads, sums, *scatter_refs[:3], scatter_refs[3:])
    turns = in_turn([scatter.stages() for scatter in scatters], 0.25)

    @pl.when(step == 0)
    def _():
        place.greet()
        for which in range(3):
            far_in(which).start()
        for j in range(fars):

            @pl.when(second)
            def _(j=j):
                grad_over(j).start()

            @pl.when(second)
            def _(j=j):
                grad_kept(j).start()

    for at, number in enumerate(events):

        @pl.when(step == at)
        def _(number=number):
            for unused in range(number):
                next(turns, None)

    @pl.when((step == fars) & second)
    def _():
        stats_over().start()

    @pl.when(step < pairs)
    def _():
        pair = lax.rem(step + fars, pairs)
        stats[pair] = pair_stats(pair, mix_ref, do_ref, logs_ref)

        def put(start, n, dk, dv):
            near[1, pair, start : start + n, :] = dk
            near[2, pair, start : start + n, :] = dv

        back_pair(tile, True, q_ref, k_ref, v_ref, do_ref, stats.at[pair], acc, put)
        near[0, pair] = acc[...]

    @pl.when((step >= pairs) & (step < pairs + fars))
    def _():
        j = step - pairs

        @pl.when(j == 0)
        def _():
            for which in range(3):
                far_in(which).wait()

            @pl.when(first)
            def _():
                stats_over().wait_recv()

        @pl.when(first)
        def _():
            grad_over(j).wait_recv()
            used_stats[...] = far_stats[j]

        @pl.when(second)
        def _():
            grad_kept(j).wait()
            used_stats[...] = stats[j]

        def put(start, n, dk, dv):
            far_dk[j, start : start + n, :] = dk.astype(far_dk.dtype)
            far_dv[j, start : start + n, :] = dv.astype(far_dv.dtype)

        back_pair(far_tile, False, far_q.at[j], far_k.at[j], far_v.at[j], far_do.at[j], used_stats, acc, put)
        far_dq[j] = acc[...].astype(far_dq.dtype)

        @pl.when(first)
        def _():
            back_over(0, j).start()

        @pl.when(second)
        def _():
            back_over(1, j).start()
            back_over(2, j).start()

    @pl.when(step >= pairs + fars)
    def _():
        pair = step - pairs - fars
        lower = pair < fars
        j = lax.rem(pair, fars)

        def write(ref, which, other):
            total = near[which, pair]
            if other is not None:
                total = total + other[j].astype(jnp.float32)
            ref[...] = total.astype(ref.dtype)

        @pl.when(first & lower)
        def _():
            for which in (1, 2):
                back_over(which, j).wait_recv()
            write(dq_ref, 0, None)
            write(dk_ref, 1, got_k)
            write(dv_ref, 2, got_v)

        @pl.when(first & jnp.logical_not(lower))
        def _():
            write(dq_ref, 0, None)
            write(dk_ref, 1, far_dk)
            write(dv_ref, 2, far_dv)

        @pl.when(second & lower)
        def _():
            write(dq_ref, 0, far_dq)
            write(dk_ref, 1, None)
            write(dv_ref, 2, None)

        @pl.when(second & jnp.logical_not(lower))
        def _():
            back_over(0, j).wait_recv()
            write(dq_ref, 0, got_q)
            write(dk_ref, 1, None)
            write(dv_ref, 2, None)

    @pl.when(step == 2 * pairs + fars - 1)
    def _():
        for unused in turns:
            pass
        for scatter in scatters:
            scatter.finish()

        @pl.when(first)
        def _():
            for j in range(fars):
                back_over(0, j).wait_send()

        @pl.when(second)
        def _():
            stats_over().wait_send()
            for j in range(fars):
                grad_over(j).wait_send()
                for which in (1, 2):
                    back_over(which, j).wait_send()


def pair_back(q, k, v, do, mix, logs, far, grads, collective_id, events, tile=384, far_tile=256):
    rows, width = q.shape
    pairs = width // 128
    fars = pairs // 2
    blocks, units, scratch = scatter_plan(grads, 256, SCATTER_ORDERS)
    count = len(grads)
    block = pl.BlockSpec((rows, 128), lambda i: (0, lax.rem(jnp.minimum(i, pairs - 1) + fars, pairs)))
    joined = pl.BlockSpec((rows, 128), lambda i: (0, jnp.maximum(i - pairs - fars, 0)))
    anywhere = pl.BlockSpec(memory_space=pl.ANY)
    half = pltpu.VMEM((fars, rows, 128), jnp.bfloat16)
    out = jax.ShapeDtypeStruct((rows, width), jnp.bfloat16)
    result = pl.pallas_call(
        functools.partial(pair_back_kernel, tile, far_tile, units, count, events),
        grid=(2 * pairs + fars,),
        in_specs=[block] * 5 + [pl.BlockSpec((rows, 128), lambda i: (0, 0))] + [anywhere] * (4 + count),
        out_specs=[joined] * 3 + [pl.BlockSpec(memory_space=pltpu.VMEM)] * count,
        out_shape=[out] * 3 + blocks,
        scratch_shapes=[
            pltpu.VMEM((3, pairs, rows, 128), jnp.float32), pltpu.VMEM((rows, 128), jnp.float32),
            pltpu.VMEM((pairs, 8, rows), jnp.float32), pltpu.VMEM((fars, 8, rows), jnp.float32),
            pltpu.VMEM((8, rows), jnp.float32), *[half] * 10,
            pltpu.SemaphoreType.DMA((5, fars)), pltpu.SemaphoreType.DMA((5, fars)),
            pltpu.SemaphoreType.DMA((3,)), pltpu.SemaphoreType.DMA((fars,)), *scratch,
        ],
        compiler_params=pltpu.CompilerParams(
            collective_id=collective_id, has_side_effects=True, vmem_limit_bytes=62 << 20),
        cost_estimate=pl.CostEstimate(
            flops=10 * rows * rows * width, bytes_accessed=16 * rows * width, transcendentals=rows * rows * pairs * 2),
    )(q, k, v, do, mix, logs, do, *far, *grads)
    return result[:3], result[3:]


def fast(
    frames_in, text_states, self_query, self_key, self_value, self_output, cross_query, cross_key, cross_value, cross_output,
    up_weight, down_weight, first_gain, first_bias, second_gain, second_bias, third_gain, third_bias, cotangent,
):
    row = lax.axis_index("row")
    rows, width = frames_in.shape
    half = width // 2
    piece = first_gain.shape[0]
    block_rows, block_cols = self_query.shape
    back = row % 2
    pairs = lax.axis_size("row") // 2
    forth_perm = [(2 * i, 2 * i + 1) for i in range(pairs)]
    back_perm = [(2 * i + 1, 2 * i) for i in range(pairs)]
    swap = forth_perm + back_perm

    def forth(array):
        return lax.ppermute(array, "row", forth_perm)

    def home(array):
        return lax.ppermute(array, "row", back_perm)

    def by_side(first, second):
        return jnp.where(back == 0, first, second)

    gains = jnp.zeros((1, 16, 128), jnp.bfloat16)
    gains = gains.at[0, :6, :piece].set(
        jnp.stack([first_gain, first_bias, second_gain, second_bias, third_gain, third_bias])
    )

    everyone = ("row", "col")
    places = (lax.axis_size("row"), lax.axis_size("col"))
    up_blocks = lax.all_gather(up_weight, everyone).reshape(*places, *up_weight.shape)
    down_blocks = lax.all_gather(down_weight, everyone).reshape(*places, *down_weight.shape)

    def small(block):
        return block.reshape(1, block_rows, block_cols)

    def flat(array):
        return array.reshape(-1, array.shape[-1])

    early = gather_blocks(
        [small(self_query), small(self_key), small(self_value), gains], 1, 128)
    query_self, key_self, value_self = [flat(w) for w in early[:3]]
    norm_params = early[3].reshape(pairs * 2, 16, -1, 128)[:, :6, :, :piece].transpose(1, 0, 2, 3)
    norm_params = norm_params.reshape(6, width).astype(jnp.float32)

    frames = frames_in.astype(jnp.float32)
    hidden_one = norm_forward(frames, norm_params[0], norm_params[1]).astype(jnp.bfloat16)
    self_k = matmul(hidden_one, key_self).astype(jnp.bfloat16)
    self_v = matmul(hidden_one, value_self).astype(jnp.bfloat16)
    self_q = matmul(hidden_one, query_self).astype(jnp.bfloat16)
    (self_mix, log_lanes, far_q, far_k, far_v), late = pair_attend(
        self_q, self_k, self_v, [small(w) for w in (self_output, cross_query, cross_key, cross_value, cross_output)],
        5, [3] * 12)
    out_self, query_cross, key_cross, value_cross, out_cross = [flat(w) for w in late]
    resid_one = frames + matmul(self_mix, out_self)
    hidden_two = norm_forward(resid_one, norm_params[2], norm_params[3]).astype(jnp.bfloat16)
    cross_q = matmul(hidden_two, query_cross).astype(jnp.bfloat16)
    other_text = lax.ppermute(text_states, "row", swap)
    clip_text = by_side(
        jnp.concatenate([text_states, other_text]), jnp.concatenate([other_text, text_states])
    )
    text_k = matmul(clip_text, key_cross).astype(jnp.bfloat16)
    text_v = matmul(clip_text, value_cross).astype(jnp.bfloat16)
    cross_mix, cross_logs = cross(cross_q, text_k, text_v)
    resid_two = resid_one + matmul(cross_mix, out_cross)
    hidden_three = norm_forward(resid_two, norm_params[4], norm_params[5]).astype(jnp.bfloat16)
    layer_out, grad_three, up_grad, down_grad = feed(hidden_three, cotangent, resid_two, up_blocks, down_blocks)
    up_sum = lax.psum_scatter(up_grad.reshape(-1, *up_weight.shape), everyone, scatter_dimension=0).astype(jnp.float32)

    cotan_full = cotangent.astype(jnp.float32)
    unused_three, pull_three = jax.vjp(norm_forward, resid_two, norm_params[4], norm_params[5])
    through_three, third_gain_part, third_bias_part = pull_three(grad_three)
    grad_resid_two = cotan_full + through_three
    grad_cross = grad_resid_two.astype(jnp.bfloat16)
    cross_out_grad = over_tokens(cross_mix, grad_cross)
    grad_cross_mix = by_transposed(grad_cross, out_cross).astype(jnp.bfloat16)
    grad_cross_q, text_k_part, text_v_part = cross_back(cross_q, text_k, text_v, grad_cross_mix, cross_mix, cross_logs)
    text_rows = text_states.shape[0]
    text_parts = jnp.concatenate([text_k_part, text_v_part], axis=1)
    given = lax.ppermute(by_side(text_parts[text_rows:], text_parts[:text_rows]), "row", swap)
    kept = by_side(text_parts[:text_rows], text_parts[text_rows:])
    text_parts = (kept.astype(jnp.float32) + given.astype(jnp.float32)).astype(jnp.bfloat16)
    grad_text_k, grad_text_v = text_parts[:, :width], text_parts[:, width:]
    cross_query_part = over_tokens(hidden_two, grad_cross_q)
    cross_key_part = over_tokens(text_states, grad_text_k)
    cross_value_part = over_tokens(text_states, grad_text_v)
    text_grad = by_transposed(grad_text_k, key_cross) + by_transposed(grad_text_v, value_cross)
    grad_two = by_transposed(grad_cross_q, query_cross)
    unused_two, pull_two = jax.vjp(norm_forward, resid_one, norm_params[2], norm_params[3])
    through_two, second_gain_part, second_bias_part = pull_two(grad_two)
    grad_resid_one = grad_resid_two + through_two
    grad_self = grad_resid_one.astype(jnp.bfloat16)
    self_out_grad = over_tokens(self_mix, grad_self)
    grad_self_mix = by_transposed(grad_self, out_self).astype(jnp.bfloat16)

    def by_place(grad, parts):
        return grad.astype(jnp.bfloat16).reshape(pairs, 2, parts, -1, grad.shape[-1])

    (grad_self_q, grad_self_k, grad_self_v), early_sums = pair_back(
        self_q, self_k, self_v, grad_self_mix, self_mix, log_lanes, (far_q, far_k, far_v),
        [by_place(g, 1) for g in (self_out_grad, cross_query_part, cross_key_part, cross_value_part, cross_out_grad)]
        + [by_place(down_grad, down_weight.shape[0] // block_rows)], 4, [6] * 11)
    self_query_part = over_tokens(hidden_one, grad_self_q)
    self_key_part = over_tokens(hidden_one, grad_self_k)
    self_value_part = over_tokens(hidden_one, grad_self_v)
    grad_one = (
        by_transposed(grad_self_q, query_self)
        + by_transposed(grad_self_k, key_self)
        + by_transposed(grad_self_v, value_self)
    )
    unused_one, pull_one = jax.vjp(norm_forward, frames, norm_params[0], norm_params[1])
    through_one, first_gain_part, first_bias_part = pull_one(grad_one)
    input_grad = grad_resid_one + through_one
    norm_grads = jnp.stack(
        [first_gain_part, first_bias_part, second_gain_part, second_bias_part, third_gain_part, third_bias_part]
    )
    norm_grads = norm_grads.reshape(6, 2 * pairs, -1, piece).transpose(1, 0, 2, 3)
    norm_grads = jnp.pad(norm_grads, ((0, 0), (0, 10), (0, 0), (0, 128 - piece)))

    late_sums = scatter_blocks(
        [by_place(g, 1) for g in (self_query_part, self_key_part, self_value_part)]
        + [by_place(norm_grads.reshape(2 * pairs * 16, -1), 1)], 3, 128)
    norm_parts = late_sums[3][0, :6, :piece]
    sums = [*late_sums[:3], *early_sums]
    sums = [total.reshape(-1, total.shape[-1]) for total in sums]
    return (layer_out, input_grad, text_grad, *sums[:-1], up_sum, sums[-1], *norm_parts)


def local(*arrays):
    frames_in, self_query = arrays[0], arrays[2]
    halves = 2 * frames_in.shape[0] == FRAMES and lax.axis_size("row") % 2 == 0
    if halves and lax.axis_size("col") % 2 == 0 and self_query.shape[1] % 256 == 0 and self_query.shape[0] % 128 == 0:
        return fast(*arrays)
    return general(*arrays)


def solution(mesh):
    placed = (
        P(("col", "row"), None),
        P(("col", "row"), None),
        P("row", "col"),
        P("row", "col"),
        P("row", "col"),
        P("row", "col"),
        P("row", "col"),
        P("row", "col"),
        P("row", "col"),
        P("row", "col"),
        P("row", "col"),
        P("row", "col"),
        P(("row", "col")),
        P(("row", "col")),
        P(("row", "col")),
        P(("row", "col")),
        P(("row", "col")),
        P(("row", "col")),
        P(("col", "row"), None),
    )
    return jax.shard_map(
        local,
        mesh=mesh,
        in_specs=placed,
        out_specs=(
            P(("col", "row"), None),
            P(("col", "row"), None),
            P(("col", "row"), None),
            P("row", "col"),
            P("row", "col"),
            P("row", "col"),
            P("row", "col"),
            P("row", "col"),
            P("row", "col"),
            P("row", "col"),
            P("row", "col"),
            P("row", "col"),
            P("row", "col"),
            P(("row", "col")),
            P(("row", "col")),
            P(("row", "col")),
            P(("row", "col")),
            P(("row", "col")),
            P(("row", "col")),
        ),
        check_vma=False,
    )
```
